32 devices in a mesh: groups: 2 (over y), blk: 4 (over z), tp: 4 (over x, core).
Axes of the slice: x: 2, y: 2, z: 4, core: 2. Of those that a mesh axis runs over, the one named last changes fastest.
Arguments:
- tokens: bfloat16 [3072, 4096], P(('groups', 'blk'), 'tp'), parts along dimension 0, may hold values from -6 to 6
- gate_weight: bfloat16 [4, 4096, 1024], P('blk', None, 'tp'), may hold values from -0.09375 to 0.09375
- up_weight: bfloat16 [4, 4096, 1024], P('blk', None, 'tp'), may hold values from -0.09375 to 0.09375
- down_weight: bfloat16 [4, 1024, 4096], P('blk', 'tp'), may hold values from -0.1875 to 0.1875
- route_gates: float32 [3072, 4], P(('groups', 'blk')), parts along dimension 0, may hold values from 0.1 to 1
- block_list: int32 [8, 4, 3], P(('groups', 'blk')), parts along dimension 0, may hold values from 0 to 2, as said below
- block_count: int32 [8, 4], P(('groups', 'blk')), parts along dimension 0, may hold values from 0 to 3, as said below
- owner_token: int32 [3072], P(('groups', 'blk')), parts along dimension 0, may hold values from 0 to 767, as said below
Outputs:
- combined: bfloat16 [1536, 4096], P(('groups', 'blk'), 'tp'), parts along dimension 0
The draws below stay inside these ranges and needn't reach their ends.
There are 2 independent parts, one for each index of `groups`. The reference program is written for one: setup_inputs(seed, part) draws one part's arguments, and reference() takes and returns one part's arrays. A program takes and returns all parts, laid end to end along the dimension named above; an argument that names none is the same for every part. Nothing has to cross between parts.
Inputs may be any that keep to these rules, and one draw needn't show every extreme that they name: `block_list`: in each row of a device and offset the entries are the 3 block numbers, each once, the chosen ones first. `block_count`: every device has an offset at which all 3 of its blocks are chosen. `owner_token`: token t is owned by device t // 192; the rows of one device name tokens of one owner device at most 192 times, and each device's rows reach 192 for some owner.
All inputs are finite; a program needn't handle non-finite values.
Results may differ from the reference program's by a relative error of at most 0.011.
Values may be sent and summed in bfloat16 or wider, within the bound.
No kernel may reach another device: no remote copies, remote signals or barrier semaphores. Data moves between devices by JAX's collectives and lax.ppermute only.
A program may use at most 128 MiB of HBM per device.

```python
import math
import jax
import jax.numpy as jnp
from jax import lax

D = 4096
FF = 1024
STEPS = 4
BROWS = 128
NBLK = 3
TOK_DEV = 384
TOKENS = 1536
OWN = 192
OUT_TOKENS = 768
CAP = 192
EXPERTS = 4
N_BLK = 4
N_TP = 4


def block_tables(key):
    key = jax.random.fold_in(key, 11)
    key_bits, key_full = jax.random.split(key)
    picked = jax.random.randint(key_bits, (N_BLK, STEPS, NBLK), 0, 2)
    full_offset = jax.random.randint(key_full, (N_BLK,), 0, STEPS)
    offsets = jnp.arange(STEPS, dtype=jnp.int32)[None, :, None]
    picked = jnp.where(offsets == full_offset[:, None, None], 1, picked)
    scores = (1 - picked) * NBLK + jnp.arange(NBLK, dtype=jnp.int32)[None, None, :]
    ordered = jnp.argsort(scores, axis=-1)
    return (ordered.astype(jnp.int32), jnp.sum(picked, axis=-1).astype(jnp.int32))


def draw_block_list(key, part):
    return block_tables(key)[0]


def draw_block_count(key, part):
    return block_tables(key)[1]


def owner_rows(key):
    key_full, key_slots, key_order, key_local = jax.random.split(key, 4)
    busiest = jax.random.randint(key_full, (), 0, N_BLK)
    slots = jax.random.permutation(key_slots, (N_BLK - 1) * CAP)[:TOK_DEV - CAP]
    others = slots // CAP
    others = others + (others >= busiest).astype(jnp.int32)
    target = jnp.concatenate([jnp.full((CAP,), busiest, jnp.int32), others.astype(jnp.int32)])
    target = target[jax.random.permutation(key_order, TOK_DEV)]
    local = jax.random.randint(key_local, (TOK_DEV,), 0, OWN)
    return (target * OWN + local).astype(jnp.int32)


def draw_owner_token(key, part):
    key = jax.random.fold_in(key, 5)
    device_keys = jax.random.split(key, N_BLK)
    return jax.vmap(owner_rows)(device_keys).reshape(TOKENS)


def shard_levels(stream_key, extent, pieces, smallest, top_value):
    factor_of = 1.0
    for position, parts in pieces:
        draws = jax.random.uniform(jax.random.fold_in(jax.random.fold_in(stream_key, 6), position), (parts,), jnp.float32, smallest / len(pieces), top_value / len(pieces))
        factor_of = factor_of * jnp.repeat(jnp.exp(draws), extent[position] // parts).reshape((-1,) + (1,) * (len(extent) - 1 - position))
    return factor_of


def scatter_about(own_key, extent, width, limit, cuts=(), held_as=jnp.bfloat16):
    drawn = jax.random.normal(own_key, extent, jnp.float32) * width
    if len(cuts) > 0:
        drawn = shard_levels(own_key, extent, cuts, -0.22, 0.18) * drawn
    return jnp.clip(drawn, min=-limit, max=limit).astype(held_as)


def setup_inputs(seed: int = 0, part: int = 0) -> dict:
    splits = jax.random.split(jax.random.key(seed), 9)
    part_splits = jax.random.split(jax.random.fold_in(splits[8], part), 9)
    return {
        "tokens": scatter_about(part_splits[0], (TOKENS, D), 1.0, 6.0, ((0, 4), (1, 4))),
        "gate_weight": scatter_about(splits[1], (EXPERTS, D, FF), D ** -0.5, 0.09375, ((0, 4), (2, 4))),
        "up_weight": scatter_about(splits[2], (EXPERTS, D, FF), D ** -0.5, 0.09375, ((0, 4), (2, 4))),
        "down_weight": scatter_about(splits[3], (EXPERTS, FF, D), FF ** -0.5, 0.1875, ((0, 4), (1, 4))),
        "route_gates": jnp.clip(jnp.exp(math.log(1.0) - 2.3025851 * jax.random.uniform(part_splits[4], (TOKENS, STEPS), jnp.float32) ** shard_levels(part_splits[4], (TOKENS, STEPS), ((0, 4),), -0.2, 0.2)), 0.1, 1.0),
        "block_list": draw_block_list(jax.random.fold_in(jax.random.fold_in(splits[8], part), 71), part),
        "block_count": draw_block_count(jax.random.fold_in(jax.random.fold_in(splits[8], part), 71), part),
        "owner_token": draw_owner_token(jax.random.fold_in(jax.random.fold_in(splits[8], part), 71), part),
    }


def reference(tokens, gate_weight, up_weight, down_weight, route_gates, block_list, block_count, owner_token):
    def device_rows(device):
        device = device.astype(jnp.int32)
        start = device * TOK_DEV
        block_rows = lax.dynamic_slice_in_dim(tokens, start, TOK_DEV, 0)
        gates_here = lax.dynamic_slice_in_dim(route_gates, start, TOK_DEV, 0)
        lists_here = lax.dynamic_index_in_dim(block_list, device, 0, keepdims=False)
        counts_here = lax.dynamic_index_in_dim(block_count, device, 0, keepdims=False)
        positions = jnp.arange(NBLK, dtype=jnp.int32)
        valid = (positions[None, :] < counts_here[:, None]).astype(jnp.float32)
        matches = (lists_here[:, :, None] == positions[None, None, :]).astype(jnp.float32)
        chosen = jnp.sum(valid[:, :, None] * matches, axis=1)
        row_chosen = jnp.repeat(chosen, BROWS, axis=1)
        partial_value = jnp.zeros((N_TP, TOK_DEV, D), jnp.float32)
        for offset in range(STEPS):
            expert = jnp.mod(device - offset, N_BLK).astype(jnp.int32)
            w_gate = lax.dynamic_index_in_dim(gate_weight, expert, 0, keepdims=False)
            w_up = lax.dynamic_index_in_dim(up_weight, expert, 0, keepdims=False)
            w_down = lax.dynamic_index_in_dim(down_weight, expert, 0, keepdims=False)
            gate_out = jnp.dot(block_rows, w_gate, preferred_element_type=jnp.float32)
            up_out = jnp.dot(block_rows, w_up, preferred_element_type=jnp.float32)
            hidden = (jax.nn.silu(gate_out) * up_out).astype(jnp.bfloat16)
            coef = gates_here[:, offset] * row_chosen[offset]
            split_hidden = hidden.astype(jnp.float32).reshape(TOK_DEV, N_TP, FF // N_TP)
            split_down = w_down.astype(jnp.float32).reshape(N_TP, FF // N_TP, D)
            terms = jnp.einsum("tkf,kfd->ktd", split_hidden, split_down)
            partial_value = partial_value + coef[None, :, None] * terms
        rounded = lax.optimization_barrier(partial_value.astype(jnp.bfloat16))
        return jnp.sum(rounded.astype(jnp.float32), axis=0).astype(jnp.bfloat16)

    rows_out = lax.map(device_rows, jnp.arange(N_BLK, dtype=jnp.int32))
    rows_out = rows_out.reshape(TOKENS, D)
    summed = jax.ops.segment_sum(rows_out.astype(jnp.float32), owner_token, num_segments=OUT_TOKENS)
    return summed.astype(jnp.bfloat16)
```

```python
import jax
import jax.numpy as jnp
from jax import lax
from jax.sharding import PartitionSpec as P


def shifted(block, axis, distance):
    devices = range(lax.axis_size(axis))
    route = [((i - distance) % len(devices), i) for i in devices]
    return lax.ppermute(block, axis, route)


def weights_travel(
    tokens, gate_weight, up_weight, down_weight, route_gates, block_list, block_count, owner_token
):
    whole_rows = lax.all_gather(tokens, "tp", axis=1, tiled=True)
    row_count = whole_rows.shape[0]
    width = whole_rows.shape[1]
    offsets_all = block_list.shape[1]
    block_total = block_list.shape[2]
    block_size = row_count // block_total
    blocks = whole_rows.reshape(block_total, block_size, width)
    gate_blocks = route_gates.reshape(block_total, block_size, offsets_all)
    totals = jnp.zeros((block_total, block_size, width), jnp.float32)

    def apply(totals, weights, offset, block_id):
        w_gate, w_up, w_down = weights
        block_rows = lax.dynamic_index_in_dim(blocks, block_id, 0, keepdims=False)
        gate_out = jnp.dot(block_rows, w_gate, preferred_element_type=jnp.float32)
        up_out = jnp.dot(block_rows, w_up, preferred_element_type=jnp.float32)
        hidden = (jax.nn.silu(gate_out) * up_out).astype(jnp.bfloat16)
        block_gates = lax.dynamic_index_in_dim(gate_blocks, block_id, 0, keepdims=False)
        factor = lax.dynamic_index_in_dim(block_gates, offset, 1, keepdims=False)
        product = jnp.dot(hidden, w_down, preferred_element_type=jnp.float32) * factor[:, None]
        before = lax.dynamic_index_in_dim(totals, block_id, 0, keepdims=False)
        return lax.dynamic_update_index_in_dim(totals, before + product, block_id, 0)

    resident = (gate_weight[0], up_weight[0], down_weight[0])
    arrived = [resident]
    holding = resident
    for offset in range(1, offsets_all):
        holding = shifted((holding[0], holding[1], holding[2]), "blk", 1)
        arrived.append(holding)
    for offset in range(offsets_all):
        weights = arrived[offset]

        def visit_block(position, totals, weights=weights, offset=offset):
            return apply(totals, weights, offset, block_list[0, offset, position])

        totals = lax.fori_loop(0, block_count[0, offset], visit_block, totals)
    summed = lax.psum_scatter(
        totals.reshape(row_count, width).astype(jnp.bfloat16), "tp", scatter_dimension=1, tiled=True
    )
    feature_share = summed.shape[1]
    cycle_size = lax.axis_size("blk")
    owned = row_count // 2
    capacity = max(2, 2 * row_count // cycle_size)
    target = owner_token // owned
    local_token = owner_token % owned
    target_table = (target[:, None] == jnp.arange(cycle_size, dtype=jnp.int32)[None, :]).astype(
        jnp.int32
    )
    running = jnp.cumsum(target_table, axis=0)
    rank = jnp.sum((running - 1) * target_table, axis=1)
    slot = target * capacity + rank
    send_rows = jnp.zeros((cycle_size * capacity, feature_share), jnp.bfloat16).at[slot].set(summed)
    send_index = jnp.full((cycle_size * capacity,), -1, jnp.int32).at[slot].set(local_token)
    send_rows = send_rows.reshape(cycle_size, capacity, feature_share)
    send_index = send_index.reshape(cycle_size, capacity)
    got_rows, got_index = (
        lax.all_to_all(send_rows, "blk", split_axis=0, concat_axis=0, tiled=True),
        lax.all_to_all(send_index, "blk", split_axis=0, concat_axis=0, tiled=True),
    )
    got_rows = got_rows.reshape(cycle_size * capacity, feature_share)
    got_index = got_index.reshape(cycle_size * capacity)
    placing = (got_index[:, None] == jnp.arange(owned, dtype=jnp.int32)[None, :]).astype(
        jnp.bfloat16
    )
    combined = lax.dot_general(
        placing, got_rows, (((0,), (0,)), ((), ())), preferred_element_type=jnp.float32
    )
    return combined.astype(jnp.bfloat16)


BESIDE = [(0, 1), (1, 0), (2, 3), (3, 2)]
MIDDLE = [(1, 2), (2, 1)]
INWARD = [(0, 1), (3, 2)]
OUTWARD = [(1, 0), (2, 3)]
SLOT_POSITION = [[0, 1, 2, 3], [1, 0, 3, 2], [2, 2, 1, 1], [3, 3, 0, 0]]
CHUNK_OWNER = [[3, 3, 0, 0], [2, 2, 1, 1], [1, 0, 3, 2], [0, 1, 2, 3]]


def across_chips(block):
    return lax.ppermute(block, "tp", [(i, i ^ 2) for i in range(4)])


def across_cores(block):
    return lax.ppermute(block, "tp", [(i, i ^ 1) for i in range(4)])


def rows_travel(
    tokens, gate_weight, up_weight, down_weight, route_gates, block_list, block_count, owner_token
):
    position = lax.axis_index("blk")
    share = lax.axis_index("tp")
    row_count, width = tokens.shape
    units = gate_weight.shape[2]
    offsets_all = block_list.shape[1]
    block_total = block_list.shape[2]
    owned = row_count // 2
    inner = (position == 1) | (position == 2)

    beside = lax.ppermute(tokens, "blk", BESIDE)
    middle = lax.ppermute(tokens, "blk", MIDDLE)
    inner_far = lax.ppermute(beside, "blk", MIDDLE)
    outer_next = lax.ppermute(middle, "blk", OUTWARD)
    outer_far = lax.ppermute(inner_far, "blk", OUTWARD)
    slots = [
        tokens,
        beside,
        jnp.where(inner, middle, outer_next),
        jnp.where(inner, inner_far, outer_far),
    ]

    order = jnp.arange(block_total, dtype=jnp.int32)
    valid = order[None, :, None] < block_count[0][:, None, None]
    chosen = jnp.any(valid & (block_list[0][:, :, None] == order[None, None, :]), axis=1)
    row_chosen = jnp.repeat(chosen.astype(jnp.float32), row_count // block_total, axis=1)
    coef = route_gates.T * row_chosen
    facts = jnp.concatenate(
        [coef, jnp.broadcast_to(owner_token.astype(jnp.float32)[None], (4, row_count))], axis=0
    )
    facts = lax.all_gather(facts, "blk")

    def by_arrival(weight):
        quarters = weight.reshape(4, width, units)
        return jnp.concatenate(
            [lax.dynamic_index_in_dim(quarters, share ^ j, 0, keepdims=False) for j in range(4)]
        )

    w_gate = by_arrival(gate_weight[0])
    w_up = by_arrival(up_weight[0])

    pieces = [
        lax.dynamic_slice_in_dim(down_weight[0], (share ^ j) * width, width, 1) for j in range(4)
    ]
    sibling = across_cores(jnp.concatenate([pieces[1], pieces[3]], axis=1))
    w_down = jnp.concatenate([jnp.concatenate([pieces[0], pieces[2]], axis=1), sibling], axis=0)

    token_of = (
        jnp.asarray(CHUNK_OWNER, jnp.int32)[:, position][:, None] * owned
        + jnp.arange(owned, dtype=jnp.int32)[None, :]
    ).reshape(4 * owned)

    collected = jnp.zeros((4 * owned, units), jnp.float32)
    for index, near in enumerate(slots):
        far = across_chips(near)
        rows = jnp.concatenate([near, across_cores(near), far, across_cores(far)], axis=1)
        gate_out = jnp.dot(rows, w_gate, preferred_element_type=jnp.float32)
        up_out = jnp.dot(rows, w_up, preferred_element_type=jnp.float32)
        hidden = (jax.nn.silu(gate_out) * up_out).astype(jnp.bfloat16)
        source = jnp.asarray(SLOT_POSITION[index], jnp.int32)[position]
        offset = (source - position) % offsets_all
        facts_here = lax.dynamic_index_in_dim(facts, source, 0, keepdims=False)
        factor = lax.dynamic_index_in_dim(facts_here, offset, 0, keepdims=False)
        owner = facts_here[offsets_all].astype(jnp.int32)
        placing = jnp.where(owner[None, :] == token_of[:, None], factor[None, :], 0.0)
        collected = collected + jnp.dot(
            placing.astype(jnp.bfloat16), hidden, preferred_element_type=jnp.float32
        )
    own_half = collected.astype(jnp.bfloat16)
    both = jnp.concatenate([own_half, across_cores(own_half)], axis=1)

    chunks = []
    for index in range(4):
        part = jnp.dot(
            both[index * owned : (index + 1) * owned], w_down, preferred_element_type=jnp.float32
        )
        got = across_chips(part[:, width:].astype(jnp.bfloat16))
        chunks.append(part[:, :width] + got.astype(jnp.float32))

    def send(block, route):
        return lax.ppermute(block.astype(jnp.bfloat16), "blk", route).astype(jnp.float32)

    first_in = send(chunks[0], INWARD)
    second_in = send(chunks[1], INWARD)
    second_mid = send(chunks[0] + first_in, MIDDLE)
    third_in = send(chunks[2], INWARD)
    third_mid = send(chunks[1] + second_in, MIDDLE)
    third_out = send(chunks[2] + second_mid, OUTWARD)
    return (chunks[3] + third_in + third_mid + third_out).astype(jnp.bfloat16)


def on_device(*args):
    block_list = args[5]
    sizes = (lax.axis_size("blk"), lax.axis_size("tp"), block_list.shape[1])
    if sizes == (4, 4, 4):
        return rows_travel(*args)
    return weights_travel(*args)


def solution(mesh):
    return jax.shard_map(
        on_device,
        mesh=mesh,
        in_specs=(
            P(("groups", "blk"), "tp"),
            P("blk", None, "tp"),
            P("blk", None, "tp"),
            P("blk", "tp", None),
            P(("groups", "blk"), None),
            P(("groups", "blk"), None, None),
            P(("groups", "blk"), None),
            P(("groups", "blk")),
        ),
        out_specs=P(("groups", "blk"), "tp"),
        check_vma=False,
    )
```

```python
import jax
import jax.numpy as jnp
from jax import lax
from jax.experimental import pallas as pl
from jax.experimental.pallas import tpu as pltpu
from jax.sharding import PartitionSpec as P


def shifted(block, axis, distance):
    devices = range(lax.axis_size(axis))
    route = [((i - distance) % len(devices), i) for i in devices]
    return lax.ppermute(block, axis, route)


def weights_travel(
    tokens, gate_weight, up_weight, down_weight, route_gates, block_list, block_count, owner_token
):
    whole_rows = lax.all_gather(tokens, "tp", axis=1, tiled=True)
    row_count = whole_rows.shape[0]
    width = whole_rows.shape[1]
    offsets_all = block_list.shape[1]
    block_total = block_list.shape[2]
    block_size = row_count // block_total
    blocks = whole_rows.reshape(block_total, block_size, width)
    gate_blocks = route_gates.reshape(block_total, block_size, offsets_all)
    totals = jnp.zeros((block_total, block_size, width), jnp.float32)

    def apply(totals, weights, offset, block_id):
        w_gate, w_up, w_down = weights
        block_rows = lax.dynamic_index_in_dim(blocks, block_id, 0, keepdims=False)
        gate_out = jnp.dot(block_rows, w_gate, preferred_element_type=jnp.float32)
        up_out = jnp.dot(block_rows, w_up, preferred_element_type=jnp.float32)
        hidden = (jax.nn.silu(gate_out) * up_out).astype(jnp.bfloat16)
        block_gates = lax.dynamic_index_in_dim(gate_blocks, block_id, 0, keepdims=False)
        factor = lax.dynamic_index_in_dim(block_gates, offset, 1, keepdims=False)
        product = jnp.dot(hidden, w_down, preferred_element_type=jnp.float32) * factor[:, None]
        before = lax.dynamic_index_in_dim(totals, block_id, 0, keepdims=False)
        return lax.dynamic_update_index_in_dim(totals, before + product, block_id, 0)

    resident = (gate_weight[0], up_weight[0], down_weight[0])
    arrived = [resident]
    holding = resident
    for offset in range(1, offsets_all):
        holding = shifted((holding[0], holding[1], holding[2]), "blk", 1)
        arrived.append(holding)
    for offset in range(offsets_all):
        weights = arrived[offset]

        def visit_block(position, totals, weights=weights, offset=offset):
            return apply(totals, weights, offset, block_list[0, offset, position])

        totals = lax.fori_loop(0, block_count[0, offset], visit_block, totals)
    summed = lax.psum_scatter(
        totals.reshape(row_count, width).astype(jnp.bfloat16), "tp", scatter_dimension=1, tiled=True
    )
    feature_share = summed.shape[1]
    cycle_size = lax.axis_size("blk")
    owned = row_count // 2
    capacity = max(2, 2 * row_count // cycle_size)
    target = owner_token // owned
    local_token = owner_token % owned
    target_table = (target[:, None] == jnp.arange(cycle_size, dtype=jnp.int32)[None, :]).astype(
        jnp.int32
    )
    running = jnp.cumsum(target_table, axis=0)
    rank = jnp.sum((running - 1) * target_table, axis=1)
    slot = target * capacity + rank
    send_rows = jnp.zeros((cycle_size * capacity, feature_share), jnp.bfloat16).at[slot].set(summed)
    send_index = jnp.full((cycle_size * capacity,), -1, jnp.int32).at[slot].set(local_token)
    send_rows = send_rows.reshape(cycle_size, capacity, feature_share)
    send_index = send_index.reshape(cycle_size, capacity)
    got_rows, got_index = (
        lax.all_to_all(send_rows, "blk", split_axis=0, concat_axis=0, tiled=True),
        lax.all_to_all(send_index, "blk", split_axis=0, concat_axis=0, tiled=True),
    )
    got_rows = got_rows.reshape(cycle_size * capacity, feature_share)
    got_index = got_index.reshape(cycle_size * capacity)
    placing = (got_index[:, None] == jnp.arange(owned, dtype=jnp.int32)[None, :]).astype(
        jnp.bfloat16
    )
    combined = lax.dot_general(
        placing, got_rows, (((0,), (0,)), ((), ())), preferred_element_type=jnp.float32
    )
    return combined.astype(jnp.bfloat16)


BESIDE = [(0, 1), (1, 0), (2, 3), (3, 2)]
MIDDLE = [(1, 2), (2, 1)]
INWARD = [(0, 1), (3, 2)]
OUTWARD = [(1, 0), (2, 3)]
SLOT_POSITION = [[0, 1, 2, 3], [1, 0, 3, 2], [2, 2, 1, 1], [3, 3, 0, 0]]
CHUNK_OWNER = [[3, 3, 0, 0], [2, 2, 1, 1], [1, 0, 3, 2], [0, 1, 2, 3]]


def across_chips(block):
    return lax.ppermute(block, "tp", [(i, i ^ 2) for i in range(4)])


def across_cores(block):
    return lax.ppermute(block, "tp", [(i, i ^ 1) for i in range(4)])


def all_there(*arrays):
    anywhere = [pl.BlockSpec(memory_space=pl.ANY)] * len(arrays)
    return pl.pallas_call(
        lambda *refs: None,
        out_shape=[jax.ShapeDtypeStruct(a.shape, a.dtype) for a in arrays],
        in_specs=anywhere,
        out_specs=anywhere,
        input_output_aliases={i: i for i in range(len(arrays))},
    )(*arrays)


def collected_rows(owned, owners, sums, got, pair, before, chunk):
    width = sums.shape[1]
    quarter = width // 4
    other = got[...].astype(jnp.float32)
    swapped = [other[:, (k ^ 1) * quarter : ((k ^ 1) + 1) * quarter] for k in range(4)]
    gate = sums[:, : width // 2] + jnp.concatenate(swapped[:2], axis=1)
    up = sums[:, width // 2 :] + jnp.concatenate(swapped[2:], axis=1)
    hidden = (gate / (1.0 + jnp.exp(-gate)) * up).astype(jnp.bfloat16)
    factor, owner = pair[0:1, :], pair[1:2, :].astype(jnp.int32)
    results = []
    for index in range(chunk):
        token = owners[index] * owned + lax.broadcasted_iota(jnp.int32, (owned, 1), 0)
        placing = jnp.where(owner == token, factor, 0.0).astype(jnp.bfloat16)
        rows = jnp.dot(placing, hidden, preferred_element_type=jnp.float32)
        if before is not None:
            rows = rows + before[index * owned : (index + 1) * owned, :]
        results.append(rows)
    return results


def collect(owned, owners, sums, got, pair, before):
    chunks = owners.shape[0]
    vmem = pl.BlockSpec(memory_space=pltpu.VMEM)
    operands = [owners, sums, got, pair] + ([] if before is None else [before])

    def body(owners_ref, sums_ref, got_ref, pair_ref, *rest):
        before_ref = rest[0] if before is not None else None
        rows = collected_rows(
            owned, owners_ref, sums_ref, got_ref, pair_ref, before_ref, chunks
        )
        for index in range(chunks):
            rest[-1][index * owned : (index + 1) * owned, :] = rows[index]

    return pl.pallas_call(
        body,
        out_shape=jax.ShapeDtypeStruct((chunks * owned, sums.shape[1] // 2), jnp.float32),
        in_specs=[pl.BlockSpec(memory_space=pltpu.SMEM)] + [vmem] * (len(operands) - 1),
        out_specs=vmem,
        compiler_params=pltpu.CompilerParams(vmem_limit_bytes=40 * 2**20),
    )(*operands)


def finish(owned, owners, sums, got, pair, before, w_down):
    chunks = owners.shape[0]
    width = w_down.shape[1] // 2
    vmem = pl.BlockSpec(memory_space=pltpu.VMEM)

    def body(owners_ref, sums_ref, got_ref, pair_ref, before_ref, w_ref, *out_refs):
        rows = collected_rows(
            owned, owners_ref, sums_ref, got_ref, pair_ref, before_ref, chunks
        )
        for index in range(chunks):
            held = rows[index].astype(jnp.bfloat16)
            keep = jnp.dot(held, w_ref[:, :width], preferred_element_type=jnp.float32)
            sent = jnp.dot(held, w_ref[:, width:], preferred_element_type=jnp.float32)
            out_refs[index][...] = sent.astype(jnp.bfloat16)
            out_refs[chunks + index][...] = keep

    results = pl.pallas_call(
        body,
        out_shape=[jax.ShapeDtypeStruct((owned, width), jnp.bfloat16)] * chunks
        + [jax.ShapeDtypeStruct((owned, width), jnp.float32)] * chunks,
        in_specs=[pl.BlockSpec(memory_space=pltpu.SMEM)] + [vmem] * 5,
        out_specs=[vmem] * (2 * chunks),
        compiler_params=pltpu.CompilerParams(vmem_limit_bytes=40 * 2**20),
    )(owners, sums, got, pair, before, w_down)
    return results[:chunks], results[chunks:]


def rows_travel(
    tokens, gate_weight, up_weight, down_weight, route_gates, block_list, block_count, owner_token
):
    position = lax.axis_index("blk")
    share = lax.axis_index("tp")
    row_count, width = tokens.shape
    units = gate_weight.shape[2]
    offsets_all = block_list.shape[1]
    block_total = block_list.shape[2]
    owned = row_count // 2
    half = row_count // 2
    inner = (position == 1) | (position == 2)

    beside = lax.ppermute(tokens, "blk", BESIDE)
    middle = lax.ppermute(tokens, "blk", MIDDLE)
    own_far = across_chips(tokens)

    order = jnp.arange(block_total, dtype=jnp.int32)
    valid = order[None, :, None] < block_count[0][:, None, None]
    chosen = jnp.any(valid & (block_list[0][:, :, None] == order[None, None, :]), axis=1)
    row_chosen = jnp.repeat(chosen.astype(jnp.float32), row_count // block_total, axis=1)
    coef = route_gates.T * row_chosen
    owner_float = owner_token.astype(jnp.float32)
    facts = []
    for offset in range(offsets_all):
        pair = jnp.stack([coef[offset], owner_float])
        if offset > 0:
            pair = shifted(pair, "blk", offsets_all - offset)
        facts.append(pair)
    facts = jnp.stack(facts)

    gate_quarters = gate_weight[0].reshape(4, width, units)
    up_quarters = up_weight[0].reshape(4, width, units)

    def quarter(j):
        index = share ^ j
        return [
            lax.dynamic_index_in_dim(q, index, 0, keepdims=False)
            for q in (gate_quarters, up_quarters)
        ]

    lend = jnp.concatenate([jnp.concatenate(quarter(j), axis=1) for j in (1, 3)])

    pieces = [
        lax.dynamic_slice_in_dim(down_weight[0], (share ^ j) * width, width, 1) for j in range(4)
    ]
    lend_down = jnp.concatenate([pieces[1], pieces[3]], axis=1)

    owners = jnp.asarray(CHUNK_OWNER, jnp.int32)[:, position]

    def partial(rows, weight):
        return jnp.dot(rows, weight, preferred_element_type=jnp.float32)

    def slot_pair(index):
        source = jnp.asarray(SLOT_POSITION[index], jnp.int32)[position]
        offset = (source - position) % offsets_all
        return lax.dynamic_index_in_dim(facts, offset, 0, keepdims=False)

    def exchanged(sums):
        return across_cores(sums.astype(jnp.bfloat16))

    beside, middle, own_far, lend, lend_down = all_there(
        beside, middle, own_far, lend, lend_down
    )
    inner_last = lax.ppermute(beside, "blk", MIDDLE)
    outer_next = lax.ppermute(middle, "blk", OUTWARD)
    inward_far = lax.ppermute(own_far[half:], "blk", INWARD)
    beside_far = across_chips(beside)
    lent = across_cores(lend)
    w_in = []
    for index, j in enumerate((0, 2)):
        gate_own, up_own = quarter(j)
        other = lent[index * width : (index + 1) * width]
        w_in.append(
            jnp.concatenate([gate_own, other[:, :units], up_own, other[:, units:]], axis=1)
        )
    w_near, w_far = w_in
    sums_0 = partial(tokens, w_near) + partial(own_far, w_far)
    got_0 = exchanged(sums_0)

    inner_last, outer_next, inward_far, beside_far, sums_0, got_0 = all_there(
        inner_last, outer_next, inward_far, beside_far, sums_0, got_0
    )
    outer_last = lax.ppermute(inner_last, "blk", OUTWARD)
    middle_far = lax.ppermute(inward_far, "blk", MIDDLE)
    second = jnp.where(inner, middle, outer_next)
    second_far = across_chips(second)
    lent_down = across_cores(lend_down)
    w_down = jnp.concatenate([jnp.concatenate([pieces[0], pieces[2]], axis=1), lent_down], axis=0)
    total = collect(owned, owners, sums_0, got_0, slot_pair(0), None)
    sums_1 = partial(beside, w_near) + partial(beside_far, w_far)
    got_1 = exchanged(sums_1)

    outer_last, middle_far, second_far, total, sums_1, got_1, w_down = all_there(
        outer_last, middle_far, second_far, total, sums_1, got_1, w_down
    )
    outward_far = lax.ppermute(middle_far, "blk", OUTWARD)
    last = jnp.where(inner, inner_last, outer_last)
    last_far = across_chips(last[:half])
    total = collect(owned, owners, sums_1, got_1, slot_pair(1), total)
    sums_2 = partial(second, w_near) + partial(second_far, w_far)
    got_2 = exchanged(sums_2)
    total = collect(owned, owners, sums_2, got_2, slot_pair(2), total)
    last_sums = partial(last, w_near)

    last_far, outward_far, total, last_sums = all_there(last_far, outward_far, total, last_sums)
    last_far = jnp.concatenate([last_far, jnp.where(inner, middle_far, outward_far)])
    sums_3 = last_sums + partial(last_far, w_far)
    sent, kept = finish(owned, owners, sums_3, exchanged(sums_3), slot_pair(3), total, w_down)
    chunks = [k + across_chips(s).astype(jnp.float32) for s, k in zip(sent, kept)]

    def send(block, route):
        return lax.ppermute(block.astype(jnp.bfloat16), "blk", route).astype(jnp.float32)

    first_in = send(chunks[0], INWARD)
    second_in = send(chunks[1], INWARD)
    second_mid = send(chunks[0] + first_in, MIDDLE)
    third_in = send(chunks[2], INWARD)
    third_mid = send(chunks[1] + second_in, MIDDLE)
    third_out = send(chunks[2] + second_mid, OUTWARD)
    return (chunks[3] + third_in + third_mid + third_out).astype(jnp.bfloat16)


def on_device(*args):
    block_list = args[5]
    sizes = (lax.axis_size("blk"), lax.axis_size("tp"), block_list.shape[1])
    if sizes == (4, 4, 4):
        return rows_travel(*args)
    return weights_travel(*args)


def solution(mesh):
    return jax.shard_map(
        on_device,
        mesh=mesh,
        in_specs=(
            P(("groups", "blk"), "tp"),
            P("blk", None, "tp"),
            P("blk", None, "tp"),
            P("blk", "tp", None),
            P(("groups", "blk"), None),
            P(("groups", "blk"), None, None),
            P(("groups", "blk"), None),
            P(("groups", "blk")),
        ),
        out_specs=P(("groups", "blk"), "tp"),
        check_vma=False,
    )
```

```python
import jax
import jax.numpy as jnp
from jax import lax
from jax.experimental import pallas as pl
from jax.experimental.pallas import tpu as pltpu
from jax.sharding import PartitionSpec as P


def shifted(block, axis, distance):
    devices = range(lax.axis_size(axis))
    route = [((i - distance) % len(devices), i) for i in devices]
    return lax.ppermute(block, axis, route)


def weights_travel(
    tokens, gate_weight, up_weight, down_weight, route_gates, block_list, block_count, owner_token
):
    whole_rows = lax.all_gather(tokens, "tp", axis=1, tiled=True)
    row_count = whole_rows.shape[0]
    width = whole_rows.shape[1]
    offsets_all = block_list.shape[1]
    block_total = block_list.shape[2]
    block_size = row_count // block_total
    blocks = whole_rows.reshape(block_total, block_size, width)
    gate_blocks = route_gates.reshape(block_total, block_size, offsets_all)
    totals = jnp.zeros((block_total, block_size, width), jnp.float32)

    def apply(totals, weights, offset, block_id):
        w_gate, w_up, w_down = weights
        block_rows = lax.dynamic_index_in_dim(blocks, block_id, 0, keepdims=False)
        gate_out = jnp.dot(block_rows, w_gate, preferred_element_type=jnp.float32)
        up_out = jnp.dot(block_rows, w_up, preferred_element_type=jnp.float32)
        hidden = (jax.nn.silu(gate_out) * up_out).astype(jnp.bfloat16)
        block_gates = lax.dynamic_index_in_dim(gate_blocks, block_id, 0, keepdims=False)
        factor = lax.dynamic_index_in_dim(block_gates, offset, 1, keepdims=False)
        product = jnp.dot(hidden, w_down, preferred_element_type=jnp.float32) * factor[:, None]
        before = lax.dynamic_index_in_dim(totals, block_id, 0, keepdims=False)
        return lax.dynamic_update_index_in_dim(totals, before + product, block_id, 0)

    resident = (gate_weight[0], up_weight[0], down_weight[0])
    arrived = [resident]
    holding = resident
    for offset in range(1, offsets_all):
        holding = shifted((holding[0], holding[1], holding[2]), "blk", 1)
        arrived.append(holding)
    for offset in range(offsets_all):
        weights = arrived[offset]

        def visit_block(position, totals, weights=weights, offset=offset):
            return apply(totals, weights, offset, block_list[0, offset, position])

        totals = lax.fori_loop(0, block_count[0, offset], visit_block, totals)
    summed = lax.psum_scatter(
        totals.reshape(row_count, width).astype(jnp.bfloat16), "tp", scatter_dimension=1, tiled=True
    )
    feature_share = summed.shape[1]
    cycle_size = lax.axis_size("blk")
    owned = row_count // 2
    capacity = max(2, 2 * row_count // cycle_size)
    target = owner_token // owned
    local_token = owner_token % owned
    target_table = (target[:, None] == jnp.arange(cycle_size, dtype=jnp.int32)[None, :]).astype(
        jnp.int32
    )
    running = jnp.cumsum(target_table, axis=0)
    rank = jnp.sum((running - 1) * target_table, axis=1)
    slot = target * capacity + rank
    send_rows = jnp.zeros((cycle_size * capacity, feature_share), jnp.bfloat16).at[slot].set(summed)
    send_index = jnp.full((cycle_size * capacity,), -1, jnp.int32).at[slot].set(local_token)
    send_rows = send_rows.reshape(cycle_size, capacity, feature_share)
    send_index = send_index.reshape(cycle_size, capacity)
    got_rows, got_index = (
        lax.all_to_all(send_rows, "blk", split_axis=0, concat_axis=0, tiled=True),
        lax.all_to_all(send_index, "blk", split_axis=0, concat_axis=0, tiled=True),
    )
    got_rows = got_rows.reshape(cycle_size * capacity, feature_share)
    got_index = got_index.reshape(cycle_size * capacity)
    placing = (got_index[:, None] == jnp.arange(owned, dtype=jnp.int32)[None, :]).astype(
        jnp.bfloat16
    )
    combined = lax.dot_general(
        placing, got_rows, (((0,), (0,)), ((), ())), preferred_element_type=jnp.float32
    )
    return combined.astype(jnp.bfloat16)


BESIDE = [(0, 1), (1, 0), (2, 3), (3, 2)]
MIDDLE = [(1, 2), (2, 1)]
INWARD = [(0, 1), (3, 2)]
OUTWARD = [(1, 0), (2, 3)]
PLAN = [
    [3, 2, 1, 0, 0, 1, 2, 3],
    [3, 2, 0, 1, 0, 3, 1, 2],
    [0, 1, 3, 2, 0, 1, 3, 2],
    [0, 1, 2, 3, 0, 3, 2, 1],
]
FACT_ROWS = 16
VMEM = pl.BlockSpec(memory_space=pltpu.VMEM)
SMEM = pl.BlockSpec(memory_space=pltpu.SMEM)
ANYWHERE = pl.BlockSpec(memory_space=pl.ANY)


def across_chips(block):
    return lax.ppermute(block, "tp", [(i, i ^ 2) for i in range(4)])


def across_cores(block):
    return lax.ppermute(block, "tp", [(i, i ^ 1) for i in range(4)])


def along(block, route):
    return lax.ppermute(block, "blk", route)


def on_core(body, out_shape, in_specs, flops=1024):
    return pl.pallas_call(
        body,
        out_shape=out_shape,
        in_specs=in_specs,
        out_specs=jax.tree.map(lambda _: VMEM, out_shape),
        compiler_params=pltpu.CompilerParams(vmem_limit_bytes=40 * 2**20),
        cost_estimate=pl.CostEstimate(flops=flops, bytes_accessed=1024, transcendentals=0),
    )


def all_there(*arrays):
    return pl.pallas_call(
        lambda *refs: None,
        out_shape=[jax.ShapeDtypeStruct(a.shape, a.dtype) for a in arrays],
        in_specs=[ANYWHERE] * len(arrays),
        out_specs=[ANYWHERE] * len(arrays),
        input_output_aliases={i: i for i in range(len(arrays))},
    )(*arrays)


def two_halves(tokens, gates, block_list, block_count, owner):
    rows, width = tokens.shape
    half = rows // 2
    offsets, blocks = block_list.shape

    def body(tokens_ref, gates_ref, list_ref, count_ref, owner_ref, a_ref, b_ref):
        a_ref[...] = tokens_ref[:half, :]
        b_ref[:half, :] = tokens_ref[half:, :]
        block_of = lax.broadcasted_iota(jnp.int32, (1, rows), 1) // (rows // blocks)
        facts = []
        for offset in range(offsets):
            mask = jnp.zeros((1, rows), jnp.float32)
            for block in range(blocks):
                used = jnp.int32(0)
                for place in range(blocks):
                    found = (list_ref[offset, place] == block) & (place < count_ref[offset])
                    used = used | found.astype(jnp.int32)
                mask = mask + jnp.where(block_of == block, used.astype(jnp.float32), 0.0)
            facts.append(gates_ref[offset : offset + 1, :] * mask)
        facts.append((owner_ref[...] >> 8).astype(jnp.float32))
        facts.append((owner_ref[...] & 255).astype(jnp.float32))
        facts.append(jnp.zeros((FACT_ROWS - len(facts), rows), jnp.float32))
        b_ref[half:, :] = jnp.zeros((FACT_ROWS, width), jnp.bfloat16)
        b_ref[half:, :rows] = jnp.concatenate(facts, axis=0).astype(jnp.bfloat16)

    return on_core(
        body,
        [
            jax.ShapeDtypeStruct((half, width), tokens.dtype),
            jax.ShapeDtypeStruct((half + FACT_ROWS, width), tokens.dtype),
        ],
        [VMEM, VMEM, SMEM, SMEM, VMEM],
    )(tokens, gates, block_list, block_count, owner)


def partial_sums(rows, parts, weights, places, before=None, send=True, flops=1024):
    width = parts[0][0].shape[1]
    columns = weights[0].shape[1]
    operands = [block for part in parts for block in part] + list(weights)
    if before is not None:
        operands.append(before)

    def body(*refs):
        blocks, results = refs[: len(parts) * len(places)], refs[len(operands) :]
        weight_refs = refs[len(blocks) : len(blocks) + len(weights)]
        for part in range(len(parts)):
            span = slice(part * rows, (part + 1) * rows)
            for side in range(2):
                at = slice(side * columns, (side + 1) * columns)
                total = None if before is None else refs[len(operands) - 1][span, at]
                for index, place in enumerate(places):
                    product = jnp.dot(
                        blocks[part * len(places) + index][:rows, :],
                        weight_refs[side][place * width : (place + 1) * width, :],
                        preferred_element_type=jnp.float32,
                    )
                    total = product if total is None else total + product
                results[0][span, at] = total
                if send:
                    results[1][span, at] = total.astype(jnp.bfloat16)

    size = (len(parts) * rows, 2 * columns)
    shapes = [jax.ShapeDtypeStruct(size, jnp.float32)]
    if send:
        shapes.append(jax.ShapeDtypeStruct(size, jnp.bfloat16))
    return on_core(body, shapes, [VMEM] * len(operands), flops)(*operands)


def collected_rows(owned, slot, plan, sums_parts, got_parts, facts, before):
    units = sums_parts[0].shape[1] // 4
    hidden = []
    for sums, got in zip(sums_parts, got_parts):
        part = []
        for core in range(2):
            here, there = 2 * core * units, 2 * (1 - core) * units
            gate = sums[:, here : here + units] + got[:, there : there + units].astype(jnp.float32)
            up = sums[:, here + units : here + 2 * units]
            up = up + got[:, there + units : there + 2 * units].astype(jnp.float32)
            part.append((gate / (1.0 + jnp.exp(-gate)) * up).astype(jnp.bfloat16))
        hidden.append(jnp.concatenate(part, axis=1))
    hidden = jnp.concatenate(hidden, axis=0)
    values = facts[...].astype(jnp.float32)
    kind = lax.broadcasted_iota(jnp.int32, (FACT_ROWS, 1), 0)
    factor = jnp.sum(jnp.where(kind == plan[4 + slot], values, 0.0), axis=0, keepdims=True)
    owner = (values[4:5, :] * 256.0 + values[5:6, :]).astype(jnp.int32)
    results = []
    for index in range(4):
        token = plan[index] * owned + lax.broadcasted_iota(jnp.int32, (owned, 1), 0)
        placing = jnp.where(owner == token, factor, 0.0).astype(jnp.bfloat16)
        rows = jnp.dot(placing, hidden, preferred_element_type=jnp.float32)
        if before is not None:
            rows = rows + before[index * owned : (index + 1) * owned, :]
        results.append(rows)
    return results


def collect(owned, slot, plan, sums, got, facts, before):
    operands = [plan, sums, got, facts] + ([] if before is None else [before])

    def body(plan_ref, sums_ref, got_ref, facts_ref, *rest):
        before_ref = rest[0] if before is not None else None
        rows = collected_rows(
            owned, slot, plan_ref, [sums_ref], [got_ref], facts_ref, before_ref
        )
        for index in range(4):
            rest[-1][index * owned : (index + 1) * owned, :] = rows[index]

    shape = jax.ShapeDtypeStruct((4 * owned, sums.shape[1] // 2), jnp.float32)
    return on_core(body, shape, [SMEM] + [VMEM] * (len(operands) - 1))(*operands)


def finish(owned, slot, plan, sums, got, facts, before, down_own, down_lent):
    units = down_own.shape[0]
    width = down_own.shape[1] // 2
    count = len(sums)

    def body(plan_ref, *refs):
        sums_refs, got_refs = refs[:count], refs[count : 2 * count]
        facts_ref, before_ref, own_ref, lent_ref, *out_refs = refs[2 * count :]
        rows = collected_rows(owned, slot, plan_ref, sums_refs, got_refs, facts_ref, before_ref)
        for index in range(4):
            held = rows[index].astype(jnp.bfloat16)
            for out, at in ((4 + index, slice(0, width)), (index, slice(width, 2 * width))):
                result = jnp.dot(
                    held[:, :units], own_ref[:, at], preferred_element_type=jnp.float32
                ) + jnp.dot(held[:, units:], lent_ref[:, at], preferred_element_type=jnp.float32)
                out_refs[out][...] = result.astype(out_refs[out].dtype)

    results = on_core(
        body,
        [jax.ShapeDtypeStruct((owned, width), jnp.bfloat16)] * 4
        + [jax.ShapeDtypeStruct((owned, width), jnp.float32)] * 4,
        [SMEM] + [VMEM] * (2 * count + 4),
    )(plan, *sums, *got, facts, before, down_own, down_lent)
    return results[:4], results[4:]


def rows_travel(
    tokens, gate_weight, up_weight, down_weight, route_gates, block_list, block_count, owner_token
):
    position = lax.axis_index("blk")
    share = lax.axis_index("tp")
    row_count, width = tokens.shape
    units = gate_weight.shape[2]
    owned = row_count // 2
    half = row_count // 2
    inner = (position == 1) | (position == 2)
    plan = jnp.asarray(PLAN, jnp.int32)[position]

    own_a, own_b = two_halves(
        tokens, route_gates.T, block_list[0], block_count[0], owner_token[None]
    )

    gate_quarters = gate_weight[0].reshape(4, width, units)
    up_quarters = up_weight[0].reshape(4, width, units)

    def quarter(j):
        pair = [
            lax.dynamic_index_in_dim(q, share ^ j, 0, keepdims=False)
            for q in (gate_quarters, up_quarters)
        ]
        return jnp.concatenate(pair, axis=1)

    def down_part(j):
        return lax.dynamic_slice_in_dim(down_weight[0], (share ^ j) * width, width, 1)

    kept_in = jnp.concatenate([quarter(0), quarter(2)])
    lend_in = jnp.concatenate([quarter(1), quarter(3)])
    kept_down = jnp.concatenate([down_part(0), down_part(2)], axis=1)
    lend_down = jnp.concatenate([down_part(1), down_part(3)], axis=1)

    def facts_of(second_half):
        return second_half[half:, :row_count]

    beside_a = along(own_a, BESIDE)
    middle_a = along(own_a, MIDDLE)
    own_far_a = across_chips(own_a)
    beside_b = along(own_b, BESIDE)
    middle_b = along(own_b, MIDDLE)
    own_far_b = across_chips(own_b)

    beside_a, middle_a, own_far_a, lend_in, lend_down, kept_in, kept_down = all_there(
        beside_a, middle_a, own_far_a, lend_in, lend_down, kept_in, kept_down
    )
    inner_last_a = along(beside_a, MIDDLE)
    outer_next_a = along(middle_a, OUTWARD)
    beside_far_a = across_chips(beside_a)
    lent_in = across_cores(lend_in)
    lent_down = across_cores(lend_down)

    beside_b, middle_b, own_far_b = all_there(beside_b, middle_b, own_far_b)
    inner_last_b = along(beside_b, MIDDLE)
    outer_next_b = along(middle_b, OUTWARD)
    beside_far_b = across_chips(beside_b)
    inward_far = along(own_far_b, INWARD)

    inner_last_a, outer_next_a, beside_far_a = all_there(inner_last_a, outer_next_a, beside_far_a)
    outer_last_a = along(inner_last_a, OUTWARD)
    second_a = jnp.where(inner, middle_a, outer_next_a)
    second_far_a = across_chips(second_a)

    inner_last_b, outer_next_b, beside_far_b, inward_far, lent_in, lent_down = all_there(
        inner_last_b, outer_next_b, beside_far_b, inward_far, lent_in, lent_down
    )
    outer_last_b = along(inner_last_b, OUTWARD)
    second_b = jnp.where(inner, middle_b, outer_next_b)
    second_far_b = across_chips(second_b)
    middle_far = along(inward_far, MIDDLE)
    weights = (kept_in, lent_in)
    sums_0, send_0 = partial_sums(half, [(own_a, own_far_a), (own_b, own_far_b)], weights, (0, 1))
    got_0 = across_cores(send_0)

    outer_last_a, second_far_a, sums_0, got_0 = all_there(
        outer_last_a, second_far_a, sums_0, got_0
    )
    last_a = jnp.where(inner, inner_last_a, outer_last_a)
    last_far_a = across_chips(last_a)
    total = collect(owned, 0, plan, sums_0, got_0, facts_of(own_b), None)
    sums_1, send_1 = partial_sums(
        half, [(beside_a, beside_far_a), (beside_b, beside_far_b)], weights, (0, 1)
    )
    got_1 = across_cores(send_1)

    outer_last_b, second_far_b, middle_far, total, sums_1, got_1 = all_there(
        outer_last_b, second_far_b, middle_far, total, sums_1, got_1
    )
    outward_far = along(middle_far, OUTWARD)
    last_b = jnp.where(inner, inner_last_b, outer_last_b)
    total = collect(owned, 1, plan, sums_1, got_1, facts_of(beside_b), total)
    sums_2, send_2 = partial_sums(
        half, [(second_a, second_far_a), (second_b, second_far_b)], weights, (0, 1)
    )
    got_2 = across_cores(send_2)
    near_a = partial_sums(half, [(last_a,)], weights, (0,), send=False)[0]
    near_b = partial_sums(half, [(last_b,)], weights, (0,), send=False)[0]
    total = collect(owned, 2, plan, sums_2, got_2, facts_of(second_b), total)

    last_far_a, near_a, near_b, total = all_there(last_far_a, near_a, near_b, total)
    sums_a, send_a = partial_sums(
        half, [(last_far_a,)], weights, (1,), before=near_a, flops=3 * 2**30
    )
    sums_a, got_a, outward_far = all_there(sums_a, across_cores(send_a), outward_far)
    last_far_b = jnp.where(inner, middle_far, outward_far)
    sums_b, send_b = partial_sums(half, [(last_far_b,)], weights, (1,), before=near_b)
    got_b = across_cores(send_b)
    sent, kept = finish(
        owned,
        3,
        plan,
        (sums_a, sums_b),
        (got_a, got_b),
        facts_of(last_b),
        total,
        kept_down,
        lent_down,
    )
    chunks = [k + across_chips(s).astype(jnp.float32) for s, k in zip(sent, kept)]

    def send(block, route):
        return along(block.astype(jnp.bfloat16), route).astype(jnp.float32)

    first_in = send(chunks[0], INWARD)
    second_in = send(chunks[1], INWARD)
    second_mid = send(chunks[0] + first_in, MIDDLE)
    third_in = send(chunks[2], INWARD)
    third_mid = send(chunks[1] + second_in, MIDDLE)
    third_out = send(chunks[2] + second_mid, OUTWARD)
    return (chunks[3] + third_in + third_mid + third_out).astype(jnp.bfloat16)


def on_device(*args):
    block_list = args[5]
    sizes = (lax.axis_size("blk"), lax.axis_size("tp"), block_list.shape[1])
    if sizes == (4, 4, 4):
        return rows_travel(*args)
    return weights_travel(*args)


def solution(mesh):
    return jax.shard_map(
        on_device,
        mesh=mesh,
        in_specs=(
            P(("groups", "blk"), "tp"),
            P("blk", None, "tp"),
            P("blk", None, "tp"),
            P("blk", "tp", None),
            P(("groups", "blk"), None),
            P(("groups", "blk"), None, None),
            P(("groups", "blk"), None),
            P(("groups", "blk")),
        ),
        out_specs=P(("groups", "blk"), "tp"),
        check_vma=False,
    )
```

```python
import jax
import jax.numpy as jnp
from jax import lax
from jax.experimental import pallas as pl
from jax.experimental.pallas import tpu as pltpu
from jax.sharding import PartitionSpec as P


def shifted(block, axis, distance):
    devices = range(lax.axis_size(axis))
    route = [((i - distance) % len(devices), i) for i in devices]
    return lax.ppermute(block, axis, route)


def weights_travel(
    tokens, gate_weight, up_weight, down_weight, route_gates, block_list, block_count, owner_token
):
    whole_rows = lax.all_gather(tokens, "tp", axis=1, tiled=True)
    row_count = whole_rows.shape[0]
    width = whole_rows.shape[1]
    offsets_all = block_list.shape[1]
    block_total = block_list.shape[2]
    block_size = row_count // block_total
    blocks = whole_rows.reshape(block_total, block_size, width)
    gate_blocks = route_gates.reshape(block_total, block_size, offsets_all)
    totals = jnp.zeros((block_total, block_size, width), jnp.float32)

    def apply(totals, weights, offset, block_id):
        w_gate, w_up, w_down = weights
        block_rows = lax.dynamic_index_in_dim(blocks, block_id, 0, keepdims=False)
        gate_out = jnp.dot(block_rows, w_gate, preferred_element_type=jnp.float32)
        up_out = jnp.dot(block_rows, w_up, preferred_element_type=jnp.float32)
        hidden = (jax.nn.silu(gate_out) * up_out).astype(jnp.bfloat16)
        block_gates = lax.dynamic_index_in_dim(gate_blocks, block_id, 0, keepdims=False)
        factor = lax.dynamic_index_in_dim(block_gates, offset, 1, keepdims=False)
        product = jnp.dot(hidden, w_down, preferred_element_type=jnp.float32) * factor[:, None]
        before = lax.dynamic_index_in_dim(totals, block_id, 0, keepdims=False)
        return lax.dynamic_update_index_in_dim(totals, before + product, block_id, 0)

    resident = (gate_weight[0], up_weight[0], down_weight[0])
    arrived = [resident]
    holding = resident
    for offset in range(1, offsets_all):
        holding = shifted((holding[0], holding[1], holding[2]), "blk", 1)
        arrived.append(holding)
    for offset in range(offsets_all):
        weights = arrived[offset]

        def visit_block(position, totals, weights=weights, offset=offset):
            return apply(totals, weights, offset, block_list[0, offset, position])

        totals = lax.fori_loop(0, block_count[0, offset], visit_block, totals)
    summed = lax.psum_scatter(
        totals.reshape(row_count, width).astype(jnp.bfloat16), "tp", scatter_dimension=1, tiled=True
    )
    feature_share = summed.shape[1]
    cycle_size = lax.axis_size("blk")
    owned = row_count // 2
    capacity = max(2, 2 * row_count // cycle_size)
    target = owner_token // owned
    local_token = owner_token % owned
    target_table = (target[:, None] == jnp.arange(cycle_size, dtype=jnp.int32)[None, :]).astype(
        jnp.int32
    )
    running = jnp.cumsum(target_table, axis=0)
    rank = jnp.sum((running - 1) * target_table, axis=1)
    slot = target * capacity + rank
    send_rows = jnp.zeros((cycle_size * capacity, feature_share), jnp.bfloat16).at[slot].set(summed)
    send_index = jnp.full((cycle_size * capacity,), -1, jnp.int32).at[slot].set(local_token)
    send_rows = send_rows.reshape(cycle_size, capacity, feature_share)
    send_index = send_index.reshape(cycle_size, capacity)
    got_rows, got_index = (
        lax.all_to_all(send_rows, "blk", split_axis=0, concat_axis=0, tiled=True),
        lax.all_to_all(send_index, "blk", split_axis=0, concat_axis=0, tiled=True),
    )
    got_rows = got_rows.reshape(cycle_size * capacity, feature_share)
    got_index = got_index.reshape(cycle_size * capacity)
    placing = (got_index[:, None] == jnp.arange(owned, dtype=jnp.int32)[None, :]).astype(
        jnp.bfloat16
    )
    combined = lax.dot_general(
        placing, got_rows, (((0,), (0,)), ((), ())), preferred_element_type=jnp.float32
    )
    return combined.astype(jnp.bfloat16)


MIDDLE = [(1, 2), (2, 1)]
INWARD = [(0, 1), (3, 2)]
OUTWARD = [(1, 0), (2, 3)]
CHUNK_OWNER = [[3, 2, 1, 0], [3, 2, 0, 1], [0, 1, 3, 2], [0, 1, 2, 3]]
FACT_ROWS = 16
VMEM = pl.BlockSpec(memory_space=pltpu.VMEM)
SMEM = pl.BlockSpec(memory_space=pltpu.SMEM)
ANYWHERE = pl.BlockSpec(memory_space=pl.ANY)


def across_chips(block):
    return lax.ppermute(block, "tp", [(i, i ^ 2) for i in range(4)])


def across_cores(block):
    return lax.ppermute(block, "tp", [(i, i ^ 1) for i in range(4)])


def along(block, route):
    return lax.ppermute(block, "blk", route)


def on_core(body, out_shape, in_specs, flops=1024):
    return pl.pallas_call(
        body,
        out_shape=out_shape,
        in_specs=in_specs,
        out_specs=jax.tree.map(lambda _: VMEM, out_shape),
        compiler_params=pltpu.CompilerParams(vmem_limit_bytes=40 * 2**20),
        cost_estimate=pl.CostEstimate(flops=flops, bytes_accessed=1024, transcendentals=0),
    )


def after(block, *others):
    return pl.pallas_call(
        lambda *refs: None,
        out_shape=jax.ShapeDtypeStruct(block.shape, block.dtype),
        in_specs=[ANYWHERE] * (1 + len(others)),
        out_specs=ANYWHERE,
        input_output_aliases={0: 0},
        cost_estimate=pl.CostEstimate(flops=16, bytes_accessed=16, transcendentals=0),
    )(block, *others)


def with_facts(rows, gates, block_list, block_count, owner):
    count, width = rows.shape
    offsets, blocks = block_list.shape
    total = owner.shape[1]

    def body(rows_ref, gates_ref, list_ref, count_ref, owner_ref, out_ref):
        out_ref[:count, :] = rows_ref[...]
        block_of = lax.broadcasted_iota(jnp.int32, (1, total), 1) // (total // blocks)
        facts = []
        for offset in range(offsets):
            mask = jnp.zeros((1, total), jnp.float32)
            for block in range(blocks):
                used = jnp.int32(0)
                for place in range(blocks):
                    found = (list_ref[offset, place] == block) & (place < count_ref[offset])
                    used = used | found.astype(jnp.int32)
                mask = mask + jnp.where(block_of == block, used.astype(jnp.float32), 0.0)
            facts.append(gates_ref[offset : offset + 1, :] * mask)
        facts.append((owner_ref[...] >> 8).astype(jnp.float32))
        facts.append((owner_ref[...] & 255).astype(jnp.float32))
        facts.append(jnp.zeros((FACT_ROWS - len(facts), total), jnp.float32))
        out_ref[count:, :] = jnp.zeros((FACT_ROWS, width), jnp.bfloat16)
        out_ref[count:, :total] = jnp.concatenate(facts, axis=0).astype(jnp.bfloat16)

    shape = jax.ShapeDtypeStruct((count + FACT_ROWS, width), rows.dtype)
    return on_core(body, shape, [VMEM, VMEM, SMEM, SMEM, VMEM])(
        rows, gates, block_list, block_count, owner
    )


def partial_sums(rows, parts, weights, places, before=None, send=True, flops=1024):
    width = parts[0][0].shape[1]
    columns = weights[0].shape[1]
    operands = [block for part in parts for block in part] + list(weights)
    if before is not None:
        operands.append(before)

    def body(*refs):
        blocks, results = refs[: len(parts) * len(places)], refs[len(operands) :]
        weight_refs = refs[len(blocks) : len(blocks) + len(weights)]
        for part in range(len(parts)):
            span = slice(part * rows, (part + 1) * rows)
            for side in range(2):
                at = slice(side * columns, (side + 1) * columns)
                total = None if before is None else refs[len(operands) - 1][span, at]
                for index, place in enumerate(places):
                    product = jnp.dot(
                        blocks[part * len(places) + index][:rows, :],
                        weight_refs[side][place * width : (place + 1) * width, :],
                        preferred_element_type=jnp.float32,
                    )
                    total = product if total is None else total + product
                results[0][span, at] = total
                if send:
                    results[1][span, at] = total.astype(jnp.bfloat16)

    size = (len(parts) * rows, 2 * columns)
    shapes = [jax.ShapeDtypeStruct(size, jnp.float32)]
    if send:
        shapes.append(jax.ShapeDtypeStruct(size, jnp.bfloat16))
    return on_core(body, shapes, [VMEM] * len(operands), flops)(*operands)


def collected_rows(owned, plan, sums, got, facts, picks, before):
    units = sums.shape[1] // 4
    hidden = []
    for core in range(2):
        here, there = 2 * core * units, 2 * (1 - core) * units
        gate = sums[:, here : here + units] + got[:, there : there + units].astype(jnp.float32)
        up = sums[:, here + units : here + 2 * units]
        up = up + got[:, there + units : there + 2 * units].astype(jnp.float32)
        hidden.append((gate / (1.0 + jnp.exp(-gate)) * up).astype(jnp.bfloat16))
    hidden = jnp.concatenate(hidden, axis=1)
    factor, owner = [], []
    for offset, start, stop in picks:
        values = facts[plan[4 + offset]].astype(jnp.float32)
        factor.append(values[offset : offset + 1, start:stop])
        owner.append(values[4:5, start:stop] * 256.0 + values[5:6, start:stop])
    factor = jnp.concatenate(factor, axis=1)
    owner = jnp.concatenate(owner, axis=1).astype(jnp.int32)
    results = []
    for index in range(4):
        token = plan[index] * owned + lax.broadcasted_iota(jnp.int32, (owned, 1), 0)
        placing = jnp.where(owner == token, factor, 0.0).astype(jnp.bfloat16)
        rows = jnp.dot(placing, hidden, preferred_element_type=jnp.float32)
        if before is not None:
            rows = rows + before[index * owned : (index + 1) * owned, :]
        results.append(rows)
    return results


def collect(owned, plan, sums, got, facts, picks, before):
    operands = [plan, sums, got, facts] + ([] if before is None else [before])

    def body(plan_ref, sums_ref, got_ref, facts_ref, *rest):
        before_ref = rest[0] if before is not None else None
        rows = collected_rows(owned, plan_ref, sums_ref, got_ref, facts_ref, picks, before_ref)
        for index in range(4):
            rest[-1][index * owned : (index + 1) * owned, :] = rows[index]

    shape = jax.ShapeDtypeStruct((4 * owned, sums.shape[1] // 2), jnp.float32)
    return on_core(body, shape, [SMEM] + [VMEM] * (len(operands) - 1))(*operands)


def finish(owned, plan, sums, got, facts, picks, before, down_own, down_lent):
    units = down_own.shape[0]
    width = down_own.shape[1] // 2

    def body(plan_ref, sums_ref, got_ref, facts_ref, before_ref, own_ref, lent_ref, *out_refs):
        rows = collected_rows(owned, plan_ref, sums_ref, got_ref, facts_ref, picks, before_ref)
        for index in range(4):
            held = rows[index].astype(jnp.bfloat16)
            for out, at in ((4 + index, slice(0, width)), (index, slice(width, 2 * width))):
                result = jnp.dot(
                    held[:, :units], own_ref[:, at], preferred_element_type=jnp.float32
                ) + jnp.dot(held[:, units:], lent_ref[:, at], preferred_element_type=jnp.float32)
                out_refs[out][...] = result.astype(out_refs[out].dtype)

    results = on_core(
        body,
        [jax.ShapeDtypeStruct((owned, width), jnp.bfloat16)] * 4
        + [jax.ShapeDtypeStruct((owned, width), jnp.float32)] * 4,
        [SMEM] + [VMEM] * 6,
    )(plan, sums, got, facts, before, down_own, down_lent)
    return results[:4], results[4:]


def rows_travel(
    tokens, gate_weight, up_weight, down_weight, route_gates, block_list, block_count, owner_token
):
    position = lax.axis_index("blk")
    share = lax.axis_index("tp")
    row_count, width = tokens.shape
    units = gate_weight.shape[2]
    owned = row_count // 2
    third = row_count // 3
    cycle = 4
    owners = jnp.asarray(CHUNK_OWNER, jnp.int32)[position]
    plan = jnp.concatenate([owners, (position + jnp.arange(cycle, dtype=jnp.int32)) % cycle])

    def others(gathered):
        rows = [
            lax.dynamic_slice(gathered, ((position + s) % cycle, 0, 0), (1, third, width))
            for s in range(1, cycle)
        ]
        return jnp.concatenate(rows).reshape((cycle - 1) * third, width)

    own_far = across_chips(tokens)
    gathered_0 = lax.all_gather(tokens[:third], "blk")
    marked = with_facts(
        tokens[third : 2 * third],
        route_gates.T,
        block_list[0],
        block_count[0],
        owner_token[None],
    )
    gathered_1 = lax.all_gather(marked, "blk")
    facts = gathered_1[:, third:, :row_count]
    rows_0 = others(gathered_0)
    far_0 = across_chips(rows_0)
    rows_1 = others(gathered_1)
    far_1 = across_chips(rows_1)
    gathered_2 = lax.all_gather(after(tokens[2 * third :], gathered_1, own_far, far_0), "blk")
    rows_2 = after(others(gathered_2), far_1)
    far_2 = across_chips(rows_2)

    gate_quarters = gate_weight[0].reshape(4, width, units)
    up_quarters = up_weight[0].reshape(4, width, units)

    def quarter(j):
        pair = [
            lax.dynamic_index_in_dim(q, share ^ j, 0, keepdims=False)
            for q in (gate_quarters, up_quarters)
        ]
        return jnp.concatenate(pair, axis=1)

    def down_part(j):
        return lax.dynamic_slice_in_dim(down_weight[0], (share ^ j) * width, width, 1)

    kept_in = jnp.concatenate([quarter(0), quarter(2)])
    lend_in = jnp.concatenate([quarter(1), quarter(3)])
    kept_down = jnp.concatenate([down_part(0), down_part(2)], axis=1)
    lend_down = jnp.concatenate([down_part(1), down_part(3)], axis=1)

    lent_in = across_cores(lend_in)
    lent_down = across_cores(lend_down)
    weights = (kept_in, lent_in)

    def sums_of(near, far):
        sums, send = partial_sums(row_count, [(near, far)], weights, (0, 1))
        return sums, across_cores(send)

    def picks(index):
        return [(s, index * third, (index + 1) * third) for s in range(1, cycle)]

    sums, got = sums_of(tokens, own_far)
    total = collect(owned, plan, sums, got, facts, [(0, 0, row_count)], None)
    sums, got = sums_of(rows_0, far_0)
    total = collect(owned, plan, sums, got, facts, picks(0), total)
    sums, got = sums_of(rows_1, far_1)
    total = collect(owned, plan, sums, got, facts, picks(1), total)
    sums, got = sums_of(rows_2, far_2)
    sent, kept = finish(owned, plan, sums, got, facts, picks(2), total, kept_down, lent_down)
    chunks = [k + across_chips(s).astype(jnp.float32) for s, k in zip(sent, kept)]

    def send(block, route):
        return along(block.astype(jnp.bfloat16), route).astype(jnp.float32)

    first_in = send(chunks[0], INWARD)
    second_in = send(chunks[1], INWARD)
    second_mid = send(chunks[0] + first_in, MIDDLE)
    third_in = send(chunks[2], INWARD)
    third_mid = send(chunks[1] + second_in, MIDDLE)
    third_out = send(chunks[2] + second_mid, OUTWARD)
    return (chunks[3] + third_in + third_mid + third_out).astype(jnp.bfloat16)


def on_device(*args):
    block_list = args[5]
    sizes = (lax.axis_size("blk"), lax.axis_size("tp"), block_list.shape[1])
    if sizes == (4, 4, 4):
        return rows_travel(*args)
    return weights_travel(*args)


def solution(mesh):
    return jax.shard_map(
        on_device,
        mesh=mesh,
        in_specs=(
            P(("groups", "blk"), "tp"),
            P("blk", None, "tp"),
            P("blk", None, "tp"),
            P("blk", "tp", None),
            P(("groups", "blk"), None),
            P(("groups", "blk"), None, None),
            P(("groups", "blk"), None),
            P(("groups", "blk")),
        ),
        out_specs=P(("groups", "blk"), "tp"),
        check_vma=False,
    )
```

```python
import jax
import jax.numpy as jnp
from jax import lax
from jax.experimental import pallas as pl
from jax.experimental.pallas import tpu as pltpu
from jax.sharding import PartitionSpec as P


def shifted(block, axis, distance):
    devices = range(lax.axis_size(axis))
    route = [((i - distance) % len(devices), i) for i in devices]
    return lax.ppermute(block, axis, route)


def weights_travel(
    tokens, gate_weight, up_weight, down_weight, route_gates, block_list, block_count, owner_token
):
    whole_rows = lax.all_gather(tokens, "tp", axis=1, tiled=True)
    row_count = whole_rows.shape[0]
    width = whole_rows.shape[1]
    offsets_all = block_list.shape[1]
    block_total = block_list.shape[2]
    block_size = row_count // block_total
    blocks = whole_rows.reshape(block_total, block_size, width)
    gate_blocks = route_gates.reshape(block_total, block_size, offsets_all)
    totals = jnp.zeros((block_total, block_size, width), jnp.float32)

    def apply(totals, weights, offset, block_id):
        w_gate, w_up, w_down = weights
        block_rows = lax.dynamic_index_in_dim(blocks, block_id, 0, keepdims=False)
        gate_out = jnp.dot(block_rows, w_gate, preferred_element_type=jnp.float32)
        up_out = jnp.dot(block_rows, w_up, preferred_element_type=jnp.float32)
        hidden = (jax.nn.silu(gate_out) * up_out).astype(jnp.bfloat16)
        block_gates = lax.dynamic_index_in_dim(gate_blocks, block_id, 0, keepdims=False)
        factor = lax.dynamic_index_in_dim(block_gates, offset, 1, keepdims=False)
        product = jnp.dot(hidden, w_down, preferred_element_type=jnp.float32) * factor[:, None]
        before = lax.dynamic_index_in_dim(totals, block_id, 0, keepdims=False)
        return lax.dynamic_update_index_in_dim(totals, before + product, block_id, 0)

    resident = (gate_weight[0], up_weight[0], down_weight[0])
    arrived = [resident]
    holding = resident
    for offset in range(1, offsets_all):
        holding = shifted((holding[0], holding[1], holding[2]), "blk", 1)
        arrived.append(holding)
    for offset in range(offsets_all):
        weights = arrived[offset]

        def visit_block(position, totals, weights=weights, offset=offset):
            return apply(totals, weights, offset, block_list[0, offset, position])

        totals = lax.fori_loop(0, block_count[0, offset], visit_block, totals)
    summed = lax.psum_scatter(
        totals.reshape(row_count, width).astype(jnp.bfloat16), "tp", scatter_dimension=1, tiled=True
    )
    feature_share = summed.shape[1]
    cycle_size = lax.axis_size("blk")
    owned = row_count // 2
    capacity = max(2, 2 * row_count // cycle_size)
    target = owner_token // owned
    local_token = owner_token % owned
    target_table = (target[:, None] == jnp.arange(cycle_size, dtype=jnp.int32)[None, :]).astype(
        jnp.int32
    )
    running = jnp.cumsum(target_table, axis=0)
    rank = jnp.sum((running - 1) * target_table, axis=1)
    slot = target * capacity + rank
    send_rows = jnp.zeros((cycle_size * capacity, feature_share), jnp.bfloat16).at[slot].set(summed)
    send_index = jnp.full((cycle_size * capacity,), -1, jnp.int32).at[slot].set(local_token)
    send_rows = send_rows.reshape(cycle_size, capacity, feature_share)
    send_index = send_index.reshape(cycle_size, capacity)
    got_rows, got_index = (
        lax.all_to_all(send_rows, "blk", split_axis=0, concat_axis=0, tiled=True),
        lax.all_to_all(send_index, "blk", split_axis=0, concat_axis=0, tiled=True),
    )
    got_rows = got_rows.reshape(cycle_size * capacity, feature_share)
    got_index = got_index.reshape(cycle_size * capacity)
    placing = (got_index[:, None] == jnp.arange(owned, dtype=jnp.int32)[None, :]).astype(
        jnp.bfloat16
    )
    combined = lax.dot_general(
        placing, got_rows, (((0,), (0,)), ((), ())), preferred_element_type=jnp.float32
    )
    return combined.astype(jnp.bfloat16)


BESIDE = [(0, 1), (1, 0), (2, 3), (3, 2)]
MIDDLE = [(1, 2), (2, 1)]
INWARD = [(0, 1), (3, 2)]
OUTWARD = [(1, 0), (2, 3)]
PLAN = [
    [3, 2, 1, 0, 0, 1, 2, 3, 0],
    [3, 2, 0, 1, 0, 3, 1, 2, 1],
    [0, 1, 3, 2, 0, 1, 3, 2, 1],
    [0, 1, 2, 3, 0, 3, 2, 1, 0],
]
OFFSETS_AT, INNER_AT = 4, 8
VMEM = pl.BlockSpec(memory_space=pltpu.VMEM)
SMEM = pl.BlockSpec(memory_space=pltpu.SMEM)
ANYWHERE = pl.BlockSpec(memory_space=pl.ANY)


def across_chips(block):
    return lax.ppermute(block, "tp", [(i, i ^ 2) for i in range(4)])


def across_cores(block):
    return lax.ppermute(block, "tp", [(i, i ^ 1) for i in range(4)])


def along(block, route):
    return lax.ppermute(block, "blk", route)


def on_core(body, out_shape, in_specs, flops=1024):
    return pl.pallas_call(
        body,
        out_shape=out_shape,
        in_specs=in_specs,
        out_specs=jax.tree.map(lambda _: VMEM, out_shape),
        compiler_params=pltpu.CompilerParams(vmem_limit_bytes=40 * 2**20),
        cost_estimate=pl.CostEstimate(flops=flops, bytes_accessed=1024, transcendentals=0),
    )


def after(block, *others):
    return pl.pallas_call(
        lambda *refs: None,
        out_shape=jax.ShapeDtypeStruct(block.shape, block.dtype),
        in_specs=[ANYWHERE] * (1 + len(others)),
        out_specs=ANYWHERE,
        input_output_aliases={0: 0},
        cost_estimate=pl.CostEstimate(flops=16, bytes_accessed=16, transcendentals=0),
    )(block, *others)


def row_facts(gates, block_list, block_count, owner):
    offsets, blocks = block_list.shape
    total = owner.shape[1]

    def body(gates_ref, list_ref, count_ref, owner_ref, *out_refs):
        block_of = lax.broadcasted_iota(jnp.int32, (1, total), 1) // (total // blocks)
        for offset in range(offsets):
            mask = jnp.zeros((1, total), jnp.float32)
            for block in range(blocks):
                used = jnp.int32(0)
                for place in range(blocks):
                    found = (list_ref[offset, place] == block) & (place < count_ref[offset])
                    used = used | found.astype(jnp.int32)
                mask = mask + jnp.where(block_of == block, used.astype(jnp.float32), 0.0)
            out_refs[offset][0:1, :] = gates_ref[offset : offset + 1, :] * mask
            out_refs[offset][1:2, :] = owner_ref[...].astype(jnp.float32)

    shapes = [jax.ShapeDtypeStruct((2, total), jnp.float32)] * offsets
    return on_core(body, shapes, [VMEM, SMEM, SMEM, VMEM])(gates, block_list, block_count, owner)


def partial_sums(parts, weights, places, before=None, send=True, choice=None, waits=()):
    width, columns = weights[0].shape[0] // 2, weights[0].shape[1]
    sizes = [part[0].shape[0] for part in parts]
    blocks = [block for part in parts for block in part]
    operands = blocks + list(weights)
    specs = [VMEM] * len(operands)
    if before is not None:
        operands.append(before)
        specs.append(VMEM)
    if choice is not None:
        operands += [choice[0], choice[1]]
        specs += [SMEM, VMEM]
    operands += waits
    specs += [ANYWHERE] * len(waits)

    def body(*refs):
        results = refs[len(operands) :]
        weight_refs = refs[len(blocks) : len(blocks) + len(weights)]
        next_ref = len(blocks) + len(weights)
        before_ref = refs[next_ref] if before is not None else None
        next_ref += before is not None
        start = 0
        for part, size in enumerate(sizes):
            span = slice(start, start + size)
            start += size
            rows = [refs[part * len(places) + index][...] for index in range(len(places))]
            if choice is not None and part == len(sizes) - 1:
                rows[0] = jnp.where(refs[next_ref][INNER_AT] == 1, refs[next_ref + 1][...], rows[0])
            for side in range(2):
                at = slice(side * columns, (side + 1) * columns)
                total = None if before is None else before_ref[span, at]
                for index, place in enumerate(places):
                    product = jnp.dot(
                        rows[index],
                        weight_refs[side][place * width : (place + 1) * width, :],
                        preferred_element_type=jnp.float32,
                    )
                    total = product if total is None else total + product
                results[0][span, at] = total
                if send:
                    results[1][span, at] = total.astype(jnp.bfloat16)

    size = (sum(sizes), 2 * columns)
    shapes = [jax.ShapeDtypeStruct(size, jnp.float32)]
    if send:
        shapes.append(jax.ShapeDtypeStruct(size, jnp.bfloat16))
    return on_core(body, shapes, specs)(*operands)


def collected_rows(owned, slot, plan, sums, got, facts, before):
    units = sums.shape[1] // 4
    hidden = []
    for core in range(2):
        here, there = 2 * core * units, 2 * (1 - core) * units
        gate = sums[:, here : here + units] + got[:, there : there + units].astype(jnp.float32)
        up = sums[:, here + units : here + 2 * units]
        up = up + got[:, there + units : there + 2 * units].astype(jnp.float32)
        hidden.append((gate / (1.0 + jnp.exp(-gate)) * up).astype(jnp.bfloat16))
    hidden = jnp.concatenate(hidden, axis=1)
    values = facts[plan[OFFSETS_AT + slot]]
    factor, owner = values[0:1, :], values[1:2, :].astype(jnp.int32)
    results = []
    for index in range(4):
        token = plan[index] * owned + lax.broadcasted_iota(jnp.int32, (owned, 1), 0)
        placing = jnp.where(owner == token, factor, 0.0).astype(jnp.bfloat16)
        rows = jnp.dot(placing, hidden, preferred_element_type=jnp.float32)
        if before is not None:
            rows = rows + before[index * owned : (index + 1) * owned, :]
        results.append(rows)
    return results


def collect(owned, slot, plan, sums, got, facts, before):
    operands = [plan, sums, got, facts] + ([] if before is None else [before])

    def body(plan_ref, sums_ref, got_ref, facts_ref, *rest):
        before_ref = rest[0] if before is not None else None
        rows = collected_rows(owned, slot, plan_ref, sums_ref, got_ref, facts_ref, before_ref)
        for index in range(4):
            rest[-1][index * owned : (index + 1) * owned, :] = rows[index]

    shape = jax.ShapeDtypeStruct((4 * owned, sums.shape[1] // 2), jnp.float32)
    return on_core(body, shape, [SMEM] + [VMEM] * (len(operands) - 1))(*operands)


def down(held, own_ref, lent_ref, sent_ref, kept_ref):
    units, width = own_ref.shape[0], kept_ref.shape[1]
    for out, at in ((kept_ref, slice(0, width)), (sent_ref, slice(width, 2 * width))):
        result = jnp.dot(held[:, :units], own_ref[:, at], preferred_element_type=jnp.float32)
        result += jnp.dot(held[:, units:], lent_ref[:, at], preferred_element_type=jnp.float32)
        out[...] = result.astype(out.dtype)


def finish(owned, slot, plan, sums, got, facts, before, down_own, down_lent):
    units = down_own.shape[0]
    width = down_own.shape[1] // 2
    pair = [
        jax.ShapeDtypeStruct((owned, width), jnp.bfloat16),
        jax.ShapeDtypeStruct((owned, width), jnp.float32),
    ]

    def first(plan_ref, sums_ref, got_ref, facts_ref, before_ref, own_ref, lent_ref, *out_refs):
        rows = collected_rows(owned, slot, plan_ref, sums_ref, got_ref, facts_ref, before_ref)
        down(rows[0].astype(jnp.bfloat16), own_ref, lent_ref, out_refs[0], out_refs[1])
        for index in range(1, 4):
            out_refs[2][(index - 1) * owned : index * owned, :] = rows[index].astype(jnp.bfloat16)

    def others(held_ref, own_ref, lent_ref, *out_refs):
        for index in range(3):
            held = held_ref[index * owned : (index + 1) * owned, :]
            down(held, own_ref, lent_ref, out_refs[2 * index], out_refs[2 * index + 1])

    held_shape = jax.ShapeDtypeStruct((3 * owned, 2 * units), jnp.bfloat16)
    sent, kept, held = on_core(first, pair + [held_shape], [SMEM] + [VMEM] * 6)(
        plan, sums, got, facts, before, down_own, down_lent
    )
    rest = on_core(others, pair * 3, [VMEM] * 3)(held, down_own, down_lent)
    return [sent, *rest[0::2]], [kept, *rest[1::2]]


def rows_travel(
    tokens, gate_weight, up_weight, down_weight, route_gates, block_list, block_count, owner_token
):
    position = lax.axis_index("blk")
    share = lax.axis_index("tp")
    row_count, width = tokens.shape
    units = gate_weight.shape[2]
    owned = row_count // 2
    half = row_count // 2
    offsets_all = block_list.shape[1]
    plan = jnp.asarray(PLAN, jnp.int32)[position]
    inner = plan[INNER_AT] == 1

    beside = along(tokens, BESIDE)
    middle = along(tokens, MIDDLE)
    own_far = across_chips(tokens)
    facts = row_facts(route_gates.T, block_list[0], block_count[0], owner_token[None])
    facts = [
        pair if offset == 0 else shifted(pair, "blk", offsets_all - offset)
        for offset, pair in enumerate(facts)
    ]
    facts = jnp.stack(facts)

    gate_quarters = gate_weight[0].reshape(4, width, units)
    up_quarters = up_weight[0].reshape(4, width, units)

    def quarter(j):
        pair = [
            lax.dynamic_index_in_dim(q, share ^ j, 0, keepdims=False)
            for q in (gate_quarters, up_quarters)
        ]
        return jnp.concatenate(pair, axis=1)

    def down_part(j):
        return lax.dynamic_slice_in_dim(down_weight[0], (share ^ j) * width, width, 1)

    kept_in = jnp.concatenate([quarter(0), quarter(2)])
    lend_in = jnp.concatenate([quarter(1), quarter(3)])
    kept_down = jnp.concatenate([down_part(0), down_part(2)], axis=1)
    lend_down = jnp.concatenate([down_part(1), down_part(3)], axis=1)


    inner_last = along(beside, MIDDLE)
    outer_next = along(middle, OUTWARD)
    beside_far = across_chips(beside)
    inward_far = along(own_far[half:], INWARD)
    lent_in = across_cores(after(lend_in, beside, own_far, facts))
    weights = (kept_in, lent_in)
    sums_0, send_0 = partial_sums([(tokens, own_far)], weights, (0, 1))
    got_0 = across_cores(send_0)

    outer_last = along(inner_last, OUTWARD)
    second = after(
        jnp.where(inner, middle, outer_next), beside_far, inner_last, inward_far
    )
    second_far = across_chips(second)
    middle_far = along(inward_far, MIDDLE)
    lent_down = across_cores(after(lend_down, inner_last))
    total = collect(owned, 0, plan, sums_0, got_0, facts, None)
    sums_1, send_1 = partial_sums([(beside, beside_far)], weights, (0, 1))
    got_1 = across_cores(send_1)

    last_a = after(
        jnp.where(inner, inner_last[:half], outer_last[:half]),
        second_far,
        middle_far,
        sums_1,
        total,
    )
    last_b = jnp.where(inner, inner_last[half:], outer_last[half:])
    last_far_a = across_chips(last_a)
    outward_far = along(middle_far, OUTWARD)
    total = collect(owned, 1, plan, sums_1, got_1, facts, total)
    sums_2, send_2 = partial_sums([(second, second_far)], weights, (0, 1))
    got_2 = across_cores(send_2)
    near = partial_sums([(last_a,), (last_b,)], weights, (0,), send=False)[0]
    total = collect(owned, 2, plan, sums_2, got_2, facts, total)
    sums_3, send_3 = partial_sums(
        [(last_far_a,), (outward_far,)],
        weights,
        (1,),
        before=near,
        choice=(plan, middle_far),
        waits=(total,),
    )
    got_3 = across_cores(send_3)
    sent, kept = finish(
        owned, 3, plan, sums_3, got_3, facts, total, kept_down, lent_down
    )
    chunks = [k + across_chips(s).astype(jnp.float32) for s, k in zip(sent, kept)]

    def send(block, route):
        return along(block.astype(jnp.bfloat16), route).astype(jnp.float32)

    first_in = send(chunks[0], INWARD)
    second_in = send(chunks[1], INWARD)
    second_mid = send(chunks[0] + first_in, MIDDLE)
    third_in = send(chunks[2], INWARD)
    third_mid = send(chunks[1] + second_in, MIDDLE)
    third_out = send(chunks[2] + second_mid, OUTWARD)
    return (chunks[3] + third_in + third_mid + third_out).astype(jnp.bfloat16)


def on_device(*args):
    block_list = args[5]
    sizes = (lax.axis_size("blk"), lax.axis_size("tp"), block_list.shape[1])
    if sizes == (4, 4, 4):
        return rows_travel(*args)
    return weights_travel(*args)


def solution(mesh):
    return jax.shard_map(
        on_device,
        mesh=mesh,
        in_specs=(
            P(("groups", "blk"), "tp"),
            P("blk", None, "tp"),
            P("blk", None, "tp"),
            P("blk", "tp", None),
            P(("groups", "blk"), None),
            P(("groups", "blk"), None, None),
            P(("groups", "blk"), None),
            P(("groups", "blk")),
        ),
        out_specs=P(("groups", "blk"), "tp"),
        check_vma=False,
    )
```

```python
import jax
import jax.numpy as jnp
from jax import lax
from jax.experimental import pallas as pl
from jax.experimental.pallas import tpu as pltpu
from jax.sharding import PartitionSpec as P


def shifted(block, axis, distance):
    devices = range(lax.axis_size(axis))
    route = [((i - distance) % len(devices), i) for i in devices]
    return lax.ppermute(block, axis, route)


def weights_travel(
    tokens, gate_weight, up_weight, down_weight, route_gates, block_list, block_count, owner_token
):
    whole_rows = lax.all_gather(tokens, "tp", axis=1, tiled=True)
    row_count = whole_rows.shape[0]
    width = whole_rows.shape[1]
    offsets_all = block_list.shape[1]
    block_total = block_list.shape[2]
    block_size = row_count // block_total
    blocks = whole_rows.reshape(block_total, block_size, width)
    gate_blocks = route_gates.reshape(block_total, block_size, offsets_all)
    totals = jnp.zeros((block_total, block_size, width), jnp.float32)

    def apply(totals, weights, offset, block_id):
        w_gate, w_up, w_down = weights
        block_rows = lax.dynamic_index_in_dim(blocks, block_id, 0, keepdims=False)
        gate_out = jnp.dot(block_rows, w_gate, preferred_element_type=jnp.float32)
        up_out = jnp.dot(block_rows, w_up, preferred_element_type=jnp.float32)
        hidden = (jax.nn.silu(gate_out) * up_out).astype(jnp.bfloat16)
        block_gates = lax.dynamic_index_in_dim(gate_blocks, block_id, 0, keepdims=False)
        factor = lax.dynamic_index_in_dim(block_gates, offset, 1, keepdims=False)
        product = jnp.dot(hidden, w_down, preferred_element_type=jnp.float32) * factor[:, None]
        before = lax.dynamic_index_in_dim(totals, block_id, 0, keepdims=False)
        return lax.dynamic_update_index_in_dim(totals, before + product, block_id, 0)

    resident = (gate_weight[0], up_weight[0], down_weight[0])
    arrived = [resident]
    holding = resident
    for offset in range(1, offsets_all):
        holding = shifted((holding[0], holding[1], holding[2]), "blk", 1)
        arrived.append(holding)
    for offset in range(offsets_all):
        weights = arrived[offset]

        def visit_block(position, totals, weights=weights, offset=offset):
            return apply(totals, weights, offset, block_list[0, offset, position])

        totals = lax.fori_loop(0, block_count[0, offset], visit_block, totals)
    summed = lax.psum_scatter(
        totals.reshape(row_count, width).astype(jnp.bfloat16), "tp", scatter_dimension=1, tiled=True
    )
    feature_share = summed.shape[1]
    cycle_size = lax.axis_size("blk")
    owned = row_count // 2
    capacity = max(2, 2 * row_count // cycle_size)
    target = owner_token // owned
    local_token = owner_token % owned
    target_table = (target[:, None] == jnp.arange(cycle_size, dtype=jnp.int32)[None, :]).astype(
        jnp.int32
    )
    running = jnp.cumsum(target_table, axis=0)
    rank = jnp.sum((running - 1) * target_table, axis=1)
    slot = target * capacity + rank
    send_rows = jnp.zeros((cycle_size * capacity, feature_share), jnp.bfloat16).at[slot].set(summed)
    send_index = jnp.full((cycle_size * capacity,), -1, jnp.int32).at[slot].set(local_token)
    send_rows = send_rows.reshape(cycle_size, capacity, feature_share)
    send_index = send_index.reshape(cycle_size, capacity)
    got_rows, got_index = (
        lax.all_to_all(send_rows, "blk", split_axis=0, concat_axis=0, tiled=True),
        lax.all_to_all(send_index, "blk", split_axis=0, concat_axis=0, tiled=True),
    )
    got_rows = got_rows.reshape(cycle_size * capacity, feature_share)
    got_index = got_index.reshape(cycle_size * capacity)
    placing = (got_index[:, None] == jnp.arange(owned, dtype=jnp.int32)[None, :]).astype(
        jnp.bfloat16
    )
    combined = lax.dot_general(
        placing, got_rows, (((0,), (0,)), ((), ())), preferred_element_type=jnp.float32
    )
    return combined.astype(jnp.bfloat16)


BESIDE = [(0, 1), (1, 0), (2, 3), (3, 2)]
MIDDLE = [(1, 2), (2, 1)]
INWARD = [(0, 1), (3, 2)]
OUTWARD = [(1, 0), (2, 3)]
TWO_ON = [(0, 2), (3, 1), (1, 3), (2, 0)]
PLAN = [
    [3, 2, 1, 0, 0, 1, 2, 3, 0],
    [2, 3, 0, 1, 0, 3, 1, 2, 1],
    [1, 0, 3, 2, 0, 1, 3, 2, 1],
    [0, 1, 2, 3, 0, 3, 2, 1, 0],
]
OFFSETS_AT, INNER_AT = 4, 8
FACT_ROWS = 16
VMEM = pl.BlockSpec(memory_space=pltpu.VMEM)
SMEM = pl.BlockSpec(memory_space=pltpu.SMEM)
ANYWHERE = pl.BlockSpec(memory_space=pl.ANY)


def across_chips(block):
    return lax.ppermute(block, "tp", [(i, i ^ 2) for i in range(4)])


def across_cores(block):
    return lax.ppermute(block, "tp", [(i, i ^ 1) for i in range(4)])


def along(block, route):
    return lax.ppermute(block, "blk", route)


def on_core(body, out_shape, in_specs, flops=1024):
    return pl.pallas_call(
        body,
        out_shape=out_shape,
        in_specs=in_specs,
        out_specs=jax.tree.map(lambda _: VMEM, out_shape),
        compiler_params=pltpu.CompilerParams(vmem_limit_bytes=40 * 2**20),
        cost_estimate=pl.CostEstimate(flops=flops, bytes_accessed=1024, transcendentals=0),
    )


def after(block, *others):
    return pl.pallas_call(
        lambda *refs: None,
        out_shape=jax.ShapeDtypeStruct(block.shape, block.dtype),
        in_specs=[ANYWHERE] * (1 + len(others)),
        out_specs=ANYWHERE,
        input_output_aliases={0: 0},
        cost_estimate=pl.CostEstimate(flops=16, bytes_accessed=16, transcendentals=0),
    )(block, *others)


def chosen(plan, if_inner, if_outer, spans, *others):
    width = if_inner.shape[1]

    def body(plan_ref, inner_ref, outer_ref, *rest):
        out_refs, sems = rest[len(others) : -1], rest[-1]

        def copy_from(source):
            copies = [
                pltpu.make_async_copy(source.at[pl.ds(start, size)], out, sems.at[index])
                for index, ((start, size), out) in enumerate(zip(spans, out_refs))
            ]
            for copy in copies:
                copy.start()
            for copy in copies:
                copy.wait()

        @pl.when(plan_ref[INNER_AT] == 1)
        def _():
            copy_from(inner_ref)

        @pl.when(plan_ref[INNER_AT] == 0)
        def _():
            copy_from(outer_ref)

    return pl.pallas_call(
        body,
        out_shape=[jax.ShapeDtypeStruct((size, width), if_inner.dtype) for _, size in spans],
        in_specs=[SMEM] + [ANYWHERE] * (2 + len(others)),
        out_specs=[ANYWHERE] * len(spans),
        scratch_shapes=[pltpu.SemaphoreType.DMA((len(spans),))],
        cost_estimate=pl.CostEstimate(flops=16, bytes_accessed=16, transcendentals=0),
    )(plan, if_inner, if_outer, *others)


def with_facts(rows, gates, block_list, block_count, owner):
    count, width = rows.shape
    offsets, blocks = block_list.shape
    total = owner.shape[1]

    def body(rows_ref, gates_ref, list_ref, count_ref, owner_ref, out_ref, sem):
        copy = pltpu.make_async_copy(rows_ref, out_ref.at[pl.ds(0, count)], sem)
        copy.start()
        block_of = lax.broadcasted_iota(jnp.int32, (1, total), 1) // (total // blocks)
        facts = []
        for offset in range(offsets):
            mask = jnp.zeros((1, total), jnp.float32)
            for block in range(blocks):
                used = jnp.int32(0)
                for place in range(blocks):
                    found = (list_ref[offset, place] == block) & (place < count_ref[offset])
                    used = used | found.astype(jnp.int32)
                mask = mask + jnp.where(block_of == block, used.astype(jnp.float32), 0.0)
            facts.append(gates_ref[offset : offset + 1, :] * mask)
        facts.append((owner_ref[...] >> 8).astype(jnp.float32))
        facts.append((owner_ref[...] & 255).astype(jnp.float32))
        facts.append(jnp.zeros((FACT_ROWS - len(facts), total), jnp.float32))
        out_ref[count:, :] = jnp.zeros((FACT_ROWS, width), jnp.bfloat16)
        out_ref[count:, :total] = jnp.concatenate(facts, axis=0).astype(jnp.bfloat16)
        copy.wait()

    return pl.pallas_call(
        body,
        out_shape=jax.ShapeDtypeStruct((count + FACT_ROWS, width), rows.dtype),
        in_specs=[ANYWHERE, VMEM, SMEM, SMEM, VMEM],
        out_specs=VMEM,
        scratch_shapes=[pltpu.SemaphoreType.DMA],
        compiler_params=pltpu.CompilerParams(vmem_limit_bytes=40 * 2**20),
        cost_estimate=pl.CostEstimate(flops=1024, bytes_accessed=1024, transcendentals=0),
    )(rows, gates, block_list, block_count, owner)


def partial_sums(
    sizes, parts, weights, places, before=None, send=True, choice=None, waits=()
):
    width, columns = weights[0].shape[0] // 2, weights[0].shape[1]
    blocks = [block for part in parts for block in part]
    operands = blocks + list(weights)
    specs = [VMEM] * len(operands)
    if before is not None:
        operands.append(before)
        specs.append(VMEM)
    if choice is not None:
        operands += [choice[0], choice[1]]
        specs += [SMEM, VMEM]
    operands += waits
    specs += [ANYWHERE] * len(waits)

    def body(*refs):
        results = refs[len(operands) :]
        weight_refs = refs[len(blocks) : len(blocks) + len(weights)]
        next_ref = len(blocks) + len(weights)
        before_ref = refs[next_ref] if before is not None else None
        next_ref += before is not None
        start = 0
        for part, size in enumerate(sizes):
            span = slice(start, start + size)
            start += size
            rows = [refs[part * len(places) + index][:size, :] for index in range(len(places))]
            if choice is not None and part == len(sizes) - 1:
                rows[0] = jnp.where(refs[next_ref][INNER_AT] == 1, refs[next_ref + 1][:size, :], rows[0])
            for side in range(2):
                at = slice(side * columns, (side + 1) * columns)
                total = None if before is None else before_ref[span, at]
                for index, place in enumerate(places):
                    product = jnp.dot(
                        rows[index],
                        weight_refs[side][place * width : (place + 1) * width, :],
                        preferred_element_type=jnp.float32,
                    )
                    total = product if total is None else total + product
                results[0][span, at] = total
                if send:
                    results[1][span, at] = total.astype(jnp.bfloat16)

    size = (sum(sizes), 2 * columns)
    shapes = [jax.ShapeDtypeStruct(size, jnp.float32)]
    if send:
        shapes.append(jax.ShapeDtypeStruct(size, jnp.bfloat16))
    return on_core(body, shapes, specs)(*operands)


def collected_rows(owned, slot, plan, sums, got, facts, before):
    units = sums.shape[1] // 4
    hidden = []
    for core in range(2):
        here, there = 2 * core * units, 2 * (1 - core) * units
        gate = sums[:, here : here + units] + got[:, there : there + units].astype(jnp.float32)
        up = sums[:, here + units : here + 2 * units]
        up = up + got[:, there + units : there + 2 * units].astype(jnp.float32)
        hidden.append((gate / (1.0 + jnp.exp(-gate)) * up).astype(jnp.bfloat16))
    hidden = jnp.concatenate(hidden, axis=1)
    values = facts[:, : sums.shape[0]].astype(jnp.float32)
    kind = lax.broadcasted_iota(jnp.int32, (FACT_ROWS, 1), 0)
    mine = kind == plan[OFFSETS_AT + slot]
    factor = jnp.sum(jnp.where(mine, values, 0.0), axis=0, keepdims=True)
    owner = (values[4:5, :] * 256.0 + values[5:6, :]).astype(jnp.int32)
    results = []
    for index in range(4):
        token = plan[index] * owned + lax.broadcasted_iota(jnp.int32, (owned, 1), 0)
        placing = jnp.where(owner == token, factor, 0.0).astype(jnp.bfloat16)
        rows = jnp.dot(placing, hidden, preferred_element_type=jnp.float32)
        if before is not None:
            rows = rows + before[index * owned : (index + 1) * owned, :]
        results.append(rows)
    return results


def collect(owned, slot, plan, sums, got, facts, before):
    operands = [plan, sums, got, facts] + ([] if before is None else [before])

    def body(plan_ref, sums_ref, got_ref, facts_ref, *rest):
        before_ref = rest[0] if before is not None else None
        rows = collected_rows(owned, slot, plan_ref, sums_ref, got_ref, facts_ref, before_ref)
        for index in range(4):
            rest[-1][index * owned : (index + 1) * owned, :] = rows[index]

    shape = jax.ShapeDtypeStruct((4 * owned, sums.shape[1] // 2), jnp.float32)
    return on_core(body, shape, [SMEM] + [VMEM] * (len(operands) - 1))(*operands)


def down(held, own_ref, lent_ref, sent_ref, kept_ref):
    units, width = own_ref.shape[0], kept_ref.shape[1]
    for out, at in ((kept_ref, slice(0, width)), (sent_ref, slice(width, 2 * width))):
        result = jnp.dot(held[:, :units], own_ref[:, at], preferred_element_type=jnp.float32)
        result += jnp.dot(held[:, units:], lent_ref[:, at], preferred_element_type=jnp.float32)
        out[...] = result.astype(out.dtype)


def finish(owned, slot, plan, sums, got, facts, before, down_own, down_lent):
    units = down_own.shape[0]
    width = down_own.shape[1] // 2
    pair = [
        jax.ShapeDtypeStruct((owned, width), jnp.bfloat16),
        jax.ShapeDtypeStruct((owned, width), jnp.float32),
    ]

    def first(plan_ref, sums_ref, got_ref, facts_ref, before_ref, own_ref, lent_ref, *out_refs):
        rows = collected_rows(owned, slot, plan_ref, sums_ref, got_ref, facts_ref, before_ref)
        down(rows[0].astype(jnp.bfloat16), own_ref, lent_ref, out_refs[0], out_refs[1])
        for index in range(1, 4):
            out_refs[2][(index - 1) * owned : index * owned, :] = rows[index].astype(jnp.bfloat16)

    def others(held_ref, own_ref, lent_ref, *out_refs):
        for index in range(3):
            held = held_ref[index * owned : (index + 1) * owned, :]
            down(held, own_ref, lent_ref, out_refs[2 * index], out_refs[2 * index + 1])

    held_shape = jax.ShapeDtypeStruct((3 * owned, 2 * units), jnp.bfloat16)
    sent, kept, held = on_core(first, pair + [held_shape], [SMEM] + [VMEM] * 6)(
        plan, sums, got, facts, before, down_own, down_lent
    )
    rest = on_core(others, pair * 3, [VMEM] * 3)(held, down_own, down_lent)
    return [sent, *rest[0::2]], [kept, *rest[1::2]]


def rows_travel(
    tokens, gate_weight, up_weight, down_weight, route_gates, block_list, block_count, owner_token
):
    position = lax.axis_index("blk")
    share = lax.axis_index("tp")
    row_count, width = tokens.shape
    units = gate_weight.shape[2]
    owned = row_count // 2
    half = row_count // 2
    plan = jnp.asarray(PLAN, jnp.int32)[position]

    own_far = across_chips(tokens)
    own = with_facts(
        tokens, route_gates.T, block_list[0], block_count[0], owner_token[None]
    )
    beside = along(own, BESIDE)
    middle = along(own, MIDDLE)

    gate_quarters = gate_weight[0].reshape(4, width, units)
    up_quarters = up_weight[0].reshape(4, width, units)

    def quarter(j):
        pair = [
            lax.dynamic_index_in_dim(q, share ^ j, 0, keepdims=False)
            for q in (gate_quarters, up_quarters)
        ]
        return jnp.concatenate(pair, axis=1)

    def down_part(j):
        return lax.dynamic_slice_in_dim(down_weight[0], (share ^ j) * width, width, 1)

    kept_in = jnp.concatenate([quarter(0), quarter(2)])
    lend_in = jnp.concatenate([quarter(1), quarter(3)])
    kept_down = jnp.concatenate([down_part(0), down_part(2)], axis=1)
    lend_down = jnp.concatenate([down_part(1), down_part(3)], axis=1)


    inner_last = along(beside, MIDDLE)
    outer_next = along(middle, OUTWARD)
    beside_far = across_chips(beside)
    inward_far = along(own_far[half:], INWARD)
    lent_in = across_cores(after(lend_in, beside, middle, own_far))
    weights = (kept_in, lent_in)
    sums_0, send_0 = partial_sums([row_count], [(tokens, own_far)], weights, (0, 1))
    got_0 = across_cores(send_0)

    outer_last = along(inner_last, OUTWARD)
    (second, second_facts) = chosen(
        plan,
        middle,
        outer_next,
        [(0, row_count), (row_count, FACT_ROWS)],
        beside_far,
        inner_last,
        inward_far,
    )
    second_far = across_chips(second)
    middle_far = along(inward_far, MIDDLE)
    lent_down = across_cores(after(lend_down, inner_last))
    sums_1, send_1 = partial_sums([row_count], [(beside, beside_far)], weights, (0, 1))
    got_1 = across_cores(send_1)

    last_a, last_b, last_facts = chosen(
        plan,
        inner_last,
        outer_last,
        [(0, half), (half, half), (row_count, FACT_ROWS)],
        second_far,
        middle_far,
        sums_0,
        sums_1,
    )
    last_far_a = across_chips(last_a)
    outward_far = along(middle_far, OUTWARD)
    total = collect(owned, 0, plan, sums_0, got_0, own[row_count:], None)
    total = collect(owned, 1, plan, sums_1, got_1, beside[row_count:], total)
    sums_2, send_2 = partial_sums([row_count], [(second, second_far)], weights, (0, 1))
    got_2 = across_cores(send_2)
    near = partial_sums([half, half], [(last_a,), (last_b,)], weights, (0,), send=False)[0]
    sums_3, send_3 = partial_sums(
        [half, half],
        [(last_far_a,), (outward_far,)],
        weights,
        (1,),
        before=near,
        choice=(plan, middle_far),
        waits=(total,),
    )
    got_3 = across_cores(send_3)
    total = collect(owned, 2, plan, sums_2, got_2, second_facts, total)
    sent, kept = finish(
        owned, 3, plan, sums_3, got_3, last_facts, total, kept_down, lent_down
    )
    chunks = [k + across_chips(s).astype(jnp.float32) for s, k in zip(sent, kept)]

    def send(block, route):
        return along(block.astype(jnp.bfloat16), route).astype(jnp.float32)

    inward = send(chunks[0], INWARD)
    middle = send(chunks[0], MIDDLE)
    two_on = send(chunks[1] + inward, TWO_ON)
    beside = send(chunks[2], BESIDE)
    return (chunks[3] + middle + two_on + beside).astype(jnp.bfloat16)


def on_device(*args):
    block_list = args[5]
    sizes = (lax.axis_size("blk"), lax.axis_size("tp"), block_list.shape[1])
    if sizes == (4, 4, 4):
        return rows_travel(*args)
    return weights_travel(*args)


def solution(mesh):
    return jax.shard_map(
        on_device,
        mesh=mesh,
        in_specs=(
            P(("groups", "blk"), "tp"),
            P("blk", None, "tp"),
            P("blk", None, "tp"),
            P("blk", "tp", None),
            P(("groups", "blk"), None),
            P(("groups", "blk"), None, None),
            P(("groups", "blk"), None),
            P(("groups", "blk")),
        ),
        out_specs=P(("groups", "blk"), "tp"),
        check_vma=False,
    )
```

```python
import jax
import jax.numpy as jnp
from jax import lax
from jax.experimental import pallas as pl
from jax.experimental.pallas import tpu as pltpu
from jax.sharding import PartitionSpec as P


def shifted(block, axis, distance):
    devices = range(lax.axis_size(axis))
    route = [((i - distance) % len(devices), i) for i in devices]
    return lax.ppermute(block, axis, route)


def weights_travel(
    tokens, gate_weight, up_weight, down_weight, route_gates, block_list, block_count, owner_token
):
    whole_rows = lax.all_gather(tokens, "tp", axis=1, tiled=True)
    row_count = whole_rows.shape[0]
    width = whole_rows.shape[1]
    offsets_all = block_list.shape[1]
    block_total = block_list.shape[2]
    block_size = row_count // block_total
    blocks = whole_rows.reshape(block_total, block_size, width)
    gate_blocks = route_gates.reshape(block_total, block_size, offsets_all)
    totals = jnp.zeros((block_total, block_size, width), jnp.float32)

    def apply(totals, weights, offset, block_id):
        w_gate, w_up, w_down = weights
        block_rows = lax.dynamic_index_in_dim(blocks, block_id, 0, keepdims=False)
        gate_out = jnp.dot(block_rows, w_gate, preferred_element_type=jnp.float32)
        up_out = jnp.dot(block_rows, w_up, preferred_element_type=jnp.float32)
        hidden = (jax.nn.silu(gate_out) * up_out).astype(jnp.bfloat16)
        block_gates = lax.dynamic_index_in_dim(gate_blocks, block_id, 0, keepdims=False)
        factor = lax.dynamic_index_in_dim(block_gates, offset, 1, keepdims=False)
        product = jnp.dot(hidden, w_down, preferred_element_type=jnp.float32) * factor[:, None]
        before = lax.dynamic_index_in_dim(totals, block_id, 0, keepdims=False)
        return lax.dynamic_update_index_in_dim(totals, before + product, block_id, 0)

    resident = (gate_weight[0], up_weight[0], down_weight[0])
    arrived = [resident]
    holding = resident
    for offset in range(1, offsets_all):
        holding = shifted((holding[0], holding[1], holding[2]), "blk", 1)
        arrived.append(holding)
    for offset in range(offsets_all):
        weights = arrived[offset]

        def visit_block(position, totals, weights=weights, offset=offset):
            return apply(totals, weights, offset, block_list[0, offset, position])

        totals = lax.fori_loop(0, block_count[0, offset], visit_block, totals)
    summed = lax.psum_scatter(
        totals.reshape(row_count, width).astype(jnp.bfloat16), "tp", scatter_dimension=1, tiled=True
    )
    feature_share = summed.shape[1]
    cycle_size = lax.axis_size("blk")
    owned = row_count // 2
    capacity = max(2, 2 * row_count // cycle_size)
    target = owner_token // owned
    local_token = owner_token % owned
    target_table = (target[:, None] == jnp.arange(cycle_size, dtype=jnp.int32)[None, :]).astype(
        jnp.int32
    )
    running = jnp.cumsum(target_table, axis=0)
    rank = jnp.sum((running - 1) * target_table, axis=1)
    slot = target * capacity + rank
    send_rows = jnp.zeros((cycle_size * capacity, feature_share), jnp.bfloat16).at[slot].set(summed)
    send_index = jnp.full((cycle_size * capacity,), -1, jnp.int32).at[slot].set(local_token)
    send_rows = send_rows.reshape(cycle_size, capacity, feature_share)
    send_index = send_index.reshape(cycle_size, capacity)
    got_rows, got_index = (
        lax.all_to_all(send_rows, "blk", split_axis=0, concat_axis=0, tiled=True),
        lax.all_to_all(send_index, "blk", split_axis=0, concat_axis=0, tiled=True),
    )
    got_rows = got_rows.reshape(cycle_size * capacity, feature_share)
    got_index = got_index.reshape(cycle_size * capacity)
    placing = (got_index[:, None] == jnp.arange(owned, dtype=jnp.int32)[None, :]).astype(
        jnp.bfloat16
    )
    combined = lax.dot_general(
        placing, got_rows, (((0,), (0,)), ((), ())), preferred_element_type=jnp.float32
    )
    return combined.astype(jnp.bfloat16)


BESIDE = [(0, 1), (1, 0), (2, 3), (3, 2)]
MIDDLE = [(1, 2), (2, 1)]
INWARD = [(0, 1), (3, 2)]
OUTWARD = [(1, 0), (2, 3)]
TWO_IN = [(0, 2), (3, 1)]
TWO_OUT = [(1, 3), (2, 0)]
PLAN = [
    [3, 2, 1, 0, 0, 1, 2, 3, 0],
    [2, 3, 0, 1, 0, 3, 1, 2, 1],
    [1, 0, 3, 2, 0, 1, 3, 2, 1],
    [0, 1, 2, 3, 0, 3, 2, 1, 0],
]
OFFSETS_AT, INNER_AT = 4, 8
FACT_ROWS = 16
VMEM = pl.BlockSpec(memory_space=pltpu.VMEM)
SMEM = pl.BlockSpec(memory_space=pltpu.SMEM)
ANYWHERE = pl.BlockSpec(memory_space=pl.ANY)


def across_chips(block):
    return lax.ppermute(block, "tp", [(i, i ^ 2) for i in range(4)])


def across_cores(block):
    return lax.ppermute(block, "tp", [(i, i ^ 1) for i in range(4)])


def along(block, route):
    return lax.ppermute(block, "blk", route)


def on_core(body, out_shape, in_specs, flops=1024):
    return pl.pallas_call(
        body,
        out_shape=out_shape,
        in_specs=in_specs,
        out_specs=jax.tree.map(lambda _: VMEM, out_shape),
        compiler_params=pltpu.CompilerParams(vmem_limit_bytes=40 * 2**20),
        cost_estimate=pl.CostEstimate(flops=flops, bytes_accessed=1024, transcendentals=0),
    )


def after(block, *others):
    return pl.pallas_call(
        lambda *refs: None,
        out_shape=jax.ShapeDtypeStruct(block.shape, block.dtype),
        in_specs=[ANYWHERE] * (1 + len(others)),
        out_specs=ANYWHERE,
        input_output_aliases={0: 0},
        cost_estimate=pl.CostEstimate(flops=16, bytes_accessed=16, transcendentals=0),
    )(block, *others)


def lower_half(block):
    rows = block.shape[0] // 2

    def body(block_ref, out_ref, sem):
        copy = pltpu.make_async_copy(block_ref.at[pl.ds(rows, rows)], out_ref, sem)
        copy.start()
        copy.wait()

    return pl.pallas_call(
        body,
        out_shape=jax.ShapeDtypeStruct((rows, block.shape[1]), block.dtype),
        in_specs=[ANYWHERE],
        out_specs=VMEM,
        scratch_shapes=[pltpu.SemaphoreType.DMA],
        cost_estimate=pl.CostEstimate(flops=1024, bytes_accessed=1024, transcendentals=0),
    )(block)


def chosen(plan, if_inner, if_outer, spans, *others):
    width = if_inner.shape[1]

    def body(plan_ref, inner_ref, outer_ref, *rest):
        out_refs, sems = rest[len(others) : -1], rest[-1]

        def copy_from(source):
            copies = [
                pltpu.make_async_copy(source.at[pl.ds(start, size)], out, sems.at[index])
                for index, ((start, size), out) in enumerate(zip(spans, out_refs))
            ]
            for copy in copies:
                copy.start()
            for copy in copies:
                copy.wait()

        @pl.when(plan_ref[INNER_AT] == 1)
        def _():
            copy_from(inner_ref)

        @pl.when(plan_ref[INNER_AT] == 0)
        def _():
            copy_from(outer_ref)

    return pl.pallas_call(
        body,
        out_shape=[jax.ShapeDtypeStruct((size, width), if_inner.dtype) for _, size in spans],
        in_specs=[SMEM] + [ANYWHERE] * (2 + len(others)),
        out_specs=[VMEM] * len(spans),
        scratch_shapes=[pltpu.SemaphoreType.DMA((len(spans),))],
        cost_estimate=pl.CostEstimate(flops=16, bytes_accessed=16, transcendentals=0),
    )(plan, if_inner, if_outer, *others)


def with_facts(rows, gates, block_list, block_count, owner):
    count, width = rows.shape
    offsets, blocks = block_list.shape
    total = owner.shape[1]

    def body(rows_ref, gates_ref, list_ref, count_ref, owner_ref, out_ref, sem):
        copy = pltpu.make_async_copy(rows_ref, out_ref.at[pl.ds(0, count)], sem)
        copy.start()
        block_of = lax.broadcasted_iota(jnp.int32, (1, total), 1) // (total // blocks)
        facts = []
        for offset in range(offsets):
            mask = jnp.zeros((1, total), jnp.float32)
            for block in range(blocks):
                used = jnp.int32(0)
                for place in range(blocks):
                    found = (list_ref[offset, place] == block) & (place < count_ref[offset])
                    used = used | found.astype(jnp.int32)
                mask = mask + jnp.where(block_of == block, used.astype(jnp.float32), 0.0)
            facts.append(gates_ref[offset : offset + 1, :] * mask)
        facts.append((owner_ref[...] >> 8).astype(jnp.float32))
        facts.append((owner_ref[...] & 255).astype(jnp.float32))
        facts.append(jnp.zeros((FACT_ROWS - len(facts), total), jnp.float32))
        out_ref[count:, :] = jnp.zeros((FACT_ROWS, width), jnp.bfloat16)
        out_ref[count:, :total] = jnp.concatenate(facts, axis=0).astype(jnp.bfloat16)
        copy.wait()

    return pl.pallas_call(
        body,
        out_shape=jax.ShapeDtypeStruct((count + FACT_ROWS, width), rows.dtype),
        in_specs=[ANYWHERE, VMEM, SMEM, SMEM, VMEM],
        out_specs=VMEM,
        scratch_shapes=[pltpu.SemaphoreType.DMA],
        compiler_params=pltpu.CompilerParams(vmem_limit_bytes=40 * 2**20),
        cost_estimate=pl.CostEstimate(flops=1024, bytes_accessed=1024, transcendentals=0),
    )(rows, gates, block_list, block_count, owner)


def partial_sums(
    sizes, parts, weights, places, before=None, send=True, choice=None, waits=()
):
    width, columns = weights[0].shape
    blocks = [block for part in parts for block in part]
    used = [weights[place] for place in places] + [weights[2]]
    operands = blocks + used
    specs = [VMEM] * len(operands)
    if before is not None:
        operands.append(before)
        specs.append(VMEM)
    if choice is not None:
        operands += [choice[0], choice[1]]
        specs += [SMEM, VMEM]
    operands += waits
    specs += [ANYWHERE] * len(waits)

    def body(*refs):
        results = refs[len(operands) :]
        weight_refs = refs[len(blocks) : len(blocks) + len(used)]
        next_ref = len(blocks) + len(used)
        before_ref = refs[next_ref] if before is not None else None
        next_ref += before is not None
        start = 0
        for part, size in enumerate(sizes):
            span = slice(start, start + size)
            start += size
            rows = [refs[part * len(places) + index][:size, :] for index in range(len(places))]
            if choice is not None and part == len(sizes) - 1:
                rows[0] = jnp.where(refs[next_ref][INNER_AT] == 1, refs[next_ref + 1][:size, :], rows[0])
            for side in range(2):
                at = slice(side * columns, (side + 1) * columns)
                total = None if before is None else before_ref[span, at]
                for index, place in enumerate(places):
                    if side == 0:
                        weight = weight_refs[index][...]
                    else:
                        weight = weight_refs[-1][place * width : (place + 1) * width, :]
                    product = jnp.dot(rows[index], weight, preferred_element_type=jnp.float32)
                    total = product if total is None else total + product
                results[0][span, at] = total
                if send:
                    results[1][span, at] = total.astype(jnp.bfloat16)

    size = (sum(sizes), 2 * columns)
    shapes = [jax.ShapeDtypeStruct(size, jnp.float32)]
    if send:
        shapes.append(jax.ShapeDtypeStruct(size, jnp.bfloat16))
    return on_core(body, shapes, specs)(*operands)


def collected_rows(owned, slot, plan, sums, got, facts, before):
    units = sums.shape[1] // 4
    hidden = []
    for core in range(2):
        here, there = 2 * core * units, 2 * (1 - core) * units
        gate = sums[:, here : here + units] + got[:, there : there + units].astype(jnp.float32)
        up = sums[:, here + units : here + 2 * units]
        up = up + got[:, there + units : there + 2 * units].astype(jnp.float32)
        hidden.append((gate / (1.0 + jnp.exp(-gate)) * up).astype(jnp.bfloat16))
    hidden = jnp.concatenate(hidden, axis=1)
    values = facts[:, : sums.shape[0]].astype(jnp.float32)
    kind = lax.broadcasted_iota(jnp.int32, (FACT_ROWS, 1), 0)
    mine = kind == plan[OFFSETS_AT + slot]
    factor = jnp.sum(jnp.where(mine, values, 0.0), axis=0, keepdims=True)
    owner = (values[4:5, :] * 256.0 + values[5:6, :]).astype(jnp.int32)
    results = []
    for index in range(4):
        token = plan[index] * owned + lax.broadcasted_iota(jnp.int32, (owned, 1), 0)
        placing = jnp.where(owner == token, factor, 0.0).astype(jnp.bfloat16)
        rows = jnp.dot(placing, hidden, preferred_element_type=jnp.float32)
        if before is not None:
            rows = rows + before[index * owned : (index + 1) * owned, :]
        results.append(rows)
    return results


def collect(owned, slot, plan, sums, got, facts, before):
    operands = [plan, sums, got, facts] + ([] if before is None else [before])

    def body(plan_ref, sums_ref, got_ref, facts_ref, *rest):
        before_ref = rest[0] if before is not None else None
        rows = collected_rows(owned, slot, plan_ref, sums_ref, got_ref, facts_ref, before_ref)
        for index in range(4):
            rest[-1][index * owned : (index + 1) * owned, :] = rows[index]

    shape = jax.ShapeDtypeStruct((4 * owned, sums.shape[1] // 2), jnp.float32)
    return on_core(body, shape, [SMEM] + [VMEM] * (len(operands) - 1))(*operands)


def down(held, own_ref, lent_ref, sent_ref, kept_ref):
    units, width = own_ref.shape[0], kept_ref.shape[1]
    for out, at in ((kept_ref, slice(0, width)), (sent_ref, slice(width, 2 * width))):
        result = jnp.dot(held[:, :units], own_ref[:, at], preferred_element_type=jnp.float32)
        result += jnp.dot(held[:, units:], lent_ref[:, at], preferred_element_type=jnp.float32)
        out[...] = result.astype(out.dtype)


def finish(owned, slot, plan, sums, got, facts, before, down_own, down_lent):
    units = down_own.shape[0]
    width = down_own.shape[1] // 2
    pair = [
        jax.ShapeDtypeStruct((owned, width), jnp.bfloat16),
        jax.ShapeDtypeStruct((owned, width), jnp.float32),
    ]

    def first(plan_ref, sums_ref, got_ref, facts_ref, before_ref, own_ref, lent_ref, *out_refs):
        rows = collected_rows(owned, slot, plan_ref, sums_ref, got_ref, facts_ref, before_ref)
        down(rows[0].astype(jnp.bfloat16), own_ref, lent_ref, out_refs[0], out_refs[1])
        for index in range(1, 4):
            out_refs[2][(index - 1) * owned : index * owned, :] = rows[index].astype(jnp.bfloat16)

    def others(indices, waits):
        def body(held_ref, own_ref, lent_ref, *refs):
            out_refs = refs[len(waits) :]
            for place, index in enumerate(indices):
                held = held_ref[(index - 1) * owned : index * owned, :]
                down(held, own_ref, lent_ref, out_refs[2 * place], out_refs[2 * place + 1])

        specs = [VMEM] * 3 + [ANYWHERE] * len(waits)
        return on_core(body, pair * len(indices), specs)(held, down_own, down_lent, *waits)

    def joined(sent, kept):
        return kept + across_chips(sent).astype(jnp.float32)

    held_shape = jax.ShapeDtypeStruct((3 * owned, 2 * units), jnp.bfloat16)
    sent, kept, held = on_core(first, pair + [held_shape], [SMEM] + [VMEM] * 6)(
        plan, sums, got, facts, before, down_own, down_lent
    )
    got_first = across_chips(sent)
    chunks = [kept + got_first.astype(jnp.float32), joined(*others([1], []))]
    rest = others([2, 3], [got_first])
    return chunks + [joined(rest[0], rest[1]), joined(rest[2], rest[3])]


def rows_travel(
    tokens, gate_weight, up_weight, down_weight, route_gates, block_list, block_count, owner_token
):
    position = lax.axis_index("blk")
    share = lax.axis_index("tp")
    row_count, width = tokens.shape
    units = gate_weight.shape[2]
    owned = row_count // 2
    half = row_count // 2
    plan = jnp.asarray(PLAN, jnp.int32)[position]

    own_far = across_chips(tokens)
    own = with_facts(
        tokens, route_gates.T, block_list[0], block_count[0], owner_token[None]
    )
    beside = along(own, BESIDE)
    middle = along(own, MIDDLE)

    gate_quarters = gate_weight[0].reshape(4, width, units)
    up_quarters = up_weight[0].reshape(4, width, units)

    def quarter(j):
        pair = [
            lax.dynamic_index_in_dim(q, share ^ j, 0, keepdims=False)
            for q in (gate_quarters, up_quarters)
        ]
        return jnp.concatenate(pair, axis=1)

    def down_part(j):
        return lax.dynamic_slice_in_dim(down_weight[0], (share ^ j) * width, width, 1)

    kept_down = jnp.concatenate([down_part(0), down_part(2)], axis=1)
    lend_down = jnp.concatenate([down_part(1), down_part(3)], axis=1)


    inner_last = along(beside, MIDDLE)
    outer_next = along(middle, OUTWARD)
    beside_far = across_chips(beside)
    inward_far = along(lower_half(own_far), INWARD)
    lend = jnp.concatenate([quarter(1), quarter(3)])
    lent = across_cores(after(lend, beside, middle, own_far))
    weights = [quarter(0), quarter(2), lent]
    sums_0, send_0 = partial_sums([row_count], [(tokens, own_far)], weights, (0, 1))
    got_0 = across_cores(send_0)
    lent_down = across_cores(lend_down)

    outer_last = along(inner_last, OUTWARD)
    (second, second_facts) = chosen(
        plan,
        middle,
        outer_next,
        [(0, row_count), (row_count, FACT_ROWS)],
        beside_far,
        inner_last,
        inward_far,
        lend_down,
        weights[0],
        weights[1],
    )
    second_far = across_chips(second)
    middle_far = along(inward_far, MIDDLE)
    sums_1, send_1 = partial_sums([row_count], [(beside, beside_far)], weights, (0, 1))
    got_1 = across_cores(send_1)

    last_a, last_b, last_facts = chosen(
        plan,
        inner_last,
        outer_last,
        [(0, half), (half, half), (row_count, FACT_ROWS)],
        second_far,
        middle_far,
        sums_0,
        sums_1,
    )
    last_far_a = across_chips(last_a)
    outward_far = along(middle_far, OUTWARD)
    total = collect(owned, 0, plan, sums_0, got_0, own[row_count:], None)
    total = collect(owned, 1, plan, sums_1, got_1, beside[row_count:], total)
    sums_2, send_2 = partial_sums([row_count], [(second, second_far)], weights, (0, 1))
    got_2 = across_cores(send_2)
    near = partial_sums([half, half], [(last_a,), (last_b,)], weights, (0,), send=False)[0]
    sums_3, send_3 = partial_sums(
        [half, half],
        [(last_far_a,), (outward_far,)],
        weights,
        (1,),
        before=near,
        choice=(plan, middle_far),
        waits=(total,),
    )
    got_3 = across_cores(send_3)
    total = collect(owned, 2, plan, sums_2, got_2, second_facts, total)
    chunks = finish(
        owned, 3, plan, sums_3, got_3, last_facts, total, kept_down, lent_down
    )

    def send(block, route):
        return along(block.astype(jnp.bfloat16), route).astype(jnp.float32)

    inward = send(chunks[0], INWARD)
    middle = send(chunks[0], MIDDLE)
    two_in = send(chunks[1], TWO_IN)
    two_out = send(chunks[1] + inward, TWO_OUT)
    beside = send(chunks[2], BESIDE)
    return (chunks[3] + middle + two_in + two_out + beside).astype(jnp.bfloat16)


def on_device(*args):
    block_list = args[5]
    sizes = (lax.axis_size("blk"), lax.axis_size("tp"), block_list.shape[1])
    if sizes == (4, 4, 4):
        return rows_travel(*args)
    return weights_travel(*args)


def solution(mesh):
    return jax.shard_map(
        on_device,
        mesh=mesh,
        in_specs=(
            P(("groups", "blk"), "tp"),
            P("blk", None, "tp"),
            P("blk", None, "tp"),
            P("blk", "tp", None),
            P(("groups", "blk"), None),
            P(("groups", "blk"), None, None),
            P(("groups", "blk"), None),
            P(("groups", "blk")),
        ),
        out_specs=P(("groups", "blk"), "tp"),
        check_vma=False,
    )
```

```python
import jax
import jax.numpy as jnp
from jax import lax
from jax.experimental import pallas as pl
from jax.experimental.pallas import tpu as pltpu
from jax.sharding import PartitionSpec as P


def shifted(block, axis, distance):
    devices = range(lax.axis_size(axis))
    route = [((i - distance) % len(devices), i) for i in devices]
    return lax.ppermute(block, axis, route)


def weights_travel(
    tokens, gate_weight, up_weight, down_weight, route_gates, block_list, block_count, owner_token
):
    whole_rows = lax.all_gather(tokens, "tp", axis=1, tiled=True)
    row_count = whole_rows.shape[0]
    width = whole_rows.shape[1]
    offsets_all = block_list.shape[1]
    block_total = block_list.shape[2]
    block_size = row_count // block_total
    blocks = whole_rows.reshape(block_total, block_size, width)
    gate_blocks = route_gates.reshape(block_total, block_size, offsets_all)
    totals = jnp.zeros((block_total, block_size, width), jnp.float32)

    def apply(totals, weights, offset, block_id):
        w_gate, w_up, w_down = weights
        block_rows = lax.dynamic_index_in_dim(blocks, block_id, 0, keepdims=False)
        gate_out = jnp.dot(block_rows, w_gate, preferred_element_type=jnp.float32)
        up_out = jnp.dot(block_rows, w_up, preferred_element_type=jnp.float32)
        hidden = (jax.nn.silu(gate_out) * up_out).astype(jnp.bfloat16)
        block_gates = lax.dynamic_index_in_dim(gate_blocks, block_id, 0, keepdims=False)
        factor = lax.dynamic_index_in_dim(block_gates, offset, 1, keepdims=False)
        product = jnp.dot(hidden, w_down, preferred_element_type=jnp.float32) * factor[:, None]
        before = lax.dynamic_index_in_dim(totals, block_id, 0, keepdims=False)
        return lax.dynamic_update_index_in_dim(totals, before + product, block_id, 0)

    resident = (gate_weight[0], up_weight[0], down_weight[0])
    arrived = [resident]
    holding = resident
    for offset in range(1, offsets_all):
        holding = shifted((holding[0], holding[1], holding[2]), "blk", 1)
        arrived.append(holding)
    for offset in range(offsets_all):
        weights = arrived[offset]

        def visit_block(position, totals, weights=weights, offset=offset):
            return apply(totals, weights, offset, block_list[0, offset, position])

        totals = lax.fori_loop(0, block_count[0, offset], visit_block, totals)
    summed = lax.psum_scatter(
        totals.reshape(row_count, width).astype(jnp.bfloat16), "tp", scatter_dimension=1, tiled=True
    )
    feature_share = summed.shape[1]
    cycle_size = lax.axis_size("blk")
    owned = row_count // 2
    capacity = max(2, 2 * row_count // cycle_size)
    target = owner_token // owned
    local_token = owner_token % owned
    target_table = (target[:, None] == jnp.arange(cycle_size, dtype=jnp.int32)[None, :]).astype(
        jnp.int32
    )
    running = jnp.cumsum(target_table, axis=0)
    rank = jnp.sum((running - 1) * target_table, axis=1)
    slot = target * capacity + rank
    send_rows = jnp.zeros((cycle_size * capacity, feature_share), jnp.bfloat16).at[slot].set(summed)
    send_index = jnp.full((cycle_size * capacity,), -1, jnp.int32).at[slot].set(local_token)
    send_rows = send_rows.reshape(cycle_size, capacity, feature_share)
    send_index = send_index.reshape(cycle_size, capacity)
    got_rows, got_index = (
        lax.all_to_all(send_rows, "blk", split_axis=0, concat_axis=0, tiled=True),
        lax.all_to_all(send_index, "blk", split_axis=0, concat_axis=0, tiled=True),
    )
    got_rows = got_rows.reshape(cycle_size * capacity, feature_share)
    got_index = got_index.reshape(cycle_size * capacity)
    placing = (got_index[:, None] == jnp.arange(owned, dtype=jnp.int32)[None, :]).astype(
        jnp.bfloat16
    )
    combined = lax.dot_general(
        placing, got_rows, (((0,), (0,)), ((), ())), preferred_element_type=jnp.float32
    )
    return combined.astype(jnp.bfloat16)


BESIDE = [(0, 1), (1, 0), (2, 3), (3, 2)]
MIDDLE = [(1, 2), (2, 1)]
INWARD = [(0, 1), (3, 2)]
OUTWARD = [(1, 0), (2, 3)]
TWO_IN = [(0, 2), (3, 1)]
TWO_OUT = [(1, 3), (2, 0)]
PLAN = [
    [3, 2, 1, 0, 0, 1, 2, 3, 0],
    [2, 3, 0, 1, 0, 3, 1, 2, 1],
    [1, 0, 3, 2, 0, 1, 3, 2, 1],
    [0, 1, 2, 3, 0, 3, 2, 1, 0],
]
OFFSETS_AT, INNER_AT = 4, 8
FACT_ROWS = 16
VMEM = pl.BlockSpec(memory_space=pltpu.VMEM)
SMEM = pl.BlockSpec(memory_space=pltpu.SMEM)
ANYWHERE = pl.BlockSpec(memory_space=pl.ANY)


def across_chips(block):
    return lax.ppermute(block, "tp", [(i, i ^ 2) for i in range(4)])


def across_cores(block):
    return lax.ppermute(block, "tp", [(i, i ^ 1) for i in range(4)])


def along(block, route):
    return lax.ppermute(block, "blk", route)


def cheap():
    return pl.CostEstimate(flops=1024, bytes_accessed=1024, transcendentals=0)


TOKEN = jax.ShapeDtypeStruct((8, 128), jnp.float32)
VMEM_LIMIT = 40 * 2**20


def on_core(body, out_shape, in_specs, scratch=()):
    return pl.pallas_call(
        body,
        out_shape=out_shape,
        in_specs=in_specs,
        out_specs=jax.tree.map(lambda _: VMEM, out_shape),
        scratch_shapes=scratch,
        compiler_params=pltpu.CompilerParams(vmem_limit_bytes=VMEM_LIMIT),
        cost_estimate=cheap(),
    )


def copies(source, start, target, size, pieces, sems, first):
    step = size // pieces
    return [
        pltpu.make_async_copy(
            source.at[pl.ds(start + index * step, step)],
            target.at[pl.ds(index * step, step)],
            sems.at[first + index],
        )
        for index in range(pieces)
    ]


def after(block, *others):
    return pl.pallas_call(
        lambda *refs: None,
        out_shape=jax.ShapeDtypeStruct(block.shape, block.dtype),
        in_specs=[ANYWHERE] * (1 + len(others)),
        out_specs=ANYWHERE,
        input_output_aliases={0: 0},
        cost_estimate=cheap(),
    )(block, *others)


def moved(sources_of, shapes_out, operands, specs, flag=False, flops=1024):
    kinds = sources_of if flag else [sources_of]
    total = sum(pieces for _, _, _, pieces in kinds[0])

    def body(*refs):
        out_refs = refs[len(operands) : len(operands) + len(shapes_out)]
        buffers = refs[len(operands) + len(shapes_out) : -2]
        in_sems, out_sems = refs[-2:]

        def run(sources):
            first, inward, outward = 0, [], []
            for (index, start, size, pieces), out, buffer in zip(sources, out_refs, buffers):
                inward += copies(refs[index], start, buffer, size, pieces, in_sems, first)
                outward += copies(buffer, 0, out, size, pieces, out_sems, first)
                first += pieces
            for copy in inward:
                copy.start()
            for copy, next_copy in zip(inward, outward):
                copy.wait()
                next_copy.start()
            for copy in outward:
                copy.wait()

        if flag:
            for kind, sources in enumerate(kinds):

                @pl.when(refs[0][INNER_AT] == kind)
                def _(sources=sources):
                    run(sources)

        else:
            run(kinds[0])

    return pl.pallas_call(
        body,
        out_shape=shapes_out,
        in_specs=specs,
        out_specs=[ANYWHERE] * len(shapes_out),
        scratch_shapes=[pltpu.VMEM(shape.shape, shape.dtype) for shape in shapes_out]
        + [pltpu.SemaphoreType.DMA((total,))] * 2,
        compiler_params=pltpu.CompilerParams(vmem_limit_bytes=VMEM_LIMIT),
        cost_estimate=pl.CostEstimate(flops=flops, bytes_accessed=1024, transcendentals=0),
    )(*operands)


def lower_half(block):
    rows = block.shape[0] // 2
    shape = jax.ShapeDtypeStruct((rows, block.shape[1]), block.dtype)
    return moved([(0, rows, rows, 4)], [shape], [block], [ANYWHERE], flops=8 * 2**30)[0]


def chosen(plan, if_inner, if_outer, spans, *others):
    shapes = [
        jax.ShapeDtypeStruct((size, if_inner.shape[1]), if_inner.dtype) for _, size, _ in spans
    ]
    kinds = [[(index, *span) for span in spans] for index in (2, 1)]
    operands = [plan, if_inner, if_outer, *others]
    return moved(kinds, shapes, operands, [SMEM] + [ANYWHERE] * (len(operands) - 1), flag=True)


def with_facts(rows, gates, block_list, block_count, owner):
    count, width = rows.shape
    blocks, _, offsets = block_list.shape
    total = owner.shape[0]

    def body(rows_ref, gates_ref, list_ref, count_ref, owner_ref, out_ref, sems):
        moves = copies(rows_ref, 0, out_ref, count, 4, sems, 0)
        for copy in moves:
            copy.start()
        block_of = lax.broadcasted_iota(jnp.int32, (1, total), 1) // (total // blocks)
        facts = []
        for offset in range(offsets):
            mask = jnp.zeros((1, total), jnp.float32)
            for block in range(blocks):
                used = jnp.int32(0)
                for place in range(blocks):
                    found = (list_ref[place, 0, offset] == block) & (place < count_ref[0, offset])
                    used = used | found.astype(jnp.int32)
                mask = mask + jnp.where(block_of == block, used.astype(jnp.float32), 0.0)
            facts.append(gates_ref[offset : offset + 1, :] * mask)
        numbers = owner_ref[...].reshape(1, total)
        facts.append((numbers >> 8).astype(jnp.float32))
        facts.append((numbers & 255).astype(jnp.float32))
        facts.append(jnp.zeros((FACT_ROWS - len(facts), total), jnp.float32))
        out_ref[count:, :] = jnp.zeros((FACT_ROWS, width), jnp.bfloat16)
        out_ref[count:, :total] = jnp.concatenate(facts, axis=0).astype(jnp.bfloat16)
        for copy in moves:
            copy.wait()

    shape = jax.ShapeDtypeStruct((count + FACT_ROWS, width), rows.dtype)
    return on_core(
        body, shape, [ANYWHERE, VMEM, SMEM, SMEM, VMEM], [pltpu.SemaphoreType.DMA((4,))]
    )(rows, gates, block_list, block_count, owner)


def partial_sums(
    sizes, parts, weights, places, before=None, send=True, choice=None, waits=()
):
    width, columns = weights[0].shape
    rows, count = sum(sizes), len(places)
    blocks = [block for part in parts for block in part]
    operands = blocks + [weights[place] for place in places] + [weights[2]]
    specs = [ANYWHERE] * len(operands)
    flag_at = len(operands)
    if choice is not None:
        operands += [choice[0], choice[1]]
        specs += [SMEM, ANYWHERE]
    before_at = len(operands)
    if before is not None:
        operands.append(before)
        specs.append(VMEM)
    operands += waits
    specs += [VMEM] * len(waits)
    row_pieces, weight_pieces = 2, 2
    row_sems = len(blocks) * row_pieces

    def body(*refs):
        results = refs[len(operands) : -4]
        row_buffer, weight_buffer, sems, weight_sems = refs[-4:]
        row_moves, weight_moves = [], [[], []]
        for part, size in enumerate(sizes):
            for index in range(count):
                block = part * count + index
                target = row_buffer.at[index, pl.ds(sum(sizes[:part]), size)]
                first = block * row_pieces
                move = copies(refs[block], 0, target, size, row_pieces, sems, first)
                if choice is not None and part == len(sizes) - 1:
                    source = refs[flag_at + 1]
                    other = copies(source, 0, target, size, row_pieces, sems, first)
                    for kind, group in enumerate((move, other)):

                        @pl.when(refs[flag_at][INNER_AT] == kind)
                        def _(group=group):
                            for copy in group:
                                copy.start()

                else:
                    for copy in move:
                        copy.start()
                row_moves += move
        for side in range(2):
            for index, place in enumerate(places):
                source = refs[len(blocks) + index] if side == 0 else refs[len(blocks) + count]
                weight_moves[side] += copies(
                    source,
                    0 if side == 0 else place * width,
                    weight_buffer.at[side, index],
                    width,
                    weight_pieces,
                    weight_sems,
                    (side * count + index) * weight_pieces,
                )
            for copy in weight_moves[side]:
                copy.start()
        for copy in row_moves:
            copy.wait()
        for side in range(2):
            for copy in weight_moves[side]:
                copy.wait()
            at = slice(side * columns, (side + 1) * columns)
            total = None if before is None else refs[before_at][:, at]
            for index in range(count):
                product = jnp.dot(
                    row_buffer[index],
                    weight_buffer[side, index],
                    preferred_element_type=jnp.float32,
                )
                total = product if total is None else total + product
            results[0][:, at] = total
            if send:
                results[1][:, at] = total.astype(jnp.bfloat16)
        results[-1][...] = jnp.zeros(TOKEN.shape, TOKEN.dtype)

    shapes = [jax.ShapeDtypeStruct((rows, 2 * columns), jnp.float32)]
    if send:
        shapes.append(jax.ShapeDtypeStruct((rows, 2 * columns), jnp.bfloat16))
    scratch = [
        pltpu.VMEM((count, rows, width), jnp.bfloat16),
        pltpu.VMEM((2, count, width, columns), jnp.bfloat16),
        pltpu.SemaphoreType.DMA((row_sems,)),
        pltpu.SemaphoreType.DMA((2 * count * weight_pieces,)),
    ]
    return on_core(body, shapes + [TOKEN], specs, scratch)(*operands)


def collected_rows(owned, slot, plan, sums, got, facts, before):
    units = sums.shape[1] // 4
    hidden = []
    for core in range(2):
        here, there = 2 * core * units, 2 * (1 - core) * units
        gate = sums[:, here : here + units] + got[:, there : there + units].astype(jnp.float32)
        up = sums[:, here + units : here + 2 * units]
        up = up + got[:, there + units : there + 2 * units].astype(jnp.float32)
        hidden.append((gate / (1.0 + jnp.exp(-gate)) * up).astype(jnp.bfloat16))
    hidden = jnp.concatenate(hidden, axis=1)
    values = facts[:, : sums.shape[0]].astype(jnp.float32)
    kind = lax.broadcasted_iota(jnp.int32, (FACT_ROWS, 1), 0)
    mine = kind == plan[OFFSETS_AT + slot]
    factor = jnp.sum(jnp.where(mine, values, 0.0), axis=0, keepdims=True)
    owner = (values[4:5, :] * 256.0 + values[5:6, :]).astype(jnp.int32)
    results = []
    for index in range(4):
        token = plan[index] * owned + lax.broadcasted_iota(jnp.int32, (owned, 1), 0)
        placing = jnp.where(owner == token, factor, 0.0).astype(jnp.bfloat16)
        rows = jnp.dot(placing, hidden, preferred_element_type=jnp.float32)
        if before is not None:
            rows = rows + before[index * owned : (index + 1) * owned, :]
        results.append(rows)
    return results


def fact_scratch(width):
    return [pltpu.VMEM((FACT_ROWS, width), jnp.bfloat16), pltpu.SemaphoreType.DMA((1,))]


def facts_of(facts_ref, buffer, sem):
    last = facts_ref.shape[0] - FACT_ROWS
    (copy,) = copies(facts_ref, last, buffer, FACT_ROWS, 1, sem, 0)
    copy.start()
    copy.wait()
    return buffer


def collect(owned, slot, plan, sums, got, facts, before):
    operands = [plan, sums, got, facts] + ([] if before is None else [before])

    def body(plan_ref, sums_ref, got_ref, facts_ref, *rest):
        before_ref = rest[0] if before is not None else None
        out_ref, token_ref, buffer, sem = rest[-4:]
        facts_here = facts_of(facts_ref, buffer, sem)
        rows = collected_rows(owned, slot, plan_ref, sums_ref, got_ref, facts_here, before_ref)
        for index in range(4):
            out_ref[index * owned : (index + 1) * owned, :] = rows[index]
        token_ref[...] = jnp.zeros(TOKEN.shape, TOKEN.dtype)

    shape = jax.ShapeDtypeStruct((4 * owned, sums.shape[1] // 2), jnp.float32)
    specs = [SMEM, VMEM, VMEM, ANYWHERE] + [VMEM] * (len(operands) - 4)
    return on_core(body, [shape, TOKEN], specs, fact_scratch(facts.shape[1]))(*operands)


def added(block, other, wait):
    def body(block_ref, other_ref, _, out_ref):
        total = block_ref[...].astype(jnp.float32) + other_ref[...].astype(jnp.float32)
        out_ref[...] = total.astype(out_ref.dtype)

    shape = jax.ShapeDtypeStruct(block.shape, block.dtype)
    return on_core(body, shape, [VMEM, VMEM, ANYWHERE])(block, other, wait)


def down(held, own_ref, lent_ref, sent_ref, kept_ref):
    units, width = own_ref.shape[0], kept_ref.shape[1]
    for out, at in ((kept_ref, slice(0, width)), (sent_ref, slice(width, 2 * width))):
        result = jnp.dot(held[:, :units], own_ref[:, at], preferred_element_type=jnp.float32)
        result += jnp.dot(held[:, units:], lent_ref[:, at], preferred_element_type=jnp.float32)
        out[...] = result.astype(out.dtype)


def finish(owned, slot, plan, sums, got, facts, before, down_own, down_lent):
    units = down_own.shape[0]
    width = down_own.shape[1] // 2
    pair = [
        jax.ShapeDtypeStruct((owned, width), jnp.bfloat16),
        jax.ShapeDtypeStruct((owned, width), jnp.float32),
    ]

    def first(plan_ref, sums_ref, got_ref, facts_ref, before_ref, own_ref, lent_ref, *out_refs):
        facts_here = facts_of(facts_ref, *out_refs[3:])
        rows = collected_rows(owned, slot, plan_ref, sums_ref, got_ref, facts_here, before_ref)
        down(rows[0].astype(jnp.bfloat16), own_ref, lent_ref, out_refs[0], out_refs[1])
        for index in range(1, 4):
            out_refs[2][(index - 1) * owned : index * owned, :] = rows[index].astype(jnp.bfloat16)

    def others(indices, waits):
        def body(held_ref, own_ref, lent_ref, *refs):
            out_refs = refs[len(waits) :]
            for place, index in enumerate(indices):
                held = held_ref[(index - 1) * owned : index * owned, :]
                down(held, own_ref, lent_ref, out_refs[2 * place], out_refs[2 * place + 1])

        specs = [VMEM] * 3 + [ANYWHERE] * len(waits)
        return on_core(body, pair * len(indices), specs)(held, down_own, down_lent, *waits)

    def joined(sent, kept):
        return kept + across_chips(sent).astype(jnp.float32)

    held_shape = jax.ShapeDtypeStruct((3 * owned, 2 * units), jnp.bfloat16)
    specs = [SMEM, VMEM, VMEM, ANYWHERE] + [VMEM] * 3
    sent, kept, held = on_core(first, pair + [held_shape], specs, fact_scratch(facts.shape[1]))(
        plan, sums, got, facts, before, down_own, down_lent
    )
    got_first = across_chips(sent)
    chunks = [kept + got_first.astype(jnp.float32), joined(*others([1], []))]
    rest = others([2, 3], [got_first])
    return chunks + [joined(rest[0], rest[1]), joined(rest[2], rest[3])]


def rows_travel(
    tokens, gate_weight, up_weight, down_weight, route_gates, block_list, block_count, owner_token
):
    position = lax.axis_index("blk")
    share = lax.axis_index("tp")
    row_count, width = tokens.shape
    units = gate_weight.shape[2]
    owned = row_count // 2
    half = row_count // 2
    plan = jnp.asarray(PLAN, jnp.int32)[position]

    own_far = across_chips(tokens)
    own = with_facts(
        tokens, route_gates.T, jnp.transpose(block_list, (2, 0, 1)), block_count, owner_token
    )
    beside = along(own, BESIDE)
    middle = along(own, MIDDLE)

    gate_quarters = gate_weight[0].reshape(4, width, units)
    up_quarters = up_weight[0].reshape(4, width, units)

    def quarter(j):
        pair = [
            lax.dynamic_index_in_dim(q, share ^ j, 0, keepdims=False)
            for q in (gate_quarters, up_quarters)
        ]
        return jnp.concatenate(pair, axis=1)

    def down_part(j):
        return lax.dynamic_slice_in_dim(down_weight[0], (share ^ j) * width, width, 1)

    kept_down = jnp.concatenate([down_part(0), down_part(2)], axis=1)
    lend_down = jnp.concatenate([down_part(1), down_part(3)], axis=1)


    inner_last = along(beside, MIDDLE)
    outer_next = along(middle, OUTWARD)
    beside_far = across_chips(beside)
    own_far_half = lower_half(own_far)
    inward_far = along(own_far_half, INWARD)
    lend = jnp.concatenate([quarter(1), quarter(3)])
    lent = across_cores(after(lend, own))
    weights = [quarter(0), quarter(2), lent]
    sums_0, send_0, ready_0 = partial_sums([row_count], [(tokens, own_far)], weights, (0, 1))
    got_0 = across_cores(send_0)
    lent_down = across_cores(lend_down)

    outer_last = along(inner_last, OUTWARD)
    (second, second_facts) = chosen(
        plan,
        middle,
        outer_next,
        [(0, row_count, 4), (row_count, FACT_ROWS, 1)],
        beside_far,
        inner_last,
        inward_far,
        lend_down,
        weights[0],
        weights[1],
    )
    second_far = across_chips(second)
    middle_far = along(inward_far, MIDDLE)
    sums_1, send_1, ready_1 = partial_sums([row_count], [(beside, beside_far)], weights, (0, 1))
    got_1 = across_cores(send_1)

    total, _ = collect(owned, 0, plan, sums_0, got_0, own, None)

    last_a, last_b, last_facts = chosen(
        plan,
        inner_last,
        outer_last,
        [(0, half, 4), (half, half, 4), (row_count, FACT_ROWS, 1)],
        second_far,
        middle_far,
        ready_0,
        ready_1,
    )
    last_far_a = across_chips(last_a)
    outward_far = along(middle_far, OUTWARD)
    total, collected_1 = collect(owned, 1, plan, sums_1, got_1, beside, total)
    sums_2, send_2, ready_2 = partial_sums([row_count], [(second, second_far)], weights, (0, 1))
    got_2 = across_cores(send_2)
    near = partial_sums([half, half], [(last_a,), (last_b,)], weights, (0,), send=False)[0]
    sums_3, send_3, _ = partial_sums(
        [half, half],
        [(last_far_a,), (outward_far,)],
        weights,
        (1,),
        before=near,
        choice=(plan, middle_far),
        waits=[collected_1],
    )
    got_3 = across_cores(send_3)
    total, _ = collect(owned, 2, plan, sums_2, got_2, second_facts, total)
    chunks = finish(
        owned, 3, plan, sums_3, got_3, last_facts, total, kept_down, lent_down
    )

    first, second, third = [chunk.astype(jnp.bfloat16) for chunk in chunks[:3]]
    middle = along(first, MIDDLE)
    inward = along(first, INWARD)
    two_in = along(second, TWO_IN)
    two_out = along(added(second, inward, middle), TWO_OUT)
    beside = along(third, BESIDE)
    arrived = [block.astype(jnp.float32) for block in (middle, two_in, two_out, beside)]
    return (chunks[3] + sum(arrived)).astype(jnp.bfloat16)


def on_device(*args):
    block_list = args[5]
    sizes = (lax.axis_size("blk"), lax.axis_size("tp"), block_list.shape[1])
    if sizes == (4, 4, 4):
        return rows_travel(*args)
    return weights_travel(*args)


def solution(mesh):
    return jax.shard_map(
        on_device,
        mesh=mesh,
        in_specs=(
            P(("groups", "blk"), "tp"),
            P("blk", None, "tp"),
            P("blk", None, "tp"),
            P("blk", "tp", None),
            P(("groups", "blk"), None),
            P(("groups", "blk"), None, None),
            P(("groups", "blk"), None),
            P(("groups", "blk")),
        ),
        out_specs=P(("groups", "blk"), "tp"),
        check_vma=False,
    )
```

```python
import jax
import jax.numpy as jnp
from jax import lax
from jax.experimental import pallas as pl
from jax.experimental.pallas import tpu as pltpu
from jax.sharding import PartitionSpec as P


def shifted(block, axis, distance):
    devices = range(lax.axis_size(axis))
    route = [((i - distance) % len(devices), i) for i in devices]
    return lax.ppermute(block, axis, route)


def weights_travel(
    tokens, gate_weight, up_weight, down_weight, route_gates, block_list, block_count, owner_token
):
    whole_rows = lax.all_gather(tokens, "tp", axis=1, tiled=True)
    row_count = whole_rows.shape[0]
    width = whole_rows.shape[1]
    offsets_all = block_list.shape[1]
    block_total = block_list.shape[2]
    block_size = row_count // block_total
    blocks = whole_rows.reshape(block_total, block_size, width)
    gate_blocks = route_gates.reshape(block_total, block_size, offsets_all)
    totals = jnp.zeros((block_total, block_size, width), jnp.float32)

    def apply(totals, weights, offset, block_id):
        w_gate, w_up, w_down = weights
        block_rows = lax.dynamic_index_in_dim(blocks, block_id, 0, keepdims=False)
        gate_out = jnp.dot(block_rows, w_gate, preferred_element_type=jnp.float32)
        up_out = jnp.dot(block_rows, w_up, preferred_element_type=jnp.float32)
        hidden = (jax.nn.silu(gate_out) * up_out).astype(jnp.bfloat16)
        block_gates = lax.dynamic_index_in_dim(gate_blocks, block_id, 0, keepdims=False)
        factor = lax.dynamic_index_in_dim(block_gates, offset, 1, keepdims=False)
        product = jnp.dot(hidden, w_down, preferred_element_type=jnp.float32) * factor[:, None]
        before = lax.dynamic_index_in_dim(totals, block_id, 0, keepdims=False)
        return lax.dynamic_update_index_in_dim(totals, before + product, block_id, 0)

    resident = (gate_weight[0], up_weight[0], down_weight[0])
    arrived = [resident]
    holding = resident
    for offset in range(1, offsets_all):
        holding = shifted((holding[0], holding[1], holding[2]), "blk", 1)
        arrived.append(holding)
    for offset in range(offsets_all):
        weights = arrived[offset]

        def visit_block(position, totals, weights=weights, offset=offset):
            return apply(totals, weights, offset, block_list[0, offset, position])

        totals = lax.fori_loop(0, block_count[0, offset], visit_block, totals)
    summed = lax.psum_scatter(
        totals.reshape(row_count, width).astype(jnp.bfloat16), "tp", scatter_dimension=1, tiled=True
    )
    feature_share = summed.shape[1]
    cycle_size = lax.axis_size("blk")
    owned = row_count // 2
    capacity = max(2, 2 * row_count // cycle_size)
    target = owner_token // owned
    local_token = owner_token % owned
    target_table = (target[:, None] == jnp.arange(cycle_size, dtype=jnp.int32)[None, :]).astype(
        jnp.int32
    )
    running = jnp.cumsum(target_table, axis=0)
    rank = jnp.sum((running - 1) * target_table, axis=1)
    slot = target * capacity + rank
    send_rows = jnp.zeros((cycle_size * capacity, feature_share), jnp.bfloat16).at[slot].set(summed)
    send_index = jnp.full((cycle_size * capacity,), -1, jnp.int32).at[slot].set(local_token)
    send_rows = send_rows.reshape(cycle_size, capacity, feature_share)
    send_index = send_index.reshape(cycle_size, capacity)
    got_rows, got_index = (
        lax.all_to_all(send_rows, "blk", split_axis=0, concat_axis=0, tiled=True),
        lax.all_to_all(send_index, "blk", split_axis=0, concat_axis=0, tiled=True),
    )
    got_rows = got_rows.reshape(cycle_size * capacity, feature_share)
    got_index = got_index.reshape(cycle_size * capacity)
    placing = (got_index[:, None] == jnp.arange(owned, dtype=jnp.int32)[None, :]).astype(
        jnp.bfloat16
    )
    combined = lax.dot_general(
        placing, got_rows, (((0,), (0,)), ((), ())), preferred_element_type=jnp.float32
    )
    return combined.astype(jnp.bfloat16)


BESIDE = [(0, 1), (1, 0), (2, 3), (3, 2)]
MIDDLE = [(1, 2), (2, 1)]
INWARD = [(0, 1), (3, 2)]
OUTWARD = [(1, 0), (2, 3)]
TWO_IN = [(0, 2), (3, 1)]
TWO_OUT = [(1, 3), (2, 0)]
PLAN = [
    [3, 2, 1, 0, 0, 1, 2, 3, 0],
    [2, 3, 0, 1, 0, 3, 1, 2, 1],
    [1, 0, 3, 2, 0, 1, 3, 2, 1],
    [0, 1, 2, 3, 0, 3, 2, 1, 0],
]
OFFSETS_AT, INNER_AT = 4, 8
FACT_ROWS = 16
VMEM = pl.BlockSpec(memory_space=pltpu.VMEM)
SMEM = pl.BlockSpec(memory_space=pltpu.SMEM)
ANYWHERE = pl.BlockSpec(memory_space=pl.ANY)


def across_chips(block):
    return lax.ppermute(block, "tp", [(i, i ^ 2) for i in range(4)])


def across_cores(block):
    return lax.ppermute(block, "tp", [(i, i ^ 1) for i in range(4)])


def along(block, route):
    return lax.ppermute(block, "blk", route)


def cheap():
    return pl.CostEstimate(flops=1024, bytes_accessed=1024, transcendentals=0)


TOKEN = jax.ShapeDtypeStruct((8, 128), jnp.float32)
VMEM_LIMIT = 40 * 2**20


def on_core(body, out_shape, in_specs, scratch=()):
    return pl.pallas_call(
        body,
        out_shape=out_shape,
        in_specs=in_specs,
        out_specs=jax.tree.map(lambda _: VMEM, out_shape),
        scratch_shapes=scratch,
        compiler_params=pltpu.CompilerParams(vmem_limit_bytes=VMEM_LIMIT),
        cost_estimate=cheap(),
    )


def copies(source, start, target, size, pieces, sems, first):
    step = size // pieces
    return [
        pltpu.make_async_copy(
            source.at[pl.ds(start + index * step, step)],
            target.at[pl.ds(index * step, step)],
            sems.at[first + index],
        )
        for index in range(pieces)
    ]


def after(block, *others, flops=1024):
    return pl.pallas_call(
        lambda *refs: None,
        out_shape=jax.ShapeDtypeStruct(block.shape, block.dtype),
        in_specs=[ANYWHERE] * (1 + len(others)),
        out_specs=ANYWHERE,
        input_output_aliases={0: 0},
        cost_estimate=pl.CostEstimate(flops=flops, bytes_accessed=1024, transcendentals=0),
    )(block, *others)


def by_kind(plan_ref, kinds, run):
    if kinds[0] is kinds[1]:
        run(kinds[0])
        return
    for kind, value in zip(kinds, (1, 0)):

        @pl.when(plan_ref[INNER_AT] == value)
        def _(kind=kind):
            run(kind)


def part_of(plan, if_inner, if_outer, start, size, *others, flops=1024):
    shape = jax.ShapeDtypeStruct((size, if_inner.shape[1]), if_inner.dtype)
    pieces = 4

    def body(plan_ref, inner_ref, outer_ref, *rest):
        out_ref, buffer, in_sems, out_sems = rest[len(others) :]

        def run(source):
            inward = copies(source, start, buffer, size, pieces, in_sems, 0)
            outward = copies(buffer, 0, out_ref, size, pieces, out_sems, 0)
            for copy in inward:
                copy.start()
            for copy, next_copy in zip(inward, outward):
                copy.wait()
                next_copy.start()
            for copy in outward:
                copy.wait()

        by_kind(plan_ref, (inner_ref, inner_ref if if_outer is if_inner else outer_ref), run)

    return pl.pallas_call(
        body,
        out_shape=shape,
        in_specs=[SMEM] + [ANYWHERE] * (2 + len(others)),
        out_specs=ANYWHERE,
        scratch_shapes=[pltpu.VMEM(shape.shape, shape.dtype)]
        + [pltpu.SemaphoreType.DMA((pieces,))] * 2,
        compiler_params=pltpu.CompilerParams(vmem_limit_bytes=VMEM_LIMIT),
        cost_estimate=pl.CostEstimate(flops=flops, bytes_accessed=1024, transcendentals=0),
    )(plan, if_inner, if_outer, *others)


def with_facts(rows, gates, block_list, block_count, owner):
    count, width = rows.shape
    blocks, _, offsets = block_list.shape
    total = owner.shape[0]

    def body(rows_ref, gates_hbm, list_hbm, count_hbm, owner_hbm, out_ref, *scratch):
        gates_ref, list_ref, count_ref, owner_ref, sems, small_sems = scratch
        moves = copies(rows_ref, 0, out_ref, count, 4, sems, 0)
        small = [
            pltpu.make_async_copy(source, target, small_sems.at[index])
            for index, (source, target) in enumerate(
                zip((gates_hbm, list_hbm, count_hbm, owner_hbm), scratch[:4])
            )
        ]
        for copy in small + moves:
            copy.start()
        for copy in small:
            copy.wait()
        block_of = lax.broadcasted_iota(jnp.int32, (1, total), 1) // (total // blocks)
        facts = []
        for offset in range(offsets):
            mask = jnp.zeros((1, total), jnp.float32)
            for block in range(blocks):
                used = jnp.int32(0)
                for place in range(blocks):
                    found = (list_ref[place, 0, offset] == block) & (place < count_ref[0, offset])
                    used = used | found.astype(jnp.int32)
                mask = mask + jnp.where(block_of == block, used.astype(jnp.float32), 0.0)
            facts.append(gates_ref[offset : offset + 1, :] * mask)
        numbers = owner_ref[...].reshape(1, total)
        facts.append((numbers >> 8).astype(jnp.float32))
        facts.append((numbers & 255).astype(jnp.float32))
        facts.append(jnp.zeros((FACT_ROWS - len(facts), total), jnp.float32))
        out_ref[count:, :] = jnp.zeros((FACT_ROWS, width), jnp.bfloat16)
        out_ref[count:, :total] = jnp.concatenate(facts, axis=0).astype(jnp.bfloat16)
        for copy in moves:
            copy.wait()

    shape = jax.ShapeDtypeStruct((count + FACT_ROWS, width), rows.dtype)
    scratch = [
        pltpu.VMEM(gates.shape, gates.dtype),
        pltpu.SMEM(block_list.shape, block_list.dtype),
        pltpu.SMEM(block_count.shape, block_count.dtype),
        pltpu.VMEM(owner.shape, owner.dtype),
        pltpu.SemaphoreType.DMA((4,)),
        pltpu.SemaphoreType.DMA((4,)),
    ]
    return on_core(body, shape, [ANYWHERE] * 5, scratch)(
        rows, gates, block_list, block_count, owner
    )


def partial_sums(plan, sizes, parts, weights, places, before=None, send=True, waits=()):
    width, columns = weights[0].shape
    rows, count = sum(sizes), len(places)
    pairs = [
        block if isinstance(block, tuple) else (block, block) for part in parts for block in part
    ]
    sources = [array for pair in pairs for array in pair]
    operands = [plan] + sources + [weights[place] for place in places] + [weights[2]]
    if before is not None:
        operands.append(before)
    specs = [SMEM] + [ANYWHERE] * (len(operands) - 1) + [VMEM] * len(waits)
    row_pieces, weight_pieces, before_pieces = 2, 4, 4
    has_before = before is not None

    def body(plan_ref, *refs):
        source_refs = refs[: len(sources)]
        weight_refs = refs[len(sources) : len(sources) + count + 1]
        before_ref = refs[len(sources) + count + 1] if has_before else None
        scratch = refs[len(operands) - 1 + len(waits) :]
        results = scratch[: 3 if send else 2]
        row_buffer, weight_buffer, row_sems, weight_sems = scratch[len(results) :][:4]
        row_moves, weight_moves, before_moves = [], [[], []], []

        def start(moves):
            for copy in moves:
                copy.start()

        for part, size in enumerate(sizes):
            for index in range(count):
                block = part * count + index
                target = row_buffer.at[index, pl.ds(sum(sizes[:part]), size)]
                first = block * row_pieces
                kinds = [
                    copies(source_refs[2 * block], 0, target, size, row_pieces, row_sems, first)
                ]
                if pairs[block][0] is pairs[block][1]:
                    kinds.append(kinds[0])
                else:
                    source = source_refs[2 * block + 1]
                    kinds.append(copies(source, 0, target, size, row_pieces, row_sems, first))
                by_kind(plan_ref, kinds, start)
                row_moves += kinds[0]
        for side in range(2):
            for index, place in enumerate(places):
                weight_moves[side] += copies(
                    weight_refs[index if side == 0 else count],
                    0 if side == 0 else place * width,
                    weight_buffer.at[side, index],
                    width,
                    weight_pieces,
                    weight_sems,
                    (side * count + index) * weight_pieces,
                )
            start(weight_moves[side])
        if has_before:
            before_buffer, before_sems = scratch[-2:]
            before_moves = copies(
                before_ref, 0, before_buffer, rows, before_pieces, before_sems, 0
            )
            start(before_moves)
        for copy in row_moves + before_moves:
            copy.wait()
        for side in range(2):
            for copy in weight_moves[side]:
                copy.wait()
            at = slice(side * columns, (side + 1) * columns)
            total = before_buffer[:, at] if has_before else None
            for index in range(count):
                product = jnp.dot(
                    row_buffer[index],
                    weight_buffer[side, index],
                    preferred_element_type=jnp.float32,
                )
                total = product if total is None else total + product
            results[0][:, at] = total
            if send:
                results[1][:, at] = total.astype(jnp.bfloat16)
        results[-1][...] = jnp.zeros(TOKEN.shape, TOKEN.dtype)

    shapes = [jax.ShapeDtypeStruct((rows, 2 * columns), jnp.float32)]
    if send:
        shapes.append(jax.ShapeDtypeStruct((rows, 2 * columns), jnp.bfloat16))
    scratch = [
        pltpu.VMEM((count, rows, width), jnp.bfloat16),
        pltpu.VMEM((2, count, width, columns), jnp.bfloat16),
        pltpu.SemaphoreType.DMA((len(pairs) * row_pieces,)),
        pltpu.SemaphoreType.DMA((2 * count * weight_pieces,)),
    ]
    if has_before:
        scratch += [
            pltpu.VMEM((rows, 2 * columns), jnp.float32),
            pltpu.SemaphoreType.DMA((before_pieces,)),
        ]
    return on_core(body, shapes + [TOKEN], specs, scratch)(*operands, *waits)


def collected_rows(owned, slot, plan, sums, got, facts, before):
    units = sums.shape[1] // 4
    hidden = []
    for core in range(2):
        here, there = 2 * core * units, 2 * (1 - core) * units
        gate = sums[:, here : here + units] + got[:, there : there + units].astype(jnp.float32)
        up = sums[:, here + units : here + 2 * units]
        up = up + got[:, there + units : there + 2 * units].astype(jnp.float32)
        hidden.append((gate / (1.0 + jnp.exp(-gate)) * up).astype(jnp.bfloat16))
    hidden = jnp.concatenate(hidden, axis=1)
    values = facts[:, : sums.shape[0]].astype(jnp.float32)
    kind = lax.broadcasted_iota(jnp.int32, (FACT_ROWS, 1), 0)
    mine = kind == plan[OFFSETS_AT + slot]
    factor = jnp.sum(jnp.where(mine, values, 0.0), axis=0, keepdims=True)
    owner = (values[4:5, :] * 256.0 + values[5:6, :]).astype(jnp.int32)
    results = []
    for index in range(4):
        token = plan[index] * owned + lax.broadcasted_iota(jnp.int32, (owned, 1), 0)
        placing = jnp.where(owner == token, factor, 0.0).astype(jnp.bfloat16)
        rows = jnp.dot(placing, hidden, preferred_element_type=jnp.float32)
        if before is not None:
            rows = rows + before[index * owned : (index + 1) * owned, :]
        results.append(rows)
    return results


def fact_scratch(width):
    return [pltpu.VMEM((FACT_ROWS, width), jnp.bfloat16), pltpu.SemaphoreType.DMA((1,))]


def facts_of(plan_ref, inner_ref, outer_ref, buffer, sem):
    last = inner_ref.shape[0] - FACT_ROWS

    def run(source):
        (copy,) = copies(source, last, buffer, FACT_ROWS, 1, sem, 0)
        copy.start()
        copy.wait()

    by_kind(plan_ref, (inner_ref, outer_ref), run)
    return buffer


def collect(owned, slot, plan, sums, got, facts, before):
    operands = [plan, sums, got, *facts] + ([] if before is None else [before])

    def body(plan_ref, sums_ref, got_ref, inner_ref, outer_ref, *rest):
        before_ref = rest[0] if before is not None else None
        out_ref, token_ref, buffer, sem = rest[-4:]
        facts_here = facts_of(plan_ref, inner_ref, outer_ref, buffer, sem)
        rows = collected_rows(owned, slot, plan_ref, sums_ref, got_ref, facts_here, before_ref)
        for index in range(4):
            out_ref[index * owned : (index + 1) * owned, :] = rows[index]
        token_ref[...] = jnp.zeros(TOKEN.shape, TOKEN.dtype)

    shape = jax.ShapeDtypeStruct((4 * owned, sums.shape[1] // 2), jnp.float32)
    specs = [SMEM, VMEM, VMEM, ANYWHERE, ANYWHERE] + [VMEM] * (len(operands) - 5)
    return on_core(body, [shape, TOKEN], specs, fact_scratch(facts[0].shape[1]))(*operands)


def added(block, other, *waits, flops=1024):
    def body(block_ref, other_ref, *rest):
        total = block_ref[...].astype(jnp.float32) + other_ref[...].astype(jnp.float32)
        rest[-1][...] = total.astype(jnp.bfloat16)

    return pl.pallas_call(
        body,
        out_shape=jax.ShapeDtypeStruct(block.shape, jnp.bfloat16),
        in_specs=[VMEM, VMEM] + [ANYWHERE] * len(waits),
        out_specs=VMEM,
        cost_estimate=pl.CostEstimate(flops=flops, bytes_accessed=1024, transcendentals=0),
    )(block, other, *waits)


def down(held, own_ref, lent_ref, sent_ref, kept_ref):
    units, width = own_ref.shape[0], kept_ref.shape[1]
    for out, at in ((kept_ref, slice(0, width)), (sent_ref, slice(width, 2 * width))):
        result = jnp.dot(held[:, :units], own_ref[:, at], preferred_element_type=jnp.float32)
        result += jnp.dot(held[:, units:], lent_ref[:, at], preferred_element_type=jnp.float32)
        out[...] = result.astype(out.dtype)


def finish(owned, slot, plan, sums, got, facts, before, down_own, down_lent):
    units = down_own.shape[0]
    width = down_own.shape[1] // 2
    pair = [
        jax.ShapeDtypeStruct((owned, width), jnp.bfloat16),
        jax.ShapeDtypeStruct((owned, width), jnp.float32),
    ]

    def first(plan_ref, sums_ref, got_ref, inner_ref, outer_ref, before_ref, *refs):
        own_ref, lent_ref, sent_ref, kept_ref, held_ref, buffer, sem = refs
        facts_here = facts_of(plan_ref, inner_ref, outer_ref, buffer, sem)
        rows = collected_rows(owned, slot, plan_ref, sums_ref, got_ref, facts_here, before_ref)
        down(rows[0].astype(jnp.bfloat16), own_ref, lent_ref, sent_ref, kept_ref)
        for index in range(1, 4):
            held_ref[(index - 1) * owned : index * owned, :] = rows[index].astype(jnp.bfloat16)

    def others(held_ref, own_ref, lent_ref, *refs):
        for index in range(3):
            held = held_ref[index * owned : (index + 1) * owned, :]
            down(held, own_ref, lent_ref, refs[2 * index], refs[2 * index + 1])

    held_shape = jax.ShapeDtypeStruct((3 * owned, 2 * units), jnp.bfloat16)
    specs = [SMEM, VMEM, VMEM, ANYWHERE, ANYWHERE] + [VMEM] * 3
    sent, kept, held = on_core(
        first, pair + [held_shape], specs, fact_scratch(facts[0].shape[1])
    )(plan, sums, got, *facts, before, down_own, down_lent)
    rest = on_core(others, pair * 3, [VMEM] * 3)(held, down_own, down_lent)
    return [sent, *rest[0::2]], [kept, *rest[1::2]]


def rows_travel(
    tokens, gate_weight, up_weight, down_weight, route_gates, block_list, block_count, owner_token
):
    position = lax.axis_index("blk")
    share = lax.axis_index("tp")
    row_count, width = tokens.shape
    units = gate_weight.shape[2]
    owned = row_count // 2
    half = row_count // 2
    plan = jnp.asarray(PLAN, jnp.int32)[position]

    own_far = across_chips(tokens)
    own = with_facts(
        tokens, route_gates.T, jnp.transpose(block_list, (2, 0, 1)), block_count, owner_token
    )
    beside = along(own, BESIDE)
    middle = along(own, MIDDLE)

    gate_quarters = gate_weight[0].reshape(4, width, units)
    up_quarters = up_weight[0].reshape(4, width, units)

    def quarter(j):
        pair = [
            lax.dynamic_index_in_dim(q, share ^ j, 0, keepdims=False)
            for q in (gate_quarters, up_quarters)
        ]
        return jnp.concatenate(pair, axis=1)

    def down_part(j):
        return lax.dynamic_slice_in_dim(down_weight[0], (share ^ j) * width, width, 1)

    kept_down = jnp.concatenate([down_part(0), down_part(2)], axis=1)
    lend_down = jnp.concatenate([down_part(1), down_part(3)], axis=1)


    def at_kind(block, positions):
        pairs = [(4 * p + i, 4 * p + (i ^ 2)) for p in positions for i in range(4)]
        return lax.ppermute(block, ("blk", "tp"), pairs)

    beside = after(beside, middle)
    inner_last = along(beside, MIDDLE)
    outer_next = after(along(middle, OUTWARD), flops=3 * 2**30)
    beside_far = across_chips(beside)
    own_far_half = part_of(plan, own_far, own_far, half, half, flops=6 * 2**30)
    inward_far = along(own_far_half, INWARD)
    lend = jnp.concatenate([quarter(1), quarter(3)])
    lent = across_cores(after(lend, own))
    weights = [quarter(0), quarter(2), lent]
    whole = [row_count]
    sums_0, send_0, ready_0 = partial_sums(
        plan, whole, [(tokens, own_far)], weights, (0, 1)
    )
    got_0 = across_cores(send_0)
    lent_down = across_cores(lend_down)

    outer_last = along(inner_last, OUTWARD)
    outer_next = after(
        outer_next,
        beside_far,
        inner_last,
        inward_far,
        lend_down,
        weights[0],
        weights[1],
    )
    second = (middle, outer_next)
    second_far = (at_kind(middle, (1, 2)), at_kind(outer_next, (0, 3)))
    middle_far = along(inward_far, MIDDLE)
    sums_1, send_1, ready_1 = partial_sums(
        plan, whole, [(beside, beside_far)], weights, (0, 1)
    )
    got_1 = across_cores(send_1)

    last = (inner_last, outer_last)
    last_far_a = across_chips(
        part_of(plan, *last, 0, half, *second_far, middle_far, ready_0, ready_1)
    )
    outward_far = along(middle_far, OUTWARD)
    total, _ = collect(owned, 0, plan, sums_0, got_0, (own, own), None)
    total, collected_1 = collect(owned, 1, plan, sums_1, got_1, (beside, beside), total)
    sums_2, send_2, _ = partial_sums(plan, whole, [(second, second_far)], weights, (0, 1))
    got_2 = across_cores(send_2)
    near, _ = partial_sums(plan, whole, [(last,)], weights, (0,), send=False)
    sums_3, send_3, _ = partial_sums(
        plan,
        [half, half],
        [(last_far_a,), ((middle_far, outward_far),)],
        weights,
        (1,),
        before=near,
        waits=[collected_1],
    )
    got_3 = across_cores(send_3)
    total, _ = collect(owned, 2, plan, sums_2, got_2, second, total)
    sent, kept = finish(owned, 3, plan, sums_3, got_3, last, total, kept_down, lent_down)

    far = [across_chips(block) for block in sent]
    first = added(kept[0], far[0])
    middle = along(first, MIDDLE)
    inward = along(first, INWARD)
    second = added(kept[1], far[1], flops=4 * 2**30)
    two_in = along(second, TWO_IN)
    two_out = along(added(second, inward, middle), TWO_OUT)
    beside = along(added(kept[2], far[2], flops=4 * 2**30), BESIDE)
    arrived = [block.astype(jnp.float32) for block in (far[3], middle, two_in, two_out, beside)]
    return (kept[3] + sum(arrived)).astype(jnp.bfloat16)


def on_device(*args):
    block_list = args[5]
    sizes = (lax.axis_size("blk"), lax.axis_size("tp"), block_list.shape[1])
    if sizes == (4, 4, 4):
        return rows_travel(*args)
    return weights_travel(*args)


def solution(mesh):
    return jax.shard_map(
        on_device,
        mesh=mesh,
        in_specs=(
            P(("groups", "blk"), "tp"),
            P("blk", None, "tp"),
            P("blk", None, "tp"),
            P("blk", "tp", None),
            P(("groups", "blk"), None),
            P(("groups", "blk"), None, None),
            P(("groups", "blk"), None),
            P(("groups", "blk")),
        ),
        out_specs=P(("groups", "blk"), "tp"),
        check_vma=False,
    )
```

```python
import jax
import jax.numpy as jnp
from jax import lax
from jax.experimental import pallas as pl
from jax.experimental.pallas import tpu as pltpu
from jax.sharding import PartitionSpec as P


def shifted(block, axis, distance):
    devices = range(lax.axis_size(axis))
    route = [((i - distance) % len(devices), i) for i in devices]
    return lax.ppermute(block, axis, route)


def weights_travel(
    tokens, gate_weight, up_weight, down_weight, route_gates, block_list, block_count, owner_token
):
    whole_rows = lax.all_gather(tokens, "tp", axis=1, tiled=True)
    row_count = whole_rows.shape[0]
    width = whole_rows.shape[1]
    offsets_all = block_list.shape[1]
    block_total = block_list.shape[2]
    block_size = row_count // block_total
    blocks = whole_rows.reshape(block_total, block_size, width)
    gate_blocks = route_gates.reshape(block_total, block_size, offsets_all)
    totals = jnp.zeros((block_total, block_size, width), jnp.float32)

    def apply(totals, weights, offset, block_id):
        w_gate, w_up, w_down = weights
        block_rows = lax.dynamic_index_in_dim(blocks, block_id, 0, keepdims=False)
        gate_out = jnp.dot(block_rows, w_gate, preferred_element_type=jnp.float32)
        up_out = jnp.dot(block_rows, w_up, preferred_element_type=jnp.float32)
        hidden = (jax.nn.silu(gate_out) * up_out).astype(jnp.bfloat16)
        block_gates = lax.dynamic_index_in_dim(gate_blocks, block_id, 0, keepdims=False)
        factor = lax.dynamic_index_in_dim(block_gates, offset, 1, keepdims=False)
        product = jnp.dot(hidden, w_down, preferred_element_type=jnp.float32) * factor[:, None]
        before = lax.dynamic_index_in_dim(totals, block_id, 0, keepdims=False)
        return lax.dynamic_update_index_in_dim(totals, before + product, block_id, 0)

    resident = (gate_weight[0], up_weight[0], down_weight[0])
    arrived = [resident]
    holding = resident
    for offset in range(1, offsets_all):
        holding = shifted((holding[0], holding[1], holding[2]), "blk", 1)
        arrived.append(holding)
    for offset in range(offsets_all):
        weights = arrived[offset]

        def visit_block(position, totals, weights=weights, offset=offset):
            return apply(totals, weights, offset, block_list[0, offset, position])

        totals = lax.fori_loop(0, block_count[0, offset], visit_block, totals)
    summed = lax.psum_scatter(
        totals.reshape(row_count, width).astype(jnp.bfloat16), "tp", scatter_dimension=1, tiled=True
    )
    feature_share = summed.shape[1]
    cycle_size = lax.axis_size("blk")
    owned = row_count // 2
    capacity = max(2, 2 * row_count // cycle_size)
    target = owner_token // owned
    local_token = owner_token % owned
    target_table = (target[:, None] == jnp.arange(cycle_size, dtype=jnp.int32)[None, :]).astype(
        jnp.int32
    )
    running = jnp.cumsum(target_table, axis=0)
    rank = jnp.sum((running - 1) * target_table, axis=1)
    slot = target * capacity + rank
    send_rows = jnp.zeros((cycle_size * capacity, feature_share), jnp.bfloat16).at[slot].set(summed)
    send_index = jnp.full((cycle_size * capacity,), -1, jnp.int32).at[slot].set(local_token)
    send_rows = send_rows.reshape(cycle_size, capacity, feature_share)
    send_index = send_index.reshape(cycle_size, capacity)
    got_rows, got_index = (
        lax.all_to_all(send_rows, "blk", split_axis=0, concat_axis=0, tiled=True),
        lax.all_to_all(send_index, "blk", split_axis=0, concat_axis=0, tiled=True),
    )
    got_rows = got_rows.reshape(cycle_size * capacity, feature_share)
    got_index = got_index.reshape(cycle_size * capacity)
    placing = (got_index[:, None] == jnp.arange(owned, dtype=jnp.int32)[None, :]).astype(
        jnp.bfloat16
    )
    combined = lax.dot_general(
        placing, got_rows, (((0,), (0,)), ((), ())), preferred_element_type=jnp.float32
    )
    return combined.astype(jnp.bfloat16)


BESIDE = [(0, 1), (1, 0), (2, 3), (3, 2)]
MIDDLE = [(1, 2), (2, 1)]
INWARD = [(0, 1), (3, 2)]
OUTWARD = [(1, 0), (2, 3)]
TWO_IN = [(0, 2), (3, 1)]
TWO_OUT = [(1, 3), (2, 0)]
PLAN = [
    [3, 2, 1, 0, 0, 1, 2, 3, 0],
    [2, 3, 0, 1, 0, 3, 1, 2, 1],
    [1, 0, 3, 2, 0, 1, 3, 2, 1],
    [0, 1, 2, 3, 0, 3, 2, 1, 0],
]
OFFSETS_AT, INNER_AT = 4, 8
FACT_ROWS = 16
VMEM = pl.BlockSpec(memory_space=pltpu.VMEM)
SMEM = pl.BlockSpec(memory_space=pltpu.SMEM)
ANYWHERE = pl.BlockSpec(memory_space=pl.ANY)


def across_chips(block):
    return lax.ppermute(block, "tp", [(i, i ^ 2) for i in range(4)])


def across_cores(block):
    return lax.ppermute(block, "tp", [(i, i ^ 1) for i in range(4)])


def along(block, route):
    return lax.ppermute(block, "blk", route)


def cheap():
    return pl.CostEstimate(flops=1024, bytes_accessed=1024, transcendentals=0)


TOKEN = jax.ShapeDtypeStruct((8, 128), jnp.float32)
VMEM_LIMIT = 18 * 2**20


def on_core(body, out_shape, in_specs, scratch=()):
    return pl.pallas_call(
        body,
        out_shape=out_shape,
        in_specs=in_specs,
        out_specs=jax.tree.map(lambda _: VMEM, out_shape),
        scratch_shapes=scratch,
        compiler_params=pltpu.CompilerParams(vmem_limit_bytes=VMEM_LIMIT),
        cost_estimate=cheap(),
    )


def copies(source, start, target, size, pieces, sems, first):
    step = size // pieces
    return [
        pltpu.make_async_copy(
            source.at[pl.ds(start + index * step, step)],
            target.at[pl.ds(index * step, step)],
            sems.at[first + index],
        )
        for index in range(pieces)
    ]


def after(block, *others, flops=1024):
    return pl.pallas_call(
        lambda *refs: None,
        out_shape=jax.ShapeDtypeStruct(block.shape, block.dtype),
        in_specs=[ANYWHERE] * (1 + len(others)),
        out_specs=ANYWHERE,
        input_output_aliases={0: 0},
        cost_estimate=pl.CostEstimate(flops=flops, bytes_accessed=1024, transcendentals=0),
    )(block, *others)


def by_kind(plan_ref, kinds, run):
    if kinds[0] is kinds[1]:
        run(kinds[0])
        return
    for kind, value in zip(kinds, (1, 0)):

        @pl.when(plan_ref[INNER_AT] == value)
        def _(kind=kind):
            run(kind)


def part_of(plan, if_inner, if_outer, start, size, *others, flops=1024):
    shape = jax.ShapeDtypeStruct((size, if_inner.shape[1]), if_inner.dtype)
    pieces = 4

    def body(plan_ref, inner_ref, outer_ref, *rest):
        out_ref, buffer, in_sems, out_sems = rest[len(others) :]

        def run(source):
            inward = copies(source, start, buffer, size, pieces, in_sems, 0)
            outward = copies(buffer, 0, out_ref, size, pieces, out_sems, 0)
            for copy in inward:
                copy.start()
            for copy, next_copy in zip(inward, outward):
                copy.wait()
                next_copy.start()
            for copy in outward:
                copy.wait()

        by_kind(plan_ref, (inner_ref, inner_ref if if_outer is if_inner else outer_ref), run)

    return pl.pallas_call(
        body,
        out_shape=shape,
        in_specs=[SMEM] + [ANYWHERE] * (2 + len(others)),
        out_specs=ANYWHERE,
        scratch_shapes=[pltpu.VMEM(shape.shape, shape.dtype)]
        + [pltpu.SemaphoreType.DMA((pieces,))] * 2,
        compiler_params=pltpu.CompilerParams(vmem_limit_bytes=VMEM_LIMIT),
        cost_estimate=pl.CostEstimate(flops=flops, bytes_accessed=1024, transcendentals=0),
    )(plan, if_inner, if_outer, *others)


def with_facts(rows, gates, block_list, block_count, owner):
    count, width = rows.shape
    blocks, _, offsets = block_list.shape
    total = owner.shape[0]

    def body(rows_ref, gates_ref, list_ref, count_ref, owner_ref, out_ref, sems):
        moves = copies(rows_ref, 0, out_ref, count, 4, sems, 0)
        for copy in moves:
            copy.start()
        block_of = lax.broadcasted_iota(jnp.int32, (1, total), 1) // (total // blocks)
        facts = []
        for offset in range(offsets):
            mask = jnp.zeros((1, total), jnp.float32)
            for block in range(blocks):
                used = jnp.int32(0)
                for place in range(blocks):
                    found = (list_ref[place, 0, offset] == block) & (place < count_ref[0, offset])
                    used = used | found.astype(jnp.int32)
                mask = mask + jnp.where(block_of == block, used.astype(jnp.float32), 0.0)
            facts.append(gates_ref[offset : offset + 1, :] * mask)
        numbers = owner_ref[...].reshape(1, total)
        facts.append((numbers >> 8).astype(jnp.float32))
        facts.append((numbers & 255).astype(jnp.float32))
        facts.append(jnp.zeros((FACT_ROWS - len(facts), total), jnp.float32))
        out_ref[count:, :] = jnp.zeros((FACT_ROWS, width), jnp.bfloat16)
        out_ref[count:, :total] = jnp.concatenate(facts, axis=0).astype(jnp.bfloat16)
        for copy in moves:
            copy.wait()

    shape = jax.ShapeDtypeStruct((count + FACT_ROWS, width), rows.dtype)
    return on_core(
        body, shape, [ANYWHERE, VMEM, SMEM, SMEM, VMEM], [pltpu.SemaphoreType.DMA((4,))]
    )(rows, gates, block_list, block_count, owner)


def partial_sums(plan, sizes, parts, weights, places, before=None, send=True, waits=()):
    width, columns = weights[0].shape
    blocks = [
        block if isinstance(block, tuple) else (block,) for part in parts for block in part
    ]
    sources = [array for block in blocks for array in block]
    operands = [plan] + sources + [weights[place] for place in places] + [weights[2]]
    if before is not None:
        operands.append(before)
    specs = [SMEM] + [VMEM] * (len(operands) - 1 + len(waits))
    has_before = before is not None

    def body(plan_ref, *refs):
        source_refs, refs = refs[: len(sources)], refs[len(sources) :]
        weight_refs, refs = refs[: len(places) + 1], refs[len(places) + 1 :]
        before_ref, refs = (refs[0], refs[1:]) if has_before else (None, refs)
        results = refs[len(waits) :]
        start, source = 0, 0
        for part, size in enumerate(sizes):
            span = slice(start, start + size)
            start += size
            rows = []
            for index in range(len(places)):
                block = blocks[part * len(places) + index]
                value = source_refs[source][:size, :]
                if len(block) > 1:
                    other = source_refs[source + 1][:size, :]
                    value = jnp.where(plan_ref[INNER_AT] == 1, value, other)
                source += len(block)
                rows.append(value)
            for side in range(2):
                at = slice(side * columns, (side + 1) * columns)
                total = before_ref[span, at] if has_before else None
                for index, place in enumerate(places):
                    if side == 0:
                        weight = weight_refs[index][...]
                    else:
                        weight = weight_refs[-1][place * width : (place + 1) * width, :]
                    product = jnp.dot(rows[index], weight, preferred_element_type=jnp.float32)
                    total = product if total is None else total + product
                results[0][span, at] = total
                if send:
                    results[1][span, at] = total.astype(jnp.bfloat16)
        results[-1][...] = jnp.zeros(TOKEN.shape, TOKEN.dtype)

    shapes = [jax.ShapeDtypeStruct((sum(sizes), 2 * columns), jnp.float32)]
    if send:
        shapes.append(jax.ShapeDtypeStruct((sum(sizes), 2 * columns), jnp.bfloat16))
    return on_core(body, shapes + [TOKEN], specs)(*operands, *waits)


def collected_rows(owned, slot, plan, sums, got, facts, before):
    units = sums.shape[1] // 4
    hidden = []
    for core in range(2):
        here, there = 2 * core * units, 2 * (1 - core) * units
        gate = sums[:, here : here + units] + got[:, there : there + units].astype(jnp.float32)
        up = sums[:, here + units : here + 2 * units]
        up = up + got[:, there + units : there + 2 * units].astype(jnp.float32)
        hidden.append((gate / (1.0 + jnp.exp(-gate)) * up).astype(jnp.bfloat16))
    hidden = jnp.concatenate(hidden, axis=1)
    values = facts[:, : sums.shape[0]].astype(jnp.float32)
    kind = lax.broadcasted_iota(jnp.int32, (FACT_ROWS, 1), 0)
    mine = kind == plan[OFFSETS_AT + slot]
    factor = jnp.sum(jnp.where(mine, values, 0.0), axis=0, keepdims=True)
    owner = (values[4:5, :] * 256.0 + values[5:6, :]).astype(jnp.int32)
    results = []
    for index in range(4):
        token = plan[index] * owned + lax.broadcasted_iota(jnp.int32, (owned, 1), 0)
        placing = jnp.where(owner == token, factor, 0.0).astype(jnp.bfloat16)
        rows = jnp.dot(placing, hidden, preferred_element_type=jnp.float32)
        if before is not None:
            rows = rows + before[index * owned : (index + 1) * owned, :]
        results.append(rows)
    return results


def fact_scratch(width):
    return [pltpu.VMEM((FACT_ROWS, width), jnp.bfloat16), pltpu.SemaphoreType.DMA((1,))]


def facts_of(plan_ref, inner_ref, outer_ref, buffer, sem):
    last = inner_ref.shape[0] - FACT_ROWS

    def run(source):
        (copy,) = copies(source, last, buffer, FACT_ROWS, 1, sem, 0)
        copy.start()
        copy.wait()

    by_kind(plan_ref, (inner_ref, outer_ref), run)
    return buffer


def collect(owned, slot, plan, sums, got, facts, before):
    operands = [plan, sums, got, *facts] + ([] if before is None else [before])

    def body(plan_ref, sums_ref, got_ref, inner_ref, outer_ref, *rest):
        before_ref = rest[0] if before is not None else None
        out_ref, token_ref, buffer, sem = rest[-4:]
        facts_here = facts_of(plan_ref, inner_ref, outer_ref, buffer, sem)
        rows = collected_rows(owned, slot, plan_ref, sums_ref, got_ref, facts_here, before_ref)
        for index in range(4):
            out_ref[index * owned : (index + 1) * owned, :] = rows[index]
        token_ref[...] = jnp.zeros(TOKEN.shape, TOKEN.dtype)

    shape = jax.ShapeDtypeStruct((4 * owned, sums.shape[1] // 2), jnp.float32)
    specs = [SMEM, VMEM, VMEM, ANYWHERE, ANYWHERE] + [VMEM] * (len(operands) - 5)
    return on_core(body, [shape, TOKEN], specs, fact_scratch(facts[0].shape[1]))(*operands)


def added(block, other, *waits, flops=1024):
    def body(block_ref, other_ref, *rest):
        total = block_ref[...].astype(jnp.float32) + other_ref[...].astype(jnp.float32)
        rest[-1][...] = total.astype(jnp.bfloat16)

    return pl.pallas_call(
        body,
        out_shape=jax.ShapeDtypeStruct(block.shape, jnp.bfloat16),
        in_specs=[VMEM, VMEM] + [ANYWHERE] * len(waits),
        out_specs=VMEM,
        cost_estimate=pl.CostEstimate(flops=flops, bytes_accessed=1024, transcendentals=0),
    )(block, other, *waits)


def down(held, own_ref, lent_ref, sent_ref, kept_ref):
    units, width = own_ref.shape[0], kept_ref.shape[1]
    for out, at in ((kept_ref, slice(0, width)), (sent_ref, slice(width, 2 * width))):
        result = jnp.dot(held[:, :units], own_ref[:, at], preferred_element_type=jnp.float32)
        result += jnp.dot(held[:, units:], lent_ref[:, at], preferred_element_type=jnp.float32)
        out[...] = result.astype(out.dtype)


def finish(owned, slot, plan, sums, got, facts, before, down_own, down_lent):
    units = down_own.shape[0]
    width = down_own.shape[1] // 2
    pair = [
        jax.ShapeDtypeStruct((owned, width), jnp.bfloat16),
        jax.ShapeDtypeStruct((owned, width), jnp.float32),
    ]

    def first(plan_ref, sums_ref, got_ref, inner_ref, outer_ref, before_ref, *refs):
        own_ref, lent_ref, sent_ref, kept_ref, held_ref, buffer, sem = refs
        facts_here = facts_of(plan_ref, inner_ref, outer_ref, buffer, sem)
        rows = collected_rows(owned, slot, plan_ref, sums_ref, got_ref, facts_here, before_ref)
        down(rows[0].astype(jnp.bfloat16), own_ref, lent_ref, sent_ref, kept_ref)
        for index in range(1, 4):
            held_ref[(index - 1) * owned : index * owned, :] = rows[index].astype(jnp.bfloat16)

    def others(held_ref, own_ref, lent_ref, *refs):
        for index in range(3):
            held = held_ref[index * owned : (index + 1) * owned, :]
            down(held, own_ref, lent_ref, refs[2 * index], refs[2 * index + 1])

    held_shape = jax.ShapeDtypeStruct((3 * owned, 2 * units), jnp.bfloat16)
    specs = [SMEM, VMEM, VMEM, ANYWHERE, ANYWHERE] + [VMEM] * 3
    sent, kept, held = on_core(
        first, pair + [held_shape], specs, fact_scratch(facts[0].shape[1])
    )(plan, sums, got, *facts, before, down_own, down_lent)
    rest = on_core(others, pair * 3, [VMEM] * 3)(held, down_own, down_lent)
    return [sent, *rest[0::2]], [kept, *rest[1::2]]


def rows_travel(
    tokens, gate_weight, up_weight, down_weight, route_gates, block_list, block_count, owner_token
):
    position = lax.axis_index("blk")
    share = lax.axis_index("tp")
    row_count, width = tokens.shape
    units = gate_weight.shape[2]
    owned = row_count // 2
    half = row_count // 2
    plan = jnp.asarray(PLAN, jnp.int32)[position]

    own_far = across_chips(tokens)
    own = with_facts(
        tokens, route_gates.T, jnp.transpose(block_list, (2, 0, 1)), block_count, owner_token
    )
    beside = along(own, BESIDE)
    middle = along(own, MIDDLE)

    gate_quarters = gate_weight[0].reshape(4, width, units)
    up_quarters = up_weight[0].reshape(4, width, units)

    def quarter(j):
        pair = [
            lax.dynamic_index_in_dim(q, share ^ j, 0, keepdims=False)
            for q in (gate_quarters, up_quarters)
        ]
        return jnp.concatenate(pair, axis=1)

    def down_part(j):
        return lax.dynamic_slice_in_dim(down_weight[0], (share ^ j) * width, width, 1)

    kept_down = jnp.concatenate([down_part(0), down_part(2)], axis=1)
    lend_down = jnp.concatenate([down_part(1), down_part(3)], axis=1)


    def at_kind(block, positions):
        pairs = [(4 * p + i, 4 * p + (i ^ 2)) for p in positions for i in range(4)]
        return lax.ppermute(block, ("blk", "tp"), pairs)

    beside = after(beside, middle)
    inner_last = along(beside, MIDDLE)
    outer_next = after(along(middle, OUTWARD), flops=3 * 2**30)
    beside_far = across_chips(beside)
    own_far_half = part_of(plan, own_far, own_far, half, half, flops=6 * 2**30)
    inward_far = along(own_far_half, INWARD)
    lend = jnp.concatenate([quarter(1), quarter(3)])
    lent = across_cores(after(lend, own))
    weights = [quarter(0), quarter(2), lent]
    whole = [row_count]
    sums_0, send_0, ready_0 = partial_sums(
        plan, whole, [(tokens, own_far)], weights, (0, 1)
    )
    got_0 = across_cores(send_0)
    lent_down = across_cores(lend_down)

    outer_last = along(inner_last, OUTWARD)
    outer_next = after(outer_next, beside_far, lend_down, weights[0], weights[1])
    second = (middle, outer_next)
    second_far = (at_kind(middle, (1, 2)), at_kind(outer_next, (0, 3)))
    middle_far = along(inward_far, MIDDLE)
    sums_1, send_1, ready_1 = partial_sums(
        plan, whole, [(beside, beside_far)], weights, (0, 1)
    )
    got_1 = across_cores(send_1)

    last = (inner_last, outer_last)
    last_far_a = across_chips(
        part_of(plan, *last, 0, half, *second_far, middle_far, ready_0, ready_1)
    )
    outward_far = along(middle_far, OUTWARD)
    total, _ = collect(owned, 0, plan, sums_0, got_0, (own, own), None)
    total, collected_1 = collect(owned, 1, plan, sums_1, got_1, (beside, beside), total)
    sums_2, send_2, _ = partial_sums(plan, whole, [(second, second_far)], weights, (0, 1))
    got_2 = across_cores(send_2)
    near, _ = partial_sums(plan, whole, [(last,)], weights, (0,), send=False)
    sums_3, send_3, _ = partial_sums(
        plan,
        [half, half],
        [(last_far_a,), ((middle_far, outward_far),)],
        weights,
        (1,),
        before=near,
        waits=[collected_1],
    )
    got_3 = across_cores(send_3)
    total, _ = collect(owned, 2, plan, sums_2, got_2, second, total)
    sent, kept = finish(owned, 3, plan, sums_3, got_3, last, total, kept_down, lent_down)

    far = [across_chips(block) for block in sent]
    first = added(kept[0], far[0])
    middle = along(first, MIDDLE)
    inward = along(first, INWARD)
    second = added(kept[1], far[1], flops=4 * 2**30)
    two_in = along(second, TWO_IN)
    two_out = along(added(second, inward, middle), TWO_OUT)
    beside = along(added(kept[2], far[2], flops=4 * 2**30), BESIDE)
    arrived = [block.astype(jnp.float32) for block in (far[3], middle, two_in, two_out, beside)]
    return (kept[3] + sum(arrived)).astype(jnp.bfloat16)


def on_device(*args):
    block_list = args[5]
    sizes = (lax.axis_size("blk"), lax.axis_size("tp"), block_list.shape[1])
    if sizes == (4, 4, 4):
        return rows_travel(*args)
    return weights_travel(*args)


def solution(mesh):
    return jax.shard_map(
        on_device,
        mesh=mesh,
        in_specs=(
            P(("groups", "blk"), "tp"),
            P("blk", None, "tp"),
            P("blk", None, "tp"),
            P("blk", "tp", None),
            P(("groups", "blk"), None),
            P(("groups", "blk"), None, None),
            P(("groups", "blk"), None),
            P(("groups", "blk")),
        ),
        out_specs=P(("groups", "blk"), "tp"),
        check_vma=False,
    )
```

```python
import jax
import jax.numpy as jnp
from jax import lax
from jax.experimental import pallas as pl
from jax.experimental.pallas import tpu as pltpu
from jax.sharding import PartitionSpec as P


def shifted(block, axis, distance):
    devices = range(lax.axis_size(axis))
    route = [((i - distance) % len(devices), i) for i in devices]
    return lax.ppermute(block, axis, route)


def weights_travel(
    tokens, gate_weight, up_weight, down_weight, route_gates, block_list, block_count, owner_token
):
    whole_rows = lax.all_gather(tokens, "tp", axis=1, tiled=True)
    row_count = whole_rows.shape[0]
    width = whole_rows.shape[1]
    offsets_all = block_list.shape[1]
    block_total = block_list.shape[2]
    block_size = row_count // block_total
    blocks = whole_rows.reshape(block_total, block_size, width)
    gate_blocks = route_gates.reshape(block_total, block_size, offsets_all)
    totals = jnp.zeros((block_total, block_size, width), jnp.float32)

    def apply(totals, weights, offset, block_id):
        w_gate, w_up, w_down = weights
        block_rows = lax.dynamic_index_in_dim(blocks, block_id, 0, keepdims=False)
        gate_out = jnp.dot(block_rows, w_gate, preferred_element_type=jnp.float32)
        up_out = jnp.dot(block_rows, w_up, preferred_element_type=jnp.float32)
        hidden = (jax.nn.silu(gate_out) * up_out).astype(jnp.bfloat16)
        block_gates = lax.dynamic_index_in_dim(gate_blocks, block_id, 0, keepdims=False)
        factor = lax.dynamic_index_in_dim(block_gates, offset, 1, keepdims=False)
        product = jnp.dot(hidden, w_down, preferred_element_type=jnp.float32) * factor[:, None]
        before = lax.dynamic_index_in_dim(totals, block_id, 0, keepdims=False)
        return lax.dynamic_update_index_in_dim(totals, before + product, block_id, 0)

    resident = (gate_weight[0], up_weight[0], down_weight[0])
    arrived = [resident]
    holding = resident
    for offset in range(1, offsets_all):
        holding = shifted((holding[0], holding[1], holding[2]), "blk", 1)
        arrived.append(holding)
    for offset in range(offsets_all):
        weights = arrived[offset]

        def visit_block(position, totals, weights=weights, offset=offset):
            return apply(totals, weights, offset, block_list[0, offset, position])

        totals = lax.fori_loop(0, block_count[0, offset], visit_block, totals)
    summed = lax.psum_scatter(
        totals.reshape(row_count, width).astype(jnp.bfloat16), "tp", scatter_dimension=1, tiled=True
    )
    feature_share = summed.shape[1]
    cycle_size = lax.axis_size("blk")
    owned = row_count // 2
    capacity = max(2, 2 * row_count // cycle_size)
    target = owner_token // owned
    local_token = owner_token % owned
    target_table = (target[:, None] == jnp.arange(cycle_size, dtype=jnp.int32)[None, :]).astype(
        jnp.int32
    )
    running = jnp.cumsum(target_table, axis=0)
    rank = jnp.sum((running - 1) * target_table, axis=1)
    slot = target * capacity + rank
    send_rows = jnp.zeros((cycle_size * capacity, feature_share), jnp.bfloat16).at[slot].set(summed)
    send_index = jnp.full((cycle_size * capacity,), -1, jnp.int32).at[slot].set(local_token)
    send_rows = send_rows.reshape(cycle_size, capacity, feature_share)
    send_index = send_index.reshape(cycle_size, capacity)
    got_rows, got_index = (
        lax.all_to_all(send_rows, "blk", split_axis=0, concat_axis=0, tiled=True),
        lax.all_to_all(send_index, "blk", split_axis=0, concat_axis=0, tiled=True),
    )
    got_rows = got_rows.reshape(cycle_size * capacity, feature_share)
    got_index = got_index.reshape(cycle_size * capacity)
    placing = (got_index[:, None] == jnp.arange(owned, dtype=jnp.int32)[None, :]).astype(
        jnp.bfloat16
    )
    combined = lax.dot_general(
        placing, got_rows, (((0,), (0,)), ((), ())), preferred_element_type=jnp.float32
    )
    return combined.astype(jnp.bfloat16)


BESIDE = [(0, 1), (1, 0), (2, 3), (3, 2)]
MIDDLE = [(1, 2), (2, 1)]
INWARD = [(0, 1), (3, 2)]
OUTWARD = [(1, 0), (2, 3)]
TWO_IN = [(0, 2), (3, 1)]
TWO_OUT = [(1, 3), (2, 0)]
PLAN = [
    [3, 2, 1, 0, 0, 1, 2, 3, 0],
    [2, 3, 0, 1, 0, 3, 1, 2, 1],
    [1, 0, 3, 2, 0, 1, 3, 2, 1],
    [0, 1, 2, 3, 0, 3, 2, 1, 0],
]
OFFSETS_AT, INNER_AT = 4, 8
FACT_ROWS = 16
VMEM = pl.BlockSpec(memory_space=pltpu.VMEM)
SMEM = pl.BlockSpec(memory_space=pltpu.SMEM)
ANYWHERE = pl.BlockSpec(memory_space=pl.ANY)


def across_chips(block):
    return lax.ppermute(block, "tp", [(i, i ^ 2) for i in range(4)])


def across_cores(block):
    return lax.ppermute(block, "tp", [(i, i ^ 1) for i in range(4)])


def along(block, route):
    return lax.ppermute(block, "blk", route)


def cheap():
    return pl.CostEstimate(flops=1024, bytes_accessed=1024, transcendentals=0)


TOKEN = jax.ShapeDtypeStruct((8, 128), jnp.float32)
VMEM_LIMIT = 40 * 2**20


def on_core(body, out_shape, in_specs, scratch=()):
    return pl.pallas_call(
        body,
        out_shape=out_shape,
        in_specs=in_specs,
        out_specs=jax.tree.map(lambda _: VMEM, out_shape),
        scratch_shapes=scratch,
        compiler_params=pltpu.CompilerParams(vmem_limit_bytes=VMEM_LIMIT),
        cost_estimate=cheap(),
    )


def copies(source, start, target, size, pieces, sems, first):
    step = size // pieces
    return [
        pltpu.make_async_copy(
            source.at[pl.ds(start + index * step, step)],
            target.at[pl.ds(index * step, step)],
            sems.at[first + index],
        )
        for index in range(pieces)
    ]


def after(block, *others, flops=1024):
    return pl.pallas_call(
        lambda *refs: None,
        out_shape=jax.ShapeDtypeStruct(block.shape, block.dtype),
        in_specs=[ANYWHERE] * (1 + len(others)),
        out_specs=ANYWHERE,
        input_output_aliases={0: 0},
        cost_estimate=pl.CostEstimate(flops=flops, bytes_accessed=1024, transcendentals=0),
    )(block, *others)


def by_kind(plan_ref, kinds, run):
    if kinds[0] is kinds[1]:
        run(kinds[0])
        return
    for kind, value in zip(kinds, (1, 0)):

        @pl.when(plan_ref[INNER_AT] == value)
        def _(kind=kind):
            run(kind)


def part_of(plan, if_inner, if_outer, start, size, *others, flops=1024):
    shape = jax.ShapeDtypeStruct((size, if_inner.shape[1]), if_inner.dtype)
    pieces = 4

    def body(plan_ref, inner_ref, outer_ref, *rest):
        out_ref, buffer, in_sems, out_sems = rest[len(others) :]

        def run(source):
            inward = copies(source, start, buffer, size, pieces, in_sems, 0)
            outward = copies(buffer, 0, out_ref, size, pieces, out_sems, 0)
            for copy in inward:
                copy.start()
            for copy, next_copy in zip(inward, outward):
                copy.wait()
                next_copy.start()
            for copy in outward:
                copy.wait()

        by_kind(plan_ref, (inner_ref, inner_ref if if_outer is if_inner else outer_ref), run)

    return pl.pallas_call(
        body,
        out_shape=shape,
        in_specs=[SMEM] + [ANYWHERE] * (2 + len(others)),
        out_specs=ANYWHERE,
        scratch_shapes=[pltpu.VMEM(shape.shape, shape.dtype)]
        + [pltpu.SemaphoreType.DMA((pieces,))] * 2,
        compiler_params=pltpu.CompilerParams(vmem_limit_bytes=VMEM_LIMIT),
        cost_estimate=pl.CostEstimate(flops=flops, bytes_accessed=1024, transcendentals=0),
    )(plan, if_inner, if_outer, *others)


def with_facts(rows, gates, block_list, block_count, owner):
    count, width = rows.shape
    blocks, _, offsets = block_list.shape
    total = owner.shape[0]

    def body(rows_ref, gates_ref, list_ref, count_ref, owner_ref, out_ref, sems):
        moves = copies(rows_ref, 0, out_ref, count, 4, sems, 0)
        for copy in moves:
            copy.start()
        block_of = lax.broadcasted_iota(jnp.int32, (1, total), 1) // (total // blocks)
        facts = []
        for offset in range(offsets):
            mask = jnp.zeros((1, total), jnp.float32)
            for block in range(blocks):
                used = jnp.int32(0)
                for place in range(blocks):
                    found = (list_ref[place, 0, offset] == block) & (place < count_ref[0, offset])
                    used = used | found.astype(jnp.int32)
                mask = mask + jnp.where(block_of == block, used.astype(jnp.float32), 0.0)
            facts.append(gates_ref[offset : offset + 1, :] * mask)
        numbers = owner_ref[...].reshape(1, total)
        facts.append((numbers >> 8).astype(jnp.float32))
        facts.append((numbers & 255).astype(jnp.float32))
        facts.append(jnp.zeros((FACT_ROWS - len(facts), total), jnp.float32))
        out_ref[count:, :] = jnp.zeros((FACT_ROWS, width), jnp.bfloat16)
        out_ref[count:, :total] = jnp.concatenate(facts, axis=0).astype(jnp.bfloat16)
        for copy in moves:
            copy.wait()

    shape = jax.ShapeDtypeStruct((count + FACT_ROWS, width), rows.dtype)
    return on_core(
        body, shape, [ANYWHERE, VMEM, SMEM, SMEM, VMEM], [pltpu.SemaphoreType.DMA((4,))]
    )(rows, gates, block_list, block_count, owner)


def partial_sums(plan, sizes, parts, weights, places, before=None, send=True, waits=()):
    width, columns = weights[0].shape
    blocks = [
        block if isinstance(block, tuple) else (block,) for part in parts for block in part
    ]
    sources = [array for block in blocks for array in block]
    operands = [plan] + sources + [weights[place] for place in places] + [weights[2]]
    if before is not None:
        operands.append(before)
    specs = [SMEM] + [VMEM] * (len(operands) - 1 + len(waits))
    has_before = before is not None

    def body(plan_ref, *refs):
        source_refs, refs = refs[: len(sources)], refs[len(sources) :]
        weight_refs, refs = refs[: len(places) + 1], refs[len(places) + 1 :]
        before_ref, refs = (refs[0], refs[1:]) if has_before else (None, refs)
        results = refs[len(waits) :]
        start, source = 0, 0
        for part, size in enumerate(sizes):
            span = slice(start, start + size)
            start += size
            rows = []
            for index in range(len(places)):
                block = blocks[part * len(places) + index]
                value = source_refs[source][:size, :]
                if len(block) > 1:
                    other = source_refs[source + 1][:size, :]
                    value = jnp.where(plan_ref[INNER_AT] == 1, value, other)
                source += len(block)
                rows.append(value)
            for side in range(2):
                at = slice(side * columns, (side + 1) * columns)
                total = before_ref[span, at] if has_before else None
                for index, place in enumerate(places):
                    if side == 0:
                        weight = weight_refs[index][...]
                    else:
                        weight = weight_refs[-1][place * width : (place + 1) * width, :]
                    product = jnp.dot(rows[index], weight, preferred_element_type=jnp.float32)
                    total = product if total is None else total + product
                results[0][span, at] = total
                if send:
                    results[1][span, at] = total.astype(jnp.bfloat16)
        results[-1][...] = jnp.zeros(TOKEN.shape, TOKEN.dtype)

    shapes = [jax.ShapeDtypeStruct((sum(sizes), 2 * columns), jnp.float32)]
    if send:
        shapes.append(jax.ShapeDtypeStruct((sum(sizes), 2 * columns), jnp.bfloat16))
    return on_core(body, shapes + [TOKEN], specs)(*operands, *waits)


def collected_rows(owned, slot, plan, sums, got, facts, before):
    units = sums.shape[1] // 4
    hidden = []
    for core in range(2):
        here, there = 2 * core * units, 2 * (1 - core) * units
        gate = sums[:, here : here + units] + got[:, there : there + units].astype(jnp.float32)
        up = sums[:, here + units : here + 2 * units]
        up = up + got[:, there + units : there + 2 * units].astype(jnp.float32)
        hidden.append((gate / (1.0 + jnp.exp(-gate)) * up).astype(jnp.bfloat16))
    hidden = jnp.concatenate(hidden, axis=1)
    values = facts[:, : sums.shape[0]].astype(jnp.float32)
    kind = lax.broadcasted_iota(jnp.int32, (FACT_ROWS, 1), 0)
    mine = kind == plan[OFFSETS_AT + slot]
    factor = jnp.sum(jnp.where(mine, values, 0.0), axis=0, keepdims=True)
    owner = (values[4:5, :] * 256.0 + values[5:6, :]).astype(jnp.int32)
    results = []
    for index in range(4):
        token = plan[index] * owned + lax.broadcasted_iota(jnp.int32, (owned, 1), 0)
        placing = jnp.where(owner == token, factor, 0.0).astype(jnp.bfloat16)
        rows = jnp.dot(placing, hidden, preferred_element_type=jnp.float32)
        if before is not None:
            rows = rows + before[index * owned : (index + 1) * owned, :]
        results.append(rows)
    return results


def fact_scratch(width):
    return [pltpu.VMEM((FACT_ROWS, width), jnp.bfloat16), pltpu.SemaphoreType.DMA((1,))]


def facts_of(plan_ref, inner_ref, outer_ref, buffer, sem):
    last = inner_ref.shape[0] - FACT_ROWS

    def run(source):
        (copy,) = copies(source, last, buffer, FACT_ROWS, 1, sem, 0)
        copy.start()
        copy.wait()

    by_kind(plan_ref, (inner_ref, outer_ref), run)
    return buffer


def collect(owned, slot, plan, sums, got, facts, before):
    operands = [plan, sums, got, *facts] + ([] if before is None else [before])

    def body(plan_ref, sums_ref, got_ref, inner_ref, outer_ref, *rest):
        before_ref = rest[0] if before is not None else None
        out_ref, token_ref, buffer, sem = rest[-4:]
        facts_here = facts_of(plan_ref, inner_ref, outer_ref, buffer, sem)
        rows = collected_rows(owned, slot, plan_ref, sums_ref, got_ref, facts_here, before_ref)
        for index in range(4):
            out_ref[index * owned : (index + 1) * owned, :] = rows[index]
        token_ref[...] = jnp.zeros(TOKEN.shape, TOKEN.dtype)

    shape = jax.ShapeDtypeStruct((4 * owned, sums.shape[1] // 2), jnp.float32)
    specs = [SMEM, VMEM, VMEM, ANYWHERE, ANYWHERE] + [VMEM] * (len(operands) - 5)
    return on_core(body, [shape, TOKEN], specs, fact_scratch(facts[0].shape[1]))(*operands)


def added(block, other, *waits, flops=1024):
    def body(block_ref, other_ref, *rest):
        total = block_ref[...].astype(jnp.float32) + other_ref[...].astype(jnp.float32)
        rest[-1][...] = total.astype(jnp.bfloat16)

    return pl.pallas_call(
        body,
        out_shape=jax.ShapeDtypeStruct(block.shape, jnp.bfloat16),
        in_specs=[VMEM, VMEM] + [ANYWHERE] * len(waits),
        out_specs=VMEM,
        cost_estimate=pl.CostEstimate(flops=flops, bytes_accessed=1024, transcendentals=0),
    )(block, other, *waits)


def down(held, own_ref, lent_ref, sent_ref, kept_ref):
    units, width = own_ref.shape[0], kept_ref.shape[1]
    for out, at in ((kept_ref, slice(0, width)), (sent_ref, slice(width, 2 * width))):
        result = jnp.dot(held[:, :units], own_ref[:, at], preferred_element_type=jnp.float32)
        result += jnp.dot(held[:, units:], lent_ref[:, at], preferred_element_type=jnp.float32)
        out[...] = result.astype(out.dtype)


def finish(owned, slot, plan, sums, got, facts, before, down_own, down_lent):
    units = down_own.shape[0]
    width = down_own.shape[1] // 2
    pair = [
        jax.ShapeDtypeStruct((owned, width), jnp.bfloat16),
        jax.ShapeDtypeStruct((owned, width), jnp.float32),
    ]

    def first(plan_ref, sums_ref, got_ref, inner_ref, outer_ref, before_ref, *refs):
        own_ref, lent_ref, sent_ref, kept_ref, held_ref, buffer, sem = refs
        facts_here = facts_of(plan_ref, inner_ref, outer_ref, buffer, sem)
        rows = collected_rows(owned, slot, plan_ref, sums_ref, got_ref, facts_here, before_ref)
        down(rows[0].astype(jnp.bfloat16), own_ref, lent_ref, sent_ref, kept_ref)
        for index in range(1, 4):
            held_ref[(index - 1) * owned : index * owned, :] = rows[index].astype(jnp.bfloat16)

    def others(held_ref, own_ref, lent_ref, *refs):
        for index in range(3):
            held = held_ref[index * owned : (index + 1) * owned, :]
            down(held, own_ref, lent_ref, refs[2 * index], refs[2 * index + 1])

    held_shape = jax.ShapeDtypeStruct((3 * owned, 2 * units), jnp.bfloat16)
    specs = [SMEM, VMEM, VMEM, ANYWHERE, ANYWHERE] + [VMEM] * 3
    sent, kept, held = on_core(
        first, pair + [held_shape], specs, fact_scratch(facts[0].shape[1])
    )(plan, sums, got, *facts, before, down_own, down_lent)
    rest = on_core(others, pair * 3, [VMEM] * 3)(held, down_own, down_lent)
    return [sent, *rest[0::2]], [kept, *rest[1::2]]


def rows_travel(
    tokens, gate_weight, up_weight, down_weight, route_gates, block_list, block_count, owner_token
):
    position = lax.axis_index("blk")
    share = lax.axis_index("tp")
    row_count, width = tokens.shape
    units = gate_weight.shape[2]
    owned = row_count // 2
    half = row_count // 2
    plan = jnp.asarray(PLAN, jnp.int32)[position]

    own_far = across_chips(tokens)
    own = with_facts(
        tokens, route_gates.T, jnp.transpose(block_list, (2, 0, 1)), block_count, owner_token
    )
    beside = along(own, BESIDE)
    middle = along(own, MIDDLE)

    gate_quarters = gate_weight[0].reshape(4, width, units)
    up_quarters = up_weight[0].reshape(4, width, units)

    def quarter(j):
        pair = [
            lax.dynamic_index_in_dim(q, share ^ j, 0, keepdims=False)
            for q in (gate_quarters, up_quarters)
        ]
        return jnp.concatenate(pair, axis=1)

    def down_part(j):
        return lax.dynamic_slice_in_dim(down_weight[0], (share ^ j) * width, width, 1)

    kept_down = jnp.concatenate([down_part(0), down_part(2)], axis=1)
    lend_down = jnp.concatenate([down_part(1), down_part(3)], axis=1)


    def at_kind(block, positions):
        pairs = [(4 * p + i, 4 * p + (i ^ 2)) for p in positions for i in range(4)]
        return lax.ppermute(block, ("blk", "tp"), pairs)

    inner_last = along(beside, MIDDLE)
    outer_next = along(middle, OUTWARD)
    beside_far = across_chips(beside)
    own_far_half = part_of(plan, own_far, own_far, half, half, flops=12 * 2**30)
    inward_far = along(own_far_half, INWARD)
    lend = jnp.concatenate([quarter(1), quarter(3)])
    lent = across_cores(after(lend, own))
    weights = [quarter(0), quarter(2), lent]
    whole = [row_count]
    sums_0, send_0, ready_0 = partial_sums(
        plan, whole, [(tokens, own_far)], weights, (0, 1)
    )
    got_0 = across_cores(send_0)
    lent_down = across_cores(lend_down)

    outer_last = along(inner_last, OUTWARD)
    outer_next = after(
        outer_next, beside_far, inner_last, inward_far, lend_down, weights[0], weights[1]
    )
    second = (middle, outer_next)
    second_far = (at_kind(middle, (1, 2)), at_kind(outer_next, (0, 3)))
    middle_far = along(inward_far, MIDDLE)
    sums_1, send_1, ready_1 = partial_sums(
        plan, whole, [(beside, beside_far)], weights, (0, 1)
    )
    got_1 = across_cores(send_1)

    last = (inner_last, outer_last)
    last_far_a = across_chips(
        part_of(plan, *last, 0, half, *second_far, middle_far, ready_0, ready_1)
    )
    outward_far = along(middle_far, OUTWARD)
    total, _ = collect(owned, 0, plan, sums_0, got_0, (own, own), None)
    total, collected_1 = collect(owned, 1, plan, sums_1, got_1, (beside, beside), total)
    sums_2, send_2, _ = partial_sums(plan, whole, [(second, second_far)], weights, (0, 1))
    got_2 = across_cores(send_2)
    near, _ = partial_sums(plan, whole, [(last,)], weights, (0,), send=False)
    sums_3, send_3, _ = partial_sums(
        plan,
        [half, half],
        [(last_far_a,), ((middle_far, outward_far),)],
        weights,
        (1,),
        before=near,
        waits=[collected_1],
    )
    got_3 = across_cores(send_3)
    total, _ = collect(owned, 2, plan, sums_2, got_2, second, total)
    sent, kept = finish(owned, 3, plan, sums_3, got_3, last, total, kept_down, lent_down)

    joined = [k + across_chips(s).astype(jnp.float32) for s, k in zip(sent, kept)]
    first, second, third = [block.astype(jnp.bfloat16) for block in joined[:3]]
    inward = along(first, INWARD)
    middle = along(first, MIDDLE)
    two_in = along(second, TWO_IN)
    two_out = along(added(second, inward), TWO_OUT)
    beside = along(third, BESIDE)
    arrived = [block.astype(jnp.float32) for block in (middle, two_in, two_out, beside)]
    return (joined[3] + sum(arrived)).astype(jnp.bfloat16)


def on_device(*args):
    block_list = args[5]
    sizes = (lax.axis_size("blk"), lax.axis_size("tp"), block_list.shape[1])
    if sizes == (4, 4, 4):
        return rows_travel(*args)
    return weights_travel(*args)


def solution(mesh):
    return jax.shard_map(
        on_device,
        mesh=mesh,
        in_specs=(
            P(("groups", "blk"), "tp"),
            P("blk", None, "tp"),
            P("blk", None, "tp"),
            P("blk", "tp", None),
            P(("groups", "blk"), None),
            P(("groups", "blk"), None, None),
            P(("groups", "blk"), None),
            P(("groups", "blk")),
        ),
        out_specs=P(("groups", "blk"), "tp"),
        check_vma=False,
    )
```

```python
import jax
import jax.numpy as jnp
from jax import lax
from jax.experimental import pallas as pl
from jax.experimental.pallas import tpu as pltpu
from jax.sharding import PartitionSpec as P


def shifted(block, axis, distance):
    devices = range(lax.axis_size(axis))
    route = [((i - distance) % len(devices), i) for i in devices]
    return lax.ppermute(block, axis, route)


def weights_travel(
    tokens, gate_weight, up_weight, down_weight, route_gates, block_list, block_count, owner_token
):
    whole_rows = lax.all_gather(tokens, "tp", axis=1, tiled=True)
    row_count = whole_rows.shape[0]
    width = whole_rows.shape[1]
    offsets_all = block_list.shape[1]
    block_total = block_list.shape[2]
    block_size = row_count // block_total
    blocks = whole_rows.reshape(block_total, block_size, width)
    gate_blocks = route_gates.reshape(block_total, block_size, offsets_all)
    totals = jnp.zeros((block_total, block_size, width), jnp.float32)

    def apply(totals, weights, offset, block_id):
        w_gate, w_up, w_down = weights
        block_rows = lax.dynamic_index_in_dim(blocks, block_id, 0, keepdims=False)
        gate_out = jnp.dot(block_rows, w_gate, preferred_element_type=jnp.float32)
        up_out = jnp.dot(block_rows, w_up, preferred_element_type=jnp.float32)
        hidden = (jax.nn.silu(gate_out) * up_out).astype(jnp.bfloat16)
        block_gates = lax.dynamic_index_in_dim(gate_blocks, block_id, 0, keepdims=False)
        factor = lax.dynamic_index_in_dim(block_gates, offset, 1, keepdims=False)
        product = jnp.dot(hidden, w_down, preferred_element_type=jnp.float32) * factor[:, None]
        before = lax.dynamic_index_in_dim(totals, block_id, 0, keepdims=False)
        return lax.dynamic_update_index_in_dim(totals, before + product, block_id, 0)

    resident = (gate_weight[0], up_weight[0], down_weight[0])
    arrived = [resident]
    holding = resident
    for offset in range(1, offsets_all):
        holding = shifted((holding[0], holding[1], holding[2]), "blk", 1)
        arrived.append(holding)
    for offset in range(offsets_all):
        weights = arrived[offset]

        def visit_block(position, totals, weights=weights, offset=offset):
            return apply(totals, weights, offset, block_list[0, offset, position])

        totals = lax.fori_loop(0, block_count[0, offset], visit_block, totals)
    summed = lax.psum_scatter(
        totals.reshape(row_count, width).astype(jnp.bfloat16), "tp", scatter_dimension=1, tiled=True
    )
    feature_share = summed.shape[1]
    cycle_size = lax.axis_size("blk")
    owned = row_count // 2
    capacity = max(2, 2 * row_count // cycle_size)
    target = owner_token // owned
    local_token = owner_token % owned
    target_table = (target[:, None] == jnp.arange(cycle_size, dtype=jnp.int32)[None, :]).astype(
        jnp.int32
    )
    running = jnp.cumsum(target_table, axis=0)
    rank = jnp.sum((running - 1) * target_table, axis=1)
    slot = target * capacity + rank
    send_rows = jnp.zeros((cycle_size * capacity, feature_share), jnp.bfloat16).at[slot].set(summed)
    send_index = jnp.full((cycle_size * capacity,), -1, jnp.int32).at[slot].set(local_token)
    send_rows = send_rows.reshape(cycle_size, capacity, feature_share)
    send_index = send_index.reshape(cycle_size, capacity)
    got_rows, got_index = (
        lax.all_to_all(send_rows, "blk", split_axis=0, concat_axis=0, tiled=True),
        lax.all_to_all(send_index, "blk", split_axis=0, concat_axis=0, tiled=True),
    )
    got_rows = got_rows.reshape(cycle_size * capacity, feature_share)
    got_index = got_index.reshape(cycle_size * capacity)
    placing = (got_index[:, None] == jnp.arange(owned, dtype=jnp.int32)[None, :]).astype(
        jnp.bfloat16
    )
    combined = lax.dot_general(
        placing, got_rows, (((0,), (0,)), ((), ())), preferred_element_type=jnp.float32
    )
    return combined.astype(jnp.bfloat16)


BESIDE = [(0, 1), (1, 0), (2, 3), (3, 2)]
MIDDLE = [(1, 2), (2, 1)]
INWARD = [(0, 1), (3, 2)]
OUTWARD = [(1, 0), (2, 3)]
TWO_IN = [(0, 2), (3, 1)]
TWO_OUT = [(1, 3), (2, 0)]
PLAN = [
    [3, 2, 1, 0, 0, 1, 2, 3, 0],
    [2, 3, 0, 1, 0, 3, 1, 2, 1],
    [1, 0, 3, 2, 0, 1, 3, 2, 1],
    [0, 1, 2, 3, 0, 3, 2, 1, 0],
]
OFFSETS_AT, INNER_AT = 4, 8
FACT_ROWS = 16
VMEM = pl.BlockSpec(memory_space=pltpu.VMEM)
SMEM = pl.BlockSpec(memory_space=pltpu.SMEM)
ANYWHERE = pl.BlockSpec(memory_space=pl.ANY)


def across_chips(block):
    return lax.ppermute(block, "tp", [(i, i ^ 2) for i in range(4)])


def across_cores(block):
    return lax.ppermute(block, "tp", [(i, i ^ 1) for i in range(4)])


def along(block, route):
    return lax.ppermute(block, "blk", route)


def cheap():
    return pl.CostEstimate(flops=1024, bytes_accessed=1024, transcendentals=0)


TOKEN = jax.ShapeDtypeStruct((8, 128), jnp.float32)
VMEM_LIMIT = 40 * 2**20


def on_core(body, out_shape, in_specs, scratch=()):
    return pl.pallas_call(
        body,
        out_shape=out_shape,
        in_specs=in_specs,
        out_specs=jax.tree.map(lambda _: VMEM, out_shape),
        scratch_shapes=scratch,
        compiler_params=pltpu.CompilerParams(vmem_limit_bytes=VMEM_LIMIT),
        cost_estimate=cheap(),
    )


def copies(source, start, target, size, pieces, sems, first):
    step = size // pieces
    return [
        pltpu.make_async_copy(
            source.at[pl.ds(start + index * step, step)],
            target.at[pl.ds(index * step, step)],
            sems.at[first + index],
        )
        for index in range(pieces)
    ]


def after(block, *others, flops=1024):
    return pl.pallas_call(
        lambda *refs: None,
        out_shape=jax.ShapeDtypeStruct(block.shape, block.dtype),
        in_specs=[ANYWHERE] * (1 + len(others)),
        out_specs=ANYWHERE,
        input_output_aliases={0: 0},
        cost_estimate=pl.CostEstimate(flops=flops, bytes_accessed=1024, transcendentals=0),
    )(block, *others)


def by_kind(plan_ref, kinds, run):
    if kinds[0] is kinds[1]:
        run(kinds[0])
        return
    for kind, value in zip(kinds, (1, 0)):

        @pl.when(plan_ref[INNER_AT] == value)
        def _(kind=kind):
            run(kind)


def part_of(plan, if_inner, if_outer, start, size, *others, flops=1024):
    shape = jax.ShapeDtypeStruct((size, if_inner.shape[1]), if_inner.dtype)
    pieces = 4

    def body(plan_ref, inner_ref, outer_ref, *rest):
        out_ref, buffer, in_sems, out_sems = rest[len(others) :]

        def run(source):
            inward = copies(source, start, buffer, size, pieces, in_sems, 0)
            outward = copies(buffer, 0, out_ref, size, pieces, out_sems, 0)
            for copy in inward:
                copy.start()
            for copy, next_copy in zip(inward, outward):
                copy.wait()
                next_copy.start()
            for copy in outward:
                copy.wait()

        by_kind(plan_ref, (inner_ref, inner_ref if if_outer is if_inner else outer_ref), run)

    return pl.pallas_call(
        body,
        out_shape=shape,
        in_specs=[SMEM] + [ANYWHERE] * (2 + len(others)),
        out_specs=ANYWHERE,
        scratch_shapes=[pltpu.VMEM(shape.shape, shape.dtype)]
        + [pltpu.SemaphoreType.DMA((pieces,))] * 2,
        compiler_params=pltpu.CompilerParams(vmem_limit_bytes=VMEM_LIMIT),
        cost_estimate=pl.CostEstimate(flops=flops, bytes_accessed=1024, transcendentals=0),
    )(plan, if_inner, if_outer, *others)


def with_facts(rows, gates, block_list, block_count, owner):
    count, width = rows.shape
    blocks, _, offsets = block_list.shape
    total = owner.shape[0]

    def body(rows_ref, gates_ref, list_ref, count_ref, owner_ref, out_ref, sems):
        moves = copies(rows_ref, 0, out_ref, count, 4, sems, 0)
        for copy in moves:
            copy.start()
        block_of = lax.broadcasted_iota(jnp.int32, (1, total), 1) // (total // blocks)
        facts = []
        for offset in range(offsets):
            mask = jnp.zeros((1, total), jnp.float32)
            for block in range(blocks):
                used = jnp.int32(0)
                for place in range(blocks):
                    found = (list_ref[place, 0, offset] == block) & (place < count_ref[0, offset])
                    used = used | found.astype(jnp.int32)
                mask = mask + jnp.where(block_of == block, used.astype(jnp.float32), 0.0)
            facts.append(gates_ref[offset : offset + 1, :] * mask)
        numbers = owner_ref[...].reshape(1, total)
        facts.append((numbers >> 8).astype(jnp.float32))
        facts.append((numbers & 255).astype(jnp.float32))
        facts.append(jnp.zeros((FACT_ROWS - len(facts), total), jnp.float32))
        out_ref[count:, :] = jnp.zeros((FACT_ROWS, width), jnp.bfloat16)
        out_ref[count:, :total] = jnp.concatenate(facts, axis=0).astype(jnp.bfloat16)
        for copy in moves:
            copy.wait()

    shape = jax.ShapeDtypeStruct((count + FACT_ROWS, width), rows.dtype)
    return on_core(
        body, shape, [ANYWHERE, VMEM, SMEM, SMEM, VMEM], [pltpu.SemaphoreType.DMA((4,))]
    )(rows, gates, block_list, block_count, owner)


def partial_sums(plan, sizes, parts, weights, places, before=None, send=True, waits=()):
    width, columns = weights[0].shape
    blocks = [
        block if isinstance(block, tuple) else (block,) for part in parts for block in part
    ]
    sources = [array for block in blocks for array in block]
    operands = [plan] + sources + [weights[place] for place in places] + [weights[2]]
    if before is not None:
        operands.append(before)
    specs = [SMEM] + [VMEM] * (len(operands) - 1 + len(waits))
    has_before = before is not None

    def body(plan_ref, *refs):
        source_refs, refs = refs[: len(sources)], refs[len(sources) :]
        weight_refs, refs = refs[: len(places) + 1], refs[len(places) + 1 :]
        before_ref, refs = (refs[0], refs[1:]) if has_before else (None, refs)
        results = refs[len(waits) :]
        start, source = 0, 0
        for part, size in enumerate(sizes):
            span = slice(start, start + size)
            start += size
            rows = []
            for index in range(len(places)):
                block = blocks[part * len(places) + index]
                value = source_refs[source][:size, :]
                if len(block) > 1:
                    other = source_refs[source + 1][:size, :]
                    value = jnp.where(plan_ref[INNER_AT] == 1, value, other)
                source += len(block)
                rows.append(value)
            for side in range(2):
                at = slice(side * columns, (side + 1) * columns)
                total = before_ref[span, at] if has_before else None
                for index, place in enumerate(places):
                    if side == 0:
                        weight = weight_refs[index][...]
                    else:
                        weight = weight_refs[-1][place * width : (place + 1) * width, :]
                    product = jnp.dot(rows[index], weight, preferred_element_type=jnp.float32)
                    total = product if total is None else total + product
                results[0][span, at] = total
                if send:
                    results[1][span, at] = total.astype(jnp.bfloat16)
        results[-1][...] = jnp.zeros(TOKEN.shape, TOKEN.dtype)

    shapes = [jax.ShapeDtypeStruct((sum(sizes), 2 * columns), jnp.float32)]
    if send:
        shapes.append(jax.ShapeDtypeStruct((sum(sizes), 2 * columns), jnp.bfloat16))
    return on_core(body, shapes + [TOKEN], specs)(*operands, *waits)


def collected_rows(owned, slot, plan, sums, got, facts, before):
    units = sums.shape[1] // 4
    hidden = []
    for core in range(2):
        here, there = 2 * core * units, 2 * (1 - core) * units
        gate = sums[:, here : here + units] + got[:, there : there + units].astype(jnp.float32)
        up = sums[:, here + units : here + 2 * units]
        up = up + got[:, there + units : there + 2 * units].astype(jnp.float32)
        hidden.append((gate / (1.0 + jnp.exp(-gate)) * up).astype(jnp.bfloat16))
    hidden = jnp.concatenate(hidden, axis=1)
    values = facts[:, : sums.shape[0]].astype(jnp.float32)
    kind = lax.broadcasted_iota(jnp.int32, (FACT_ROWS, 1), 0)
    mine = kind == plan[OFFSETS_AT + slot]
    factor = jnp.sum(jnp.where(mine, values, 0.0), axis=0, keepdims=True)
    owner = (values[4:5, :] * 256.0 + values[5:6, :]).astype(jnp.int32)
    results = []
    for index in range(4):
        token = plan[index] * owned + lax.broadcasted_iota(jnp.int32, (owned, 1), 0)
        placing = jnp.where(owner == token, factor, 0.0).astype(jnp.bfloat16)
        rows = jnp.dot(placing, hidden, preferred_element_type=jnp.float32)
        if before is not None:
            rows = rows + before[index * owned : (index + 1) * owned, :]
        results.append(rows)
    return results


def fact_scratch(width):
    return [pltpu.VMEM((FACT_ROWS, width), jnp.bfloat16), pltpu.SemaphoreType.DMA((1,))]


def facts_of(plan_ref, inner_ref, outer_ref, buffer, sem):
    last = inner_ref.shape[0] - FACT_ROWS

    def run(source):
        (copy,) = copies(source, last, buffer, FACT_ROWS, 1, sem, 0)
        copy.start()
        copy.wait()

    by_kind(plan_ref, (inner_ref, outer_ref), run)
    return buffer


def collect(owned, slot, plan, sums, got, facts, before):
    operands = [plan, sums, got, *facts] + ([] if before is None else [before])

    def body(plan_ref, sums_ref, got_ref, inner_ref, outer_ref, *rest):
        before_ref = rest[0] if before is not None else None
        out_ref, token_ref, buffer, sem = rest[-4:]
        facts_here = facts_of(plan_ref, inner_ref, outer_ref, buffer, sem)
        rows = collected_rows(owned, slot, plan_ref, sums_ref, got_ref, facts_here, before_ref)
        for index in range(4):
            out_ref[index * owned : (index + 1) * owned, :] = rows[index]
        token_ref[...] = jnp.zeros(TOKEN.shape, TOKEN.dtype)

    shape = jax.ShapeDtypeStruct((4 * owned, sums.shape[1] // 2), jnp.float32)
    specs = [SMEM, VMEM, VMEM, ANYWHERE, ANYWHERE] + [VMEM] * (len(operands) - 5)
    return on_core(body, [shape, TOKEN], specs, fact_scratch(facts[0].shape[1]))(*operands)


def down(held, own_ref, lent_ref, sent_ref, kept_ref):
    units, width = own_ref.shape[0], kept_ref.shape[1]
    for out, at in ((kept_ref, slice(0, width)), (sent_ref, slice(width, 2 * width))):
        result = jnp.dot(held[:, :units], own_ref[:, at], preferred_element_type=jnp.float32)
        result += jnp.dot(held[:, units:], lent_ref[:, at], preferred_element_type=jnp.float32)
        out[...] = result.astype(out.dtype)


def finish(owned, slot, plan, sums, got, facts, before, down_own, down_lent):
    units = down_own.shape[0]
    width = down_own.shape[1] // 2
    pair = [
        jax.ShapeDtypeStruct((owned, width), jnp.bfloat16),
        jax.ShapeDtypeStruct((owned, width), jnp.float32),
    ]

    def first(plan_ref, sums_ref, got_ref, inner_ref, outer_ref, before_ref, *refs):
        own_ref, lent_ref, sent_ref, kept_ref, held_ref, buffer, sem = refs
        facts_here = facts_of(plan_ref, inner_ref, outer_ref, buffer, sem)
        rows = collected_rows(owned, slot, plan_ref, sums_ref, got_ref, facts_here, before_ref)
        down(rows[0].astype(jnp.bfloat16), own_ref, lent_ref, sent_ref, kept_ref)
        for index in range(1, 4):
            held_ref[(index - 1) * owned : index * owned, :] = rows[index].astype(jnp.bfloat16)

    def others(held_ref, own_ref, lent_ref, *refs):
        for index in range(3):
            held = held_ref[index * owned : (index + 1) * owned, :]
            down(held, own_ref, lent_ref, refs[2 * index], refs[2 * index + 1])

    held_shape = jax.ShapeDtypeStruct((3 * owned, 2 * units), jnp.bfloat16)
    specs = [SMEM, VMEM, VMEM, ANYWHERE, ANYWHERE] + [VMEM] * 3
    sent, kept, held = on_core(
        first, pair + [held_shape], specs, fact_scratch(facts[0].shape[1])
    )(plan, sums, got, *facts, before, down_own, down_lent)
    rest = on_core(others, pair * 3, [VMEM] * 3)(held, down_own, down_lent)
    return [sent, *rest[0::2]], [kept, *rest[1::2]]


def rows_travel(
    tokens, gate_weight, up_weight, down_weight, route_gates, block_list, block_count, owner_token
):
    position = lax.axis_index("blk")
    share = lax.axis_index("tp")
    row_count, width = tokens.shape
    units = gate_weight.shape[2]
    owned = row_count // 2
    half = row_count // 2
    plan = jnp.asarray(PLAN, jnp.int32)[position]

    own_far = across_chips(tokens)
    own = with_facts(
        tokens, route_gates.T, jnp.transpose(block_list, (2, 0, 1)), block_count, owner_token
    )
    beside = along(own, BESIDE)
    middle = along(own, MIDDLE)

    gate_quarters = gate_weight[0].reshape(4, width, units)
    up_quarters = up_weight[0].reshape(4, width, units)

    def quarter(j):
        pair = [
            lax.dynamic_index_in_dim(q, share ^ j, 0, keepdims=False)
            for q in (gate_quarters, up_quarters)
        ]
        return jnp.concatenate(pair, axis=1)

    def down_part(j):
        return lax.dynamic_slice_in_dim(down_weight[0], (share ^ j) * width, width, 1)

    kept_down = jnp.concatenate([down_part(0), down_part(2)], axis=1)
    lend_down = jnp.concatenate([down_part(1), down_part(3)], axis=1)


    def at_kind(block, positions):
        pairs = [(4 * p + i, 4 * p + (i ^ 2)) for p in positions for i in range(4)]
        return lax.ppermute(block, ("blk", "tp"), pairs)

    inner_last = along(beside, MIDDLE)
    outer_next = along(middle, OUTWARD)
    beside_far = across_chips(beside)
    own_far_half = part_of(plan, own_far, own_far, half, half, flops=16 * 2**30)
    inward_far = along(own_far_half, INWARD)
    lend = jnp.concatenate([quarter(1), quarter(3)])
    lent = across_cores(after(lend, own))
    weights = [quarter(0), quarter(2), lent]
    whole = [row_count]
    sums_0, send_0, ready_0 = partial_sums(
        plan, whole, [(tokens, own_far)], weights, (0, 1)
    )
    got_0 = across_cores(send_0)
    lent_down = across_cores(lend_down)

    outer_last = along(inner_last, OUTWARD)
    outer_next = after(
        outer_next, beside_far, inner_last, inward_far, lend_down, weights[0], weights[1], ready_0
    )
    second = (middle, outer_next)
    second_far = (at_kind(middle, (1, 2)), at_kind(outer_next, (0, 3)))
    middle_far = along(inward_far, MIDDLE)
    sums_1, send_1, ready_1 = partial_sums(
        plan, whole, [(beside, beside_far)], weights, (0, 1)
    )
    got_1 = across_cores(send_1)

    last = (inner_last, outer_last)
    last_far_a = across_chips(
        part_of(plan, *last, 0, half, *second_far, middle_far, ready_0, ready_1)
    )
    outward_far = along(middle_far, OUTWARD)
    total, _ = collect(owned, 0, plan, sums_0, got_0, (own, own), None)
    total, collected_1 = collect(owned, 1, plan, sums_1, got_1, (beside, beside), total)
    sums_2, send_2, _ = partial_sums(plan, whole, [(second, second_far)], weights, (0, 1))
    got_2 = across_cores(send_2)
    near, _ = partial_sums(plan, whole, [(last,)], weights, (0,), send=False)
    sums_3, send_3, _ = partial_sums(
        plan,
        [half, half],
        [(last_far_a,), ((middle_far, outward_far),)],
        weights,
        (1,),
        before=near,
        waits=[collected_1],
    )
    got_3 = across_cores(send_3)
    total, _ = collect(owned, 2, plan, sums_2, got_2, second, total)
    sent, kept = finish(owned, 3, plan, sums_3, got_3, last, total, kept_down, lent_down)

    joined = [k + across_chips(s).astype(jnp.float32) for s, k in zip(sent, kept)]
    first, second, third = [block.astype(jnp.bfloat16) for block in joined[:3]]
    second = lax.optimization_barrier(second)
    inward = along(first, INWARD)
    middle = along(first, MIDDLE)
    two_in = along(second, TWO_IN)
    passed = second.astype(jnp.float32) + inward.astype(jnp.float32)
    two_out = along(passed.astype(jnp.bfloat16), TWO_OUT)
    beside = along(third, BESIDE)
    arrived = [block.astype(jnp.float32) for block in (middle, two_in, two_out)]
    total = lax.optimization_barrier(joined[3] + sum(arrived))
    return (total + beside.astype(jnp.float32)).astype(jnp.bfloat16)


def on_device(*args):
    block_list = args[5]
    sizes = (lax.axis_size("blk"), lax.axis_size("tp"), block_list.shape[1])
    if sizes == (4, 4, 4):
        return rows_travel(*args)
    return weights_travel(*args)


def solution(mesh):
    return jax.shard_map(
        on_device,
        mesh=mesh,
        in_specs=(
            P(("groups", "blk"), "tp"),
            P("blk", None, "tp"),
            P("blk", None, "tp"),
            P("blk", "tp", None),
            P(("groups", "blk"), None),
            P(("groups", "blk"), None, None),
            P(("groups", "blk"), None),
            P(("groups", "blk")),
        ),
        out_specs=P(("groups", "blk"), "tp"),
        check_vma=False,
    )
```

```python
import jax
import jax.numpy as jnp
from jax import lax
from jax.experimental import pallas as pl
from jax.experimental.pallas import tpu as pltpu
from jax.sharding import PartitionSpec as P


def shifted(block, axis, distance):
    devices = range(lax.axis_size(axis))
    route = [((i - distance) % len(devices), i) for i in devices]
    return lax.ppermute(block, axis, route)


def weights_travel(
    tokens, gate_weight, up_weight, down_weight, route_gates, block_list, block_count, owner_token
):
    whole_rows = lax.all_gather(tokens, "tp", axis=1, tiled=True)
    row_count = whole_rows.shape[0]
    width = whole_rows.shape[1]
    offsets_all = block_list.shape[1]
    block_total = block_list.shape[2]
    block_size = row_count // block_total
    blocks = whole_rows.reshape(block_total, block_size, width)
    gate_blocks = route_gates.reshape(block_total, block_size, offsets_all)
    totals = jnp.zeros((block_total, block_size, width), jnp.float32)

    def apply(totals, weights, offset, block_id):
        w_gate, w_up, w_down = weights
        block_rows = lax.dynamic_index_in_dim(blocks, block_id, 0, keepdims=False)
        gate_out = jnp.dot(block_rows, w_gate, preferred_element_type=jnp.float32)
        up_out = jnp.dot(block_rows, w_up, preferred_element_type=jnp.float32)
        hidden = (jax.nn.silu(gate_out) * up_out).astype(jnp.bfloat16)
        block_gates = lax.dynamic_index_in_dim(gate_blocks, block_id, 0, keepdims=False)
        factor = lax.dynamic_index_in_dim(block_gates, offset, 1, keepdims=False)
        product = jnp.dot(hidden, w_down, preferred_element_type=jnp.float32) * factor[:, None]
        before = lax.dynamic_index_in_dim(totals, block_id, 0, keepdims=False)
        return lax.dynamic_update_index_in_dim(totals, before + product, block_id, 0)

    resident = (gate_weight[0], up_weight[0], down_weight[0])
    arrived = [resident]
    holding = resident
    for offset in range(1, offsets_all):
        holding = shifted((holding[0], holding[1], holding[2]), "blk", 1)
        arrived.append(holding)
    for offset in range(offsets_all):
        weights = arrived[offset]

        def visit_block(position, totals, weights=weights, offset=offset):
            return apply(totals, weights, offset, block_list[0, offset, position])

        totals = lax.fori_loop(0, block_count[0, offset], visit_block, totals)
    summed = lax.psum_scatter(
        totals.reshape(row_count, width).astype(jnp.bfloat16), "tp", scatter_dimension=1, tiled=True
    )
    feature_share = summed.shape[1]
    cycle_size = lax.axis_size("blk")
    owned = row_count // 2
    capacity = max(2, 2 * row_count // cycle_size)
    target = owner_token // owned
    local_token = owner_token % owned
    target_table = (target[:, None] == jnp.arange(cycle_size, dtype=jnp.int32)[None, :]).astype(
        jnp.int32
    )
    running = jnp.cumsum(target_table, axis=0)
    rank = jnp.sum((running - 1) * target_table, axis=1)
    slot = target * capacity + rank
    send_rows = jnp.zeros((cycle_size * capacity, feature_share), jnp.bfloat16).at[slot].set(summed)
    send_index = jnp.full((cycle_size * capacity,), -1, jnp.int32).at[slot].set(local_token)
    send_rows = send_rows.reshape(cycle_size, capacity, feature_share)
    send_index = send_index.reshape(cycle_size, capacity)
    got_rows, got_index = (
        lax.all_to_all(send_rows, "blk", split_axis=0, concat_axis=0, tiled=True),
        lax.all_to_all(send_index, "blk", split_axis=0, concat_axis=0, tiled=True),
    )
    got_rows = got_rows.reshape(cycle_size * capacity, feature_share)
    got_index = got_index.reshape(cycle_size * capacity)
    placing = (got_index[:, None] == jnp.arange(owned, dtype=jnp.int32)[None, :]).astype(
        jnp.bfloat16
    )
    combined = lax.dot_general(
        placing, got_rows, (((0,), (0,)), ((), ())), preferred_element_type=jnp.float32
    )
    return combined.astype(jnp.bfloat16)


BESIDE = [(0, 1), (1, 0), (2, 3), (3, 2)]
MIDDLE = [(1, 2), (2, 1)]
INWARD = [(0, 1), (3, 2)]
OUTWARD = [(1, 0), (2, 3)]
TWO_IN = [(0, 2), (3, 1)]
TWO_OUT = [(1, 3), (2, 0)]
PLAN = [
    [3, 2, 1, 0, 0, 1, 2, 3, 0],
    [2, 3, 0, 1, 0, 3, 1, 2, 1],
    [1, 0, 3, 2, 0, 1, 3, 2, 1],
    [0, 1, 2, 3, 0, 3, 2, 1, 0],
]
OFFSETS_AT, INNER_AT = 4, 8
FACT_ROWS = 16
VMEM = pl.BlockSpec(memory_space=pltpu.VMEM)
SMEM = pl.BlockSpec(memory_space=pltpu.SMEM)
ANYWHERE = pl.BlockSpec(memory_space=pl.ANY)


def across_chips(block):
    return lax.ppermute(block, "tp", [(i, i ^ 2) for i in range(4)])


def across_cores(block):
    return lax.ppermute(block, "tp", [(i, i ^ 1) for i in range(4)])


def along(block, route):
    return lax.ppermute(block, "blk", route)


def cheap():
    return pl.CostEstimate(flops=1024, bytes_accessed=1024, transcendentals=0)


TOKEN = jax.ShapeDtypeStruct((8, 128), jnp.float32)
VMEM_LIMIT = 40 * 2**20


def on_core(body, out_shape, in_specs, scratch=()):
    return pl.pallas_call(
        body,
        out_shape=out_shape,
        in_specs=in_specs,
        out_specs=jax.tree.map(lambda _: VMEM, out_shape),
        scratch_shapes=scratch,
        compiler_params=pltpu.CompilerParams(vmem_limit_bytes=VMEM_LIMIT),
        cost_estimate=cheap(),
    )


def copies(source, start, target, size, pieces, sems, first):
    step = size // pieces
    return [
        pltpu.make_async_copy(
            source.at[pl.ds(start + index * step, step)],
            target.at[pl.ds(index * step, step)],
            sems.at[first + index],
        )
        for index in range(pieces)
    ]


def after(block, *others, flops=1024):
    return pl.pallas_call(
        lambda *refs: None,
        out_shape=jax.ShapeDtypeStruct(block.shape, block.dtype),
        in_specs=[ANYWHERE] * (1 + len(others)),
        out_specs=ANYWHERE,
        input_output_aliases={0: 0},
        cost_estimate=pl.CostEstimate(flops=flops, bytes_accessed=1024, transcendentals=0),
    )(block, *others)


def by_kind(plan_ref, kinds, run):
    if kinds[0] is kinds[1]:
        run(kinds[0])
        return
    for kind, value in zip(kinds, (1, 0)):

        @pl.when(plan_ref[INNER_AT] == value)
        def _(kind=kind):
            run(kind)


def part_of(plan, if_inner, if_outer, start, size, *others, flops=1024):
    shape = jax.ShapeDtypeStruct((size, if_inner.shape[1]), if_inner.dtype)
    pieces = 4

    def body(plan_ref, inner_ref, outer_ref, *rest):
        out_ref, buffer, in_sems, out_sems = rest[len(others) :]

        def run(source):
            inward = copies(source, start, buffer, size, pieces, in_sems, 0)
            outward = copies(buffer, 0, out_ref, size, pieces, out_sems, 0)
            for copy in inward:
                copy.start()
            for copy, next_copy in zip(inward, outward):
                copy.wait()
                next_copy.start()
            for copy in outward:
                copy.wait()

        by_kind(plan_ref, (inner_ref, inner_ref if if_outer is if_inner else outer_ref), run)

    return pl.pallas_call(
        body,
        out_shape=shape,
        in_specs=[SMEM] + [ANYWHERE] * (2 + len(others)),
        out_specs=ANYWHERE,
        scratch_shapes=[pltpu.VMEM(shape.shape, shape.dtype)]
        + [pltpu.SemaphoreType.DMA((pieces,))] * 2,
        compiler_params=pltpu.CompilerParams(vmem_limit_bytes=VMEM_LIMIT),
        cost_estimate=pl.CostEstimate(flops=flops, bytes_accessed=1024, transcendentals=0),
    )(plan, if_inner, if_outer, *others)


def with_facts(rows, gates, block_list, block_count, owner):
    count, width = rows.shape
    blocks, _, offsets = block_list.shape
    total = owner.shape[0]

    def body(rows_ref, gates_ref, list_ref, count_ref, owner_ref, out_ref, sems):
        moves = copies(rows_ref, 0, out_ref, count, 4, sems, 0)
        for copy in moves:
            copy.start()
        block_of = lax.broadcasted_iota(jnp.int32, (1, total), 1) // (total // blocks)
        facts = []
        for offset in range(offsets):
            mask = jnp.zeros((1, total), jnp.float32)
            for block in range(blocks):
                used = jnp.int32(0)
                for place in range(blocks):
                    found = (list_ref[place, 0, offset] == block) & (place < count_ref[0, offset])
                    used = used | found.astype(jnp.int32)
                mask = mask + jnp.where(block_of == block, used.astype(jnp.float32), 0.0)
            facts.append(gates_ref[offset : offset + 1, :] * mask)
        numbers = owner_ref[...].reshape(1, total)
        facts.append((numbers >> 8).astype(jnp.float32))
        facts.append((numbers & 255).astype(jnp.float32))
        facts.append(jnp.zeros((FACT_ROWS - len(facts), total), jnp.float32))
        out_ref[count:, :] = jnp.zeros((FACT_ROWS, width), jnp.bfloat16)
        out_ref[count:, :total] = jnp.concatenate(facts, axis=0).astype(jnp.bfloat16)
        for copy in moves:
            copy.wait()

    shape = jax.ShapeDtypeStruct((count + FACT_ROWS, width), rows.dtype)
    return on_core(
        body, shape, [ANYWHERE, VMEM, SMEM, SMEM, VMEM], [pltpu.SemaphoreType.DMA((4,))]
    )(rows, gates, block_list, block_count, owner)


def partial_sums(plan, sizes, parts, weights, places, before=None, send=True, waits=()):
    width, columns = weights[0].shape
    blocks = [
        block if isinstance(block, tuple) else (block,) for part in parts for block in part
    ]
    sources = [array for block in blocks for array in block]
    operands = [plan] + sources + [weights[place] for place in places] + [weights[2]]
    if before is not None:
        operands.append(before)
    specs = [SMEM] + [VMEM] * (len(operands) - 1 + len(waits))
    has_before = before is not None

    def body(plan_ref, *refs):
        source_refs, refs = refs[: len(sources)], refs[len(sources) :]
        weight_refs, refs = refs[: len(places) + 1], refs[len(places) + 1 :]
        before_ref, refs = (refs[0], refs[1:]) if has_before else (None, refs)
        results = refs[len(waits) :]
        start, source = 0, 0
        for part, size in enumerate(sizes):
            span = slice(start, start + size)
            start += size
            rows = []
            for index in range(len(places)):
                block = blocks[part * len(places) + index]
                value = source_refs[source][:size, :]
                if len(block) > 1:
                    other = source_refs[source + 1][:size, :]
                    value = jnp.where(plan_ref[INNER_AT] == 1, value, other)
                source += len(block)
                rows.append(value)
            for side in range(2):
                at = slice(side * columns, (side + 1) * columns)
                total = before_ref[span, at] if has_before else None
                for index, place in enumerate(places):
                    if side == 0:
                        weight = weight_refs[index][...]
                    else:
                        weight = weight_refs[-1][place * width : (place + 1) * width, :]
                    product = jnp.dot(rows[index], weight, preferred_element_type=jnp.float32)
                    total = product if total is None else total + product
                results[0][span, at] = total
                if send:
                    results[1][span, at] = total.astype(jnp.bfloat16)
        results[-1][...] = jnp.zeros(TOKEN.shape, TOKEN.dtype)

    shapes = [jax.ShapeDtypeStruct((sum(sizes), 2 * columns), jnp.float32)]
    if send:
        shapes.append(jax.ShapeDtypeStruct((sum(sizes), 2 * columns), jnp.bfloat16))
    return on_core(body, shapes + [TOKEN], specs)(*operands, *waits)


def collected_rows(owned, slot, plan, sums, got, facts, before):
    units = sums.shape[1] // 4
    hidden = []
    for core in range(2):
        here, there = 2 * core * units, 2 * (1 - core) * units
        gate = sums[:, here : here + units] + got[:, there : there + units].astype(jnp.float32)
        up = sums[:, here + units : here + 2 * units]
        up = up + got[:, there + units : there + 2 * units].astype(jnp.float32)
        hidden.append((gate / (1.0 + jnp.exp(-gate)) * up).astype(jnp.bfloat16))
    hidden = jnp.concatenate(hidden, axis=1)
    values = facts[:, : sums.shape[0]].astype(jnp.float32)
    kind = lax.broadcasted_iota(jnp.int32, (FACT_ROWS, 1), 0)
    mine = kind == plan[OFFSETS_AT + slot]
    factor = jnp.sum(jnp.where(mine, values, 0.0), axis=0, keepdims=True)
    owner = (values[4:5, :] * 256.0 + values[5:6, :]).astype(jnp.int32)
    results = []
    for index in range(4):
        token = plan[index] * owned + lax.broadcasted_iota(jnp.int32, (owned, 1), 0)
        placing = jnp.where(owner == token, factor, 0.0).astype(jnp.bfloat16)
        rows = jnp.dot(placing, hidden, preferred_element_type=jnp.float32)
        if before is not None:
            rows = rows + before[index * owned : (index + 1) * owned, :]
        results.append(rows)
    return results


def fact_scratch(width):
    return [pltpu.VMEM((FACT_ROWS, width), jnp.bfloat16), pltpu.SemaphoreType.DMA((1,))]


def facts_of(plan_ref, inner_ref, outer_ref, buffer, sem):
    last = inner_ref.shape[0] - FACT_ROWS

    def run(source):
        (copy,) = copies(source, last, buffer, FACT_ROWS, 1, sem, 0)
        copy.start()
        copy.wait()

    by_kind(plan_ref, (inner_ref, outer_ref), run)
    return buffer


def collect(owned, slot, plan, sums, got, facts, before):
    operands = [plan, sums, got, *facts] + ([] if before is None else [before])

    def body(plan_ref, sums_ref, got_ref, inner_ref, outer_ref, *rest):
        before_ref = rest[0] if before is not None else None
        out_ref, token_ref, buffer, sem = rest[-4:]
        facts_here = facts_of(plan_ref, inner_ref, outer_ref, buffer, sem)
        rows = collected_rows(owned, slot, plan_ref, sums_ref, got_ref, facts_here, before_ref)
        for index in range(4):
            out_ref[index * owned : (index + 1) * owned, :] = rows[index]
        token_ref[...] = jnp.zeros(TOKEN.shape, TOKEN.dtype)

    shape = jax.ShapeDtypeStruct((4 * owned, sums.shape[1] // 2), jnp.float32)
    specs = [SMEM, VMEM, VMEM, ANYWHERE, ANYWHERE] + [VMEM] * (len(operands) - 5)
    return on_core(body, [shape, TOKEN], specs, fact_scratch(facts[0].shape[1]))(*operands)


def down(held, own_ref, lent_ref, sent_ref, kept_ref):
    units, width = own_ref.shape[0], kept_ref.shape[1]
    for out, at in ((kept_ref, slice(0, width)), (sent_ref, slice(width, 2 * width))):
        result = jnp.dot(held[:, :units], own_ref[:, at], preferred_element_type=jnp.float32)
        result += jnp.dot(held[:, units:], lent_ref[:, at], preferred_element_type=jnp.float32)
        out[...] = result.astype(out.dtype)


def finish(owned, slot, plan, sums, got, facts, before, down_own, down_lent):
    units = down_own.shape[0]
    width = down_own.shape[1] // 2
    pair = [
        jax.ShapeDtypeStruct((owned, width), jnp.bfloat16),
        jax.ShapeDtypeStruct((owned, width), jnp.float32),
    ]

    def first(plan_ref, sums_ref, got_ref, inner_ref, outer_ref, before_ref, *refs):
        own_ref, lent_ref, sent_ref, kept_ref, both_ref, held_ref, buffer, sem = refs
        facts_here = facts_of(plan_ref, inner_ref, outer_ref, buffer, sem)
        rows = collected_rows(owned, slot, plan_ref, sums_ref, got_ref, facts_here, before_ref)
        down(rows[0].astype(jnp.bfloat16), own_ref, lent_ref, sent_ref, kept_ref)
        both_ref[:, :width] = kept_ref[...].astype(jnp.bfloat16)
        both_ref[:, width:] = sent_ref[...]
        for index in range(1, 4):
            held_ref[(index - 1) * owned : index * owned, :] = rows[index].astype(jnp.bfloat16)

    def others(held_ref, own_ref, lent_ref, *refs):
        for index in range(3):
            held = held_ref[index * owned : (index + 1) * owned, :]
            down(held, own_ref, lent_ref, refs[2 * index], refs[2 * index + 1])

    held_shape = jax.ShapeDtypeStruct((3 * owned, 2 * units), jnp.bfloat16)
    specs = [SMEM, VMEM, VMEM, ANYWHERE, ANYWHERE] + [VMEM] * 3
    both_shape = jax.ShapeDtypeStruct((owned, 2 * width), jnp.bfloat16)
    sent, kept, both, held = on_core(
        first, pair + [both_shape, held_shape], specs, fact_scratch(facts[0].shape[1])
    )(plan, sums, got, *facts, before, down_own, down_lent)
    rest = on_core(others, pair * 3, [VMEM] * 3)(held, down_own, down_lent)
    return [sent, *rest[0::2]], [kept, *rest[1::2]], both


def rows_travel(
    tokens, gate_weight, up_weight, down_weight, route_gates, block_list, block_count, owner_token
):
    position = lax.axis_index("blk")
    share = lax.axis_index("tp")
    row_count, width = tokens.shape
    units = gate_weight.shape[2]
    owned = row_count // 2
    half = row_count // 2
    plan = jnp.asarray(PLAN, jnp.int32)[position]

    own_far = across_chips(tokens)
    own = with_facts(
        tokens, route_gates.T, jnp.transpose(block_list, (2, 0, 1)), block_count, owner_token
    )
    beside = along(own, BESIDE)
    middle = along(own, MIDDLE)

    gate_quarters = gate_weight[0].reshape(4, width, units)
    up_quarters = up_weight[0].reshape(4, width, units)

    def quarter(j):
        pair = [
            lax.dynamic_index_in_dim(q, share ^ j, 0, keepdims=False)
            for q in (gate_quarters, up_quarters)
        ]
        return jnp.concatenate(pair, axis=1)

    def down_part(j):
        return lax.dynamic_slice_in_dim(down_weight[0], (share ^ j) * width, width, 1)

    kept_down = jnp.concatenate([down_part(0), down_part(2)], axis=1)
    lend_down = jnp.concatenate([down_part(1), down_part(3)], axis=1)


    def at_kind(block, positions):
        pairs = [(4 * p + i, 4 * p + (i ^ 2)) for p in positions for i in range(4)]
        return lax.ppermute(block, ("blk", "tp"), pairs)

    inner_last = along(beside, MIDDLE)
    outer_next = along(middle, OUTWARD)
    beside_far = across_chips(beside)
    own_far_half = part_of(plan, own_far, own_far, half, half, flops=16 * 2**30)
    inward_far = along(own_far_half, INWARD)
    lend = jnp.concatenate([quarter(1), quarter(3)])
    lent = across_cores(after(lend, own))
    weights = [quarter(0), quarter(2), lent]
    whole = [row_count]
    sums_0, send_0, ready_0 = partial_sums(
        plan, whole, [(tokens, own_far)], weights, (0, 1)
    )
    got_0 = across_cores(send_0)
    lent_down = across_cores(lend_down)

    outer_last = along(inner_last, OUTWARD)
    outer_next = after(
        outer_next, beside_far, inner_last, inward_far, lend_down, weights[0], weights[1], ready_0
    )
    second = (middle, outer_next)
    second_far = (at_kind(middle, (1, 2)), at_kind(outer_next, (0, 3)))
    middle_far = along(inward_far, MIDDLE)
    sums_1, send_1, ready_1 = partial_sums(
        plan, whole, [(beside, beside_far)], weights, (0, 1)
    )
    got_1 = across_cores(send_1)

    last = (inner_last, outer_last)
    last_far_a = across_chips(
        part_of(plan, *last, 0, half, *second_far, middle_far, ready_0, ready_1)
    )
    outward_far = along(middle_far, OUTWARD)
    total, _ = collect(owned, 0, plan, sums_0, got_0, (own, own), None)
    total, collected_1 = collect(owned, 1, plan, sums_1, got_1, (beside, beside), total)
    sums_2, send_2, _ = partial_sums(plan, whole, [(second, second_far)], weights, (0, 1))
    got_2 = across_cores(send_2)
    near, _ = partial_sums(plan, whole, [(last,)], weights, (0,), send=False)
    sums_3, send_3, _ = partial_sums(
        plan,
        [half, half],
        [(last_far_a,), ((middle_far, outward_far),)],
        weights,
        (1,),
        before=near,
        waits=[collected_1],
    )
    got_3 = across_cores(send_3)
    total, _ = collect(owned, 2, plan, sums_2, got_2, second, total)
    sent, kept, both = finish(owned, 3, plan, sums_3, got_3, last, total, kept_down, lent_down)

    def joined(kept_part, sent_part):
        return kept_part + across_chips(sent_part).astype(jnp.float32)

    middle = along(both, MIDDLE).astype(jnp.float32)
    first = kept[0] + at_kind(sent[0], (0, 3)).astype(jnp.float32)
    inward = along(first.astype(jnp.bfloat16), INWARD)
    second = lax.optimization_barrier(joined(kept[1], sent[1]).astype(jnp.bfloat16))
    two_in = along(second, TWO_IN)
    passed = second.astype(jnp.float32) + inward.astype(jnp.float32)
    two_out = along(passed.astype(jnp.bfloat16), TWO_OUT)
    beside = along(joined(kept[2], sent[2]).astype(jnp.bfloat16), BESIDE)
    own_sent = (sent[3].astype(jnp.float32) + middle[:, width:]).astype(jnp.bfloat16)
    own_sum = joined(kept[3] + middle[:, :width], own_sent)
    arrived = [block.astype(jnp.float32) for block in (two_in, two_out)]
    total = lax.optimization_barrier(own_sum + sum(arrived))
    return (total + beside.astype(jnp.float32)).astype(jnp.bfloat16)


def on_device(*args):
    block_list = args[5]
    sizes = (lax.axis_size("blk"), lax.axis_size("tp"), block_list.shape[1])
    if sizes == (4, 4, 4):
        return rows_travel(*args)
    return weights_travel(*args)


def solution(mesh):
    return jax.shard_map(
        on_device,
        mesh=mesh,
        in_specs=(
            P(("groups", "blk"), "tp"),
            P("blk", None, "tp"),
            P("blk", None, "tp"),
            P("blk", "tp", None),
            P(("groups", "blk"), None),
            P(("groups", "blk"), None, None),
            P(("groups", "blk"), None),
            P(("groups", "blk")),
        ),
        out_specs=P(("groups", "blk"), "tp"),
        check_vma=False,
    )
```

```python
import jax
import jax.numpy as jnp
from jax import lax
from jax.experimental import pallas as pl
from jax.experimental.pallas import tpu as pltpu
from jax.sharding import PartitionSpec as P


def shifted(block, axis, distance):
    devices = range(lax.axis_size(axis))
    route = [((i - distance) % len(devices), i) for i in devices]
    return lax.ppermute(block, axis, route)


def weights_travel(
    tokens, gate_weight, up_weight, down_weight, route_gates, block_list, block_count, owner_token
):
    whole_rows = lax.all_gather(tokens, "tp", axis=1, tiled=True)
    row_count = whole_rows.shape[0]
    width = whole_rows.shape[1]
    offsets_all = block_list.shape[1]
    block_total = block_list.shape[2]
    block_size = row_count // block_total
    blocks = whole_rows.reshape(block_total, block_size, width)
    gate_blocks = route_gates.reshape(block_total, block_size, offsets_all)
    totals = jnp.zeros((block_total, block_size, width), jnp.float32)

    def apply(totals, weights, offset, block_id):
        w_gate, w_up, w_down = weights
        block_rows = lax.dynamic_index_in_dim(blocks, block_id, 0, keepdims=False)
        gate_out = jnp.dot(block_rows, w_gate, preferred_element_type=jnp.float32)
        up_out = jnp.dot(block_rows, w_up, preferred_element_type=jnp.float32)
        hidden = (jax.nn.silu(gate_out) * up_out).astype(jnp.bfloat16)
        block_gates = lax.dynamic_index_in_dim(gate_blocks, block_id, 0, keepdims=False)
        factor = lax.dynamic_index_in_dim(block_gates, offset, 1, keepdims=False)
        product = jnp.dot(hidden, w_down, preferred_element_type=jnp.float32) * factor[:, None]
        before = lax.dynamic_index_in_dim(totals, block_id, 0, keepdims=False)
        return lax.dynamic_update_index_in_dim(totals, before + product, block_id, 0)

    resident = (gate_weight[0], up_weight[0], down_weight[0])
    arrived = [resident]
    holding = resident
    for offset in range(1, offsets_all):
        holding = shifted((holding[0], holding[1], holding[2]), "blk", 1)
        arrived.append(holding)
    for offset in range(offsets_all):
        weights = arrived[offset]

        def visit_block(position, totals, weights=weights, offset=offset):
            return apply(totals, weights, offset, block_list[0, offset, position])

        totals = lax.fori_loop(0, block_count[0, offset], visit_block, totals)
    summed = lax.psum_scatter(
        totals.reshape(row_count, width).astype(jnp.bfloat16), "tp", scatter_dimension=1, tiled=True
    )
    feature_share = summed.shape[1]
    cycle_size = lax.axis_size("blk")
    owned = row_count // 2
    capacity = max(2, 2 * row_count // cycle_size)
    target = owner_token // owned
    local_token = owner_token % owned
    target_table = (target[:, None] == jnp.arange(cycle_size, dtype=jnp.int32)[None, :]).astype(
        jnp.int32
    )
    running = jnp.cumsum(target_table, axis=0)
    rank = jnp.sum((running - 1) * target_table, axis=1)
    slot = target * capacity + rank
    send_rows = jnp.zeros((cycle_size * capacity, feature_share), jnp.bfloat16).at[slot].set(summed)
    send_index = jnp.full((cycle_size * capacity,), -1, jnp.int32).at[slot].set(local_token)
    send_rows = send_rows.reshape(cycle_size, capacity, feature_share)
    send_index = send_index.reshape(cycle_size, capacity)
    got_rows, got_index = (
        lax.all_to_all(send_rows, "blk", split_axis=0, concat_axis=0, tiled=True),
        lax.all_to_all(send_index, "blk", split_axis=0, concat_axis=0, tiled=True),
    )
    got_rows = got_rows.reshape(cycle_size * capacity, feature_share)
    got_index = got_index.reshape(cycle_size * capacity)
    placing = (got_index[:, None] == jnp.arange(owned, dtype=jnp.int32)[None, :]).astype(
        jnp.bfloat16
    )
    combined = lax.dot_general(
        placing, got_rows, (((0,), (0,)), ((), ())), preferred_element_type=jnp.float32
    )
    return combined.astype(jnp.bfloat16)


BESIDE = [(0, 1), (1, 0), (2, 3), (3, 2)]
MIDDLE = [(1, 2), (2, 1)]
INWARD = [(0, 1), (3, 2)]
OUTWARD = [(1, 0), (2, 3)]
TWO_IN = [(0, 2), (3, 1)]
TWO_OUT = [(1, 3), (2, 0)]
PLAN = [
    [3, 2, 1, 0, 0, 1, 2, 3, 0],
    [2, 3, 0, 1, 0, 3, 1, 2, 1],
    [1, 0, 3, 2, 0, 1, 3, 2, 1],
    [0, 1, 2, 3, 0, 3, 2, 1, 0],
]
OFFSETS_AT, INNER_AT = 4, 8
FACT_ROWS = 16
VMEM = pl.BlockSpec(memory_space=pltpu.VMEM)
SMEM = pl.BlockSpec(memory_space=pltpu.SMEM)
ANYWHERE = pl.BlockSpec(memory_space=pl.ANY)


def across_chips(block):
    return lax.ppermute(block, "tp", [(i, i ^ 2) for i in range(4)])


def across_cores(block):
    return lax.ppermute(block, "tp", [(i, i ^ 1) for i in range(4)])


def along(block, route):
    return lax.ppermute(block, "blk", route)


def cheap():
    return pl.CostEstimate(flops=1024, bytes_accessed=1024, transcendentals=0)


TOKEN = jax.ShapeDtypeStruct((8, 128), jnp.float32)
VMEM_LIMIT = 40 * 2**20


def on_core(body, out_shape, in_specs, scratch=()):
    return pl.pallas_call(
        body,
        out_shape=out_shape,
        in_specs=in_specs,
        out_specs=jax.tree.map(lambda _: VMEM, out_shape),
        scratch_shapes=scratch,
        compiler_params=pltpu.CompilerParams(vmem_limit_bytes=VMEM_LIMIT),
        cost_estimate=cheap(),
    )


def copies(source, start, target, size, pieces, sems, first):
    step = size // pieces
    return [
        pltpu.make_async_copy(
            source.at[pl.ds(start + index * step, step)],
            target.at[pl.ds(index * step, step)],
            sems.at[first + index],
        )
        for index in range(pieces)
    ]


def after(block, *others, flops=1024):
    return pl.pallas_call(
        lambda *refs: None,
        out_shape=jax.ShapeDtypeStruct(block.shape, block.dtype),
        in_specs=[ANYWHERE] * (1 + len(others)),
        out_specs=ANYWHERE,
        input_output_aliases={0: 0},
        cost_estimate=pl.CostEstimate(flops=flops, bytes_accessed=1024, transcendentals=0),
    )(block, *others)


def by_kind(plan_ref, kinds, run):
    if kinds[0] is kinds[1]:
        run(kinds[0])
        return
    for kind, value in zip(kinds, (1, 0)):

        @pl.when(plan_ref[INNER_AT] == value)
        def _(kind=kind):
            run(kind)


def part_of(plan, if_inner, if_outer, start, size, *others, flops=1024):
    shape = jax.ShapeDtypeStruct((size, if_inner.shape[1]), if_inner.dtype)
    pieces = 4

    def body(plan_ref, inner_ref, outer_ref, *rest):
        out_ref, buffer, in_sems, out_sems = rest[len(others) :]

        def run(source):
            inward = copies(source, start, buffer, size, pieces, in_sems, 0)
            outward = copies(buffer, 0, out_ref, size, pieces, out_sems, 0)
            for copy in inward:
                copy.start()
            for copy, next_copy in zip(inward, outward):
                copy.wait()
                next_copy.start()
            for copy in outward:
                copy.wait()

        by_kind(plan_ref, (inner_ref, inner_ref if if_outer is if_inner else outer_ref), run)

    return pl.pallas_call(
        body,
        out_shape=shape,
        in_specs=[SMEM] + [ANYWHERE] * (2 + len(others)),
        out_specs=ANYWHERE,
        scratch_shapes=[pltpu.VMEM(shape.shape, shape.dtype)]
        + [pltpu.SemaphoreType.DMA((pieces,))] * 2,
        compiler_params=pltpu.CompilerParams(vmem_limit_bytes=VMEM_LIMIT),
        cost_estimate=pl.CostEstimate(flops=flops, bytes_accessed=1024, transcendentals=0),
    )(plan, if_inner, if_outer, *others)


def with_facts(rows, gates, block_list, block_count, owner):
    count, width = rows.shape
    blocks, _, offsets = block_list.shape
    total = owner.shape[0]

    def body(rows_ref, gates_ref, list_ref, count_ref, owner_ref, out_ref, sems):
        moves = copies(rows_ref, 0, out_ref, count, 4, sems, 0)
        for copy in moves:
            copy.start()
        block_of = lax.broadcasted_iota(jnp.int32, (1, total), 1) // (total // blocks)
        facts = []
        for offset in range(offsets):
            mask = jnp.zeros((1, total), jnp.float32)
            for block in range(blocks):
                used = jnp.int32(0)
                for place in range(blocks):
                    found = (list_ref[place, 0, offset] == block) & (place < count_ref[0, offset])
                    used = used | found.astype(jnp.int32)
                mask = mask + jnp.where(block_of == block, used.astype(jnp.float32), 0.0)
            facts.append(gates_ref[offset : offset + 1, :] * mask)
        numbers = owner_ref[...].reshape(1, total)
        facts.append((numbers >> 8).astype(jnp.float32))
        facts.append((numbers & 255).astype(jnp.float32))
        facts.append(jnp.zeros((FACT_ROWS - len(facts), total), jnp.float32))
        out_ref[count:, :] = jnp.zeros((FACT_ROWS, width), jnp.bfloat16)
        out_ref[count:, :total] = jnp.concatenate(facts, axis=0).astype(jnp.bfloat16)
        for copy in moves:
            copy.wait()

    shape = jax.ShapeDtypeStruct((count + FACT_ROWS, width), rows.dtype)
    return on_core(
        body, shape, [ANYWHERE, VMEM, SMEM, SMEM, VMEM], [pltpu.SemaphoreType.DMA((4,))]
    )(rows, gates, block_list, block_count, owner)


def partial_sums(plan, sizes, parts, weights, places, before=None, send=True, waits=()):
    width, columns = weights[0].shape
    blocks = [
        block if isinstance(block, tuple) else (block,) for part in parts for block in part
    ]
    sources = [array for block in blocks for array in block]
    operands = [plan] + sources + [weights[place] for place in places] + [weights[2]]
    if before is not None:
        operands.append(before)
    specs = [SMEM] + [VMEM] * (len(operands) - 1 + len(waits))
    has_before = before is not None

    def body(plan_ref, *refs):
        source_refs, refs = refs[: len(sources)], refs[len(sources) :]
        weight_refs, refs = refs[: len(places) + 1], refs[len(places) + 1 :]
        before_ref, refs = (refs[0], refs[1:]) if has_before else (None, refs)
        results = refs[len(waits) :]
        start, source = 0, 0
        for part, size in enumerate(sizes):
            span = slice(start, start + size)
            start += size
            rows = []
            for index in range(len(places)):
                block = blocks[part * len(places) + index]
                value = source_refs[source][:size, :]
                if len(block) > 1:
                    other = source_refs[source + 1][:size, :]
                    value = jnp.where(plan_ref[INNER_AT] == 1, value, other)
                source += len(block)
                rows.append(value)
            for side in range(2):
                at = slice(side * columns, (side + 1) * columns)
                total = before_ref[span, at] if has_before else None
                for index, place in enumerate(places):
                    if side == 0:
                        weight = weight_refs[index][...]
                    else:
                        weight = weight_refs[-1][place * width : (place + 1) * width, :]
                    product = jnp.dot(rows[index], weight, preferred_element_type=jnp.float32)
                    total = product if total is None else total + product
                results[0][span, at] = total
                if send:
                    results[1][span, at] = total.astype(jnp.bfloat16)
        results[-1][...] = jnp.zeros(TOKEN.shape, TOKEN.dtype)

    shapes = [jax.ShapeDtypeStruct((sum(sizes), 2 * columns), jnp.float32)]
    if send:
        shapes.append(jax.ShapeDtypeStruct((sum(sizes), 2 * columns), jnp.bfloat16))
    return on_core(body, shapes + [TOKEN], specs)(*operands, *waits)


def collected_rows(owned, slot, plan, sums, got, facts, before):
    units = sums.shape[1] // 4
    hidden = []
    for core in range(2):
        here, there = 2 * core * units, 2 * (1 - core) * units
        gate = sums[:, here : here + units] + got[:, there : there + units].astype(jnp.float32)
        up = sums[:, here + units : here + 2 * units]
        up = up + got[:, there + units : there + 2 * units].astype(jnp.float32)
        hidden.append((gate / (1.0 + jnp.exp(-gate)) * up).astype(jnp.bfloat16))
    hidden = jnp.concatenate(hidden, axis=1)
    values = facts[:, : sums.shape[0]].astype(jnp.float32)
    kind = lax.broadcasted_iota(jnp.int32, (FACT_ROWS, 1), 0)
    mine = kind == plan[OFFSETS_AT + slot]
    factor = jnp.sum(jnp.where(mine, values, 0.0), axis=0, keepdims=True)
    owner = (values[4:5, :] * 256.0 + values[5:6, :]).astype(jnp.int32)
    results = []
    for index in range(4):
        token = plan[index] * owned + lax.broadcasted_iota(jnp.int32, (owned, 1), 0)
        placing = jnp.where(owner == token, factor, 0.0).astype(jnp.bfloat16)
        rows = jnp.dot(placing, hidden, preferred_element_type=jnp.float32)
        if before is not None:
            rows = rows + before[index * owned : (index + 1) * owned, :]
        results.append(rows)
    return results


def fact_scratch(width):
    return [pltpu.VMEM((FACT_ROWS, width), jnp.bfloat16), pltpu.SemaphoreType.DMA((1,))]


def facts_of(plan_ref, inner_ref, outer_ref, buffer, sem):
    last = inner_ref.shape[0] - FACT_ROWS

    def run(source):
        (copy,) = copies(source, last, buffer, FACT_ROWS, 1, sem, 0)
        copy.start()
        copy.wait()

    by_kind(plan_ref, (inner_ref, outer_ref), run)
    return buffer


def collect(owned, slot, plan, sums, got, facts, before):
    operands = [plan, sums, got, *facts] + ([] if before is None else [before])

    def body(plan_ref, sums_ref, got_ref, inner_ref, outer_ref, *rest):
        before_ref = rest[0] if before is not None else None
        out_ref, token_ref, buffer, sem = rest[-4:]
        facts_here = facts_of(plan_ref, inner_ref, outer_ref, buffer, sem)
        rows = collected_rows(owned, slot, plan_ref, sums_ref, got_ref, facts_here, before_ref)
        for index in range(4):
            out_ref[index * owned : (index + 1) * owned, :] = rows[index]
        token_ref[...] = jnp.zeros(TOKEN.shape, TOKEN.dtype)

    shape = jax.ShapeDtypeStruct((4 * owned, sums.shape[1] // 2), jnp.float32)
    specs = [SMEM, VMEM, VMEM, ANYWHERE, ANYWHERE] + [VMEM] * (len(operands) - 5)
    return on_core(body, [shape, TOKEN], specs, fact_scratch(facts[0].shape[1]))(*operands)


def down(held, own_ref, lent_ref, sent_ref, kept_ref):
    units, width = own_ref.shape[0], kept_ref.shape[1]
    for out, at in ((kept_ref, slice(0, width)), (sent_ref, slice(width, 2 * width))):
        result = jnp.dot(held[:, :units], own_ref[:, at], preferred_element_type=jnp.float32)
        result += jnp.dot(held[:, units:], lent_ref[:, at], preferred_element_type=jnp.float32)
        out[...] = result.astype(out.dtype)


def finish(owned, slot, plan, sums, got, facts, before, down_own, down_lent):
    units = down_own.shape[0]
    width = down_own.shape[1] // 2
    pair = [
        jax.ShapeDtypeStruct((owned, width), jnp.bfloat16),
        jax.ShapeDtypeStruct((owned, width), jnp.float32),
    ]

    def first(plan_ref, sums_ref, got_ref, inner_ref, outer_ref, before_ref, *refs):
        own_ref, lent_ref, sent_ref, kept_ref, both_ref, held_ref, buffer, sem = refs
        facts_here = facts_of(plan_ref, inner_ref, outer_ref, buffer, sem)
        rows = collected_rows(owned, slot, plan_ref, sums_ref, got_ref, facts_here, before_ref)
        down(rows[0].astype(jnp.bfloat16), own_ref, lent_ref, sent_ref, kept_ref)
        both_ref[:, :width] = kept_ref[...].astype(jnp.bfloat16)
        both_ref[:, width:] = sent_ref[...]
        for index in range(1, 4):
            held_ref[(index - 1) * owned : index * owned, :] = rows[index].astype(jnp.bfloat16)

    def others(held_ref, own_ref, lent_ref, *refs):
        for index in range(3):
            held = held_ref[index * owned : (index + 1) * owned, :]
            down(held, own_ref, lent_ref, refs[2 * index], refs[2 * index + 1])

    held_shape = jax.ShapeDtypeStruct((3 * owned, 2 * units), jnp.bfloat16)
    specs = [SMEM, VMEM, VMEM, ANYWHERE, ANYWHERE] + [VMEM] * 3
    both_shape = jax.ShapeDtypeStruct((owned, 2 * width), jnp.bfloat16)
    sent, kept, both, held = on_core(
        first, pair + [both_shape, held_shape], specs, fact_scratch(facts[0].shape[1])
    )(plan, sums, got, *facts, before, down_own, down_lent)
    rest = on_core(others, pair * 3, [VMEM] * 3)(held, down_own, down_lent)
    return [sent, *rest[0::2]], [kept, *rest[1::2]], both


def rows_travel(
    tokens, gate_weight, up_weight, down_weight, route_gates, block_list, block_count, owner_token
):
    position = lax.axis_index("blk")
    share = lax.axis_index("tp")
    row_count, width = tokens.shape
    units = gate_weight.shape[2]
    owned = row_count // 2
    half = row_count // 2
    plan = jnp.asarray(PLAN, jnp.int32)[position]

    own_far = across_chips(tokens)
    own = with_facts(
        tokens, route_gates.T, jnp.transpose(block_list, (2, 0, 1)), block_count, owner_token
    )
    beside = along(own, BESIDE)
    middle = along(own, MIDDLE)

    gate_quarters = gate_weight[0].reshape(4, width, units)
    up_quarters = up_weight[0].reshape(4, width, units)

    def quarter(j):
        pair = [
            lax.dynamic_index_in_dim(q, share ^ j, 0, keepdims=False)
            for q in (gate_quarters, up_quarters)
        ]
        return jnp.concatenate(pair, axis=1)

    def down_part(j):
        return lax.dynamic_slice_in_dim(down_weight[0], (share ^ j) * width, width, 1)

    kept_down = jnp.concatenate([down_part(0), down_part(2)], axis=1)
    lend_down = jnp.concatenate([down_part(1), down_part(3)], axis=1)


    def at_kind(block, positions):
        pairs = [(4 * p + i, 4 * p + (i ^ 2)) for p in positions for i in range(4)]
        return lax.ppermute(block, ("blk", "tp"), pairs)

    inner_last = along(beside, MIDDLE)
    outer_next = along(middle, OUTWARD)
    beside_far = across_chips(beside)
    own_far_half = part_of(plan, own_far, own_far, half, half, flops=16 * 2**30)
    inward_far = along(own_far_half, INWARD)
    lend = jnp.concatenate([quarter(1), quarter(3)])
    lent = across_cores(after(lend, own))
    weights = [quarter(0), quarter(2), lent]
    whole = [row_count]
    sums_0, send_0, ready_0 = partial_sums(
        plan, whole, [(tokens, own_far)], weights, (0, 1)
    )
    got_0 = across_cores(send_0)
    lent_down = across_cores(lend_down)

    outer_last = along(inner_last, OUTWARD)
    outer_next = after(
        outer_next, beside_far, inner_last, inward_far, lend_down, weights[0], weights[1], ready_0
    )
    second = (middle, outer_next)
    second_far = (at_kind(middle, (1, 2)), at_kind(outer_next, (0, 3)))
    middle_far = along(inward_far, MIDDLE)
    sums_1, send_1, ready_1 = partial_sums(
        plan, whole, [(beside, beside_far)], weights, (0, 1)
    )
    got_1 = across_cores(send_1)

    last = (inner_last, outer_last)
    last_far_a = across_chips(
        part_of(plan, *last, 0, half, *second_far, middle_far, ready_0, ready_1)
    )
    outward_far = along(middle_far, OUTWARD)
    total, _ = collect(owned, 0, plan, sums_0, got_0, (own, own), None)
    total, collected_1 = collect(owned, 1, plan, sums_1, got_1, (beside, beside), total)
    sums_2, send_2, _ = partial_sums(plan, whole, [(second, second_far)], weights, (0, 1))
    got_2 = across_cores(send_2)
    near, _ = partial_sums(plan, whole, [(last,)], weights, (0,), send=False)
    sums_3, send_3, _ = partial_sums(
        plan,
        [half, half],
        [(last_far_a,), ((middle_far, outward_far),)],
        weights,
        (1,),
        before=near,
        waits=[collected_1],
    )
    got_3 = across_cores(send_3)
    total, _ = collect(owned, 2, plan, sums_2, got_2, second, total)
    sent, kept, both = finish(owned, 3, plan, sums_3, got_3, last, total, kept_down, lent_down)

    def joined(kept_part, sent_part):
        return kept_part + across_chips(sent_part).astype(jnp.float32)

    middle = along(both, MIDDLE).astype(jnp.float32)
    first = kept[0] + at_kind(sent[0], (0, 3)).astype(jnp.float32)
    inward = along(first.astype(jnp.bfloat16), INWARD)
    second = lax.optimization_barrier(joined(kept[1], sent[1]).astype(jnp.bfloat16))
    two_in = along(second, TWO_IN)
    passed = second.astype(jnp.float32) + inward.astype(jnp.float32)
    two_out = along(passed.astype(jnp.bfloat16), TWO_OUT)
    beside = along(joined(kept[2], sent[2]).astype(jnp.bfloat16), BESIDE)
    own_sent = (sent[3].astype(jnp.float32) + middle[:, width:]).astype(jnp.bfloat16)
    own_sum = joined(kept[3] + middle[:, :width], own_sent)
    total = lax.optimization_barrier(two_in.astype(jnp.float32) + two_out.astype(jnp.float32))
    return (total + own_sum + beside.astype(jnp.float32)).astype(jnp.bfloat16)


def on_device(*args):
    block_list = args[5]
    sizes = (lax.axis_size("blk"), lax.axis_size("tp"), block_list.shape[1])
    if sizes == (4, 4, 4):
        return rows_travel(*args)
    return weights_travel(*args)


def solution(mesh):
    return jax.shard_map(
        on_device,
        mesh=mesh,
        in_specs=(
            P(("groups", "blk"), "tp"),
            P("blk", None, "tp"),
            P("blk", None, "tp"),
            P("blk", "tp", None),
            P(("groups", "blk"), None),
            P(("groups", "blk"), None, None),
            P(("groups", "blk"), None),
            P(("groups", "blk")),
        ),
        out_specs=P(("groups", "blk"), "tp"),
        check_vma=False,
    )
```

```python
import jax
import jax.numpy as jnp
from jax import lax
from jax.experimental import pallas as pl
from jax.experimental.pallas import tpu as pltpu
from jax.sharding import PartitionSpec as P


def shifted(block, axis, distance):
    devices = range(lax.axis_size(axis))
    route = [((i - distance) % len(devices), i) for i in devices]
    return lax.ppermute(block, axis, route)


def weights_travel(
    tokens, gate_weight, up_weight, down_weight, route_gates, block_list, block_count, owner_token
):
    whole_rows = lax.all_gather(tokens, "tp", axis=1, tiled=True)
    row_count = whole_rows.shape[0]
    width = whole_rows.shape[1]
    offsets_all = block_list.shape[1]
    block_total = block_list.shape[2]
    block_size = row_count // block_total
    blocks = whole_rows.reshape(block_total, block_size, width)
    gate_blocks = route_gates.reshape(block_total, block_size, offsets_all)
    totals = jnp.zeros((block_total, block_size, width), jnp.float32)

    def apply(totals, weights, offset, block_id):
        w_gate, w_up, w_down = weights
        block_rows = lax.dynamic_index_in_dim(blocks, block_id, 0, keepdims=False)
        gate_out = jnp.dot(block_rows, w_gate, preferred_element_type=jnp.float32)
        up_out = jnp.dot(block_rows, w_up, preferred_element_type=jnp.float32)
        hidden = (jax.nn.silu(gate_out) * up_out).astype(jnp.bfloat16)
        block_gates = lax.dynamic_index_in_dim(gate_blocks, block_id, 0, keepdims=False)
        factor = lax.dynamic_index_in_dim(block_gates, offset, 1, keepdims=False)
        product = jnp.dot(hidden, w_down, preferred_element_type=jnp.float32) * factor[:, None]
        before = lax.dynamic_index_in_dim(totals, block_id, 0, keepdims=False)
        return lax.dynamic_update_index_in_dim(totals, before + product, block_id, 0)

    resident = (gate_weight[0], up_weight[0], down_weight[0])
    arrived = [resident]
    holding = resident
    for offset in range(1, offsets_all):
        holding = shifted((holding[0], holding[1], holding[2]), "blk", 1)
        arrived.append(holding)
    for offset in range(offsets_all):
        weights = arrived[offset]

        def visit_block(position, totals, weights=weights, offset=offset):
            return apply(totals, weights, offset, block_list[0, offset, position])

        totals = lax.fori_loop(0, block_count[0, offset], visit_block, totals)
    summed = lax.psum_scatter(
        totals.reshape(row_count, width).astype(jnp.bfloat16), "tp", scatter_dimension=1, tiled=True
    )
    feature_share = summed.shape[1]
    cycle_size = lax.axis_size("blk")
    owned = row_count // 2
    capacity = max(2, 2 * row_count // cycle_size)
    target = owner_token // owned
    local_token = owner_token % owned
    target_table = (target[:, None] == jnp.arange(cycle_size, dtype=jnp.int32)[None, :]).astype(
        jnp.int32
    )
    running = jnp.cumsum(target_table, axis=0)
    rank = jnp.sum((running - 1) * target_table, axis=1)
    slot = target * capacity + rank
    send_rows = jnp.zeros((cycle_size * capacity, feature_share), jnp.bfloat16).at[slot].set(summed)
    send_index = jnp.full((cycle_size * capacity,), -1, jnp.int32).at[slot].set(local_token)
    send_rows = send_rows.reshape(cycle_size, capacity, feature_share)
    send_index = send_index.reshape(cycle_size, capacity)
    got_rows, got_index = (
        lax.all_to_all(send_rows, "blk", split_axis=0, concat_axis=0, tiled=True),
        lax.all_to_all(send_index, "blk", split_axis=0, concat_axis=0, tiled=True),
    )
    got_rows = got_rows.reshape(cycle_size * capacity, feature_share)
    got_index = got_index.reshape(cycle_size * capacity)
    placing = (got_index[:, None] == jnp.arange(owned, dtype=jnp.int32)[None, :]).astype(
        jnp.bfloat16
    )
    combined = lax.dot_general(
        placing, got_rows, (((0,), (0,)), ((), ())), preferred_element_type=jnp.float32
    )
    return combined.astype(jnp.bfloat16)


BESIDE = [(0, 1), (1, 0), (2, 3), (3, 2)]
MIDDLE = [(1, 2), (2, 1)]
INWARD = [(0, 1), (3, 2)]
OUTWARD = [(1, 0), (2, 3)]
TWO_IN = [(0, 2), (3, 1)]
TWO_OUT = [(1, 3), (2, 0)]
PLAN = [
    [3, 2, 1, 0, 0, 1, 2, 3, 0],
    [2, 3, 0, 1, 0, 3, 1, 2, 1],
    [1, 0, 3, 2, 0, 1, 3, 2, 1],
    [0, 1, 2, 3, 0, 3, 2, 1, 0],
]
OFFSETS_AT, INNER_AT = 4, 8
FACT_ROWS = 16
VMEM = pl.BlockSpec(memory_space=pltpu.VMEM)
SMEM = pl.BlockSpec(memory_space=pltpu.SMEM)
ANYWHERE = pl.BlockSpec(memory_space=pl.ANY)


def across_chips(block):
    return lax.ppermute(block, "tp", [(i, i ^ 2) for i in range(4)])


def across_cores(block):
    return lax.ppermute(block, "tp", [(i, i ^ 1) for i in range(4)])


def along(block, route):
    return lax.ppermute(block, "blk", route)


def cheap():
    return pl.CostEstimate(flops=1024, bytes_accessed=1024, transcendentals=0)


TOKEN = jax.ShapeDtypeStruct((8, 128), jnp.float32)
VMEM_LIMIT = 40 * 2**20


def on_core(body, out_shape, in_specs, scratch=()):
    return pl.pallas_call(
        body,
        out_shape=out_shape,
        in_specs=in_specs,
        out_specs=jax.tree.map(lambda _: VMEM, out_shape),
        scratch_shapes=scratch,
        compiler_params=pltpu.CompilerParams(vmem_limit_bytes=VMEM_LIMIT),
        cost_estimate=cheap(),
    )


def copies(source, start, target, size, pieces, sems, first):
    step = size // pieces
    return [
        pltpu.make_async_copy(
            source.at[pl.ds(start + index * step, step)],
            target.at[pl.ds(index * step, step)],
            sems.at[first + index],
        )
        for index in range(pieces)
    ]


def after(block, *others, flops=1024):
    return pl.pallas_call(
        lambda *refs: None,
        out_shape=jax.ShapeDtypeStruct(block.shape, block.dtype),
        in_specs=[ANYWHERE] * (1 + len(others)),
        out_specs=ANYWHERE,
        input_output_aliases={0: 0},
        cost_estimate=pl.CostEstimate(flops=flops, bytes_accessed=1024, transcendentals=0),
    )(block, *others)


def by_kind(plan_ref, kinds, run):
    if kinds[0] is kinds[1]:
        run(kinds[0])
        return
    for kind, value in zip(kinds, (1, 0)):

        @pl.when(plan_ref[INNER_AT] == value)
        def _(kind=kind):
            run(kind)


def part_of(plan, if_inner, if_outer, start, size, *others, flops=1024):
    shape = jax.ShapeDtypeStruct((size, if_inner.shape[1]), if_inner.dtype)
    pieces = 4

    def body(plan_ref, inner_ref, outer_ref, *rest):
        out_ref, buffer, in_sems, out_sems = rest[len(others) :]

        def run(source):
            inward = copies(source, start, buffer, size, pieces, in_sems, 0)
            outward = copies(buffer, 0, out_ref, size, pieces, out_sems, 0)
            for copy in inward:
                copy.start()
            for copy, next_copy in zip(inward, outward):
                copy.wait()
                next_copy.start()
            for copy in outward:
                copy.wait()

        by_kind(plan_ref, (inner_ref, inner_ref if if_outer is if_inner else outer_ref), run)

    return pl.pallas_call(
        body,
        out_shape=shape,
        in_specs=[SMEM] + [ANYWHERE] * (2 + len(others)),
        out_specs=ANYWHERE,
        scratch_shapes=[pltpu.VMEM(shape.shape, shape.dtype)]
        + [pltpu.SemaphoreType.DMA((pieces,))] * 2,
        compiler_params=pltpu.CompilerParams(vmem_limit_bytes=VMEM_LIMIT),
        cost_estimate=pl.CostEstimate(flops=flops, bytes_accessed=1024, transcendentals=0),
    )(plan, if_inner, if_outer, *others)


def with_facts(rows, gates, block_list, block_count, owner):
    count, width = rows.shape
    blocks, _, offsets = block_list.shape
    total = owner.shape[0]

    def body(rows_ref, gates_ref, list_ref, count_ref, owner_ref, out_ref, sems):
        moves = copies(rows_ref, 0, out_ref, count, 4, sems, 0)
        for copy in moves:
            copy.start()
        block_of = lax.broadcasted_iota(jnp.int32, (1, total), 1) // (total // blocks)
        facts = []
        for offset in range(offsets):
            mask = jnp.zeros((1, total), jnp.float32)
            for block in range(blocks):
                used = jnp.int32(0)
                for place in range(blocks):
                    found = (list_ref[place, 0, offset] == block) & (place < count_ref[0, offset])
                    used = used | found.astype(jnp.int32)
                mask = mask + jnp.where(block_of == block, used.astype(jnp.float32), 0.0)
            facts.append(gates_ref[offset : offset + 1, :] * mask)
        numbers = owner_ref[...].reshape(1, total)
        facts.append((numbers >> 8).astype(jnp.float32))
        facts.append((numbers & 255).astype(jnp.float32))
        facts.append(jnp.zeros((FACT_ROWS - len(facts), total), jnp.float32))
        out_ref[count:, :] = jnp.zeros((FACT_ROWS, width), jnp.bfloat16)
        out_ref[count:, :total] = jnp.concatenate(facts, axis=0).astype(jnp.bfloat16)
        for copy in moves:
            copy.wait()

    shape = jax.ShapeDtypeStruct((count + FACT_ROWS, width), rows.dtype)
    return on_core(
        body, shape, [ANYWHERE, VMEM, SMEM, SMEM, VMEM], [pltpu.SemaphoreType.DMA((4,))]
    )(rows, gates, block_list, block_count, owner)


def partial_sums(plan, sizes, parts, weights, places, before=None, send=True, waits=()):
    width, columns = weights[0].shape
    blocks = [
        block if isinstance(block, tuple) else (block,) for part in parts for block in part
    ]
    sources = [array for block in blocks for array in block]
    operands = [plan] + sources + [weights[place] for place in places] + [weights[2]]
    if before is not None:
        operands.append(before)
    specs = [SMEM] + [VMEM] * (len(operands) - 1 + len(waits))
    has_before = before is not None

    def body(plan_ref, *refs):
        source_refs, refs = refs[: len(sources)], refs[len(sources) :]
        weight_refs, refs = refs[: len(places) + 1], refs[len(places) + 1 :]
        before_ref, refs = (refs[0], refs[1:]) if has_before else (None, refs)
        results = refs[len(waits) :]
        start, source = 0, 0
        for part, size in enumerate(sizes):
            span = slice(start, start + size)
            start += size
            rows = []
            for index in range(len(places)):
                block = blocks[part * len(places) + index]
                value = source_refs[source][:size, :]
                if len(block) > 1:
                    other = source_refs[source + 1][:size, :]
                    value = jnp.where(plan_ref[INNER_AT] == 1, value, other)
                source += len(block)
                rows.append(value)
            for side in range(2):
                at = slice(side * columns, (side + 1) * columns)
                total = before_ref[span, at] if has_before else None
                for index, place in enumerate(places):
                    if side == 0:
                        weight = weight_refs[index][...]
                    else:
                        weight = weight_refs[-1][place * width : (place + 1) * width, :]
                    product = jnp.dot(rows[index], weight, preferred_element_type=jnp.float32)
                    total = product if total is None else total + product
                results[0][span, at] = total
                if send:
                    results[1][span, at] = total.astype(jnp.bfloat16)
        results[-1][...] = jnp.zeros(TOKEN.shape, TOKEN.dtype)

    shapes = [jax.ShapeDtypeStruct((sum(sizes), 2 * columns), jnp.float32)]
    if send:
        shapes.append(jax.ShapeDtypeStruct((sum(sizes), 2 * columns), jnp.bfloat16))
    return on_core(body, shapes + [TOKEN], specs)(*operands, *waits)


def collected_rows(owned, slot, plan, sums, got, facts, before):
    units = sums.shape[1] // 4
    hidden = []
    for core in range(2):
        here, there = 2 * core * units, 2 * (1 - core) * units
        gate = sums[:, here : here + units] + got[:, there : there + units].astype(jnp.float32)
        up = sums[:, here + units : here + 2 * units]
        up = up + got[:, there + units : there + 2 * units].astype(jnp.float32)
        hidden.append((gate / (1.0 + jnp.exp(-gate)) * up).astype(jnp.bfloat16))
    hidden = jnp.concatenate(hidden, axis=1)
    values = facts[:, : sums.shape[0]].astype(jnp.float32)
    kind = lax.broadcasted_iota(jnp.int32, (FACT_ROWS, 1), 0)
    mine = kind == plan[OFFSETS_AT + slot]
    factor = jnp.sum(jnp.where(mine, values, 0.0), axis=0, keepdims=True)
    owner = (values[4:5, :] * 256.0 + values[5:6, :]).astype(jnp.int32)
    results = []
    for index in range(4):
        token = plan[index] * owned + lax.broadcasted_iota(jnp.int32, (owned, 1), 0)
        placing = jnp.where(owner == token, factor, 0.0).astype(jnp.bfloat16)
        rows = jnp.dot(placing, hidden, preferred_element_type=jnp.float32)
        if before is not None:
            rows = rows + before[index * owned : (index + 1) * owned, :]
        results.append(rows)
    return results


def fact_scratch(width):
    return [pltpu.VMEM((FACT_ROWS, width), jnp.bfloat16), pltpu.SemaphoreType.DMA((1,))]


def facts_of(plan_ref, inner_ref, outer_ref, buffer, sem):
    last = inner_ref.shape[0] - FACT_ROWS

    def run(source):
        (copy,) = copies(source, last, buffer, FACT_ROWS, 1, sem, 0)
        copy.start()
        copy.wait()

    by_kind(plan_ref, (inner_ref, outer_ref), run)
    return buffer


def collect(owned, slot, plan, sums, got, facts, before):
    operands = [plan, sums, got, *facts] + ([] if before is None else [before])

    def body(plan_ref, sums_ref, got_ref, inner_ref, outer_ref, *rest):
        before_ref = rest[0] if before is not None else None
        out_ref, token_ref, buffer, sem = rest[-4:]
        facts_here = facts_of(plan_ref, inner_ref, outer_ref, buffer, sem)
        rows = collected_rows(owned, slot, plan_ref, sums_ref, got_ref, facts_here, before_ref)
        for index in range(4):
            out_ref[index * owned : (index + 1) * owned, :] = rows[index]
        token_ref[...] = jnp.zeros(TOKEN.shape, TOKEN.dtype)

    shape = jax.ShapeDtypeStruct((4 * owned, sums.shape[1] // 2), jnp.float32)
    specs = [SMEM, VMEM, VMEM, ANYWHERE, ANYWHERE] + [VMEM] * (len(operands) - 5)
    return on_core(body, [shape, TOKEN], specs, fact_scratch(facts[0].shape[1]))(*operands)


def down(held, own_ref, lent_ref, sent_ref, kept_ref):
    units, width = own_ref.shape[0], kept_ref.shape[1]
    for out, at in ((kept_ref, slice(0, width)), (sent_ref, slice(width, 2 * width))):
        result = jnp.dot(held[:, :units], own_ref[:, at], preferred_element_type=jnp.float32)
        result += jnp.dot(held[:, units:], lent_ref[:, at], preferred_element_type=jnp.float32)
        out[...] = result.astype(out.dtype)


def finish(owned, slot, plan, sums, got, facts, before, down_own, down_lent):
    units = down_own.shape[0]
    width = down_own.shape[1] // 2
    pair = [
        jax.ShapeDtypeStruct((owned, width), jnp.bfloat16),
        jax.ShapeDtypeStruct((owned, width), jnp.float32),
    ]

    def first(plan_ref, sums_ref, got_ref, inner_ref, outer_ref, before_ref, *refs):
        own_ref, lent_ref, sent_ref, kept_ref, again_ref, held_ref, buffer, sem = refs
        facts_here = facts_of(plan_ref, inner_ref, outer_ref, buffer, sem)
        rows = collected_rows(owned, slot, plan_ref, sums_ref, got_ref, facts_here, before_ref)
        down(rows[0].astype(jnp.bfloat16), own_ref, lent_ref, sent_ref, kept_ref)
        again_ref[...] = kept_ref[...]
        for index in range(1, 4):
            held_ref[(index - 1) * owned : index * owned, :] = rows[index].astype(jnp.bfloat16)

    def others(indices, *waits):
        def body(held_ref, own_ref, lent_ref, *refs):
            out_refs = refs[len(waits) :]
            for place, index in enumerate(indices):
                held = held_ref[(index - 1) * owned : index * owned, :]
                down(held, own_ref, lent_ref, out_refs[2 * place], out_refs[2 * place + 1])

        operands = [held, down_own, down_lent, *waits]
        return on_core(body, pair * len(indices), [VMEM] * len(operands))(*operands)

    held_shape = jax.ShapeDtypeStruct((3 * owned, 2 * units), jnp.bfloat16)
    specs = [SMEM, VMEM, VMEM, ANYWHERE, ANYWHERE] + [VMEM] * 3
    sent, kept, again, held = on_core(
        first, pair + [pair[1], held_shape], specs, fact_scratch(facts[0].shape[1])
    )(plan, sums, got, *facts, before, down_own, down_lent)
    rest = others([1, 2])
    chunks = [(sent, kept), (rest[0], rest[1]), (rest[2], rest[3])]
    return chunks, again, lambda *waits: others([3], *waits)


def rows_travel(
    tokens, gate_weight, up_weight, down_weight, route_gates, block_list, block_count, owner_token
):
    position = lax.axis_index("blk")
    share = lax.axis_index("tp")
    row_count, width = tokens.shape
    units = gate_weight.shape[2]
    owned = row_count // 2
    half = row_count // 2
    plan = jnp.asarray(PLAN, jnp.int32)[position]

    own_far = across_chips(tokens)
    own = with_facts(
        tokens, route_gates.T, jnp.transpose(block_list, (2, 0, 1)), block_count, owner_token
    )
    beside = along(own, BESIDE)
    middle = along(own, MIDDLE)

    gate_quarters = gate_weight[0].reshape(4, width, units)
    up_quarters = up_weight[0].reshape(4, width, units)

    def quarter(j):
        pair = [
            lax.dynamic_index_in_dim(q, share ^ j, 0, keepdims=False)
            for q in (gate_quarters, up_quarters)
        ]
        return jnp.concatenate(pair, axis=1)

    def down_part(j):
        return lax.dynamic_slice_in_dim(down_weight[0], (share ^ j) * width, width, 1)

    kept_down = jnp.concatenate([down_part(0), down_part(2)], axis=1)
    lend_down = jnp.concatenate([down_part(1), down_part(3)], axis=1)


    def at_kind(block, positions):
        pairs = [(4 * p + i, 4 * p + (i ^ 2)) for p in positions for i in range(4)]
        return lax.ppermute(block, ("blk", "tp"), pairs)

    inner_last = along(beside, MIDDLE)
    outer_next = along(middle, OUTWARD)
    beside_far = across_chips(beside)
    own_far_half = part_of(plan, own_far, own_far, half, half, flops=16 * 2**30)
    inward_far = along(own_far_half, INWARD)
    lend = jnp.concatenate([quarter(1), quarter(3)])
    lent = across_cores(after(lend, own))
    weights = [quarter(0), quarter(2), lent]
    whole = [row_count]
    sums_0, send_0, ready_0 = partial_sums(
        plan, whole, [(tokens, own_far)], weights, (0, 1)
    )
    got_0 = across_cores(send_0)
    lent_down = across_cores(lend_down)

    outer_last = along(inner_last, OUTWARD)
    outer_next = after(
        outer_next, beside_far, inner_last, inward_far, lend_down, weights[0], weights[1], ready_0
    )
    second = (middle, outer_next)
    second_far = (at_kind(middle, (1, 2)), at_kind(outer_next, (0, 3)))
    middle_far = along(inward_far, MIDDLE)
    sums_1, send_1, ready_1 = partial_sums(
        plan, whole, [(beside, beside_far)], weights, (0, 1)
    )
    got_1 = across_cores(send_1)

    total, collected_0 = collect(owned, 0, plan, sums_0, got_0, (own, own), None)

    last = (inner_last, outer_last)
    last_far_a = across_chips(
        part_of(plan, *last, 0, half, *second_far, middle_far, collected_0, ready_1)
    )
    outward_far = along(middle_far, OUTWARD)
    total, collected_1 = collect(owned, 1, plan, sums_1, got_1, (beside, beside), total)
    sums_2, send_2, _ = partial_sums(plan, whole, [(second, second_far)], weights, (0, 1))
    got_2 = across_cores(send_2)
    near, _ = partial_sums(plan, whole, [(last,)], weights, (0,), send=False)
    sums_3, send_3, _ = partial_sums(
        plan,
        [half, half],
        [(last_far_a,), ((middle_far, outward_far),)],
        weights,
        (1,),
        before=near,
        waits=[collected_1],
    )
    got_3 = across_cores(send_3)
    total, _ = collect(owned, 2, plan, sums_2, got_2, second, total)
    chunks, again, last_chunk = finish(owned, 3, plan, sums_3, got_3, last, total, kept_down, lent_down)

    def joined(sent, kept, exchange=across_chips):
        return kept + exchange(sent).astype(jnp.float32)

    def rounded(block):
        return lax.optimization_barrier(block.astype(jnp.bfloat16))

    sent, kept = chunks[0]
    first_outer = rounded(joined(sent, kept, lambda block: at_kind(block, (0, 3))))
    first_inner = rounded(joined(sent, again, lambda block: at_kind(block, (1, 2))))
    second = rounded(joined(*chunks[1]))
    third = rounded(joined(*chunks[2]))
    inward = along(first_outer, INWARD)
    middle = along(first_inner, MIDDLE)
    two_in = along(second, TWO_IN)
    passed = second.astype(jnp.float32) + inward.astype(jnp.float32)
    two_out = along(passed.astype(jnp.bfloat16), TWO_OUT)
    beside = along(third, BESIDE)
    arrived = [block.astype(jnp.float32) for block in (middle, two_in, two_out)]
    total = lax.optimization_barrier(joined(*last_chunk(second)) + sum(arrived))
    return (total + beside.astype(jnp.float32)).astype(jnp.bfloat16)


def on_device(*args):
    block_list = args[5]
    sizes = (lax.axis_size("blk"), lax.axis_size("tp"), block_list.shape[1])
    if sizes == (4, 4, 4):
        return rows_travel(*args)
    return weights_travel(*args)


def solution(mesh):
    return jax.shard_map(
        on_device,
        mesh=mesh,
        in_specs=(
            P(("groups", "blk"), "tp"),
            P("blk", None, "tp"),
            P("blk", None, "tp"),
            P("blk", "tp", None),
            P(("groups", "blk"), None),
            P(("groups", "blk"), None, None),
            P(("groups", "blk"), None),
            P(("groups", "blk")),
        ),
        out_specs=P(("groups", "blk"), "tp"),
        check_vma=False,
    )
```

```python
import jax
import jax.numpy as jnp
from jax import lax
from jax.experimental import pallas as pl
from jax.experimental.pallas import tpu as pltpu
from jax.sharding import PartitionSpec as P


def shifted(block, axis, distance):
    devices = range(lax.axis_size(axis))
    route = [((i - distance) % len(devices), i) for i in devices]
    return lax.ppermute(block, axis, route)


def weights_travel(
    tokens, gate_weight, up_weight, down_weight, route_gates, block_list, block_count, owner_token
):
    whole_rows = lax.all_gather(tokens, "tp", axis=1, tiled=True)
    row_count = whole_rows.shape[0]
    width = whole_rows.shape[1]
    offsets_all = block_list.shape[1]
    block_total = block_list.shape[2]
    block_size = row_count // block_total
    blocks = whole_rows.reshape(block_total, block_size, width)
    gate_blocks = route_gates.reshape(block_total, block_size, offsets_all)
    totals = jnp.zeros((block_total, block_size, width), jnp.float32)

    def apply(totals, weights, offset, block_id):
        w_gate, w_up, w_down = weights
        block_rows = lax.dynamic_index_in_dim(blocks, block_id, 0, keepdims=False)
        gate_out = jnp.dot(block_rows, w_gate, preferred_element_type=jnp.float32)
        up_out = jnp.dot(block_rows, w_up, preferred_element_type=jnp.float32)
        hidden = (jax.nn.silu(gate_out) * up_out).astype(jnp.bfloat16)
        block_gates = lax.dynamic_index_in_dim(gate_blocks, block_id, 0, keepdims=False)
        factor = lax.dynamic_index_in_dim(block_gates, offset, 1, keepdims=False)
        product = jnp.dot(hidden, w_down, preferred_element_type=jnp.float32) * factor[:, None]
        before = lax.dynamic_index_in_dim(totals, block_id, 0, keepdims=False)
        return lax.dynamic_update_index_in_dim(totals, before + product, block_id, 0)

    resident = (gate_weight[0], up_weight[0], down_weight[0])
    arrived = [resident]
    holding = resident
    for offset in range(1, offsets_all):
        holding = shifted((holding[0], holding[1], holding[2]), "blk", 1)
        arrived.append(holding)
    for offset in range(offsets_all):
        weights = arrived[offset]

        def visit_block(position, totals, weights=weights, offset=offset):
            return apply(totals, weights, offset, block_list[0, offset, position])

        totals = lax.fori_loop(0, block_count[0, offset], visit_block, totals)
    summed = lax.psum_scatter(
        totals.reshape(row_count, width).astype(jnp.bfloat16), "tp", scatter_dimension=1, tiled=True
    )
    feature_share = summed.shape[1]
    cycle_size = lax.axis_size("blk")
    owned = row_count // 2
    capacity = max(2, 2 * row_count // cycle_size)
    target = owner_token // owned
    local_token = owner_token % owned
    target_table = (target[:, None] == jnp.arange(cycle_size, dtype=jnp.int32)[None, :]).astype(
        jnp.int32
    )
    running = jnp.cumsum(target_table, axis=0)
    rank = jnp.sum((running - 1) * target_table, axis=1)
    slot = target * capacity + rank
    send_rows = jnp.zeros((cycle_size * capacity, feature_share), jnp.bfloat16).at[slot].set(summed)
    send_index = jnp.full((cycle_size * capacity,), -1, jnp.int32).at[slot].set(local_token)
    send_rows = send_rows.reshape(cycle_size, capacity, feature_share)
    send_index = send_index.reshape(cycle_size, capacity)
    got_rows, got_index = (
        lax.all_to_all(send_rows, "blk", split_axis=0, concat_axis=0, tiled=True),
        lax.all_to_all(send_index, "blk", split_axis=0, concat_axis=0, tiled=True),
    )
    got_rows = got_rows.reshape(cycle_size * capacity, feature_share)
    got_index = got_index.reshape(cycle_size * capacity)
    placing = (got_index[:, None] == jnp.arange(owned, dtype=jnp.int32)[None, :]).astype(
        jnp.bfloat16
    )
    combined = lax.dot_general(
        placing, got_rows, (((0,), (0,)), ((), ())), preferred_element_type=jnp.float32
    )
    return combined.astype(jnp.bfloat16)


BESIDE = [(0, 1), (1, 0), (2, 3), (3, 2)]
MIDDLE = [(1, 2), (2, 1)]
INWARD = [(0, 1), (3, 2)]
OUTWARD = [(1, 0), (2, 3)]
TWO_IN = [(0, 2), (3, 1)]
TWO_OUT = [(1, 3), (2, 0)]
PLAN = [
    [3, 2, 1, 0, 0, 1, 2, 3, 0],
    [2, 3, 0, 1, 0, 3, 1, 2, 1],
    [1, 0, 3, 2, 0, 1, 3, 2, 1],
    [0, 1, 2, 3, 0, 3, 2, 1, 0],
]
OFFSETS_AT, INNER_AT = 4, 8
FACT_ROWS = 16
VMEM = pl.BlockSpec(memory_space=pltpu.VMEM)
SMEM = pl.BlockSpec(memory_space=pltpu.SMEM)
ANYWHERE = pl.BlockSpec(memory_space=pl.ANY)


def across_chips(block):
    return lax.ppermute(block, "tp", [(i, i ^ 2) for i in range(4)])


def across_cores(block):
    return lax.ppermute(block, "tp", [(i, i ^ 1) for i in range(4)])


def along(block, route):
    return lax.ppermute(block, "blk", route)


def cheap():
    return pl.CostEstimate(flops=1024, bytes_accessed=1024, transcendentals=0)


TOKEN = jax.ShapeDtypeStruct((8, 128), jnp.float32)
VMEM_LIMIT = 40 * 2**20


def on_core(body, out_shape, in_specs, scratch=()):
    return pl.pallas_call(
        body,
        out_shape=out_shape,
        in_specs=in_specs,
        out_specs=jax.tree.map(lambda _: VMEM, out_shape),
        scratch_shapes=scratch,
        compiler_params=pltpu.CompilerParams(vmem_limit_bytes=VMEM_LIMIT),
        cost_estimate=cheap(),
    )


def copies(source, start, target, size, pieces, sems, first):
    step = size // pieces
    return [
        pltpu.make_async_copy(
            source.at[pl.ds(start + index * step, step)],
            target.at[pl.ds(index * step, step)],
            sems.at[first + index],
        )
        for index in range(pieces)
    ]


def after(block, *others, flops=1024):
    return pl.pallas_call(
        lambda *refs: None,
        out_shape=jax.ShapeDtypeStruct(block.shape, block.dtype),
        in_specs=[ANYWHERE] * (1 + len(others)),
        out_specs=ANYWHERE,
        input_output_aliases={0: 0},
        cost_estimate=pl.CostEstimate(flops=flops, bytes_accessed=1024, transcendentals=0),
    )(block, *others)


def by_kind(plan_ref, kinds, run):
    if kinds[0] is kinds[1]:
        run(kinds[0])
        return
    for kind, value in zip(kinds, (1, 0)):

        @pl.when(plan_ref[INNER_AT] == value)
        def _(kind=kind):
            run(kind)


def part_of(plan, if_inner, if_outer, start, size, *others, flops=1024):
    shape = jax.ShapeDtypeStruct((size, if_inner.shape[1]), if_inner.dtype)
    pieces = 4

    def body(plan_ref, inner_ref, outer_ref, *rest):
        out_ref, buffer, in_sems, out_sems = rest[len(others) :]

        def run(source):
            inward = copies(source, start, buffer, size, pieces, in_sems, 0)
            outward = copies(buffer, 0, out_ref, size, pieces, out_sems, 0)
            for copy in inward:
                copy.start()
            for copy, next_copy in zip(inward, outward):
                copy.wait()
                next_copy.start()
            for copy in outward:
                copy.wait()

        by_kind(plan_ref, (inner_ref, inner_ref if if_outer is if_inner else outer_ref), run)

    return pl.pallas_call(
        body,
        out_shape=shape,
        in_specs=[SMEM] + [ANYWHERE] * (2 + len(others)),
        out_specs=ANYWHERE,
        scratch_shapes=[pltpu.VMEM(shape.shape, shape.dtype)]
        + [pltpu.SemaphoreType.DMA((pieces,))] * 2,
        compiler_params=pltpu.CompilerParams(vmem_limit_bytes=VMEM_LIMIT),
        cost_estimate=pl.CostEstimate(flops=flops, bytes_accessed=1024, transcendentals=0),
    )(plan, if_inner, if_outer, *others)


def with_facts(rows, gates, block_list, block_count, owner):
    count, width = rows.shape
    blocks, _, offsets = block_list.shape
    total = owner.shape[0]

    def body(rows_ref, gates_ref, list_ref, count_ref, owner_ref, out_ref, sems):
        moves = copies(rows_ref, 0, out_ref, count, 4, sems, 0)
        for copy in moves:
            copy.start()
        block_of = lax.broadcasted_iota(jnp.int32, (1, total), 1) // (total // blocks)
        facts = []
        for offset in range(offsets):
            mask = jnp.zeros((1, total), jnp.float32)
            for block in range(blocks):
                used = jnp.int32(0)
                for place in range(blocks):
                    found = (list_ref[place, 0, offset] == block) & (place < count_ref[0, offset])
                    used = used | found.astype(jnp.int32)
                mask = mask + jnp.where(block_of == block, used.astype(jnp.float32), 0.0)
            facts.append(gates_ref[offset : offset + 1, :] * mask)
        numbers = owner_ref[...].reshape(1, total)
        facts.append((numbers >> 8).astype(jnp.float32))
        facts.append((numbers & 255).astype(jnp.float32))
        facts.append(jnp.zeros((FACT_ROWS - len(facts), total), jnp.float32))
        out_ref[count:, :] = jnp.zeros((FACT_ROWS, width), jnp.bfloat16)
        out_ref[count:, :total] = jnp.concatenate(facts, axis=0).astype(jnp.bfloat16)
        for copy in moves:
            copy.wait()

    shape = jax.ShapeDtypeStruct((count + FACT_ROWS, width), rows.dtype)
    return on_core(
        body, shape, [ANYWHERE, VMEM, SMEM, SMEM, VMEM], [pltpu.SemaphoreType.DMA((4,))]
    )(rows, gates, block_list, block_count, owner)


def partial_sums(plan, sizes, parts, weights, places, before=None, send=True, waits=()):
    width, columns = weights[0].shape
    blocks = [
        block if isinstance(block, tuple) else (block,) for part in parts for block in part
    ]
    sources = [array for block in blocks for array in block]
    operands = [plan] + sources + [weights[place] for place in places] + [weights[2]]
    if before is not None:
        operands.append(before)
    specs = [SMEM] + [VMEM] * (len(operands) - 1 + len(waits))
    has_before = before is not None

    def body(plan_ref, *refs):
        source_refs, refs = refs[: len(sources)], refs[len(sources) :]
        weight_refs, refs = refs[: len(places) + 1], refs[len(places) + 1 :]
        before_ref, refs = (refs[0], refs[1:]) if has_before else (None, refs)
        results = refs[len(waits) :]
        start, source = 0, 0
        for part, size in enumerate(sizes):
            span = slice(start, start + size)
            start += size
            rows = []
            for index in range(len(places)):
                block = blocks[part * len(places) + index]
                value = source_refs[source][:size, :]
                if len(block) > 1:
                    other = source_refs[source + 1][:size, :]
                    value = jnp.where(plan_ref[INNER_AT] == 1, value, other)
                source += len(block)
                rows.append(value)
            for side in range(2):
                at = slice(side * columns, (side + 1) * columns)
                total = before_ref[span, at] if has_before else None
                for index, place in enumerate(places):
                    if side == 0:
                        weight = weight_refs[index][...]
                    else:
                        weight = weight_refs[-1][place * width : (place + 1) * width, :]
                    product = jnp.dot(rows[index], weight, preferred_element_type=jnp.float32)
                    total = product if total is None else total + product
                results[0][span, at] = total
                if send:
                    results[1][span, at] = total.astype(jnp.bfloat16)
        results[-1][...] = jnp.zeros(TOKEN.shape, TOKEN.dtype)

    shapes = [jax.ShapeDtypeStruct((sum(sizes), 2 * columns), jnp.float32)]
    if send:
        shapes.append(jax.ShapeDtypeStruct((sum(sizes), 2 * columns), jnp.bfloat16))
    return on_core(body, shapes + [TOKEN], specs)(*operands, *waits)


def collected_rows(owned, slot, plan, sums, got, facts, before):
    units = sums.shape[1] // 4
    hidden = []
    for core in range(2):
        here, there = 2 * core * units, 2 * (1 - core) * units
        gate = sums[:, here : here + units] + got[:, there : there + units].astype(jnp.float32)
        up = sums[:, here + units : here + 2 * units]
        up = up + got[:, there + units : there + 2 * units].astype(jnp.float32)
        hidden.append((gate / (1.0 + jnp.exp(-gate)) * up).astype(jnp.bfloat16))
    hidden = jnp.concatenate(hidden, axis=1)
    values = facts[:, : sums.shape[0]].astype(jnp.float32)
    kind = lax.broadcasted_iota(jnp.int32, (FACT_ROWS, 1), 0)
    mine = kind == plan[OFFSETS_AT + slot]
    factor = jnp.sum(jnp.where(mine, values, 0.0), axis=0, keepdims=True)
    owner = (values[4:5, :] * 256.0 + values[5:6, :]).astype(jnp.int32)
    results = []
    for index in range(4):
        token = plan[index] * owned + lax.broadcasted_iota(jnp.int32, (owned, 1), 0)
        placing = jnp.where(owner == token, factor, 0.0).astype(jnp.bfloat16)
        rows = jnp.dot(placing, hidden, preferred_element_type=jnp.float32)
        if before is not None:
            rows = rows + before[index * owned : (index + 1) * owned, :]
        results.append(rows)
    return results


def fact_scratch(width):
    return [pltpu.VMEM((FACT_ROWS, width), jnp.bfloat16), pltpu.SemaphoreType.DMA((1,))]


def facts_of(plan_ref, inner_ref, outer_ref, buffer, sem):
    last = inner_ref.shape[0] - FACT_ROWS

    def run(source):
        (copy,) = copies(source, last, buffer, FACT_ROWS, 1, sem, 0)
        copy.start()
        copy.wait()

    by_kind(plan_ref, (inner_ref, outer_ref), run)
    return buffer


def collect(owned, slot, plan, sums, got, facts, before):
    operands = [plan, sums, got, *facts] + ([] if before is None else [before])

    def body(plan_ref, sums_ref, got_ref, inner_ref, outer_ref, *rest):
        before_ref = rest[0] if before is not None else None
        out_ref, token_ref, buffer, sem = rest[-4:]
        facts_here = facts_of(plan_ref, inner_ref, outer_ref, buffer, sem)
        rows = collected_rows(owned, slot, plan_ref, sums_ref, got_ref, facts_here, before_ref)
        for index in range(4):
            out_ref[index * owned : (index + 1) * owned, :] = rows[index]
        token_ref[...] = jnp.zeros(TOKEN.shape, TOKEN.dtype)

    shape = jax.ShapeDtypeStruct((4 * owned, sums.shape[1] // 2), jnp.float32)
    specs = [SMEM, VMEM, VMEM, ANYWHERE, ANYWHERE] + [VMEM] * (len(operands) - 5)
    return on_core(body, [shape, TOKEN], specs, fact_scratch(facts[0].shape[1]))(*operands)


def down(held, own_ref, lent_ref, sent_ref, kept_ref):
    units, width = own_ref.shape[0], kept_ref.shape[1]
    for out, at in ((kept_ref, slice(0, width)), (sent_ref, slice(width, 2 * width))):
        result = jnp.dot(held[:, :units], own_ref[:, at], preferred_element_type=jnp.float32)
        result += jnp.dot(held[:, units:], lent_ref[:, at], preferred_element_type=jnp.float32)
        out[...] = result.astype(out.dtype)


def finish(owned, slot, plan, sums, got, facts, before, down_own, down_lent):
    units = down_own.shape[0]
    width = down_own.shape[1] // 2
    pair = [
        jax.ShapeDtypeStruct((owned, width), jnp.bfloat16),
        jax.ShapeDtypeStruct((owned, width), jnp.float32),
    ]

    def first(plan_ref, sums_ref, got_ref, inner_ref, outer_ref, before_ref, *refs):
        own_ref, lent_ref, sent_ref, kept_ref, held_ref, buffer, sem = refs
        facts_here = facts_of(plan_ref, inner_ref, outer_ref, buffer, sem)
        rows = collected_rows(owned, slot, plan_ref, sums_ref, got_ref, facts_here, before_ref)
        down(rows[0].astype(jnp.bfloat16), own_ref, lent_ref, sent_ref, kept_ref)
        for index in range(1, 4):
            held_ref[(index - 1) * owned : index * owned, :] = rows[index].astype(jnp.bfloat16)

    def others(held_ref, own_ref, lent_ref, *refs):
        for index in range(3):
            held = held_ref[index * owned : (index + 1) * owned, :]
            down(held, own_ref, lent_ref, refs[2 * index], refs[2 * index + 1])

    held_shape = jax.ShapeDtypeStruct((3 * owned, 2 * units), jnp.bfloat16)
    specs = [SMEM, VMEM, VMEM, ANYWHERE, ANYWHERE] + [VMEM] * 3
    sent, kept, held = on_core(
        first, pair + [held_shape], specs, fact_scratch(facts[0].shape[1])
    )(plan, sums, got, *facts, before, down_own, down_lent)
    rest = on_core(others, pair * 3, [VMEM] * 3)(held, down_own, down_lent)
    return [sent, *rest[0::2]], [kept, *rest[1::2]]


def rows_travel(
    tokens, gate_weight, up_weight, down_weight, route_gates, block_list, block_count, owner_token
):
    position = lax.axis_index("blk")
    share = lax.axis_index("tp")
    row_count, width = tokens.shape
    units = gate_weight.shape[2]
    owned = row_count // 2
    half = row_count // 2
    plan = jnp.asarray(PLAN, jnp.int32)[position]

    own_far = across_chips(tokens)
    own = with_facts(
        tokens, route_gates.T, jnp.transpose(block_list, (2, 0, 1)), block_count, owner_token
    )
    beside = along(own, BESIDE)
    middle = along(own, MIDDLE)

    gate_quarters = gate_weight[0].reshape(4, width, units)
    up_quarters = up_weight[0].reshape(4, width, units)

    def quarter(j):
        pair = [
            lax.dynamic_index_in_dim(q, share ^ j, 0, keepdims=False)
            for q in (gate_quarters, up_quarters)
        ]
        return jnp.concatenate(pair, axis=1)

    def down_part(j):
        return lax.dynamic_slice_in_dim(down_weight[0], (share ^ j) * width, width, 1)

    kept_down = jnp.concatenate([down_part(0), down_part(2)], axis=1)
    lend_down = jnp.concatenate([down_part(1), down_part(3)], axis=1)


    def at_kind(block, positions):
        pairs = [(4 * p + i, 4 * p + (i ^ 2)) for p in positions for i in range(4)]
        return lax.ppermute(block, ("blk", "tp"), pairs)

    outer_next = along(middle, OUTWARD)
    beside_far = across_chips(beside)
    own_far_half = part_of(plan, own_far, own_far, half, half, flops=16 * 2**30)
    inward_far = along(own_far_half, INWARD)
    lend = jnp.concatenate([quarter(1), quarter(3)])
    lent = across_cores(after(lend, own))
    weights = [quarter(0), quarter(2), lent]
    whole = [row_count]
    sums_0, send_0, ready_0 = partial_sums(
        plan, whole, [(tokens, own_far)], weights, (0, 1)
    )
    got_0 = across_cores(send_0)
    inner_last = after(along(beside, MIDDLE), ready_0)
    lent_down = across_cores(lend_down)

    outer_last = after(along(inner_last, OUTWARD), flops=5 * 2**30)
    outer_next = after(
        outer_next, beside_far, inner_last, inward_far, lend_down, weights[0], weights[1]
    )
    second = (middle, outer_next)
    second_far = (at_kind(middle, (1, 2)), at_kind(outer_next, (0, 3)))
    middle_far = along(inward_far, MIDDLE)
    sums_1, send_1, ready_1 = partial_sums(
        plan, whole, [(beside, beside_far)], weights, (0, 1)
    )
    got_1 = across_cores(send_1)

    total, collected_0 = collect(owned, 0, plan, sums_0, got_0, (own, own), None)

    last = (inner_last, outer_last)
    last_far_a = across_chips(
        part_of(plan, *last, 0, half, *second_far, collected_0, ready_1)
    )
    outward_far = along(middle_far, OUTWARD)
    total, collected_1 = collect(owned, 1, plan, sums_1, got_1, (beside, beside), total)
    sums_2, send_2, _ = partial_sums(plan, whole, [(second, second_far)], weights, (0, 1))
    got_2 = across_cores(send_2)
    near, _ = partial_sums(plan, whole, [(last,)], weights, (0,), send=False)
    sums_3, send_3, _ = partial_sums(
        plan,
        [half, half],
        [(last_far_a,), ((middle_far, outward_far),)],
        weights,
        (1,),
        before=near,
        waits=[collected_1],
    )
    got_3 = across_cores(send_3)
    total, _ = collect(owned, 2, plan, sums_2, got_2, second, total)
    sent, kept = finish(owned, 3, plan, sums_3, got_3, last, total, kept_down, lent_down)

    joined = [k + across_chips(s).astype(jnp.float32) for s, k in zip(sent, kept)]
    first, second, third = [block.astype(jnp.bfloat16) for block in joined[:3]]
    second = lax.optimization_barrier(second)
    inward = along(first, INWARD)
    middle = along(first, MIDDLE)
    two_in = along(second, TWO_IN)
    passed = second.astype(jnp.float32) + inward.astype(jnp.float32)
    two_out = along(passed.astype(jnp.bfloat16), TWO_OUT)
    beside = along(third, BESIDE)
    arrived = [block.astype(jnp.float32) for block in (middle, two_in, two_out)]
    total = lax.optimization_barrier(joined[3] + sum(arrived))
    return (total + beside.astype(jnp.float32)).astype(jnp.bfloat16)


def on_device(*args):
    block_list = args[5]
    sizes = (lax.axis_size("blk"), lax.axis_size("tp"), block_list.shape[1])
    if sizes == (4, 4, 4):
        return rows_travel(*args)
    return weights_travel(*args)


def solution(mesh):
    return jax.shard_map(
        on_device,
        mesh=mesh,
        in_specs=(
            P(("groups", "blk"), "tp"),
            P("blk", None, "tp"),
            P("blk", None, "tp"),
            P("blk", "tp", None),
            P(("groups", "blk"), None),
            P(("groups", "blk"), None, None),
            P(("groups", "blk"), None),
            P(("groups", "blk")),
        ),
        out_specs=P(("groups", "blk"), "tp"),
        check_vma=False,
    )
```

```python
import jax
import jax.numpy as jnp
from jax import lax
from jax.experimental import pallas as pl
from jax.experimental.pallas import tpu as pltpu
from jax.sharding import PartitionSpec as P


def shifted(block, axis, distance):
    devices = range(lax.axis_size(axis))
    route = [((i - distance) % len(devices), i) for i in devices]
    return lax.ppermute(block, axis, route)


def weights_travel(
    tokens, gate_weight, up_weight, down_weight, route_gates, block_list, block_count, owner_token
):
    whole_rows = lax.all_gather(tokens, "tp", axis=1, tiled=True)
    row_count = whole_rows.shape[0]
    width = whole_rows.shape[1]
    offsets_all = block_list.shape[1]
    block_total = block_list.shape[2]
    block_size = row_count // block_total
    blocks = whole_rows.reshape(block_total, block_size, width)
    gate_blocks = route_gates.reshape(block_total, block_size, offsets_all)
    totals = jnp.zeros((block_total, block_size, width), jnp.float32)

    def apply(totals, weights, offset, block_id):
        w_gate, w_up, w_down = weights
        block_rows = lax.dynamic_index_in_dim(blocks, block_id, 0, keepdims=False)
        gate_out = jnp.dot(block_rows, w_gate, preferred_element_type=jnp.float32)
        up_out = jnp.dot(block_rows, w_up, preferred_element_type=jnp.float32)
        hidden = (jax.nn.silu(gate_out) * up_out).astype(jnp.bfloat16)
        block_gates = lax.dynamic_index_in_dim(gate_blocks, block_id, 0, keepdims=False)
        factor = lax.dynamic_index_in_dim(block_gates, offset, 1, keepdims=False)
        product = jnp.dot(hidden, w_down, preferred_element_type=jnp.float32) * factor[:, None]
        before = lax.dynamic_index_in_dim(totals, block_id, 0, keepdims=False)
        return lax.dynamic_update_index_in_dim(totals, before + product, block_id, 0)

    resident = (gate_weight[0], up_weight[0], down_weight[0])
    arrived = [resident]
    holding = resident
    for offset in range(1, offsets_all):
        holding = shifted((holding[0], holding[1], holding[2]), "blk", 1)
        arrived.append(holding)
    for offset in range(offsets_all):
        weights = arrived[offset]

        def visit_block(position, totals, weights=weights, offset=offset):
            return apply(totals, weights, offset, block_list[0, offset, position])

        totals = lax.fori_loop(0, block_count[0, offset], visit_block, totals)
    summed = lax.psum_scatter(
        totals.reshape(row_count, width).astype(jnp.bfloat16), "tp", scatter_dimension=1, tiled=True
    )
    feature_share = summed.shape[1]
    cycle_size = lax.axis_size("blk")
    owned = row_count // 2
    capacity = max(2, 2 * row_count // cycle_size)
    target = owner_token // owned
    local_token = owner_token % owned
    target_table = (target[:, None] == jnp.arange(cycle_size, dtype=jnp.int32)[None, :]).astype(
        jnp.int32
    )
    running = jnp.cumsum(target_table, axis=0)
    rank = jnp.sum((running - 1) * target_table, axis=1)
    slot = target * capacity + rank
    send_rows = jnp.zeros((cycle_size * capacity, feature_share), jnp.bfloat16).at[slot].set(summed)
    send_index = jnp.full((cycle_size * capacity,), -1, jnp.int32).at[slot].set(local_token)
    send_rows = send_rows.reshape(cycle_size, capacity, feature_share)
    send_index = send_index.reshape(cycle_size, capacity)
    got_rows, got_index = (
        lax.all_to_all(send_rows, "blk", split_axis=0, concat_axis=0, tiled=True),
        lax.all_to_all(send_index, "blk", split_axis=0, concat_axis=0, tiled=True),
    )
    got_rows = got_rows.reshape(cycle_size * capacity, feature_share)
    got_index = got_index.reshape(cycle_size * capacity)
    placing = (got_index[:, None] == jnp.arange(owned, dtype=jnp.int32)[None, :]).astype(
        jnp.bfloat16
    )
    combined = lax.dot_general(
        placing, got_rows, (((0,), (0,)), ((), ())), preferred_element_type=jnp.float32
    )
    return combined.astype(jnp.bfloat16)


BESIDE = [(0, 1), (1, 0), (2, 3), (3, 2)]
MIDDLE = [(1, 2), (2, 1)]
INWARD = [(0, 1), (3, 2)]
OUTWARD = [(1, 0), (2, 3)]
TWO_IN = [(0, 2), (3, 1)]
TWO_OUT = [(1, 3), (2, 0)]
PLAN = [
    [3, 2, 1, 0, 0, 1, 2, 3, 0],
    [2, 3, 0, 1, 0, 3, 1, 2, 1],
    [1, 0, 3, 2, 0, 1, 3, 2, 1],
    [0, 1, 2, 3, 0, 3, 2, 1, 0],
]
OFFSETS_AT, INNER_AT = 4, 8
FACT_ROWS = 16
VMEM = pl.BlockSpec(memory_space=pltpu.VMEM)
SMEM = pl.BlockSpec(memory_space=pltpu.SMEM)
ANYWHERE = pl.BlockSpec(memory_space=pl.ANY)


def across_chips(block):
    return lax.ppermute(block, "tp", [(i, i ^ 2) for i in range(4)])


def across_cores(block):
    return lax.ppermute(block, "tp", [(i, i ^ 1) for i in range(4)])


def along(block, route):
    return lax.ppermute(block, "blk", route)


def cheap():
    return pl.CostEstimate(flops=1024, bytes_accessed=1024, transcendentals=0)


TOKEN = jax.ShapeDtypeStruct((8, 128), jnp.float32)
VMEM_LIMIT = 18 * 2**20


def on_core(body, out_shape, in_specs, scratch=()):
    return pl.pallas_call(
        body,
        out_shape=out_shape,
        in_specs=in_specs,
        out_specs=jax.tree.map(lambda _: VMEM, out_shape),
        scratch_shapes=scratch,
        compiler_params=pltpu.CompilerParams(vmem_limit_bytes=VMEM_LIMIT),
        cost_estimate=cheap(),
    )


def copies(source, start, target, size, pieces, sems, first):
    step = size // pieces
    return [
        pltpu.make_async_copy(
            source.at[pl.ds(start + index * step, step)],
            target.at[pl.ds(index * step, step)],
            sems.at[first + index],
        )
        for index in range(pieces)
    ]


def after(block, *others, flops=1024):
    return pl.pallas_call(
        lambda *refs: None,
        out_shape=jax.ShapeDtypeStruct(block.shape, block.dtype),
        in_specs=[ANYWHERE] * (1 + len(others)),
        out_specs=ANYWHERE,
        input_output_aliases={0: 0},
        cost_estimate=pl.CostEstimate(flops=flops, bytes_accessed=1024, transcendentals=0),
    )(block, *others)


def by_kind(plan_ref, kinds, run):
    if kinds[0] is kinds[1]:
        run(kinds[0])
        return
    for kind, value in zip(kinds, (1, 0)):

        @pl.when(plan_ref[INNER_AT] == value)
        def _(kind=kind):
            run(kind)


def part_of(plan, if_inner, if_outer, start, size, *others, flops=1024):
    shape = jax.ShapeDtypeStruct((size, if_inner.shape[1]), if_inner.dtype)
    pieces = 4

    def body(plan_ref, inner_ref, outer_ref, *rest):
        out_ref, buffer, in_sems, out_sems = rest[len(others) :]

        def run(source):
            inward = copies(source, start, buffer, size, pieces, in_sems, 0)
            outward = copies(buffer, 0, out_ref, size, pieces, out_sems, 0)
            for copy in inward:
                copy.start()
            for copy, next_copy in zip(inward, outward):
                copy.wait()
                next_copy.start()
            for copy in outward:
                copy.wait()

        by_kind(plan_ref, (inner_ref, inner_ref if if_outer is if_inner else outer_ref), run)

    return pl.pallas_call(
        body,
        out_shape=shape,
        in_specs=[SMEM] + [ANYWHERE] * (2 + len(others)),
        out_specs=ANYWHERE,
        scratch_shapes=[pltpu.VMEM(shape.shape, shape.dtype)]
        + [pltpu.SemaphoreType.DMA((pieces,))] * 2,
        compiler_params=pltpu.CompilerParams(vmem_limit_bytes=VMEM_LIMIT),
        cost_estimate=pl.CostEstimate(flops=flops, bytes_accessed=1024, transcendentals=0),
    )(plan, if_inner, if_outer, *others)


def with_facts(rows, gates, block_list, block_count, owner):
    count, width = rows.shape
    blocks, _, offsets = block_list.shape
    total = owner.shape[0]

    def body(rows_ref, gates_ref, list_ref, count_ref, owner_ref, out_ref, sems):
        moves = copies(rows_ref, 0, out_ref, count, 4, sems, 0)
        for copy in moves:
            copy.start()
        block_of = lax.broadcasted_iota(jnp.int32, (1, total), 1) // (total // blocks)
        facts = []
        for offset in range(offsets):
            mask = jnp.zeros((1, total), jnp.float32)
            for block in range(blocks):
                used = jnp.int32(0)
                for place in range(blocks):
                    found = (list_ref[place, 0, offset] == block) & (place < count_ref[0, offset])
                    used = used | found.astype(jnp.int32)
                mask = mask + jnp.where(block_of == block, used.astype(jnp.float32), 0.0)
            facts.append(gates_ref[offset : offset + 1, :] * mask)
        numbers = owner_ref[...].reshape(1, total)
        facts.append((numbers >> 8).astype(jnp.float32))
        facts.append((numbers & 255).astype(jnp.float32))
        facts.append(jnp.zeros((FACT_ROWS - len(facts), total), jnp.float32))
        out_ref[count:, :] = jnp.zeros((FACT_ROWS, width), jnp.bfloat16)
        out_ref[count:, :total] = jnp.concatenate(facts, axis=0).astype(jnp.bfloat16)
        for copy in moves:
            copy.wait()

    shape = jax.ShapeDtypeStruct((count + FACT_ROWS, width), rows.dtype)
    return on_core(
        body, shape, [ANYWHERE, VMEM, SMEM, SMEM, VMEM], [pltpu.SemaphoreType.DMA((4,))]
    )(rows, gates, block_list, block_count, owner)


def partial_sums(plan, sizes, parts, weights, places, before=None, send=True, waits=()):
    width, columns = weights[0].shape
    blocks = [
        block if isinstance(block, tuple) else (block,) for part in parts for block in part
    ]
    sources = [array for block in blocks for array in block]
    operands = [plan] + sources + [weights[place] for place in places] + [weights[2]]
    if before is not None:
        operands.append(before)
    specs = [SMEM] + [VMEM] * (len(operands) - 1 + len(waits))
    has_before = before is not None

    def body(plan_ref, *refs):
        source_refs, refs = refs[: len(sources)], refs[len(sources) :]
        weight_refs, refs = refs[: len(places) + 1], refs[len(places) + 1 :]
        before_ref, refs = (refs[0], refs[1:]) if has_before else (None, refs)
        results = refs[len(waits) :]
        start, source = 0, 0
        for part, size in enumerate(sizes):
            span = slice(start, start + size)
            start += size
            rows = []
            for index in range(len(places)):
                block = blocks[part * len(places) + index]
                value = source_refs[source][:size, :]
                if len(block) > 1:
                    other = source_refs[source + 1][:size, :]
                    value = jnp.where(plan_ref[INNER_AT] == 1, value, other)
                source += len(block)
                rows.append(value)
            for side in range(2):
                at = slice(side * columns, (side + 1) * columns)
                total = before_ref[span, at] if has_before else None
                for index, place in enumerate(places):
                    if side == 0:
                        weight = weight_refs[index][...]
                    else:
                        weight = weight_refs[-1][place * width : (place + 1) * width, :]
                    product = jnp.dot(rows[index], weight, preferred_element_type=jnp.float32)
                    total = product if total is None else total + product
                results[0][span, at] = total
                if send:
                    results[1][span, at] = total.astype(jnp.bfloat16)
        results[-1][...] = jnp.zeros(TOKEN.shape, TOKEN.dtype)

    shapes = [jax.ShapeDtypeStruct((sum(sizes), 2 * columns), jnp.float32)]
    if send:
        shapes.append(jax.ShapeDtypeStruct((sum(sizes), 2 * columns), jnp.bfloat16))
    return on_core(body, shapes + [TOKEN], specs)(*operands, *waits)


def collected_rows(owned, slot, plan, sums, got, facts, before):
    units = sums.shape[1] // 4
    hidden = []
    for core in range(2):
        here, there = 2 * core * units, 2 * (1 - core) * units
        gate = sums[:, here : here + units] + got[:, there : there + units].astype(jnp.float32)
        up = sums[:, here + units : here + 2 * units]
        up = up + got[:, there + units : there + 2 * units].astype(jnp.float32)
        hidden.append((gate / (1.0 + jnp.exp(-gate)) * up).astype(jnp.bfloat16))
    hidden = jnp.concatenate(hidden, axis=1)
    values = facts[:, : sums.shape[0]].astype(jnp.float32)
    kind = lax.broadcasted_iota(jnp.int32, (FACT_ROWS, 1), 0)
    mine = kind == plan[OFFSETS_AT + slot]
    factor = jnp.sum(jnp.where(mine, values, 0.0), axis=0, keepdims=True)
    owner = (values[4:5, :] * 256.0 + values[5:6, :]).astype(jnp.int32)
    results = []
    for index in range(4):
        token = plan[index] * owned + lax.broadcasted_iota(jnp.int32, (owned, 1), 0)
        placing = jnp.where(owner == token, factor, 0.0).astype(jnp.bfloat16)
        rows = jnp.dot(placing, hidden, preferred_element_type=jnp.float32)
        if before is not None:
            rows = rows + before[index * owned : (index + 1) * owned, :]
        results.append(rows)
    return results


def fact_scratch(width):
    return [pltpu.VMEM((FACT_ROWS, width), jnp.bfloat16), pltpu.SemaphoreType.DMA((1,))]


def facts_of(plan_ref, inner_ref, outer_ref, buffer, sem):
    last = inner_ref.shape[0] - FACT_ROWS

    def run(source):
        (copy,) = copies(source, last, buffer, FACT_ROWS, 1, sem, 0)
        copy.start()
        copy.wait()

    by_kind(plan_ref, (inner_ref, outer_ref), run)
    return buffer


def collect(owned, slot, plan, sums, got, facts, before):
    operands = [plan, sums, got, *facts] + ([] if before is None else [before])

    def body(plan_ref, sums_ref, got_ref, inner_ref, outer_ref, *rest):
        before_ref = rest[0] if before is not None else None
        out_ref, token_ref, buffer, sem = rest[-4:]
        facts_here = facts_of(plan_ref, inner_ref, outer_ref, buffer, sem)
        rows = collected_rows(owned, slot, plan_ref, sums_ref, got_ref, facts_here, before_ref)
        for index in range(4):
            out_ref[index * owned : (index + 1) * owned, :] = rows[index]
        token_ref[...] = jnp.zeros(TOKEN.shape, TOKEN.dtype)

    shape = jax.ShapeDtypeStruct((4 * owned, sums.shape[1] // 2), jnp.float32)
    specs = [SMEM, VMEM, VMEM, ANYWHERE, ANYWHERE] + [VMEM] * (len(operands) - 5)
    return on_core(body, [shape, TOKEN], specs, fact_scratch(facts[0].shape[1]))(*operands)


def down(held, own_ref, lent_ref, sent_ref, kept_ref):
    units, width = own_ref.shape[0], kept_ref.shape[1]
    for out, at in ((kept_ref, slice(0, width)), (sent_ref, slice(width, 2 * width))):
        result = jnp.dot(held[:, :units], own_ref[:, at], preferred_element_type=jnp.float32)
        result += jnp.dot(held[:, units:], lent_ref[:, at], preferred_element_type=jnp.float32)
        out[...] = result.astype(out.dtype)


def finish(owned, slot, plan, sums, got, facts, before, down_own, down_lent):
    units = down_own.shape[0]
    width = down_own.shape[1] // 2
    pair = [
        jax.ShapeDtypeStruct((owned, width), jnp.bfloat16),
        jax.ShapeDtypeStruct((owned, width), jnp.float32),
    ]

    def first(plan_ref, sums_ref, got_ref, inner_ref, outer_ref, before_ref, *refs):
        own_ref, lent_ref, sent_ref, kept_ref, held_ref, buffer, sem = refs
        facts_here = facts_of(plan_ref, inner_ref, outer_ref, buffer, sem)
        rows = collected_rows(owned, slot, plan_ref, sums_ref, got_ref, facts_here, before_ref)
        down(rows[0].astype(jnp.bfloat16), own_ref, lent_ref, sent_ref, kept_ref)
        for index in range(1, 4):
            held_ref[(index - 1) * owned : index * owned, :] = rows[index].astype(jnp.bfloat16)

    def others(held_ref, own_ref, lent_ref, *refs):
        for index in range(3):
            held = held_ref[index * owned : (index + 1) * owned, :]
            down(held, own_ref, lent_ref, refs[2 * index], refs[2 * index + 1])

    held_shape = jax.ShapeDtypeStruct((3 * owned, 2 * units), jnp.bfloat16)
    specs = [SMEM, VMEM, VMEM, ANYWHERE, ANYWHERE] + [VMEM] * 3
    sent, kept, held = on_core(
        first, pair + [held_shape], specs, fact_scratch(facts[0].shape[1])
    )(plan, sums, got, *facts, before, down_own, down_lent)
    rest = on_core(others, pair * 3, [VMEM] * 3)(held, down_own, down_lent)
    return [sent, *rest[0::2]], [kept, *rest[1::2]]


def rows_travel(
    tokens, gate_weight, up_weight, down_weight, route_gates, block_list, block_count, owner_token
):
    position = lax.axis_index("blk")
    share = lax.axis_index("tp")
    row_count, width = tokens.shape
    units = gate_weight.shape[2]
    owned = row_count // 2
    half = row_count // 2
    plan = jnp.asarray(PLAN, jnp.int32)[position]

    own_far = across_chips(tokens)
    own = with_facts(
        tokens, route_gates.T, jnp.transpose(block_list, (2, 0, 1)), block_count, owner_token
    )
    beside = along(own, BESIDE)
    middle = along(own, MIDDLE)

    gate_quarters = gate_weight[0].reshape(4, width, units)
    up_quarters = up_weight[0].reshape(4, width, units)

    def quarter(j):
        pair = [
            lax.dynamic_index_in_dim(q, share ^ j, 0, keepdims=False)
            for q in (gate_quarters, up_quarters)
        ]
        return jnp.concatenate(pair, axis=1)

    def down_part(j):
        return lax.dynamic_slice_in_dim(down_weight[0], (share ^ j) * width, width, 1)

    kept_down = jnp.concatenate([down_part(0), down_part(2)], axis=1)
    lend_down = jnp.concatenate([down_part(1), down_part(3)], axis=1)


    def at_kind(block, positions):
        pairs = [(4 * p + i, 4 * p + (i ^ 2)) for p in positions for i in range(4)]
        return lax.ppermute(block, ("blk", "tp"), pairs)

    inner_last = along(beside, MIDDLE)
    outer_next = along(middle, OUTWARD)
    beside_far = across_chips(beside)
    own_far_half = part_of(plan, own_far, own_far, half, half, flops=16 * 2**30)
    inward_far = along(own_far_half, INWARD)
    lend = jnp.concatenate([quarter(1), quarter(3)])
    lent = across_cores(after(lend, own))
    weights = [quarter(0), quarter(2), lent]
    whole = [row_count]
    sums_0, send_0, ready_0 = partial_sums(
        plan, whole, [(tokens, own_far)], weights, (0, 1)
    )
    got_0 = across_cores(send_0)
    lent_down = across_cores(lend_down)

    outer_last = along(inner_last, OUTWARD)
    outer_next = after(
        outer_next, beside_far, inner_last, inward_far, lend_down, weights[0], weights[1], ready_0
    )
    second = (middle, outer_next)
    second_far = (at_kind(middle, (1, 2)), at_kind(outer_next, (0, 3)))
    middle_far = along(inward_far, MIDDLE)
    sums_1, send_1, ready_1 = partial_sums(
        plan, whole, [(beside, beside_far)], weights, (0, 1)
    )
    got_1 = across_cores(send_1)

    last = (inner_last, outer_last)
    last_far_a = across_chips(
        part_of(plan, *last, 0, half, *second_far, middle_far, ready_0, ready_1)
    )
    outward_far = along(middle_far, OUTWARD)
    total, _ = collect(owned, 0, plan, sums_0, got_0, (own, own), None)
    total, collected_1 = collect(owned, 1, plan, sums_1, got_1, (beside, beside), total)
    sums_2, send_2, _ = partial_sums(plan, whole, [(second, second_far)], weights, (0, 1))
    got_2 = across_cores(send_2)
    near, _ = partial_sums(plan, whole, [(last,)], weights, (0,), send=False)
    sums_3, send_3, _ = partial_sums(
        plan,
        [half, half],
        [(last_far_a,), ((middle_far, outward_far),)],
        weights,
        (1,),
        before=near,
        waits=[collected_1],
    )
    got_3 = across_cores(send_3)
    total, _ = collect(owned, 2, plan, sums_2, got_2, second, total)
    sent, kept = finish(owned, 3, plan, sums_3, got_3, last, total, kept_down, lent_down)

    joined = [k + across_chips(s).astype(jnp.float32) for s, k in zip(sent, kept)]
    first, second, third = [block.astype(jnp.bfloat16) for block in joined[:3]]
    second = lax.optimization_barrier(second)
    inward = along(first, INWARD)
    middle = along(first, MIDDLE)
    two_in = along(second, TWO_IN)
    passed = second.astype(jnp.float32) + inward.astype(jnp.float32)
    two_out = along(passed.astype(jnp.bfloat16), TWO_OUT)
    beside = along(third, BESIDE)
    arrived = [block.astype(jnp.float32) for block in (middle, two_in, two_out)]
    total = lax.optimization_barrier(joined[3] + sum(arrived))
    return (total + beside.astype(jnp.float32)).astype(jnp.bfloat16)


def on_device(*args):
    block_list = args[5]
    sizes = (lax.axis_size("blk"), lax.axis_size("tp"), block_list.shape[1])
    if sizes == (4, 4, 4):
        return rows_travel(*args)
    return weights_travel(*args)


def solution(mesh):
    return jax.shard_map(
        on_device,
        mesh=mesh,
        in_specs=(
            P(("groups", "blk"), "tp"),
            P("blk", None, "tp"),
            P("blk", None, "tp"),
            P("blk", "tp", None),
            P(("groups", "blk"), None),
            P(("groups", "blk"), None, None),
            P(("groups", "blk"), None),
            P(("groups", "blk")),
        ),
        out_specs=P(("groups", "blk"), "tp"),
        check_vma=False,
    )
```

```python
import jax
import jax.numpy as jnp
from jax import lax
from jax.experimental import pallas as pl
from jax.experimental.pallas import tpu as pltpu
from jax.sharding import PartitionSpec as P


def shifted(block, axis, distance):
    devices = range(lax.axis_size(axis))
    route = [((i - distance) % len(devices), i) for i in devices]
    return lax.ppermute(block, axis, route)


def weights_travel(
    tokens, gate_weight, up_weight, down_weight, route_gates, block_list, block_count, owner_token
):
    whole_rows = lax.all_gather(tokens, "tp", axis=1, tiled=True)
    row_count = whole_rows.shape[0]
    width = whole_rows.shape[1]
    offsets_all = block_list.shape[1]
    block_total = block_list.shape[2]
    block_size = row_count // block_total
    blocks = whole_rows.reshape(block_total, block_size, width)
    gate_blocks = route_gates.reshape(block_total, block_size, offsets_all)
    totals = jnp.zeros((block_total, block_size, width), jnp.float32)

    def apply(totals, weights, offset, block_id):
        w_gate, w_up, w_down = weights
        block_rows = lax.dynamic_index_in_dim(blocks, block_id, 0, keepdims=False)
        gate_out = jnp.dot(block_rows, w_gate, preferred_element_type=jnp.float32)
        up_out = jnp.dot(block_rows, w_up, preferred_element_type=jnp.float32)
        hidden = (jax.nn.silu(gate_out) * up_out).astype(jnp.bfloat16)
        block_gates = lax.dynamic_index_in_dim(gate_blocks, block_id, 0, keepdims=False)
        factor = lax.dynamic_index_in_dim(block_gates, offset, 1, keepdims=False)
        product = jnp.dot(hidden, w_down, preferred_element_type=jnp.float32) * factor[:, None]
        before = lax.dynamic_index_in_dim(totals, block_id, 0, keepdims=False)
        return lax.dynamic_update_index_in_dim(totals, before + product, block_id, 0)

    resident = (gate_weight[0], up_weight[0], down_weight[0])
    arrived = [resident]
    holding = resident
    for offset in range(1, offsets_all):
        holding = shifted((holding[0], holding[1], holding[2]), "blk", 1)
        arrived.append(holding)
    for offset in range(offsets_all):
        weights = arrived[offset]

        def visit_block(position, totals, weights=weights, offset=offset):
            return apply(totals, weights, offset, block_list[0, offset, position])

        totals = lax.fori_loop(0, block_count[0, offset], visit_block, totals)
    summed = lax.psum_scatter(
        totals.reshape(row_count, width).astype(jnp.bfloat16), "tp", scatter_dimension=1, tiled=True
    )
    feature_share = summed.shape[1]
    cycle_size = lax.axis_size("blk")
    owned = row_count // 2
    capacity = max(2, 2 * row_count // cycle_size)
    target = owner_token // owned
    local_token = owner_token % owned
    target_table = (target[:, None] == jnp.arange(cycle_size, dtype=jnp.int32)[None, :]).astype(
        jnp.int32
    )
    running = jnp.cumsum(target_table, axis=0)
    rank = jnp.sum((running - 1) * target_table, axis=1)
    slot = target * capacity + rank
    send_rows = jnp.zeros((cycle_size * capacity, feature_share), jnp.bfloat16).at[slot].set(summed)
    send_index = jnp.full((cycle_size * capacity,), -1, jnp.int32).at[slot].set(local_token)
    send_rows = send_rows.reshape(cycle_size, capacity, feature_share)
    send_index = send_index.reshape(cycle_size, capacity)
    got_rows, got_index = (
        lax.all_to_all(send_rows, "blk", split_axis=0, concat_axis=0, tiled=True),
        lax.all_to_all(send_index, "blk", split_axis=0, concat_axis=0, tiled=True),
    )
    got_rows = got_rows.reshape(cycle_size * capacity, feature_share)
    got_index = got_index.reshape(cycle_size * capacity)
    placing = (got_index[:, None] == jnp.arange(owned, dtype=jnp.int32)[None, :]).astype(
        jnp.bfloat16
    )
    combined = lax.dot_general(
        placing, got_rows, (((0,), (0,)), ((), ())), preferred_element_type=jnp.float32
    )
    return combined.astype(jnp.bfloat16)


BESIDE = [(0, 1), (1, 0), (2, 3), (3, 2)]
MIDDLE = [(1, 2), (2, 1)]
INWARD = [(0, 1), (3, 2)]
OUTWARD = [(1, 0), (2, 3)]
TWO_IN = [(0, 2), (3, 1)]
TWO_OUT = [(1, 3), (2, 0)]
PLAN = [
    [3, 2, 1, 0, 0, 1, 2, 3, 0],
    [2, 3, 0, 1, 0, 3, 1, 2, 1],
    [1, 0, 3, 2, 0, 1, 3, 2, 1],
    [0, 1, 2, 3, 0, 3, 2, 1, 0],
]
OFFSETS_AT, INNER_AT = 4, 8
FACT_ROWS = 16
VMEM = pl.BlockSpec(memory_space=pltpu.VMEM)
SMEM = pl.BlockSpec(memory_space=pltpu.SMEM)
ANYWHERE = pl.BlockSpec(memory_space=pl.ANY)


def across_chips(block):
    return lax.ppermute(block, "tp", [(i, i ^ 2) for i in range(4)])


def across_cores(block):
    return lax.ppermute(block, "tp", [(i, i ^ 1) for i in range(4)])


def along(block, route):
    return lax.ppermute(block, "blk", route)


def cheap():
    return pl.CostEstimate(flops=1024, bytes_accessed=1024, transcendentals=0)


TOKEN = jax.ShapeDtypeStruct((8, 128), jnp.float32)
VMEM_LIMIT = 18 * 2**20


def on_core(body, out_shape, in_specs, scratch=()):
    return pl.pallas_call(
        body,
        out_shape=out_shape,
        in_specs=in_specs,
        out_specs=jax.tree.map(lambda _: VMEM, out_shape),
        scratch_shapes=scratch,
        compiler_params=pltpu.CompilerParams(vmem_limit_bytes=VMEM_LIMIT),
        cost_estimate=cheap(),
    )


def copies(source, start, target, size, pieces, sems, first):
    step = size // pieces
    return [
        pltpu.make_async_copy(
            source.at[pl.ds(start + index * step, step)],
            target.at[pl.ds(index * step, step)],
            sems.at[first + index],
        )
        for index in range(pieces)
    ]


def after(block, *others, flops=1024):
    return pl.pallas_call(
        lambda *refs: None,
        out_shape=jax.ShapeDtypeStruct(block.shape, block.dtype),
        in_specs=[ANYWHERE] * (1 + len(others)),
        out_specs=ANYWHERE,
        input_output_aliases={0: 0},
        cost_estimate=pl.CostEstimate(flops=flops, bytes_accessed=1024, transcendentals=0),
    )(block, *others)


def by_kind(plan_ref, kinds, run):
    if kinds[0] is kinds[1]:
        run(kinds[0])
        return
    for kind, value in zip(kinds, (1, 0)):

        @pl.when(plan_ref[INNER_AT] == value)
        def _(kind=kind):
            run(kind)


def part_of(plan, if_inner, if_outer, start, size, *others, flops=1024):
    shape = jax.ShapeDtypeStruct((size, if_inner.shape[1]), if_inner.dtype)
    pieces = 4

    def body(plan_ref, inner_ref, outer_ref, *rest):
        out_ref, buffer, in_sems, out_sems = rest[len(others) :]

        def run(source):
            inward = copies(source, start, buffer, size, pieces, in_sems, 0)
            outward = copies(buffer, 0, out_ref, size, pieces, out_sems, 0)
            for copy in inward:
                copy.start()
            for copy, next_copy in zip(inward, outward):
                copy.wait()
                next_copy.start()
            for copy in outward:
                copy.wait()

        by_kind(plan_ref, (inner_ref, inner_ref if if_outer is if_inner else outer_ref), run)

    return pl.pallas_call(
        body,
        out_shape=shape,
        in_specs=[SMEM] + [ANYWHERE] * (2 + len(others)),
        out_specs=ANYWHERE,
        scratch_shapes=[pltpu.VMEM(shape.shape, shape.dtype)]
        + [pltpu.SemaphoreType.DMA((pieces,))] * 2,
        compiler_params=pltpu.CompilerParams(vmem_limit_bytes=VMEM_LIMIT),
        cost_estimate=pl.CostEstimate(flops=flops, bytes_accessed=1024, transcendentals=0),
    )(plan, if_inner, if_outer, *others)


def with_facts(rows, gates, block_list, block_count, owner):
    count, width = rows.shape
    blocks, _, offsets = block_list.shape
    total = owner.shape[0]

    def body(rows_ref, gates_ref, list_ref, count_ref, owner_ref, out_ref, sems):
        moves = copies(rows_ref, 0, out_ref, count, 4, sems, 0)
        for copy in moves:
            copy.start()
        block_of = lax.broadcasted_iota(jnp.int32, (1, total), 1) // (total // blocks)
        facts = []
        for offset in range(offsets):
            mask = jnp.zeros((1, total), jnp.float32)
            for block in range(blocks):
                used = jnp.int32(0)
                for place in range(blocks):
                    found = (list_ref[place, 0, offset] == block) & (place < count_ref[0, offset])
                    used = used | found.astype(jnp.int32)
                mask = mask + jnp.where(block_of == block, used.astype(jnp.float32), 0.0)
            facts.append(gates_ref[offset : offset + 1, :] * mask)
        numbers = owner_ref[...].reshape(1, total)
        facts.append((numbers >> 8).astype(jnp.float32))
        facts.append((numbers & 255).astype(jnp.float32))
        facts.append(jnp.zeros((FACT_ROWS - len(facts), total), jnp.float32))
        out_ref[count:, :] = jnp.zeros((FACT_ROWS, width), jnp.bfloat16)
        out_ref[count:, :total] = jnp.concatenate(facts, axis=0).astype(jnp.bfloat16)
        for copy in moves:
            copy.wait()

    shape = jax.ShapeDtypeStruct((count + FACT_ROWS, width), rows.dtype)
    return on_core(
        body, shape, [ANYWHERE, VMEM, SMEM, SMEM, VMEM], [pltpu.SemaphoreType.DMA((4,))]
    )(rows, gates, block_list, block_count, owner)


def partial_sums(plan, sizes, parts, weights, places, before=None, send=True, waits=()):
    width, columns = weights[0].shape
    blocks = [
        block if isinstance(block, tuple) else (block,) for part in parts for block in part
    ]
    sources = [array for block in blocks for array in block]
    operands = [plan] + sources + [weights[place] for place in places] + [weights[2]]
    if before is not None:
        operands.append(before)
    specs = [SMEM] + [VMEM] * (len(operands) - 1 + len(waits))
    has_before = before is not None

    def body(plan_ref, *refs):
        source_refs, refs = refs[: len(sources)], refs[len(sources) :]
        weight_refs, refs = refs[: len(places) + 1], refs[len(places) + 1 :]
        before_ref, refs = (refs[0], refs[1:]) if has_before else (None, refs)
        results = refs[len(waits) :]
        start, source = 0, 0
        for part, size in enumerate(sizes):
            span = slice(start, start + size)
            start += size
            rows = []
            for index in range(len(places)):
                block = blocks[part * len(places) + index]
                value = source_refs[source][:size, :]
                if len(block) > 1:
                    other = source_refs[source + 1][:size, :]
                    value = jnp.where(plan_ref[INNER_AT] == 1, value, other)
                source += len(block)
                rows.append(value)
            for side in range(2):
                at = slice(side * columns, (side + 1) * columns)
                total = before_ref[span, at] if has_before else None
                for index, place in enumerate(places):
                    if side == 0:
                        weight = weight_refs[index][...]
                    else:
                        weight = weight_refs[-1][place * width : (place + 1) * width, :]
                    product = jnp.dot(rows[index], weight, preferred_element_type=jnp.float32)
                    total = product if total is None else total + product
                results[0][span, at] = total
                if send:
                    results[1][span, at] = total.astype(jnp.bfloat16)
        results[-1][...] = jnp.zeros(TOKEN.shape, TOKEN.dtype)

    shapes = [jax.ShapeDtypeStruct((sum(sizes), 2 * columns), jnp.float32)]
    if send:
        shapes.append(jax.ShapeDtypeStruct((sum(sizes), 2 * columns), jnp.bfloat16))
    return on_core(body, shapes + [TOKEN], specs)(*operands, *waits)


def collected_rows(owned, slot, plan, sums, got, facts, before):
    units = sums.shape[1] // 4
    hidden = []
    for core in range(2):
        here, there = 2 * core * units, 2 * (1 - core) * units
        gate = sums[:, here : here + units] + got[:, there : there + units].astype(jnp.float32)
        up = sums[:, here + units : here + 2 * units]
        up = up + got[:, there + units : there + 2 * units].astype(jnp.float32)
        hidden.append((gate / (1.0 + jnp.exp(-gate)) * up).astype(jnp.bfloat16))
    hidden = jnp.concatenate(hidden, axis=1)
    values = facts[:, : sums.shape[0]].astype(jnp.float32)
    kind = lax.broadcasted_iota(jnp.int32, (FACT_ROWS, 1), 0)
    mine = kind == plan[OFFSETS_AT + slot]
    factor = jnp.sum(jnp.where(mine, values, 0.0), axis=0, keepdims=True)
    owner = (values[4:5, :] * 256.0 + values[5:6, :]).astype(jnp.int32)
    results = []
    for index in range(4):
        token = plan[index] * owned + lax.broadcasted_iota(jnp.int32, (owned, 1), 0)
        placing = jnp.where(owner == token, factor, 0.0).astype(jnp.bfloat16)
        rows = jnp.dot(placing, hidden, preferred_element_type=jnp.float32)
        if before is not None:
            rows = rows + before[index * owned : (index + 1) * owned, :]
        results.append(rows)
    return results


def fact_scratch(width):
    return [pltpu.VMEM((FACT_ROWS, width), jnp.bfloat16), pltpu.SemaphoreType.DMA((1,))]


def facts_of(plan_ref, inner_ref, outer_ref, buffer, sem):
    last = inner_ref.shape[0] - FACT_ROWS

    def run(source):
        (copy,) = copies(source, last, buffer, FACT_ROWS, 1, sem, 0)
        copy.start()
        copy.wait()

    by_kind(plan_ref, (inner_ref, outer_ref), run)
    return buffer


def collect(owned, slot, plan, sums, got, facts, before):
    operands = [plan, sums, got, *facts] + ([] if before is None else [before])

    def body(plan_ref, sums_ref, got_ref, inner_ref, outer_ref, *rest):
        before_ref = rest[0] if before is not None else None
        out_ref, token_ref, buffer, sem = rest[-4:]
        facts_here = facts_of(plan_ref, inner_ref, outer_ref, buffer, sem)
        rows = collected_rows(owned, slot, plan_ref, sums_ref, got_ref, facts_here, before_ref)
        for index in range(4):
            out_ref[index * owned : (index + 1) * owned, :] = rows[index]
        token_ref[...] = jnp.zeros(TOKEN.shape, TOKEN.dtype)

    shape = jax.ShapeDtypeStruct((4 * owned, sums.shape[1] // 2), jnp.float32)
    specs = [SMEM, VMEM, VMEM, ANYWHERE, ANYWHERE] + [VMEM] * (len(operands) - 5)
    return on_core(body, [shape, TOKEN], specs, fact_scratch(facts[0].shape[1]))(*operands)


def down(held, own_ref, lent_ref, sent_ref, kept_ref):
    units, width = own_ref.shape[0], kept_ref.shape[1]
    for out, at in ((kept_ref, slice(0, width)), (sent_ref, slice(width, 2 * width))):
        result = jnp.dot(held[:, :units], own_ref[:, at], preferred_element_type=jnp.float32)
        result += jnp.dot(held[:, units:], lent_ref[:, at], preferred_element_type=jnp.float32)
        out[...] = result.astype(out.dtype)


def finish(owned, slot, plan, sums, got, facts, before, down_own, down_lent):
    units = down_own.shape[0]
    width = down_own.shape[1] // 2
    pair = [
        jax.ShapeDtypeStruct((owned, width), jnp.bfloat16),
        jax.ShapeDtypeStruct((owned, width), jnp.float32),
    ]

    def first(plan_ref, sums_ref, got_ref, inner_ref, outer_ref, before_ref, *refs):
        own_ref, lent_ref, sent_ref, kept_ref, held_ref, buffer, sem = refs
        facts_here = facts_of(plan_ref, inner_ref, outer_ref, buffer, sem)
        rows = collected_rows(owned, slot, plan_ref, sums_ref, got_ref, facts_here, before_ref)
        down(rows[0].astype(jnp.bfloat16), own_ref, lent_ref, sent_ref, kept_ref)
        for index in range(1, 4):
            held_ref[(index - 1) * owned : index * owned, :] = rows[index].astype(jnp.bfloat16)

    def others(held_ref, own_ref, lent_ref, *refs):
        for index in range(3):
            held = held_ref[index * owned : (index + 1) * owned, :]
            down(held, own_ref, lent_ref, refs[2 * index], refs[2 * index + 1])

    held_shape = jax.ShapeDtypeStruct((3 * owned, 2 * units), jnp.bfloat16)
    specs = [SMEM, VMEM, VMEM, ANYWHERE, ANYWHERE] + [VMEM] * 3
    sent, kept, held = on_core(
        first, pair + [held_shape], specs, fact_scratch(facts[0].shape[1])
    )(plan, sums, got, *facts, before, down_own, down_lent)
    rest = on_core(others, pair * 3, [VMEM] * 3)(held, down_own, down_lent)
    return [sent, *rest[0::2]], [kept, *rest[1::2]]


def rows_travel(
    tokens, gate_weight, up_weight, down_weight, route_gates, block_list, block_count, owner_token
):
    position = lax.axis_index("blk")
    share = lax.axis_index("tp")
    row_count, width = tokens.shape
    units = gate_weight.shape[2]
    owned = row_count // 2
    half = row_count // 2
    plan = jnp.asarray(PLAN, jnp.int32)[position]

    own_far = across_chips(tokens)
    own = with_facts(
        tokens, route_gates.T, jnp.transpose(block_list, (2, 0, 1)), block_count, owner_token
    )
    beside = along(own, BESIDE)
    middle = along(own, MIDDLE)

    gate_quarters = gate_weight[0].reshape(4, width, units)
    up_quarters = up_weight[0].reshape(4, width, units)

    def quarter(j):
        pair = [
            lax.dynamic_index_in_dim(q, share ^ j, 0, keepdims=False)
            for q in (gate_quarters, up_quarters)
        ]
        return jnp.concatenate(pair, axis=1)

    def down_part(j):
        return lax.dynamic_slice_in_dim(down_weight[0], (share ^ j) * width, width, 1)

    kept_down = jnp.concatenate([down_part(0), down_part(2)], axis=1)
    lend_down = jnp.concatenate([down_part(1), down_part(3)], axis=1)


    def at_kind(block, positions):
        pairs = [(4 * p + i, 4 * p + (i ^ 2)) for p in positions for i in range(4)]
        return lax.ppermute(block, ("blk", "tp"), pairs)

    inner_last = along(beside, MIDDLE)
    outer_next = along(middle, OUTWARD)
    beside_far = across_chips(beside)
    own_far_half = part_of(plan, own_far, own_far, half, half, flops=16 * 2**30)
    inward_far = along(own_far_half, INWARD)
    lend = jnp.concatenate([quarter(1), quarter(3)])
    lent = across_cores(after(lend, own))
    weights = [quarter(0), quarter(2), lent]
    whole = [row_count]
    sums_0, send_0, ready_0 = partial_sums(
        plan, whole, [(tokens, own_far)], weights, (0, 1), waits=[lend_down]
    )
    got_0 = across_cores(send_0)
    lent_down = across_cores(lend_down)

    outer_last = along(inner_last, OUTWARD)
    outer_next = after(outer_next, beside_far, inner_last, inward_far, ready_0)
    second = (middle, outer_next)
    second_far = (at_kind(middle, (1, 2)), at_kind(outer_next, (0, 3)))
    middle_far = along(inward_far, MIDDLE)
    sums_1, send_1, ready_1 = partial_sums(
        plan, whole, [(beside, beside_far)], weights, (0, 1)
    )
    got_1 = across_cores(send_1)

    last = (inner_last, outer_last)
    last_far_a = across_chips(
        part_of(plan, *last, 0, half, *second_far, middle_far, ready_0, ready_1)
    )
    outward_far = along(middle_far, OUTWARD)
    total, _ = collect(owned, 0, plan, sums_0, got_0, (own, own), None)
    total, collected_1 = collect(owned, 1, plan, sums_1, got_1, (beside, beside), total)
    sums_2, send_2, _ = partial_sums(plan, whole, [(second, second_far)], weights, (0, 1))
    got_2 = across_cores(send_2)
    near, _ = partial_sums(plan, whole, [(last,)], weights, (0,), send=False)
    sums_3, send_3, _ = partial_sums(
        plan,
        [half, half],
        [(last_far_a,), ((middle_far, outward_far),)],
        weights,
        (1,),
        before=near,
        waits=[collected_1],
    )
    got_3 = across_cores(send_3)
    total, _ = collect(owned, 2, plan, sums_2, got_2, second, total)
    sent, kept = finish(owned, 3, plan, sums_3, got_3, last, total, kept_down, lent_down)

    joined = [k + across_chips(s).astype(jnp.float32) for s, k in zip(sent, kept)]
    first, second, third = [block.astype(jnp.bfloat16) for block in joined[:3]]
    second = lax.optimization_barrier(second)
    inward = along(first, INWARD)
    middle = after(along(first, MIDDLE), flops=8 * 2**30)
    two_in = along(second, TWO_IN)
    passed = second.astype(jnp.float32) + inward.astype(jnp.float32)
    two_out = along(passed.astype(jnp.bfloat16), TWO_OUT)
    beside = along(third, BESIDE)
    arrived = [block.astype(jnp.float32) for block in (middle, two_in, two_out)]
    total = lax.optimization_barrier(joined[3] + sum(arrived))
    return (total + beside.astype(jnp.float32)).astype(jnp.bfloat16)


def on_device(*args):
    block_list = args[5]
    sizes = (lax.axis_size("blk"), lax.axis_size("tp"), block_list.shape[1])
    if sizes == (4, 4, 4):
        return rows_travel(*args)
    return weights_travel(*args)


def solution(mesh):
    return jax.shard_map(
        on_device,
        mesh=mesh,
        in_specs=(
            P(("groups", "blk"), "tp"),
            P("blk", None, "tp"),
            P("blk", None, "tp"),
            P("blk", "tp", None),
            P(("groups", "blk"), None),
            P(("groups", "blk"), None, None),
            P(("groups", "blk"), None),
            P(("groups", "blk")),
        ),
        out_specs=P(("groups", "blk"), "tp"),
        check_vma=False,
    )
```

```python
import jax
import jax.numpy as jnp
from jax import lax
from jax.experimental import pallas as pl
from jax.experimental.pallas import tpu as pltpu
from jax.sharding import PartitionSpec as P


def shifted(block, axis, distance):
    devices = range(lax.axis_size(axis))
    route = [((i - distance) % len(devices), i) for i in devices]
    return lax.ppermute(block, axis, route)


def weights_travel(
    tokens, gate_weight, up_weight, down_weight, route_gates, block_list, block_count, owner_token
):
    whole_rows = lax.all_gather(tokens, "tp", axis=1, tiled=True)
    row_count = whole_rows.shape[0]
    width = whole_rows.shape[1]
    offsets_all = block_list.shape[1]
    block_total = block_list.shape[2]
    block_size = row_count // block_total
    blocks = whole_rows.reshape(block_total, block_size, width)
    gate_blocks = route_gates.reshape(block_total, block_size, offsets_all)
    totals = jnp.zeros((block_total, block_size, width), jnp.float32)

    def apply(totals, weights, offset, block_id):
        w_gate, w_up, w_down = weights
        block_rows = lax.dynamic_index_in_dim(blocks, block_id, 0, keepdims=False)
        gate_out = jnp.dot(block_rows, w_gate, preferred_element_type=jnp.float32)
        up_out = jnp.dot(block_rows, w_up, preferred_element_type=jnp.float32)
        hidden = (jax.nn.silu(gate_out) * up_out).astype(jnp.bfloat16)
        block_gates = lax.dynamic_index_in_dim(gate_blocks, block_id, 0, keepdims=False)
        factor = lax.dynamic_index_in_dim(block_gates, offset, 1, keepdims=False)
        product = jnp.dot(hidden, w_down, preferred_element_type=jnp.float32) * factor[:, None]
        before = lax.dynamic_index_in_dim(totals, block_id, 0, keepdims=False)
        return lax.dynamic_update_index_in_dim(totals, before + product, block_id, 0)

    resident = (gate_weight[0], up_weight[0], down_weight[0])
    arrived = [resident]
    holding = resident
    for offset in range(1, offsets_all):
        holding = shifted((holding[0], holding[1], holding[2]), "blk", 1)
        arrived.append(holding)
    for offset in range(offsets_all):
        weights = arrived[offset]

        def visit_block(position, totals, weights=weights, offset=offset):
            return apply(totals, weights, offset, block_list[0, offset, position])

        totals = lax.fori_loop(0, block_count[0, offset], visit_block, totals)
    summed = lax.psum_scatter(
        totals.reshape(row_count, width).astype(jnp.bfloat16), "tp", scatter_dimension=1, tiled=True
    )
    feature_share = summed.shape[1]
    cycle_size = lax.axis_size("blk")
    owned = row_count // 2
    capacity = max(2, 2 * row_count // cycle_size)
    target = owner_token // owned
    local_token = owner_token % owned
    target_table = (target[:, None] == jnp.arange(cycle_size, dtype=jnp.int32)[None, :]).astype(
        jnp.int32
    )
    running = jnp.cumsum(target_table, axis=0)
    rank = jnp.sum((running - 1) * target_table, axis=1)
    slot = target * capacity + rank
    send_rows = jnp.zeros((cycle_size * capacity, feature_share), jnp.bfloat16).at[slot].set(summed)
    send_index = jnp.full((cycle_size * capacity,), -1, jnp.int32).at[slot].set(local_token)
    send_rows = send_rows.reshape(cycle_size, capacity, feature_share)
    send_index = send_index.reshape(cycle_size, capacity)
    got_rows, got_index = (
        lax.all_to_all(send_rows, "blk", split_axis=0, concat_axis=0, tiled=True),
        lax.all_to_all(send_index, "blk", split_axis=0, concat_axis=0, tiled=True),
    )
    got_rows = got_rows.reshape(cycle_size * capacity, feature_share)
    got_index = got_index.reshape(cycle_size * capacity)
    placing = (got_index[:, None] == jnp.arange(owned, dtype=jnp.int32)[None, :]).astype(
        jnp.bfloat16
    )
    combined = lax.dot_general(
        placing, got_rows, (((0,), (0,)), ((), ())), preferred_element_type=jnp.float32
    )
    return combined.astype(jnp.bfloat16)


BESIDE = [(0, 1), (1, 0), (2, 3), (3, 2)]
MIDDLE = [(1, 2), (2, 1)]
INWARD = [(0, 1), (3, 2)]
OUTWARD = [(1, 0), (2, 3)]
TWO_IN = [(0, 2), (3, 1)]
TWO_OUT = [(1, 3), (2, 0)]
PLAN = [
    [3, 2, 1, 0, 0, 1, 2, 3, 0],
    [2, 3, 0, 1, 0, 3, 1, 2, 1],
    [1, 0, 3, 2, 0, 1, 3, 2, 1],
    [0, 1, 2, 3, 0, 3, 2, 1, 0],
]
OFFSETS_AT, INNER_AT = 4, 8
FACT_ROWS = 16
VMEM = pl.BlockSpec(memory_space=pltpu.VMEM)
SMEM = pl.BlockSpec(memory_space=pltpu.SMEM)
ANYWHERE = pl.BlockSpec(memory_space=pl.ANY)


def across_chips(block):
    return lax.ppermute(block, "tp", [(i, i ^ 2) for i in range(4)])


def across_cores(block):
    return lax.ppermute(block, "tp", [(i, i ^ 1) for i in range(4)])


def along(block, route):
    return lax.ppermute(block, "blk", route)


def cheap():
    return pl.CostEstimate(flops=1024, bytes_accessed=1024, transcendentals=0)


TOKEN = jax.ShapeDtypeStruct((8, 128), jnp.float32)
VMEM_LIMIT = 18 * 2**20


def on_core(body, out_shape, in_specs, scratch=()):
    return pl.pallas_call(
        body,
        out_shape=out_shape,
        in_specs=in_specs,
        out_specs=jax.tree.map(lambda _: VMEM, out_shape),
        scratch_shapes=scratch,
        compiler_params=pltpu.CompilerParams(vmem_limit_bytes=VMEM_LIMIT),
        cost_estimate=cheap(),
    )


def copies(source, start, target, size, pieces, sems, first):
    step = size // pieces
    return [
        pltpu.make_async_copy(
            source.at[pl.ds(start + index * step, step)],
            target.at[pl.ds(index * step, step)],
            sems.at[first + index],
        )
        for index in range(pieces)
    ]


def after(block, *others, flops=1024):
    return pl.pallas_call(
        lambda *refs: None,
        out_shape=jax.ShapeDtypeStruct(block.shape, block.dtype),
        in_specs=[ANYWHERE] * (1 + len(others)),
        out_specs=ANYWHERE,
        input_output_aliases={0: 0},
        cost_estimate=pl.CostEstimate(flops=flops, bytes_accessed=1024, transcendentals=0),
    )(block, *others)


def by_kind(plan_ref, kinds, run):
    if kinds[0] is kinds[1]:
        run(kinds[0])
        return
    for kind, value in zip(kinds, (1, 0)):

        @pl.when(plan_ref[INNER_AT] == value)
        def _(kind=kind):
            run(kind)


def part_of(plan, if_inner, if_outer, start, size, *others, flops=1024):
    shape = jax.ShapeDtypeStruct((size, if_inner.shape[1]), if_inner.dtype)
    pieces = 4

    def body(plan_ref, inner_ref, outer_ref, *rest):
        out_ref, buffer, in_sems, out_sems = rest[len(others) :]

        def run(source):
            inward = copies(source, start, buffer, size, pieces, in_sems, 0)
            outward = copies(buffer, 0, out_ref, size, pieces, out_sems, 0)
            for copy in inward:
                copy.start()
            for copy, next_copy in zip(inward, outward):
                copy.wait()
                next_copy.start()
            for copy in outward:
                copy.wait()

        by_kind(plan_ref, (inner_ref, inner_ref if if_outer is if_inner else outer_ref), run)

    return pl.pallas_call(
        body,
        out_shape=shape,
        in_specs=[SMEM] + [ANYWHERE] * (2 + len(others)),
        out_specs=ANYWHERE,
        scratch_shapes=[pltpu.VMEM(shape.shape, shape.dtype)]
        + [pltpu.SemaphoreType.DMA((pieces,))] * 2,
        compiler_params=pltpu.CompilerParams(vmem_limit_bytes=VMEM_LIMIT),
        cost_estimate=pl.CostEstimate(flops=flops, bytes_accessed=1024, transcendentals=0),
    )(plan, if_inner, if_outer, *others)


def with_facts(rows, gates, block_list, block_count, owner):
    count, width = rows.shape
    blocks, _, offsets = block_list.shape
    total = owner.shape[0]

    def body(rows_ref, gates_ref, list_ref, count_ref, owner_ref, out_ref, sems):
        moves = copies(rows_ref, 0, out_ref, count, 4, sems, 0)
        for copy in moves:
            copy.start()
        block_of = lax.broadcasted_iota(jnp.int32, (1, total), 1) // (total // blocks)
        facts = []
        for offset in range(offsets):
            mask = jnp.zeros((1, total), jnp.float32)
            for block in range(blocks):
                used = jnp.int32(0)
                for place in range(blocks):
                    found = (list_ref[place, 0, offset] == block) & (place < count_ref[0, offset])
                    used = used | found.astype(jnp.int32)
                mask = mask + jnp.where(block_of == block, used.astype(jnp.float32), 0.0)
            facts.append(gates_ref[offset : offset + 1, :] * mask)
        numbers = owner_ref[...].reshape(1, total)
        facts.append((numbers >> 8).astype(jnp.float32))
        facts.append((numbers & 255).astype(jnp.float32))
        facts.append(jnp.zeros((FACT_ROWS - len(facts), total), jnp.float32))
        out_ref[count:, :] = jnp.zeros((FACT_ROWS, width), jnp.bfloat16)
        out_ref[count:, :total] = jnp.concatenate(facts, axis=0).astype(jnp.bfloat16)
        for copy in moves:
            copy.wait()

    shape = jax.ShapeDtypeStruct((count + FACT_ROWS, width), rows.dtype)
    return on_core(
        body, shape, [ANYWHERE, VMEM, SMEM, SMEM, VMEM], [pltpu.SemaphoreType.DMA((4,))]
    )(rows, gates, block_list, block_count, owner)


def partial_sums(plan, sizes, parts, weights, places, before=None, send=True, waits=()):
    width, columns = weights[0].shape
    blocks = [
        block if isinstance(block, tuple) else (block,) for part in parts for block in part
    ]
    sources = [array for block in blocks for array in block]
    operands = [plan] + sources + [weights[place] for place in places] + [weights[2]]
    if before is not None:
        operands.append(before)
    specs = [SMEM] + [VMEM] * (len(operands) - 1 + len(waits))
    has_before = before is not None

    def body(plan_ref, *refs):
        source_refs, refs = refs[: len(sources)], refs[len(sources) :]
        weight_refs, refs = refs[: len(places) + 1], refs[len(places) + 1 :]
        before_ref, refs = (refs[0], refs[1:]) if has_before else (None, refs)
        results = refs[len(waits) :]
        start, source = 0, 0
        for part, size in enumerate(sizes):
            span = slice(start, start + size)
            start += size
            rows = []
            for index in range(len(places)):
                block = blocks[part * len(places) + index]
                value = source_refs[source][:size, :]
                if len(block) > 1:
                    other = source_refs[source + 1][:size, :]
                    value = jnp.where(plan_ref[INNER_AT] == 1, value, other)
                source += len(block)
                rows.append(value)
            for side in range(2):
                at = slice(side * columns, (side + 1) * columns)
                total = before_ref[span, at] if has_before else None
                for index, place in enumerate(places):
                    if side == 0:
                        weight = weight_refs[index][...]
                    else:
                        weight = weight_refs[-1][place * width : (place + 1) * width, :]
                    product = jnp.dot(rows[index], weight, preferred_element_type=jnp.float32)
                    total = product if total is None else total + product
                results[0][span, at] = total
                if send:
                    results[1][span, at] = total.astype(jnp.bfloat16)
        results[-1][...] = jnp.zeros(TOKEN.shape, TOKEN.dtype)

    shapes = [jax.ShapeDtypeStruct((sum(sizes), 2 * columns), jnp.float32)]
    if send:
        shapes.append(jax.ShapeDtypeStruct((sum(sizes), 2 * columns), jnp.bfloat16))
    return on_core(body, shapes + [TOKEN], specs)(*operands, *waits)


def hidden_rows(sums, got):
    units = sums.shape[1] // 4
    hidden = []
    for core in range(2):
        here, there = 2 * core * units, 2 * (1 - core) * units
        gate = sums[:, here : here + units] + got[:, there : there + units].astype(jnp.float32)
        up = sums[:, here + units : here + 2 * units]
        up = up + got[:, there + units : there + 2 * units].astype(jnp.float32)
        hidden.append((gate / (1.0 + jnp.exp(-gate)) * up).astype(jnp.bfloat16))
    return jnp.concatenate(hidden, axis=1)


def hide(sums, got):
    def body(sums_ref, got_ref, out_ref, token_ref):
        out_ref[...] = hidden_rows(sums_ref, got_ref)
        token_ref[...] = jnp.zeros(TOKEN.shape, TOKEN.dtype)

    shape = jax.ShapeDtypeStruct((sums.shape[0], sums.shape[1] // 2), jnp.bfloat16)
    return on_core(body, [shape, TOKEN], [VMEM, VMEM])(sums, got)


def factors_of(slot, plan, facts, rows):
    values = facts[:, :rows].astype(jnp.float32)
    kind = lax.broadcasted_iota(jnp.int32, (FACT_ROWS, 1), 0)
    mine = kind == plan[OFFSETS_AT + slot]
    factor = jnp.sum(jnp.where(mine, values, 0.0), axis=0, keepdims=True)
    return factor, values[4:5, :] * 256.0 + values[5:6, :]


def chunk_rows(owned, index, plan, factor, owner, hidden):
    first = (plan[index] * owned).astype(jnp.float32)
    token = first + lax.broadcasted_iota(jnp.int32, (owned, 1), 0).astype(jnp.float32)
    placing = jnp.where(owner == token, factor, 0.0).astype(jnp.bfloat16)
    return jnp.dot(placing, hidden, preferred_element_type=jnp.float32).astype(jnp.bfloat16)


def facts_of(plan_ref, inner_ref, outer_ref, buffer, sem):
    last = inner_ref.shape[0] - FACT_ROWS

    def run(source):
        (copy,) = copies(source, last, buffer, FACT_ROWS, 1, sem, 0)
        copy.start()
        copy.wait()

    by_kind(plan_ref, (inner_ref, outer_ref), run)
    return buffer


def down(held, own_ref, lent_ref, sent_ref, kept_ref):
    units, width = own_ref.shape[0], kept_ref.shape[1]
    for out, at in ((kept_ref, slice(0, width)), (sent_ref, slice(width, 2 * width))):
        result = jnp.dot(held[:, :units], own_ref[:, at], preferred_element_type=jnp.float32)
        result += jnp.dot(held[:, units:], lent_ref[:, at], preferred_element_type=jnp.float32)
        out[...] = result.astype(out.dtype)


def finish(owned, plan, hidden, sums, got, facts, down_own, down_lent):
    rows, units = hidden[0].shape
    width = down_own.shape[1] // 2
    slots = len(facts)
    pair = [
        jax.ShapeDtypeStruct((owned, width), jnp.bfloat16),
        jax.ShapeDtypeStruct((owned, width), jnp.float32),
    ]

    def first(plan_ref, *refs):
        hidden_refs, refs = refs[:2], refs[2:]
        sums_refs, got_refs, refs = refs[:2], refs[2:4], refs[4:]
        fact_refs, refs = refs[: 2 * slots], refs[2 * slots :]
        own_ref, lent_ref, sent_ref, kept_ref, all_ref, by_row_ref, buffer, sem = refs
        for slot in range(slots):
            facts_of(plan_ref, *fact_refs[2 * slot : 2 * slot + 2], buffer, sem)
            factor, owner = factors_of(slot, plan_ref, buffer, rows)
            by_row_ref[0:1, slot * rows : (slot + 1) * rows] = factor
            by_row_ref[1:2, slot * rows : (slot + 1) * rows] = owner
        for slot in range(2):
            all_ref[slot * rows : (slot + 1) * rows, :] = hidden_refs[slot][...]
            made = hidden_rows(sums_refs[slot], got_refs[slot])
            all_ref[(slot + 2) * rows : (slot + 3) * rows, :] = made
        factor, owner = by_row_ref[0:1, :], by_row_ref[1:2, :]
        held = chunk_rows(owned, 0, plan_ref, factor, owner, all_ref[...])
        down(held, own_ref, lent_ref, sent_ref, kept_ref)

    def others(plan_ref, all_ref, by_row_ref, own_ref, lent_ref, *refs):
        factor, owner = by_row_ref[0:1, :], by_row_ref[1:2, :]
        for index in range(1, 4):
            held = chunk_rows(owned, index, plan_ref, factor, owner, all_ref[...])
            down(held, own_ref, lent_ref, refs[2 * index - 2], refs[2 * index - 1])

    all_shape = jax.ShapeDtypeStruct((slots * rows, units), jnp.bfloat16)
    by_row_shape = jax.ShapeDtypeStruct((2, slots * rows), jnp.float32)
    scratch = [
        pltpu.VMEM((FACT_ROWS, facts[0][0].shape[1]), jnp.bfloat16),
        pltpu.SemaphoreType.DMA((1,)),
    ]
    fact_blocks = [block for pair_of in facts for block in pair_of]
    specs = [SMEM] + [VMEM] * 6 + [ANYWHERE] * len(fact_blocks) + [VMEM] * 2
    sent, kept, every, by_row = on_core(
        first, pair + [all_shape, by_row_shape], specs, scratch
    )(plan, *hidden, *sums, *got, *fact_blocks, down_own, down_lent)
    rest = on_core(others, pair * 3, [SMEM] + [VMEM] * 4)(
        plan, every, by_row, down_own, down_lent
    )
    return [sent, *rest[0::2]], [kept, *rest[1::2]]


def rows_travel(
    tokens, gate_weight, up_weight, down_weight, route_gates, block_list, block_count, owner_token
):
    position = lax.axis_index("blk")
    share = lax.axis_index("tp")
    row_count, width = tokens.shape
    units = gate_weight.shape[2]
    owned = row_count // 2
    half = row_count // 2
    plan = jnp.asarray(PLAN, jnp.int32)[position]

    own_far = across_chips(tokens)
    own = with_facts(
        tokens, route_gates.T, jnp.transpose(block_list, (2, 0, 1)), block_count, owner_token
    )
    beside = along(own, BESIDE)
    middle = along(own, MIDDLE)

    gate_quarters = gate_weight[0].reshape(4, width, units)
    up_quarters = up_weight[0].reshape(4, width, units)

    def quarter(j):
        pair = [
            lax.dynamic_index_in_dim(q, share ^ j, 0, keepdims=False)
            for q in (gate_quarters, up_quarters)
        ]
        return jnp.concatenate(pair, axis=1)

    def down_part(j):
        return lax.dynamic_slice_in_dim(down_weight[0], (share ^ j) * width, width, 1)

    kept_down = jnp.concatenate([down_part(0), down_part(2)], axis=1)
    lend_down = jnp.concatenate([down_part(1), down_part(3)], axis=1)


    def at_kind(block, positions):
        pairs = [(4 * p + i, 4 * p + (i ^ 2)) for p in positions for i in range(4)]
        return lax.ppermute(block, ("blk", "tp"), pairs)

    inner_last = along(beside, MIDDLE)
    outer_next = along(middle, OUTWARD)
    beside_far = across_chips(beside)
    own_far_half = part_of(plan, own_far, own_far, half, half, flops=16 * 2**30)
    inward_far = along(own_far_half, INWARD)
    lend = jnp.concatenate([quarter(1), quarter(3)])
    lent = across_cores(after(lend, own))
    weights = [quarter(0), quarter(2), lent]
    whole = [row_count]
    sums_0, send_0, ready_0 = partial_sums(
        plan, whole, [(tokens, own_far)], weights, (0, 1), waits=[lend_down]
    )
    got_0 = across_cores(send_0)
    lent_down = across_cores(lend_down)

    outer_last = along(inner_last, OUTWARD)
    outer_next = after(outer_next, beside_far, inner_last, inward_far, ready_0)
    second = (middle, outer_next)
    second_far = (at_kind(middle, (1, 2)), at_kind(outer_next, (0, 3)))
    middle_far = along(inward_far, MIDDLE)
    sums_1, send_1, ready_1 = partial_sums(
        plan, whole, [(beside, beside_far)], weights, (0, 1)
    )
    got_1 = across_cores(send_1)

    last = (inner_last, outer_last)
    last_far_a = across_chips(
        part_of(plan, *last, 0, half, *second_far, middle_far, ready_0, ready_1)
    )
    outward_far = along(middle_far, OUTWARD)
    hidden_0, hidden_here = hide(sums_0, got_0)
    hidden_1, hidden_there = hide(sums_1, got_1)
    sums_2, send_2, _ = partial_sums(plan, whole, [(second, second_far)], weights, (0, 1))
    got_2 = across_cores(send_2)
    near, _ = partial_sums(plan, whole, [(last,)], weights, (0,), send=False)
    sums_3, send_3, _ = partial_sums(
        plan,
        [half, half],
        [(last_far_a,), ((middle_far, outward_far),)],
        weights,
        (1,),
        before=near,
        waits=[hidden_here, hidden_there],
    )
    got_3 = across_cores(send_3)
    sent, kept = finish(
        owned,
        plan,
        (hidden_0, hidden_1),
        (sums_2, sums_3),
        (got_2, got_3),
        [(own, own), (beside, beside), second, last],
        kept_down,
        lent_down,
    )

    joined = [k + across_chips(s).astype(jnp.float32) for s, k in zip(sent, kept)]
    first, second, third = [block.astype(jnp.bfloat16) for block in joined[:3]]
    second = lax.optimization_barrier(second)
    inward = along(first, INWARD)
    middle = along(first, MIDDLE)
    two_in = along(second, TWO_IN)
    passed = second.astype(jnp.float32) + inward.astype(jnp.float32)
    two_out = along(passed.astype(jnp.bfloat16), TWO_OUT)
    beside = along(third, BESIDE)
    arrived = [block.astype(jnp.float32) for block in (middle, two_in, two_out)]
    total = lax.optimization_barrier(joined[3] + sum(arrived))
    return (total + beside.astype(jnp.float32)).astype(jnp.bfloat16)


def on_device(*args):
    block_list = args[5]
    sizes = (lax.axis_size("blk"), lax.axis_size("tp"), block_list.shape[1])
    if sizes == (4, 4, 4):
        return rows_travel(*args)
    return weights_travel(*args)


def solution(mesh):
    return jax.shard_map(
        on_device,
        mesh=mesh,
        in_specs=(
            P(("groups", "blk"), "tp"),
            P("blk", None, "tp"),
            P("blk", None, "tp"),
            P("blk", "tp", None),
            P(("groups", "blk"), None),
            P(("groups", "blk"), None, None),
            P(("groups", "blk"), None),
            P(("groups", "blk")),
        ),
        out_specs=P(("groups", "blk"), "tp"),
        check_vma=False,
    )
```

```python
import jax
import jax.numpy as jnp
from jax import lax
from jax.experimental import pallas as pl
from jax.experimental.pallas import tpu as pltpu
from jax.sharding import PartitionSpec as P


def shifted(block, axis, distance):
    devices = range(lax.axis_size(axis))
    route = [((i - distance) % len(devices), i) for i in devices]
    return lax.ppermute(block, axis, route)


def weights_travel(
    tokens, gate_weight, up_weight, down_weight, route_gates, block_list, block_count, owner_token
):
    whole_rows = lax.all_gather(tokens, "tp", axis=1, tiled=True)
    row_count = whole_rows.shape[0]
    width = whole_rows.shape[1]
    offsets_all = block_list.shape[1]
    block_total = block_list.shape[2]
    block_size = row_count // block_total
    blocks = whole_rows.reshape(block_total, block_size, width)
    gate_blocks = route_gates.reshape(block_total, block_size, offsets_all)
    totals = jnp.zeros((block_total, block_size, width), jnp.float32)

    def apply(totals, weights, offset, block_id):
        w_gate, w_up, w_down = weights
        block_rows = lax.dynamic_index_in_dim(blocks, block_id, 0, keepdims=False)
        gate_out = jnp.dot(block_rows, w_gate, preferred_element_type=jnp.float32)
        up_out = jnp.dot(block_rows, w_up, preferred_element_type=jnp.float32)
        hidden = (jax.nn.silu(gate_out) * up_out).astype(jnp.bfloat16)
        block_gates = lax.dynamic_index_in_dim(gate_blocks, block_id, 0, keepdims=False)
        factor = lax.dynamic_index_in_dim(block_gates, offset, 1, keepdims=False)
        product = jnp.dot(hidden, w_down, preferred_element_type=jnp.float32) * factor[:, None]
        before = lax.dynamic_index_in_dim(totals, block_id, 0, keepdims=False)
        return lax.dynamic_update_index_in_dim(totals, before + product, block_id, 0)

    resident = (gate_weight[0], up_weight[0], down_weight[0])
    arrived = [resident]
    holding = resident
    for offset in range(1, offsets_all):
        holding = shifted((holding[0], holding[1], holding[2]), "blk", 1)
        arrived.append(holding)
    for offset in range(offsets_all):
        weights = arrived[offset]

        def visit_block(position, totals, weights=weights, offset=offset):
            return apply(totals, weights, offset, block_list[0, offset, position])

        totals = lax.fori_loop(0, block_count[0, offset], visit_block, totals)
    summed = lax.psum_scatter(
        totals.reshape(row_count, width).astype(jnp.bfloat16), "tp", scatter_dimension=1, tiled=True
    )
    feature_share = summed.shape[1]
    cycle_size = lax.axis_size("blk")
    owned = row_count // 2
    capacity = max(2, 2 * row_count // cycle_size)
    target = owner_token // owned
    local_token = owner_token % owned
    target_table = (target[:, None] == jnp.arange(cycle_size, dtype=jnp.int32)[None, :]).astype(
        jnp.int32
    )
    running = jnp.cumsum(target_table, axis=0)
    rank = jnp.sum((running - 1) * target_table, axis=1)
    slot = target * capacity + rank
    send_rows = jnp.zeros((cycle_size * capacity, feature_share), jnp.bfloat16).at[slot].set(summed)
    send_index = jnp.full((cycle_size * capacity,), -1, jnp.int32).at[slot].set(local_token)
    send_rows = send_rows.reshape(cycle_size, capacity, feature_share)
    send_index = send_index.reshape(cycle_size, capacity)
    got_rows, got_index = (
        lax.all_to_all(send_rows, "blk", split_axis=0, concat_axis=0, tiled=True),
        lax.all_to_all(send_index, "blk", split_axis=0, concat_axis=0, tiled=True),
    )
    got_rows = got_rows.reshape(cycle_size * capacity, feature_share)
    got_index = got_index.reshape(cycle_size * capacity)
    placing = (got_index[:, None] == jnp.arange(owned, dtype=jnp.int32)[None, :]).astype(
        jnp.bfloat16
    )
    combined = lax.dot_general(
        placing, got_rows, (((0,), (0,)), ((), ())), preferred_element_type=jnp.float32
    )
    return combined.astype(jnp.bfloat16)


BESIDE = [(0, 1), (1, 0), (2, 3), (3, 2)]
MIDDLE = [(1, 2), (2, 1)]
INWARD = [(0, 1), (3, 2)]
OUTWARD = [(1, 0), (2, 3)]
TWO_IN = [(0, 2), (3, 1)]
TWO_OUT = [(1, 3), (2, 0)]
PLAN = [
    [3, 2, 1, 0, 0, 1, 2, 3, 0],
    [2, 3, 0, 1, 0, 3, 1, 2, 1],
    [1, 0, 3, 2, 0, 1, 3, 2, 1],
    [0, 1, 2, 3, 0, 3, 2, 1, 0],
]
OFFSETS_AT, INNER_AT = 4, 8
FACT_ROWS = 16
VMEM = pl.BlockSpec(memory_space=pltpu.VMEM)
SMEM = pl.BlockSpec(memory_space=pltpu.SMEM)
ANYWHERE = pl.BlockSpec(memory_space=pl.ANY)


def across_chips(block):
    return lax.ppermute(block, "tp", [(i, i ^ 2) for i in range(4)])


def across_cores(block):
    return lax.ppermute(block, "tp", [(i, i ^ 1) for i in range(4)])


def along(block, route):
    return lax.ppermute(block, "blk", route)


def cheap():
    return pl.CostEstimate(flops=1024, bytes_accessed=1024, transcendentals=0)


TOKEN = jax.ShapeDtypeStruct((8, 128), jnp.float32)
VMEM_LIMIT = 18 * 2**20


def on_core(body, out_shape, in_specs, scratch=()):
    return pl.pallas_call(
        body,
        out_shape=out_shape,
        in_specs=in_specs,
        out_specs=jax.tree.map(lambda _: VMEM, out_shape),
        scratch_shapes=scratch,
        compiler_params=pltpu.CompilerParams(vmem_limit_bytes=VMEM_LIMIT),
        cost_estimate=cheap(),
    )


def copies(source, start, target, size, pieces, sems, first):
    step = size // pieces
    return [
        pltpu.make_async_copy(
            source.at[pl.ds(start + index * step, step)],
            target.at[pl.ds(index * step, step)],
            sems.at[first + index],
        )
        for index in range(pieces)
    ]


def after(block, *others, flops=1024):
    return pl.pallas_call(
        lambda *refs: None,
        out_shape=jax.ShapeDtypeStruct(block.shape, block.dtype),
        in_specs=[ANYWHERE] * (1 + len(others)),
        out_specs=ANYWHERE,
        input_output_aliases={0: 0},
        cost_estimate=pl.CostEstimate(flops=flops, bytes_accessed=1024, transcendentals=0),
    )(block, *others)


def by_kind(plan_ref, kinds, run):
    if kinds[0] is kinds[1]:
        run(kinds[0])
        return
    for kind, value in zip(kinds, (1, 0)):

        @pl.when(plan_ref[INNER_AT] == value)
        def _(kind=kind):
            run(kind)


def part_of(plan, if_inner, if_outer, start, size, *others, flops=1024):
    shape = jax.ShapeDtypeStruct((size, if_inner.shape[1]), if_inner.dtype)
    pieces = 4

    def body(plan_ref, inner_ref, outer_ref, *rest):
        out_ref, buffer, in_sems, out_sems = rest[len(others) :]

        def run(source):
            inward = copies(source, start, buffer, size, pieces, in_sems, 0)
            outward = copies(buffer, 0, out_ref, size, pieces, out_sems, 0)
            for copy in inward:
                copy.start()
            for copy, next_copy in zip(inward, outward):
                copy.wait()
                next_copy.start()
            for copy in outward:
                copy.wait()

        by_kind(plan_ref, (inner_ref, inner_ref if if_outer is if_inner else outer_ref), run)

    return pl.pallas_call(
        body,
        out_shape=shape,
        in_specs=[SMEM] + [ANYWHERE] * (2 + len(others)),
        out_specs=ANYWHERE,
        scratch_shapes=[pltpu.VMEM(shape.shape, shape.dtype)]
        + [pltpu.SemaphoreType.DMA((pieces,))] * 2,
        compiler_params=pltpu.CompilerParams(vmem_limit_bytes=VMEM_LIMIT),
        cost_estimate=pl.CostEstimate(flops=flops, bytes_accessed=1024, transcendentals=0),
    )(plan, if_inner, if_outer, *others)


def with_facts(rows, gates, block_list, block_count, owner):
    count, width = rows.shape
    blocks, _, offsets = block_list.shape
    total = owner.shape[0]

    def body(rows_ref, gates_ref, list_ref, count_ref, owner_ref, out_ref, sems):
        moves = copies(rows_ref, 0, out_ref, count, 4, sems, 0)
        for copy in moves:
            copy.start()
        block_of = lax.broadcasted_iota(jnp.int32, (1, total), 1) // (total // blocks)
        facts = []
        for offset in range(offsets):
            mask = jnp.zeros((1, total), jnp.float32)
            for block in range(blocks):
                used = jnp.int32(0)
                for place in range(blocks):
                    found = (list_ref[place, 0, offset] == block) & (place < count_ref[0, offset])
                    used = used | found.astype(jnp.int32)
                mask = mask + jnp.where(block_of == block, used.astype(jnp.float32), 0.0)
            facts.append(gates_ref[offset : offset + 1, :] * mask)
        numbers = owner_ref[...].reshape(1, total)
        facts.append((numbers >> 8).astype(jnp.float32))
        facts.append((numbers & 255).astype(jnp.float32))
        facts.append(jnp.zeros((FACT_ROWS - len(facts), total), jnp.float32))
        out_ref[count:, :] = jnp.zeros((FACT_ROWS, width), jnp.bfloat16)
        out_ref[count:, :total] = jnp.concatenate(facts, axis=0).astype(jnp.bfloat16)
        for copy in moves:
            copy.wait()

    shape = jax.ShapeDtypeStruct((count + FACT_ROWS, width), rows.dtype)
    return on_core(
        body, shape, [ANYWHERE, VMEM, SMEM, SMEM, VMEM], [pltpu.SemaphoreType.DMA((4,))]
    )(rows, gates, block_list, block_count, owner)


def partial_sums(plan, sizes, parts, weights, places, before=None, send=True, waits=()):
    width, columns = weights[0].shape
    blocks = [
        block if isinstance(block, tuple) else (block,) for part in parts for block in part
    ]
    sources = [array for block in blocks for array in block]
    operands = [plan] + sources + [weights[place] for place in places] + [weights[2]]
    if before is not None:
        operands.append(before)
    specs = [SMEM] + [VMEM] * (len(operands) - 1 + len(waits))
    has_before = before is not None

    def body(plan_ref, *refs):
        source_refs, refs = refs[: len(sources)], refs[len(sources) :]
        weight_refs, refs = refs[: len(places) + 1], refs[len(places) + 1 :]
        before_ref, refs = (refs[0], refs[1:]) if has_before else (None, refs)
        results = refs[len(waits) :]
        start, source = 0, 0
        for part, size in enumerate(sizes):
            span = slice(start, start + size)
            start += size
            rows = []
            for index in range(len(places)):
                block = blocks[part * len(places) + index]
                value = source_refs[source][:size, :]
                if len(block) > 1:
                    other = source_refs[source + 1][:size, :]
                    value = jnp.where(plan_ref[INNER_AT] == 1, value, other)
                source += len(block)
                rows.append(value)
            for side in range(2):
                at = slice(side * columns, (side + 1) * columns)
                total = before_ref[span, at] if has_before else None
                for index, place in enumerate(places):
                    if side == 0:
                        weight = weight_refs[index][...]
                    else:
                        weight = weight_refs[-1][place * width : (place + 1) * width, :]
                    product = jnp.dot(rows[index], weight, preferred_element_type=jnp.float32)
                    total = product if total is None else total + product
                results[0][span, at] = total
                if send:
                    results[1][span, at] = total.astype(jnp.bfloat16)
        results[-1][...] = jnp.zeros(TOKEN.shape, TOKEN.dtype)

    shapes = [jax.ShapeDtypeStruct((sum(sizes), 2 * columns), jnp.float32)]
    if send:
        shapes.append(jax.ShapeDtypeStruct((sum(sizes), 2 * columns), jnp.bfloat16))
    return on_core(body, shapes + [TOKEN], specs)(*operands, *waits)


def hidden_rows(sums, got):
    units = sums.shape[1] // 4
    hidden = []
    for core in range(2):
        here, there = 2 * core * units, 2 * (1 - core) * units
        gate = sums[:, here : here + units] + got[:, there : there + units].astype(jnp.float32)
        up = sums[:, here + units : here + 2 * units]
        up = up + got[:, there + units : there + 2 * units].astype(jnp.float32)
        hidden.append((gate / (1.0 + jnp.exp(-gate)) * up).astype(jnp.bfloat16))
    return jnp.concatenate(hidden, axis=1)


def hide(sums, got):
    def body(sums_ref, got_ref, out_ref, token_ref):
        out_ref[...] = hidden_rows(sums_ref, got_ref)
        token_ref[...] = jnp.zeros(TOKEN.shape, TOKEN.dtype)

    shape = jax.ShapeDtypeStruct((sums.shape[0], sums.shape[1] // 2), jnp.bfloat16)
    return on_core(body, [shape, TOKEN], [VMEM, VMEM])(sums, got)


def factors_of(slot, plan, facts, rows):
    values = facts[:, :rows].astype(jnp.float32)
    kind = lax.broadcasted_iota(jnp.int32, (FACT_ROWS, 1), 0)
    mine = kind == plan[OFFSETS_AT + slot]
    factor = jnp.sum(jnp.where(mine, values, 0.0), axis=0, keepdims=True)
    return factor, values[4:5, :] * 256.0 + values[5:6, :]


def chunk_rows(owned, index, plan, factor, owner, hidden):
    first = (plan[index] * owned).astype(jnp.float32)
    token = first + lax.broadcasted_iota(jnp.int32, (owned, 1), 0).astype(jnp.float32)
    placing = jnp.where(owner == token, factor, 0.0).astype(jnp.bfloat16)
    return jnp.dot(placing, hidden, preferred_element_type=jnp.float32)


def facts_of(plan_ref, inner_ref, outer_ref, buffer, sem):
    last = inner_ref.shape[0] - FACT_ROWS

    def run(source):
        (copy,) = copies(source, last, buffer, FACT_ROWS, 1, sem, 0)
        copy.start()
        copy.wait()

    by_kind(plan_ref, (inner_ref, outer_ref), run)
    return buffer


def down(held, own_ref, lent_ref, sent_ref, kept_ref):
    units, width = own_ref.shape[0], kept_ref.shape[1]
    for out, at in ((kept_ref, slice(0, width)), (sent_ref, slice(width, 2 * width))):
        result = jnp.dot(held[:, :units], own_ref[:, at], preferred_element_type=jnp.float32)
        result += jnp.dot(held[:, units:], lent_ref[:, at], preferred_element_type=jnp.float32)
        out[...] = result.astype(out.dtype)


def fact_scratch(width):
    return [pltpu.VMEM((FACT_ROWS, width), jnp.bfloat16), pltpu.SemaphoreType.DMA((1,))]


def collect(owned, plan, hidden, sums, got, facts):
    rows, units = hidden[0].shape
    slots = len(facts)

    def body(plan_ref, *refs):
        hidden_refs, refs = refs[: slots - 1], refs[slots - 1 :]
        sums_ref, got_ref, refs = refs[0], refs[1], refs[2:]
        fact_refs, (out_ref, buffer, sem) = refs[: 2 * slots], refs[2 * slots :]
        factors = []
        for slot in range(slots):
            facts_of(plan_ref, *fact_refs[2 * slot : 2 * slot + 2], buffer, sem)
            factors.append(factors_of(slot, plan_ref, buffer, rows))
        factor = jnp.concatenate([pair[0] for pair in factors], axis=1)
        owner = jnp.concatenate([pair[1] for pair in factors], axis=1)
        every = [ref[...] for ref in hidden_refs] + [hidden_rows(sums_ref, got_ref)]
        every = jnp.concatenate(every, axis=0)
        for index in range(4):
            span = slice(index * owned, (index + 1) * owned)
            out_ref[span, :] = chunk_rows(owned, index, plan_ref, factor, owner, every)

    fact_blocks = [block for pair_of in facts for block in pair_of]
    specs = [SMEM] + [VMEM] * (slots + 1) + [ANYWHERE] * len(fact_blocks)
    shape = jax.ShapeDtypeStruct((4 * owned, units), jnp.float32)
    return on_core(body, shape, specs, fact_scratch(facts[0][0].shape[1]))(
        plan, *hidden, sums, got, *fact_blocks
    )


def finish(owned, slot, plan, sums, got, facts, before, down_own, down_lent):
    units = down_own.shape[0]
    width = down_own.shape[1] // 2
    pair = [
        jax.ShapeDtypeStruct((owned, width), jnp.bfloat16),
        jax.ShapeDtypeStruct((owned, width), jnp.float32),
    ]

    def first(plan_ref, sums_ref, got_ref, inner_ref, outer_ref, before_ref, *refs):
        own_ref, lent_ref, sent_ref, kept_ref, held_ref, buffer, sem = refs
        facts_of(plan_ref, inner_ref, outer_ref, buffer, sem)
        factor, owner = factors_of(slot, plan_ref, buffer, sums_ref.shape[0])
        hidden = hidden_rows(sums_ref, got_ref)
        for index in range(4):
            rows = chunk_rows(owned, index, plan_ref, factor, owner, hidden)
            rows = rows + before_ref[index * owned : (index + 1) * owned, :]
            held = rows.astype(jnp.bfloat16)
            if index == 0:
                down(held, own_ref, lent_ref, sent_ref, kept_ref)
            else:
                held_ref[(index - 1) * owned : index * owned, :] = held

    def others(indices, *waits):
        def body(held_ref, own_ref, lent_ref, *refs):
            out_refs = refs[len(waits) :]
            for place, index in enumerate(indices):
                held = held_ref[(index - 1) * owned : index * owned, :]
                down(held, own_ref, lent_ref, out_refs[2 * place], out_refs[2 * place + 1])

        operands = [held, down_own, down_lent, *waits]
        return on_core(body, pair * len(indices), [VMEM] * len(operands))(*operands)

    held_shape = jax.ShapeDtypeStruct((3 * owned, 2 * units), jnp.bfloat16)
    specs = [SMEM, VMEM, VMEM, ANYWHERE, ANYWHERE] + [VMEM] * 3
    sent, kept, held = on_core(
        first, pair + [held_shape], specs, fact_scratch(facts[0].shape[1])
    )(plan, sums, got, *facts, before, down_own, down_lent)
    rest = others([1, 2])
    chunks = [(sent, kept), (rest[0], rest[1]), (rest[2], rest[3])]
    return chunks, lambda *waits: others([3], *waits)


def rows_travel(
    tokens, gate_weight, up_weight, down_weight, route_gates, block_list, block_count, owner_token
):
    position = lax.axis_index("blk")
    share = lax.axis_index("tp")
    row_count, width = tokens.shape
    units = gate_weight.shape[2]
    owned = row_count // 2
    half = row_count // 2
    plan = jnp.asarray(PLAN, jnp.int32)[position]

    own_far = across_chips(tokens)
    own = with_facts(
        tokens, route_gates.T, jnp.transpose(block_list, (2, 0, 1)), block_count, owner_token
    )
    beside = along(own, BESIDE)
    middle = along(own, MIDDLE)

    gate_quarters = gate_weight[0].reshape(4, width, units)
    up_quarters = up_weight[0].reshape(4, width, units)

    def quarter(j):
        pair = [
            lax.dynamic_index_in_dim(q, share ^ j, 0, keepdims=False)
            for q in (gate_quarters, up_quarters)
        ]
        return jnp.concatenate(pair, axis=1)

    def down_part(j):
        return lax.dynamic_slice_in_dim(down_weight[0], (share ^ j) * width, width, 1)

    kept_down = jnp.concatenate([down_part(0), down_part(2)], axis=1)
    lend_down = jnp.concatenate([down_part(1), down_part(3)], axis=1)


    def at_kind(block, positions):
        pairs = [(4 * p + i, 4 * p + (i ^ 2)) for p in positions for i in range(4)]
        return lax.ppermute(block, ("blk", "tp"), pairs)

    inner_last = along(beside, MIDDLE)
    outer_next = along(middle, OUTWARD)
    beside_far = across_chips(beside)
    own_far_half = part_of(plan, own_far, own_far, half, half, flops=16 * 2**30)
    inward_far = along(own_far_half, INWARD)
    lend = jnp.concatenate([quarter(1), quarter(3)])
    lent = across_cores(after(lend, own))
    weights = [quarter(0), quarter(2), lent]
    whole = [row_count]
    sums_0, send_0, ready_0 = partial_sums(
        plan, whole, [(tokens, own_far)], weights, (0, 1), waits=[lend_down]
    )
    got_0 = across_cores(send_0)
    lent_down = across_cores(lend_down)

    outer_last = along(inner_last, OUTWARD)
    outer_next = after(outer_next, beside_far, inner_last, inward_far, ready_0)
    second = (middle, outer_next)
    second_far = (at_kind(middle, (1, 2)), at_kind(outer_next, (0, 3)))
    middle_far = along(inward_far, MIDDLE)
    sums_1, send_1, ready_1 = partial_sums(
        plan, whole, [(beside, beside_far)], weights, (0, 1)
    )
    got_1 = across_cores(send_1)

    last = (inner_last, outer_last)
    last_far_a = across_chips(
        part_of(plan, *last, 0, half, *second_far, middle_far, ready_0, ready_1)
    )
    outward_far = along(middle_far, OUTWARD)
    hidden_0, hidden_here = hide(sums_0, got_0)
    hidden_1, hidden_there = hide(sums_1, got_1)
    sums_2, send_2, _ = partial_sums(plan, whole, [(second, second_far)], weights, (0, 1))
    got_2 = across_cores(send_2)
    near, _ = partial_sums(plan, whole, [(last,)], weights, (0,), send=False)
    sums_3, send_3, _ = partial_sums(
        plan,
        [half, half],
        [(last_far_a,), ((middle_far, outward_far),)],
        weights,
        (1,),
        before=near,
        waits=[hidden_here, hidden_there],
    )
    got_3 = across_cores(send_3)
    total = collect(
        owned,
        plan,
        (hidden_0, hidden_1),
        sums_2,
        got_2,
        [(own, own), (beside, beside), second],
    )
    chunks, last_chunk = finish(
        owned, 3, plan, sums_3, got_3, last, total, kept_down, lent_down
    )

    def joined(sent, kept):
        return kept + across_chips(sent).astype(jnp.float32)

    first, second, third = [joined(*chunk).astype(jnp.bfloat16) for chunk in chunks]
    second = lax.optimization_barrier(second)
    inward = along(first, INWARD)
    middle = along(first, MIDDLE)
    two_in = along(second, TWO_IN)
    passed = second.astype(jnp.float32) + inward.astype(jnp.float32)
    two_out = along(passed.astype(jnp.bfloat16), TWO_OUT)
    beside = along(third, BESIDE)
    arrived = [block.astype(jnp.float32) for block in (middle, two_in, two_out)]
    total = lax.optimization_barrier(joined(*last_chunk(second)) + sum(arrived))
    return (total + beside.astype(jnp.float32)).astype(jnp.bfloat16)


def on_device(*args):
    block_list = args[5]
    sizes = (lax.axis_size("blk"), lax.axis_size("tp"), block_list.shape[1])
    if sizes == (4, 4, 4):
        return rows_travel(*args)
    return weights_travel(*args)


def solution(mesh):
    return jax.shard_map(
        on_device,
        mesh=mesh,
        in_specs=(
            P(("groups", "blk"), "tp"),
            P("blk", None, "tp"),
            P("blk", None, "tp"),
            P("blk", "tp", None),
            P(("groups", "blk"), None),
            P(("groups", "blk"), None, None),
            P(("groups", "blk"), None),
            P(("groups", "blk")),
        ),
        out_specs=P(("groups", "blk"), "tp"),
        check_vma=False,
    )
```

```python
import jax
import jax.numpy as jnp
from jax import lax
from jax.experimental import pallas as pl
from jax.experimental.pallas import tpu as pltpu
from jax.sharding import PartitionSpec as P


def shifted(block, axis, distance):
    devices = range(lax.axis_size(axis))
    route = [((i - distance) % len(devices), i) for i in devices]
    return lax.ppermute(block, axis, route)


def weights_travel(
    tokens, gate_weight, up_weight, down_weight, route_gates, block_list, block_count, owner_token
):
    whole_rows = lax.all_gather(tokens, "tp", axis=1, tiled=True)
    row_count = whole_rows.shape[0]
    width = whole_rows.shape[1]
    offsets_all = block_list.shape[1]
    block_total = block_list.shape[2]
    block_size = row_count // block_total
    blocks = whole_rows.reshape(block_total, block_size, width)
    gate_blocks = route_gates.reshape(block_total, block_size, offsets_all)
    totals = jnp.zeros((block_total, block_size, width), jnp.float32)

    def apply(totals, weights, offset, block_id):
        w_gate, w_up, w_down = weights
        block_rows = lax.dynamic_index_in_dim(blocks, block_id, 0, keepdims=False)
        gate_out = jnp.dot(block_rows, w_gate, preferred_element_type=jnp.float32)
        up_out = jnp.dot(block_rows, w_up, preferred_element_type=jnp.float32)
        hidden = (jax.nn.silu(gate_out) * up_out).astype(jnp.bfloat16)
        block_gates = lax.dynamic_index_in_dim(gate_blocks, block_id, 0, keepdims=False)
        factor = lax.dynamic_index_in_dim(block_gates, offset, 1, keepdims=False)
        product = jnp.dot(hidden, w_down, preferred_element_type=jnp.float32) * factor[:, None]
        before = lax.dynamic_index_in_dim(totals, block_id, 0, keepdims=False)
        return lax.dynamic_update_index_in_dim(totals, before + product, block_id, 0)

    resident = (gate_weight[0], up_weight[0], down_weight[0])
    arrived = [resident]
    holding = resident
    for offset in range(1, offsets_all):
        holding = shifted((holding[0], holding[1], holding[2]), "blk", 1)
        arrived.append(holding)
    for offset in range(offsets_all):
        weights = arrived[offset]

        def visit_block(position, totals, weights=weights, offset=offset):
            return apply(totals, weights, offset, block_list[0, offset, position])

        totals = lax.fori_loop(0, block_count[0, offset], visit_block, totals)
    summed = lax.psum_scatter(
        totals.reshape(row_count, width).astype(jnp.bfloat16), "tp", scatter_dimension=1, tiled=True
    )
    feature_share = summed.shape[1]
    cycle_size = lax.axis_size("blk")
    owned = row_count // 2
    capacity = max(2, 2 * row_count // cycle_size)
    target = owner_token // owned
    local_token = owner_token % owned
    target_table = (target[:, None] == jnp.arange(cycle_size, dtype=jnp.int32)[None, :]).astype(
        jnp.int32
    )
    running = jnp.cumsum(target_table, axis=0)
    rank = jnp.sum((running - 1) * target_table, axis=1)
    slot = target * capacity + rank
    send_rows = jnp.zeros((cycle_size * capacity, feature_share), jnp.bfloat16).at[slot].set(summed)
    send_index = jnp.full((cycle_size * capacity,), -1, jnp.int32).at[slot].set(local_token)
    send_rows = send_rows.reshape(cycle_size, capacity, feature_share)
    send_index = send_index.reshape(cycle_size, capacity)
    got_rows, got_index = (
        lax.all_to_all(send_rows, "blk", split_axis=0, concat_axis=0, tiled=True),
        lax.all_to_all(send_index, "blk", split_axis=0, concat_axis=0, tiled=True),
    )
    got_rows = got_rows.reshape(cycle_size * capacity, feature_share)
    got_index = got_index.reshape(cycle_size * capacity)
    placing = (got_index[:, None] == jnp.arange(owned, dtype=jnp.int32)[None, :]).astype(
        jnp.bfloat16
    )
    combined = lax.dot_general(
        placing, got_rows, (((0,), (0,)), ((), ())), preferred_element_type=jnp.float32
    )
    return combined.astype(jnp.bfloat16)


BESIDE = [(0, 1), (1, 0), (2, 3), (3, 2)]
MIDDLE = [(1, 2), (2, 1)]
INWARD = [(0, 1), (3, 2)]
OUTWARD = [(1, 0), (2, 3)]
TWO_IN = [(0, 2), (3, 1)]
TWO_OUT = [(1, 3), (2, 0)]
PLAN = [
    [3, 2, 1, 0, 0, 1, 2, 3, 0],
    [2, 3, 0, 1, 0, 3, 1, 2, 1],
    [1, 0, 3, 2, 0, 1, 3, 2, 1],
    [0, 1, 2, 3, 0, 3, 2, 1, 0],
]
OFFSETS_AT, INNER_AT = 4, 8
FACT_ROWS = 16
VMEM = pl.BlockSpec(memory_space=pltpu.VMEM)
SMEM = pl.BlockSpec(memory_space=pltpu.SMEM)
ANYWHERE = pl.BlockSpec(memory_space=pl.ANY)


def across_chips(block):
    return lax.ppermute(block, "tp", [(i, i ^ 2) for i in range(4)])


def across_cores(block):
    return lax.ppermute(block, "tp", [(i, i ^ 1) for i in range(4)])


def along(block, route):
    return lax.ppermute(block, "blk", route)


def cheap():
    return pl.CostEstimate(flops=1024, bytes_accessed=1024, transcendentals=0)


TOKEN = jax.ShapeDtypeStruct((8, 128), jnp.float32)
VMEM_LIMIT = 18 * 2**20


def on_core(body, out_shape, in_specs, scratch=()):
    return pl.pallas_call(
        body,
        out_shape=out_shape,
        in_specs=in_specs,
        out_specs=jax.tree.map(lambda _: VMEM, out_shape),
        scratch_shapes=scratch,
        compiler_params=pltpu.CompilerParams(vmem_limit_bytes=VMEM_LIMIT),
        cost_estimate=cheap(),
    )


def copies(source, start, target, size, pieces, sems, first):
    step = size // pieces
    return [
        pltpu.make_async_copy(
            source.at[pl.ds(start + index * step, step)],
            target.at[pl.ds(index * step, step)],
            sems.at[first + index],
        )
        for index in range(pieces)
    ]


def waits_of(block, others):
    return [VMEM if other.shape[0] < block.shape[0] else ANYWHERE for other in others]


def after(block, *others, flops=1024):
    return pl.pallas_call(
        lambda *refs: None,
        out_shape=jax.ShapeDtypeStruct(block.shape, block.dtype),
        in_specs=[ANYWHERE] + waits_of(block, others),
        out_specs=ANYWHERE,
        input_output_aliases={0: 0},
        cost_estimate=pl.CostEstimate(flops=flops, bytes_accessed=1024, transcendentals=0),
    )(block, *others)


def by_kind(plan_ref, kinds, run):
    if kinds[0] is kinds[1]:
        run(kinds[0])
        return
    for kind, value in zip(kinds, (1, 0)):

        @pl.when(plan_ref[INNER_AT] == value)
        def _(kind=kind):
            run(kind)


def part_of(plan, if_inner, if_outer, start, size, *others, flops=1024):
    shape = jax.ShapeDtypeStruct((size, if_inner.shape[1]), if_inner.dtype)
    pieces = 4

    def body(plan_ref, inner_ref, outer_ref, *rest):
        out_ref, buffer, in_sems, out_sems = rest[len(others) :]

        def run(source):
            inward = copies(source, start, buffer, size, pieces, in_sems, 0)
            outward = copies(buffer, 0, out_ref, size, pieces, out_sems, 0)
            for copy in inward:
                copy.start()
            for copy, next_copy in zip(inward, outward):
                copy.wait()
                next_copy.start()
            for copy in outward:
                copy.wait()

        by_kind(plan_ref, (inner_ref, inner_ref if if_outer is if_inner else outer_ref), run)

    return pl.pallas_call(
        body,
        out_shape=shape,
        in_specs=[SMEM] + [ANYWHERE] * 2 + waits_of(if_inner, others),
        out_specs=ANYWHERE,
        scratch_shapes=[pltpu.VMEM(shape.shape, shape.dtype)]
        + [pltpu.SemaphoreType.DMA((pieces,))] * 2,
        compiler_params=pltpu.CompilerParams(vmem_limit_bytes=VMEM_LIMIT),
        cost_estimate=pl.CostEstimate(flops=flops, bytes_accessed=1024, transcendentals=0),
    )(plan, if_inner, if_outer, *others)


def with_facts(rows, gates, block_list, block_count, owner):
    count, width = rows.shape
    blocks, _, offsets = block_list.shape
    total = owner.shape[0]

    def body(rows_ref, gates_ref, list_ref, count_ref, owner_ref, out_ref, sems):
        moves = copies(rows_ref, 0, out_ref, count, 4, sems, 0)
        for copy in moves:
            copy.start()
        block_of = lax.broadcasted_iota(jnp.int32, (1, total), 1) // (total // blocks)
        facts = []
        for offset in range(offsets):
            mask = jnp.zeros((1, total), jnp.float32)
            for block in range(blocks):
                used = jnp.int32(0)
                for place in range(blocks):
                    found = (list_ref[place, 0, offset] == block) & (place < count_ref[0, offset])
                    used = used | found.astype(jnp.int32)
                mask = mask + jnp.where(block_of == block, used.astype(jnp.float32), 0.0)
            facts.append(gates_ref[offset : offset + 1, :] * mask)
        numbers = owner_ref[...].reshape(1, total)
        facts.append((numbers >> 8).astype(jnp.float32))
        facts.append((numbers & 255).astype(jnp.float32))
        facts.append(jnp.zeros((FACT_ROWS - len(facts), total), jnp.float32))
        out_ref[count:, :] = jnp.zeros((FACT_ROWS, width), jnp.bfloat16)
        out_ref[count:, :total] = jnp.concatenate(facts, axis=0).astype(jnp.bfloat16)
        for copy in moves:
            copy.wait()

    shape = jax.ShapeDtypeStruct((count + FACT_ROWS, width), rows.dtype)
    return on_core(
        body, shape, [ANYWHERE, VMEM, SMEM, SMEM, VMEM], [pltpu.SemaphoreType.DMA((4,))]
    )(rows, gates, block_list, block_count, owner)


def partial_sums(plan, sizes, parts, weights, places, before=None, send=True, waits=()):
    width, columns = weights[0].shape
    blocks = [
        block if isinstance(block, tuple) else (block,) for part in parts for block in part
    ]
    sources = [array for block in blocks for array in block]
    operands = [plan] + sources + [weights[place] for place in places] + [weights[2]]
    if before is not None:
        operands.append(before)
    specs = [SMEM] + [VMEM] * (len(operands) - 1 + len(waits))
    has_before = before is not None

    def body(plan_ref, *refs):
        source_refs, refs = refs[: len(sources)], refs[len(sources) :]
        weight_refs, refs = refs[: len(places) + 1], refs[len(places) + 1 :]
        before_ref, refs = (refs[0], refs[1:]) if has_before else (None, refs)
        results = refs[len(waits) :]
        start, source = 0, 0
        for part, size in enumerate(sizes):
            span = slice(start, start + size)
            start += size
            rows = []
            for index in range(len(places)):
                block = blocks[part * len(places) + index]
                value = source_refs[source][:size, :]
                if len(block) > 1:
                    other = source_refs[source + 1][:size, :]
                    value = jnp.where(plan_ref[INNER_AT] == 1, value, other)
                source += len(block)
                rows.append(value)
            for side in range(2):
                at = slice(side * columns, (side + 1) * columns)
                total = before_ref[span, at] if has_before else None
                for index, place in enumerate(places):
                    if side == 0:
                        weight = weight_refs[index][...]
                    else:
                        weight = weight_refs[-1][place * width : (place + 1) * width, :]
                    product = jnp.dot(rows[index], weight, preferred_element_type=jnp.float32)
                    total = product if total is None else total + product
                results[0][span, at] = total
                if send:
                    results[1][span, at] = total.astype(jnp.bfloat16)
        results[-1][...] = jnp.zeros(TOKEN.shape, TOKEN.dtype)

    shapes = [jax.ShapeDtypeStruct((sum(sizes), 2 * columns), jnp.float32)]
    if send:
        shapes.append(jax.ShapeDtypeStruct((sum(sizes), 2 * columns), jnp.bfloat16))
    return on_core(body, shapes + [TOKEN], specs)(*operands, *waits)


def hidden_rows(sums, got):
    units = sums.shape[1] // 4
    hidden = []
    for core in range(2):
        here, there = 2 * core * units, 2 * (1 - core) * units
        gate = sums[:, here : here + units] + got[:, there : there + units].astype(jnp.float32)
        up = sums[:, here + units : here + 2 * units]
        up = up + got[:, there + units : there + 2 * units].astype(jnp.float32)
        hidden.append((gate / (1.0 + jnp.exp(-gate)) * up).astype(jnp.bfloat16))
    return jnp.concatenate(hidden, axis=1)


def hide(sums, got):
    def body(sums_ref, got_ref, out_ref, token_ref):
        out_ref[...] = hidden_rows(sums_ref, got_ref)
        token_ref[...] = jnp.zeros(TOKEN.shape, TOKEN.dtype)

    shape = jax.ShapeDtypeStruct((sums.shape[0], sums.shape[1] // 2), jnp.bfloat16)
    return on_core(body, [shape, TOKEN], [VMEM, VMEM])(sums, got)


def factors_of(slot, plan, facts, rows):
    values = facts[:, :rows].astype(jnp.float32)
    kind = lax.broadcasted_iota(jnp.int32, (FACT_ROWS, 1), 0)
    mine = kind == plan[OFFSETS_AT + slot]
    factor = jnp.sum(jnp.where(mine, values, 0.0), axis=0, keepdims=True)
    return factor, values[4:5, :] * 256.0 + values[5:6, :]


def chunk_rows(owned, index, plan, factor, owner, hidden):
    first = (plan[index] * owned).astype(jnp.float32)
    token = first + lax.broadcasted_iota(jnp.int32, (owned, 1), 0).astype(jnp.float32)
    placing = jnp.where(owner == token, factor, 0.0).astype(jnp.bfloat16)
    return jnp.dot(placing, hidden, preferred_element_type=jnp.float32)


def facts_of(plan_ref, inner_ref, outer_ref, buffer, sem):
    last = inner_ref.shape[0] - FACT_ROWS

    def run(source):
        (copy,) = copies(source, last, buffer, FACT_ROWS, 1, sem, 0)
        copy.start()
        copy.wait()

    by_kind(plan_ref, (inner_ref, outer_ref), run)
    return buffer


def down(held, own_ref, lent_ref, sent_ref, kept_ref):
    units, width = own_ref.shape[0], kept_ref.shape[1]
    for out, at in ((kept_ref, slice(0, width)), (sent_ref, slice(width, 2 * width))):
        result = jnp.dot(held[:, :units], own_ref[:, at], preferred_element_type=jnp.float32)
        result += jnp.dot(held[:, units:], lent_ref[:, at], preferred_element_type=jnp.float32)
        out[...] = result.astype(out.dtype)


def fact_scratch(width):
    return [pltpu.VMEM((FACT_ROWS, width), jnp.bfloat16), pltpu.SemaphoreType.DMA((1,))]


def collect(owned, plan, hidden, sums, got, facts):
    rows, units = hidden[0].shape
    slots = len(facts)

    def body(plan_ref, *refs):
        hidden_refs, refs = refs[: slots - 1], refs[slots - 1 :]
        sums_ref, got_ref, refs = refs[0], refs[1], refs[2:]
        fact_refs, (out_ref, buffer, sem) = refs[: 2 * slots], refs[2 * slots :]
        factors = []
        for slot in range(slots):
            facts_of(plan_ref, *fact_refs[2 * slot : 2 * slot + 2], buffer, sem)
            factors.append(factors_of(slot, plan_ref, buffer, rows))
        factor = jnp.concatenate([pair[0] for pair in factors], axis=1)
        owner = jnp.concatenate([pair[1] for pair in factors], axis=1)
        every = [ref[...] for ref in hidden_refs] + [hidden_rows(sums_ref, got_ref)]
        every = jnp.concatenate(every, axis=0)
        for index in range(4):
            span = slice(index * owned, (index + 1) * owned)
            out_ref[span, :] = chunk_rows(owned, index, plan_ref, factor, owner, every)

    fact_blocks = [block for pair_of in facts for block in pair_of]
    specs = [SMEM] + [VMEM] * (slots + 1) + [ANYWHERE] * len(fact_blocks)
    shape = jax.ShapeDtypeStruct((4 * owned, units), jnp.float32)
    return on_core(body, shape, specs, fact_scratch(facts[0][0].shape[1]))(
        plan, *hidden, sums, got, *fact_blocks
    )


def finish(owned, slot, plan, sums, got, facts, before, down_own, down_lent):
    units = down_own.shape[0]
    width = down_own.shape[1] // 2
    pair = [
        jax.ShapeDtypeStruct((owned, width), jnp.bfloat16),
        jax.ShapeDtypeStruct((owned, width), jnp.float32),
    ]

    def first(plan_ref, sums_ref, got_ref, inner_ref, outer_ref, before_ref, *refs):
        own_ref, lent_ref, sent_ref, kept_ref, held_ref, buffer, sem = refs
        facts_of(plan_ref, inner_ref, outer_ref, buffer, sem)
        factor, owner = factors_of(slot, plan_ref, buffer, sums_ref.shape[0])
        hidden = hidden_rows(sums_ref, got_ref)
        for index in range(4):
            rows = chunk_rows(owned, index, plan_ref, factor, owner, hidden)
            rows = rows + before_ref[index * owned : (index + 1) * owned, :]
            held = rows.astype(jnp.bfloat16)
            if index == 0:
                down(held, own_ref, lent_ref, sent_ref, kept_ref)
            else:
                held_ref[(index - 1) * owned : index * owned, :] = held

    def others(indices, *waits):
        def body(held_ref, own_ref, lent_ref, *refs):
            out_refs = refs[len(waits) :]
            for place, index in enumerate(indices):
                held = held_ref[(index - 1) * owned : index * owned, :]
                down(held, own_ref, lent_ref, out_refs[2 * place], out_refs[2 * place + 1])

        operands = [held, down_own, down_lent, *waits]
        return on_core(body, pair * len(indices), [VMEM] * len(operands))(*operands)

    held_shape = jax.ShapeDtypeStruct((3 * owned, 2 * units), jnp.bfloat16)
    specs = [SMEM, VMEM, VMEM, ANYWHERE, ANYWHERE] + [VMEM] * 3
    sent, kept, held = on_core(
        first, pair + [held_shape], specs, fact_scratch(facts[0].shape[1])
    )(plan, sums, got, *facts, before, down_own, down_lent)
    rest = others([1, 2])
    chunks = [(sent, kept), (rest[0], rest[1]), (rest[2], rest[3])]
    return chunks, lambda *waits: others([3], *waits)


def rows_travel(
    tokens, gate_weight, up_weight, down_weight, route_gates, block_list, block_count, owner_token
):
    position = lax.axis_index("blk")
    share = lax.axis_index("tp")
    row_count, width = tokens.shape
    units = gate_weight.shape[2]
    owned = row_count // 2
    half = row_count // 2
    plan = jnp.asarray(PLAN, jnp.int32)[position]

    own_far = across_chips(tokens)
    own = with_facts(
        tokens, route_gates.T, jnp.transpose(block_list, (2, 0, 1)), block_count, owner_token
    )
    beside = along(own, BESIDE)
    middle = along(own, MIDDLE)

    gate_quarters = gate_weight[0].reshape(4, width, units)
    up_quarters = up_weight[0].reshape(4, width, units)

    def quarter(j):
        pair = [
            lax.dynamic_index_in_dim(q, share ^ j, 0, keepdims=False)
            for q in (gate_quarters, up_quarters)
        ]
        return jnp.concatenate(pair, axis=1)

    def down_part(j):
        return lax.dynamic_slice_in_dim(down_weight[0], (share ^ j) * width, width, 1)

    kept_down = jnp.concatenate([down_part(0), down_part(2)], axis=1)
    lend_down = jnp.concatenate([down_part(1), down_part(3)], axis=1)


    def at_kind(block, positions):
        pairs = [(4 * p + i, 4 * p + (i ^ 2)) for p in positions for i in range(4)]
        return lax.ppermute(block, ("blk", "tp"), pairs)

    inner_last = along(beside, MIDDLE)
    outer_next = along(middle, OUTWARD)
    beside_far = across_chips(beside)
    own_far_half = part_of(plan, own_far, own_far, half, half, flops=16 * 2**30)
    inward_far = along(own_far_half, INWARD)
    lend = jnp.concatenate([quarter(1), quarter(3)])
    lent = across_cores(after(lend, own))
    weights = [quarter(0), quarter(2), lent]
    whole = [row_count]
    sums_0, send_0, ready_0 = partial_sums(
        plan, whole, [(tokens, own_far)], weights, (0, 1), waits=[lend_down]
    )
    got_0 = across_cores(send_0)
    lent_down = across_cores(lend_down)

    outer_last = along(inner_last, OUTWARD)
    outer_next = after(outer_next, beside_far, inner_last, inward_far, ready_0)
    second = (middle, outer_next)
    second_far = (at_kind(middle, (1, 2)), at_kind(outer_next, (0, 3)))
    middle_far = along(inward_far, MIDDLE)
    sums_1, send_1, ready_1 = partial_sums(
        plan, whole, [(beside, beside_far)], weights, (0, 1)
    )
    got_1 = across_cores(send_1)

    last = (inner_last, outer_last)
    last_far_a = across_chips(
        part_of(plan, *last, 0, half, *second_far, middle_far, ready_0, ready_1)
    )
    outward_far = along(middle_far, OUTWARD)
    hidden_0, hidden_here = hide(sums_0, got_0)
    hidden_1, hidden_there = hide(sums_1, got_1)
    sums_2, send_2, _ = partial_sums(plan, whole, [(second, second_far)], weights, (0, 1))
    got_2 = across_cores(send_2)
    near, _ = partial_sums(plan, whole, [(last,)], weights, (0,), send=False)
    sums_3, send_3, _ = partial_sums(
        plan,
        [half, half],
        [(last_far_a,), ((middle_far, outward_far),)],
        weights,
        (1,),
        before=near,
        waits=[hidden_here, hidden_there],
    )
    got_3 = across_cores(send_3)
    total = collect(
        owned,
        plan,
        (hidden_0, hidden_1),
        sums_2,
        got_2,
        [(own, own), (beside, beside), second],
    )
    chunks, last_chunk = finish(
        owned, 3, plan, sums_3, got_3, last, total, kept_down, lent_down
    )

    def joined(sent, kept):
        return kept + across_chips(sent).astype(jnp.float32)

    first, second, third = [joined(*chunk).astype(jnp.bfloat16) for chunk in chunks]
    second = lax.optimization_barrier(second)
    inward = along(first, INWARD)
    middle = along(first, MIDDLE)
    two_in = along(second, TWO_IN)
    passed = second.astype(jnp.float32) + inward.astype(jnp.float32)
    two_out = along(passed.astype(jnp.bfloat16), TWO_OUT)
    beside = along(third, BESIDE)
    arrived = [block.astype(jnp.float32) for block in (middle, two_in, two_out)]
    total = lax.optimization_barrier(joined(*last_chunk(second)) + sum(arrived))
    return (total + beside.astype(jnp.float32)).astype(jnp.bfloat16)


def on_device(*args):
    block_list = args[5]
    sizes = (lax.axis_size("blk"), lax.axis_size("tp"), block_list.shape[1])
    if sizes == (4, 4, 4):
        return rows_travel(*args)
    return weights_travel(*args)


def solution(mesh):
    return jax.shard_map(
        on_device,
        mesh=mesh,
        in_specs=(
            P(("groups", "blk"), "tp"),
            P("blk", None, "tp"),
            P("blk", None, "tp"),
            P("blk", "tp", None),
            P(("groups", "blk"), None),
            P(("groups", "blk"), None, None),
            P(("groups", "blk"), None),
            P(("groups", "blk")),
        ),
        out_specs=P(("groups", "blk"), "tp"),
        check_vma=False,
    )
```

```python
import jax
import jax.numpy as jnp
from jax import lax
from jax.experimental import pallas as pl
from jax.experimental.pallas import tpu as pltpu
from jax.sharding import PartitionSpec as P


def shifted(block, axis, distance):
    devices = range(lax.axis_size(axis))
    route = [((i - distance) % len(devices), i) for i in devices]
    return lax.ppermute(block, axis, route)


def weights_travel(
    tokens, gate_weight, up_weight, down_weight, route_gates, block_list, block_count, owner_token
):
    whole_rows = lax.all_gather(tokens, "tp", axis=1, tiled=True)
    row_count = whole_rows.shape[0]
    width = whole_rows.shape[1]
    offsets_all = block_list.shape[1]
    block_total = block_list.shape[2]
    block_size = row_count // block_total
    blocks = whole_rows.reshape(block_total, block_size, width)
    gate_blocks = route_gates.reshape(block_total, block_size, offsets_all)
    totals = jnp.zeros((block_total, block_size, width), jnp.float32)

    def apply(totals, weights, offset, block_id):
        w_gate, w_up, w_down = weights
        block_rows = lax.dynamic_index_in_dim(blocks, block_id, 0, keepdims=False)
        gate_out = jnp.dot(block_rows, w_gate, preferred_element_type=jnp.float32)
        up_out = jnp.dot(block_rows, w_up, preferred_element_type=jnp.float32)
        hidden = (jax.nn.silu(gate_out) * up_out).astype(jnp.bfloat16)
        block_gates = lax.dynamic_index_in_dim(gate_blocks, block_id, 0, keepdims=False)
        factor = lax.dynamic_index_in_dim(block_gates, offset, 1, keepdims=False)
        product = jnp.dot(hidden, w_down, preferred_element_type=jnp.float32) * factor[:, None]
        before = lax.dynamic_index_in_dim(totals, block_id, 0, keepdims=False)
        return lax.dynamic_update_index_in_dim(totals, before + product, block_id, 0)

    resident = (gate_weight[0], up_weight[0], down_weight[0])
    arrived = [resident]
    holding = resident
    for offset in range(1, offsets_all):
        holding = shifted((holding[0], holding[1], holding[2]), "blk", 1)
        arrived.append(holding)
    for offset in range(offsets_all):
        weights = arrived[offset]

        def visit_block(position, totals, weights=weights, offset=offset):
            return apply(totals, weights, offset, block_list[0, offset, position])

        totals = lax.fori_loop(0, block_count[0, offset], visit_block, totals)
    summed = lax.psum_scatter(
        totals.reshape(row_count, width).astype(jnp.bfloat16), "tp", scatter_dimension=1, tiled=True
    )
    feature_share = summed.shape[1]
    cycle_size = lax.axis_size("blk")
    owned = row_count // 2
    capacity = max(2, 2 * row_count // cycle_size)
    target = owner_token // owned
    local_token = owner_token % owned
    target_table = (target[:, None] == jnp.arange(cycle_size, dtype=jnp.int32)[None, :]).astype(
        jnp.int32
    )
    running = jnp.cumsum(target_table, axis=0)
    rank = jnp.sum((running - 1) * target_table, axis=1)
    slot = target * capacity + rank
    send_rows = jnp.zeros((cycle_size * capacity, feature_share), jnp.bfloat16).at[slot].set(summed)
    send_index = jnp.full((cycle_size * capacity,), -1, jnp.int32).at[slot].set(local_token)
    send_rows = send_rows.reshape(cycle_size, capacity, feature_share)
    send_index = send_index.reshape(cycle_size, capacity)
    got_rows, got_index = (
        lax.all_to_all(send_rows, "blk", split_axis=0, concat_axis=0, tiled=True),
        lax.all_to_all(send_index, "blk", split_axis=0, concat_axis=0, tiled=True),
    )
    got_rows = got_rows.reshape(cycle_size * capacity, feature_share)
    got_index = got_index.reshape(cycle_size * capacity)
    placing = (got_index[:, None] == jnp.arange(owned, dtype=jnp.int32)[None, :]).astype(
        jnp.bfloat16
    )
    combined = lax.dot_general(
        placing, got_rows, (((0,), (0,)), ((), ())), preferred_element_type=jnp.float32
    )
    return combined.astype(jnp.bfloat16)


BESIDE = [(0, 1), (1, 0), (2, 3), (3, 2)]
MIDDLE = [(1, 2), (2, 1)]
INWARD = [(0, 1), (3, 2)]
OUTWARD = [(1, 0), (2, 3)]
TWO_IN = [(0, 2), (3, 1)]
TWO_OUT = [(1, 3), (2, 0)]
PLAN = [
    [3, 2, 1, 0, 0, 1, 2, 3, 0],
    [2, 3, 0, 1, 0, 3, 1, 2, 1],
    [1, 0, 3, 2, 0, 1, 3, 2, 1],
    [0, 1, 2, 3, 0, 3, 2, 1, 0],
]
OFFSETS_AT, INNER_AT = 4, 8
FACT_ROWS = 16
VMEM = pl.BlockSpec(memory_space=pltpu.VMEM)
SMEM = pl.BlockSpec(memory_space=pltpu.SMEM)
ANYWHERE = pl.BlockSpec(memory_space=pl.ANY)


def across_chips(block):
    return lax.ppermute(block, "tp", [(i, i ^ 2) for i in range(4)])


def across_cores(block):
    return lax.ppermute(block, "tp", [(i, i ^ 1) for i in range(4)])


def along(block, route):
    return lax.ppermute(block, "blk", route)


def cheap():
    return pl.CostEstimate(flops=1024, bytes_accessed=1024, transcendentals=0)


TOKEN = jax.ShapeDtypeStruct((8, 128), jnp.float32)
VMEM_LIMIT = 18 * 2**20


def on_core(body, out_shape, in_specs, scratch=()):
    return pl.pallas_call(
        body,
        out_shape=out_shape,
        in_specs=in_specs,
        out_specs=jax.tree.map(lambda _: VMEM, out_shape),
        scratch_shapes=scratch,
        compiler_params=pltpu.CompilerParams(vmem_limit_bytes=VMEM_LIMIT),
        cost_estimate=cheap(),
    )


def copies(source, start, target, size, pieces, sems, first):
    step = size // pieces
    return [
        pltpu.make_async_copy(
            source.at[pl.ds(start + index * step, step)],
            target.at[pl.ds(index * step, step)],
            sems.at[first + index],
        )
        for index in range(pieces)
    ]


def after(block, *others, flops=1024):
    return pl.pallas_call(
        lambda *refs: None,
        out_shape=jax.ShapeDtypeStruct(block.shape, block.dtype),
        in_specs=[ANYWHERE] * (1 + len(others)),
        out_specs=ANYWHERE,
        input_output_aliases={0: 0},
        cost_estimate=pl.CostEstimate(flops=flops, bytes_accessed=1024, transcendentals=0),
    )(block, *others)


def by_kind(plan_ref, kinds, run):
    if kinds[0] is kinds[1]:
        run(kinds[0])
        return
    for kind, value in zip(kinds, (1, 0)):

        @pl.when(plan_ref[INNER_AT] == value)
        def _(kind=kind):
            run(kind)


def part_of(plan, if_inner, if_outer, start, size, *others, flops=1024):
    shape = jax.ShapeDtypeStruct((size, if_inner.shape[1]), if_inner.dtype)
    pieces = 4

    def body(plan_ref, inner_ref, outer_ref, *rest):
        out_ref, buffer, in_sems, out_sems = rest[len(others) :]

        def run(source):
            inward = copies(source, start, buffer, size, pieces, in_sems, 0)
            outward = copies(buffer, 0, out_ref, size, pieces, out_sems, 0)
            for copy in inward:
                copy.start()
            for copy, next_copy in zip(inward, outward):
                copy.wait()
                next_copy.start()
            for copy in outward:
                copy.wait()

        by_kind(plan_ref, (inner_ref, inner_ref if if_outer is if_inner else outer_ref), run)

    return pl.pallas_call(
        body,
        out_shape=shape,
        in_specs=[SMEM] + [ANYWHERE] * (2 + len(others)),
        out_specs=ANYWHERE,
        scratch_shapes=[pltpu.VMEM(shape.shape, shape.dtype)]
        + [pltpu.SemaphoreType.DMA((pieces,))] * 2,
        compiler_params=pltpu.CompilerParams(vmem_limit_bytes=VMEM_LIMIT),
        cost_estimate=pl.CostEstimate(flops=flops, bytes_accessed=1024, transcendentals=0),
    )(plan, if_inner, if_outer, *others)


def with_facts(rows, gates, block_list, block_count, owner):
    count, width = rows.shape
    blocks, _, offsets = block_list.shape
    total = owner.shape[0]

    def body(rows_ref, gates_ref, list_ref, count_ref, owner_ref, out_ref, sems):
        moves = copies(rows_ref, 0, out_ref, count, 4, sems, 0)
        for copy in moves:
            copy.start()
        block_of = lax.broadcasted_iota(jnp.int32, (1, total), 1) // (total // blocks)
        facts = []
        for offset in range(offsets):
            mask = jnp.zeros((1, total), jnp.float32)
            for block in range(blocks):
                used = jnp.int32(0)
                for place in range(blocks):
                    found = (list_ref[place, 0, offset] == block) & (place < count_ref[0, offset])
                    used = used | found.astype(jnp.int32)
                mask = mask + jnp.where(block_of == block, used.astype(jnp.float32), 0.0)
            facts.append(gates_ref[offset : offset + 1, :] * mask)
        numbers = owner_ref[...].reshape(1, total)
        facts.append((numbers >> 8).astype(jnp.float32))
        facts.append((numbers & 255).astype(jnp.float32))
        facts.append(jnp.zeros((FACT_ROWS - len(facts), total), jnp.float32))
        out_ref[count:, :] = jnp.zeros((FACT_ROWS, width), jnp.bfloat16)
        out_ref[count:, :total] = jnp.concatenate(facts, axis=0).astype(jnp.bfloat16)
        for copy in moves:
            copy.wait()

    shape = jax.ShapeDtypeStruct((count + FACT_ROWS, width), rows.dtype)
    return on_core(
        body, shape, [ANYWHERE, VMEM, SMEM, SMEM, VMEM], [pltpu.SemaphoreType.DMA((4,))]
    )(rows, gates, block_list, block_count, owner)


def partial_sums(plan, sizes, parts, weights, places, before=None, send=True, waits=()):
    width, columns = weights[0].shape
    blocks = [
        block if isinstance(block, tuple) else (block,) for part in parts for block in part
    ]
    sources = [array for block in blocks for array in block]
    operands = [plan] + sources + [weights[place] for place in places] + [weights[2]]
    if before is not None:
        operands.append(before)
    specs = [SMEM] + [VMEM] * (len(operands) - 1 + len(waits))
    has_before = before is not None

    def body(plan_ref, *refs):
        source_refs, refs = refs[: len(sources)], refs[len(sources) :]
        weight_refs, refs = refs[: len(places) + 1], refs[len(places) + 1 :]
        before_ref, refs = (refs[0], refs[1:]) if has_before else (None, refs)
        results = refs[len(waits) :]
        start, source = 0, 0
        for part, size in enumerate(sizes):
            span = slice(start, start + size)
            start += size
            rows = []
            for index in range(len(places)):
                block = blocks[part * len(places) + index]
                value = source_refs[source][:size, :]
                if len(block) > 1:
                    other = source_refs[source + 1][:size, :]
                    value = jnp.where(plan_ref[INNER_AT] == 1, value, other)
                source += len(block)
                rows.append(value)
            for side in range(2):
                at = slice(side * columns, (side + 1) * columns)
                total = before_ref[span, at] if has_before else None
                for index, place in enumerate(places):
                    if side == 0:
                        weight = weight_refs[index][...]
                    else:
                        weight = weight_refs[-1][place * width : (place + 1) * width, :]
                    product = jnp.dot(rows[index], weight, preferred_element_type=jnp.float32)
                    total = product if total is None else total + product
                results[0][span, at] = total
                if send:
                    results[1][span, at] = total.astype(jnp.bfloat16)
        results[-1][...] = jnp.zeros(TOKEN.shape, TOKEN.dtype)

    shapes = [jax.ShapeDtypeStruct((sum(sizes), 2 * columns), jnp.float32)]
    if send:
        shapes.append(jax.ShapeDtypeStruct((sum(sizes), 2 * columns), jnp.bfloat16))
    return on_core(body, shapes + [TOKEN], specs)(*operands, *waits)


def hidden_rows(sums, got):
    units = sums.shape[1] // 4
    hidden = []
    for core in range(2):
        here, there = 2 * core * units, 2 * (1 - core) * units
        gate = sums[:, here : here + units] + got[:, there : there + units].astype(jnp.float32)
        up = sums[:, here + units : here + 2 * units]
        up = up + got[:, there + units : there + 2 * units].astype(jnp.float32)
        hidden.append((gate / (1.0 + jnp.exp(-gate)) * up).astype(jnp.bfloat16))
    return jnp.concatenate(hidden, axis=1)


def hide(sums, got):
    def body(sums_ref, got_ref, out_ref, token_ref):
        out_ref[...] = hidden_rows(sums_ref, got_ref)
        token_ref[...] = jnp.zeros(TOKEN.shape, TOKEN.dtype)

    shape = jax.ShapeDtypeStruct((sums.shape[0], sums.shape[1] // 2), jnp.bfloat16)
    return on_core(body, [shape, TOKEN], [VMEM, VMEM])(sums, got)


def factors_of(slot, plan, facts, rows):
    values = facts[:, :rows].astype(jnp.float32)
    kind = lax.broadcasted_iota(jnp.int32, (FACT_ROWS, 1), 0)
    mine = kind == plan[OFFSETS_AT + slot]
    factor = jnp.sum(jnp.where(mine, values, 0.0), axis=0, keepdims=True)
    return factor, values[4:5, :] * 256.0 + values[5:6, :]


def chunk_rows(owned, index, plan, factor, owner, hidden):
    first = (plan[index] * owned).astype(jnp.float32)
    token = first + lax.broadcasted_iota(jnp.int32, (owned, 1), 0).astype(jnp.float32)
    placing = jnp.where(owner == token, factor, 0.0).astype(jnp.bfloat16)
    return jnp.dot(placing, hidden, preferred_element_type=jnp.float32)


def facts_of(plan_ref, inner_ref, outer_ref, buffer, sem):
    last = inner_ref.shape[0] - FACT_ROWS

    def run(source):
        (copy,) = copies(source, last, buffer, FACT_ROWS, 1, sem, 0)
        copy.start()
        copy.wait()

    by_kind(plan_ref, (inner_ref, outer_ref), run)
    return buffer


def down(held, own_ref, lent_ref, sent_ref, kept_ref):
    units, width = own_ref.shape[0], kept_ref.shape[1]
    for out, at in ((kept_ref, slice(0, width)), (sent_ref, slice(width, 2 * width))):
        result = jnp.dot(held[:, :units], own_ref[:, at], preferred_element_type=jnp.float32)
        result += jnp.dot(held[:, units:], lent_ref[:, at], preferred_element_type=jnp.float32)
        out[...] = result.astype(out.dtype)


def fact_scratch(width):
    return [pltpu.VMEM((FACT_ROWS, width), jnp.bfloat16), pltpu.SemaphoreType.DMA((1,))]


def collect(owned, plan, hidden, sums, got, facts):
    rows, units = hidden[0].shape
    slots = len(facts)

    def body(plan_ref, *refs):
        hidden_refs, refs = refs[: slots - 1], refs[slots - 1 :]
        sums_ref, got_ref, refs = refs[0], refs[1], refs[2:]
        fact_refs, (out_ref, buffer, sem) = refs[: 2 * slots], refs[2 * slots :]
        factors = []
        for slot in range(slots):
            facts_of(plan_ref, *fact_refs[2 * slot : 2 * slot + 2], buffer, sem)
            factors.append(factors_of(slot, plan_ref, buffer, rows))
        factor = jnp.concatenate([pair[0] for pair in factors], axis=1)
        owner = jnp.concatenate([pair[1] for pair in factors], axis=1)
        every = [ref[...] for ref in hidden_refs] + [hidden_rows(sums_ref, got_ref)]
        every = jnp.concatenate(every, axis=0)
        for index in range(4):
            span = slice(index * owned, (index + 1) * owned)
            out_ref[span, :] = chunk_rows(owned, index, plan_ref, factor, owner, every)

    fact_blocks = [block for pair_of in facts for block in pair_of]
    specs = [SMEM] + [VMEM] * (slots + 1) + [ANYWHERE] * len(fact_blocks)
    shape = jax.ShapeDtypeStruct((4 * owned, units), jnp.float32)
    return on_core(body, shape, specs, fact_scratch(facts[0][0].shape[1]))(
        plan, *hidden, sums, got, *fact_blocks
    )


def finish(owned, slot, plan, sums, got, facts, before, down_own, down_lent):
    units = down_own.shape[0]
    width = down_own.shape[1] // 2
    pair = [
        jax.ShapeDtypeStruct((owned, width), jnp.bfloat16),
        jax.ShapeDtypeStruct((owned, width), jnp.float32),
    ]

    def first(plan_ref, sums_ref, got_ref, inner_ref, outer_ref, before_ref, *refs):
        own_ref, lent_ref, sent_ref, kept_ref, held_ref, buffer, sem = refs
        facts_of(plan_ref, inner_ref, outer_ref, buffer, sem)
        factor, owner = factors_of(slot, plan_ref, buffer, sums_ref.shape[0])
        hidden = hidden_rows(sums_ref, got_ref)
        for index in range(4):
            rows = chunk_rows(owned, index, plan_ref, factor, owner, hidden)
            rows = rows + before_ref[index * owned : (index + 1) * owned, :]
            held = rows.astype(jnp.bfloat16)
            if index == 0:
                down(held, own_ref, lent_ref, sent_ref, kept_ref)
            else:
                held_ref[(index - 1) * owned : index * owned, :] = held

    def others(indices, *waits):
        def body(held_ref, own_ref, lent_ref, *refs):
            out_refs = refs[len(waits) :]
            for place, index in enumerate(indices):
                held = held_ref[(index - 1) * owned : index * owned, :]
                down(held, own_ref, lent_ref, out_refs[2 * place], out_refs[2 * place + 1])

        operands = [held, down_own, down_lent, *waits]
        return on_core(body, pair * len(indices), [VMEM] * len(operands))(*operands)

    held_shape = jax.ShapeDtypeStruct((3 * owned, 2 * units), jnp.bfloat16)
    specs = [SMEM, VMEM, VMEM, ANYWHERE, ANYWHERE] + [VMEM] * 3
    sent, kept, held = on_core(
        first, pair + [held_shape], specs, fact_scratch(facts[0].shape[1])
    )(plan, sums, got, *facts, before, down_own, down_lent)
    rest = others([1, 2])
    chunks = [(sent, kept), (rest[0], rest[1]), (rest[2], rest[3])]
    return chunks, lambda *waits: others([3], *waits)


def rows_travel(
    tokens, gate_weight, up_weight, down_weight, route_gates, block_list, block_count, owner_token
):
    position = lax.axis_index("blk")
    share = lax.axis_index("tp")
    row_count, width = tokens.shape
    units = gate_weight.shape[2]
    owned = row_count // 2
    half = row_count // 2
    plan = jnp.asarray(PLAN, jnp.int32)[position]

    own_far = across_chips(tokens)
    own = with_facts(
        tokens, route_gates.T, jnp.transpose(block_list, (2, 0, 1)), block_count, owner_token
    )
    beside = along(own, BESIDE)
    middle = along(own, MIDDLE)

    gate_quarters = gate_weight[0].reshape(4, width, units)
    up_quarters = up_weight[0].reshape(4, width, units)

    def quarter(j):
        pair = [
            lax.dynamic_index_in_dim(q, share ^ j, 0, keepdims=False)
            for q in (gate_quarters, up_quarters)
        ]
        return jnp.concatenate(pair, axis=1)

    def down_part(j):
        return lax.dynamic_slice_in_dim(down_weight[0], (share ^ j) * width, width, 1)

    kept_down = jnp.concatenate([down_part(0), down_part(2)], axis=1)
    lend_down = jnp.concatenate([down_part(1), down_part(3)], axis=1)


    def at_kind(block, positions):
        pairs = [(4 * p + i, 4 * p + (i ^ 2)) for p in positions for i in range(4)]
        return lax.ppermute(block, ("blk", "tp"), pairs)

    inner_last = along(beside, MIDDLE)
    outer_next = along(middle, OUTWARD)
    beside_far = across_chips(beside)
    own_far_half = part_of(plan, own_far, own_far, half, half, flops=16 * 2**30)
    inward_far = along(own_far_half, INWARD)
    lend = jnp.concatenate([quarter(1), quarter(3)])
    lent = across_cores(after(lend, own))
    weights = [quarter(0), quarter(2), lent]
    whole = [row_count]
    sums_0, send_0, ready_0 = partial_sums(
        plan, whole, [(tokens, own_far)], weights, (0, 1), waits=[lend_down]
    )
    got_0 = across_cores(send_0)
    lent_down = across_cores(lend_down)

    outer_last = along(inner_last, OUTWARD)
    outer_next = after(outer_next, beside_far, inner_last, inward_far, ready_0)
    second = (middle, outer_next)
    second_far = (at_kind(middle, (1, 2)), at_kind(outer_next, (0, 3)))
    middle_far = along(inward_far, MIDDLE)
    sums_1, send_1, ready_1 = partial_sums(
        plan, whole, [(beside, beside_far)], weights, (0, 1)
    )
    got_1 = across_cores(send_1)

    last = (inner_last, outer_last)
    last_far_a = across_chips(
        part_of(plan, *last, 0, half, *second_far, middle_far, ready_0, ready_1)
    )
    outward_far = along(middle_far, OUTWARD)
    hidden_0, hidden_here = hide(sums_0, got_0)
    hidden_1, hidden_there = hide(sums_1, got_1)
    sums_2, send_2, _ = partial_sums(plan, whole, [(second, second_far)], weights, (0, 1))
    got_2 = across_cores(send_2)
    near, _ = partial_sums(plan, whole, [(last,)], weights, (0,), send=False)
    sums_3, send_3, _ = partial_sums(
        plan,
        [half, half],
        [(last_far_a,), ((middle_far, outward_far),)],
        weights,
        (1,),
        before=near,
        waits=[hidden_here, hidden_there],
    )
    got_3 = across_cores(send_3)
    total = collect(
        owned,
        plan,
        (hidden_0, hidden_1),
        sums_2,
        got_2,
        [(own, own), (beside, beside), second],
    )
    chunks, last_chunk = finish(
        owned, 3, plan, sums_3, got_3, last, total, kept_down, lent_down
    )

    def joined(sent, kept):
        return kept + across_chips(sent).astype(jnp.float32)

    first, second, third = [joined(*chunk).astype(jnp.bfloat16) for chunk in chunks]
    second = lax.optimization_barrier(second)
    inward = along(first, INWARD)
    middle = along(first, MIDDLE)
    two_in = along(second, TWO_IN)
    passed = second.astype(jnp.float32) + inward.astype(jnp.float32)
    two_out = along(passed.astype(jnp.bfloat16), TWO_OUT)
    beside = along(third, BESIDE)
    arrived = [block.astype(jnp.float32) for block in (middle, two_in, two_out)]
    total = lax.optimization_barrier(sum(arrived))
    own_sum = joined(*last_chunk(second))
    return (total + own_sum + beside.astype(jnp.float32)).astype(jnp.bfloat16)


def on_device(*args):
    block_list = args[5]
    sizes = (lax.axis_size("blk"), lax.axis_size("tp"), block_list.shape[1])
    if sizes == (4, 4, 4):
        return rows_travel(*args)
    return weights_travel(*args)


def solution(mesh):
    return jax.shard_map(
        on_device,
        mesh=mesh,
        in_specs=(
            P(("groups", "blk"), "tp"),
            P("blk", None, "tp"),
            P("blk", None, "tp"),
            P("blk", "tp", None),
            P(("groups", "blk"), None),
            P(("groups", "blk"), None, None),
            P(("groups", "blk"), None),
            P(("groups", "blk")),
        ),
        out_specs=P(("groups", "blk"), "tp"),
        check_vma=False,
    )
```

```python
import jax
import jax.numpy as jnp
from jax import lax
from jax.experimental import pallas as pl
from jax.experimental.pallas import tpu as pltpu
from jax.sharding import PartitionSpec as P


def shifted(block, axis, distance):
    devices = range(lax.axis_size(axis))
    route = [((i - distance) % len(devices), i) for i in devices]
    return lax.ppermute(block, axis, route)


def weights_travel(
    tokens, gate_weight, up_weight, down_weight, route_gates, block_list, block_count, owner_token
):
    whole_rows = lax.all_gather(tokens, "tp", axis=1, tiled=True)
    row_count = whole_rows.shape[0]
    width = whole_rows.shape[1]
    offsets_all = block_list.shape[1]
    block_total = block_list.shape[2]
    block_size = row_count // block_total
    blocks = whole_rows.reshape(block_total, block_size, width)
    gate_blocks = route_gates.reshape(block_total, block_size, offsets_all)
    totals = jnp.zeros((block_total, block_size, width), jnp.float32)

    def apply(totals, weights, offset, block_id):
        w_gate, w_up, w_down = weights
        block_rows = lax.dynamic_index_in_dim(blocks, block_id, 0, keepdims=False)
        gate_out = jnp.dot(block_rows, w_gate, preferred_element_type=jnp.float32)
        up_out = jnp.dot(block_rows, w_up, preferred_element_type=jnp.float32)
        hidden = (jax.nn.silu(gate_out) * up_out).astype(jnp.bfloat16)
        block_gates = lax.dynamic_index_in_dim(gate_blocks, block_id, 0, keepdims=False)
        factor = lax.dynamic_index_in_dim(block_gates, offset, 1, keepdims=False)
        product = jnp.dot(hidden, w_down, preferred_element_type=jnp.float32) * factor[:, None]
        before = lax.dynamic_index_in_dim(totals, block_id, 0, keepdims=False)
        return lax.dynamic_update_index_in_dim(totals, before + product, block_id, 0)

    resident = (gate_weight[0], up_weight[0], down_weight[0])
    arrived = [resident]
    holding = resident
    for offset in range(1, offsets_all):
        holding = shifted((holding[0], holding[1], holding[2]), "blk", 1)
        arrived.append(holding)
    for offset in range(offsets_all):
        weights = arrived[offset]

        def visit_block(position, totals, weights=weights, offset=offset):
            return apply(totals, weights, offset, block_list[0, offset, position])

        totals = lax.fori_loop(0, block_count[0, offset], visit_block, totals)
    summed = lax.psum_scatter(
        totals.reshape(row_count, width).astype(jnp.bfloat16), "tp", scatter_dimension=1, tiled=True
    )
    feature_share = summed.shape[1]
    cycle_size = lax.axis_size("blk")
    owned = row_count // 2
    capacity = max(2, 2 * row_count // cycle_size)
    target = owner_token // owned
    local_token = owner_token % owned
    target_table = (target[:, None] == jnp.arange(cycle_size, dtype=jnp.int32)[None, :]).astype(
        jnp.int32
    )
    running = jnp.cumsum(target_table, axis=0)
    rank = jnp.sum((running - 1) * target_table, axis=1)
    slot = target * capacity + rank
    send_rows = jnp.zeros((cycle_size * capacity, feature_share), jnp.bfloat16).at[slot].set(summed)
    send_index = jnp.full((cycle_size * capacity,), -1, jnp.int32).at[slot].set(local_token)
    send_rows = send_rows.reshape(cycle_size, capacity, feature_share)
    send_index = send_index.reshape(cycle_size, capacity)
    got_rows, got_index = (
        lax.all_to_all(send_rows, "blk", split_axis=0, concat_axis=0, tiled=True),
        lax.all_to_all(send_index, "blk", split_axis=0, concat_axis=0, tiled=True),
    )
    got_rows = got_rows.reshape(cycle_size * capacity, feature_share)
    got_index = got_index.reshape(cycle_size * capacity)
    placing = (got_index[:, None] == jnp.arange(owned, dtype=jnp.int32)[None, :]).astype(
        jnp.bfloat16
    )
    combined = lax.dot_general(
        placing, got_rows, (((0,), (0,)), ((), ())), preferred_element_type=jnp.float32
    )
    return combined.astype(jnp.bfloat16)


BESIDE = [(0, 1), (1, 0), (2, 3), (3, 2)]
MIDDLE = [(1, 2), (2, 1)]
INWARD = [(0, 1), (3, 2)]
OUTWARD = [(1, 0), (2, 3)]
TWO_IN = [(0, 2), (3, 1)]
TWO_OUT = [(1, 3), (2, 0)]
PLAN = [
    [3, 2, 1, 0, 0, 1, 2, 3, 0],
    [2, 3, 0, 1, 0, 3, 1, 2, 1],
    [1, 0, 3, 2, 0, 1, 3, 2, 1],
    [0, 1, 2, 3, 0, 3, 2, 1, 0],
]
OFFSETS_AT, INNER_AT = 4, 8
FACT_ROWS = 16
VMEM = pl.BlockSpec(memory_space=pltpu.VMEM)
SMEM = pl.BlockSpec(memory_space=pltpu.SMEM)
ANYWHERE = pl.BlockSpec(memory_space=pl.ANY)


def across_chips(block):
    return lax.ppermute(block, "tp", [(i, i ^ 2) for i in range(4)])


def across_cores(block):
    return lax.ppermute(block, "tp", [(i, i ^ 1) for i in range(4)])


def along(block, route):
    return lax.ppermute(block, "blk", route)


def cheap():
    return pl.CostEstimate(flops=1024, bytes_accessed=1024, transcendentals=0)


TOKEN = jax.ShapeDtypeStruct((8, 128), jnp.float32)
VMEM_LIMIT = 18 * 2**20


def on_core(body, out_shape, in_specs, scratch=()):
    return pl.pallas_call(
        body,
        out_shape=out_shape,
        in_specs=in_specs,
        out_specs=jax.tree.map(lambda _: VMEM, out_shape),
        scratch_shapes=scratch,
        compiler_params=pltpu.CompilerParams(vmem_limit_bytes=VMEM_LIMIT),
        cost_estimate=cheap(),
    )


def copies(source, start, target, size, pieces, sems, first):
    step = size // pieces
    return [
        pltpu.make_async_copy(
            source.at[pl.ds(start + index * step, step)],
            target.at[pl.ds(index * step, step)],
            sems.at[first + index],
        )
        for index in range(pieces)
    ]


def after(block, *others, flops=1024):
    return pl.pallas_call(
        lambda *refs: None,
        out_shape=jax.ShapeDtypeStruct(block.shape, block.dtype),
        in_specs=[ANYWHERE] * (1 + len(others)),
        out_specs=ANYWHERE,
        input_output_aliases={0: 0},
        cost_estimate=pl.CostEstimate(flops=flops, bytes_accessed=1024, transcendentals=0),
    )(block, *others)


def by_kind(plan_ref, kinds, run):
    if kinds[0] is kinds[1]:
        run(kinds[0])
        return
    for kind, value in zip(kinds, (1, 0)):

        @pl.when(plan_ref[INNER_AT] == value)
        def _(kind=kind):
            run(kind)


def part_of(plan, if_inner, if_outer, start, size, *others, flops=1024):
    shape = jax.ShapeDtypeStruct((size, if_inner.shape[1]), if_inner.dtype)
    pieces = 4

    def body(plan_ref, inner_ref, outer_ref, *rest):
        out_ref, buffer, in_sems, out_sems = rest[len(others) :]

        def run(source):
            inward = copies(source, start, buffer, size, pieces, in_sems, 0)
            outward = copies(buffer, 0, out_ref, size, pieces, out_sems, 0)
            for copy in inward:
                copy.start()
            for copy, next_copy in zip(inward, outward):
                copy.wait()
                next_copy.start()
            for copy in outward:
                copy.wait()

        by_kind(plan_ref, (inner_ref, inner_ref if if_outer is if_inner else outer_ref), run)

    return pl.pallas_call(
        body,
        out_shape=shape,
        in_specs=[SMEM] + [ANYWHERE] * (2 + len(others)),
        out_specs=ANYWHERE,
        scratch_shapes=[pltpu.VMEM(shape.shape, shape.dtype)]
        + [pltpu.SemaphoreType.DMA((pieces,))] * 2,
        compiler_params=pltpu.CompilerParams(vmem_limit_bytes=VMEM_LIMIT),
        cost_estimate=pl.CostEstimate(flops=flops, bytes_accessed=1024, transcendentals=0),
    )(plan, if_inner, if_outer, *others)


def with_facts(rows, gates, block_list, block_count, owner):
    count, width = rows.shape
    blocks, _, offsets = block_list.shape
    total = owner.shape[0]

    def body(rows_ref, gates_ref, list_ref, count_ref, owner_ref, out_ref, sems):
        moves = copies(rows_ref, 0, out_ref, count, 4, sems, 0)
        for copy in moves:
            copy.start()
        block_of = lax.broadcasted_iota(jnp.int32, (1, total), 1) // (total // blocks)
        facts = []
        for offset in range(offsets):
            mask = jnp.zeros((1, total), jnp.float32)
            for block in range(blocks):
                used = jnp.int32(0)
                for place in range(blocks):
                    found = (list_ref[place, 0, offset] == block) & (place < count_ref[0, offset])
                    used = used | found.astype(jnp.int32)
                mask = mask + jnp.where(block_of == block, used.astype(jnp.float32), 0.0)
            facts.append(gates_ref[offset : offset + 1, :] * mask)
        numbers = owner_ref[...].reshape(1, total)
        facts.append((numbers >> 8).astype(jnp.float32))
        facts.append((numbers & 255).astype(jnp.float32))
        facts.append(jnp.zeros((FACT_ROWS - len(facts), total), jnp.float32))
        out_ref[count:, :] = jnp.zeros((FACT_ROWS, width), jnp.bfloat16)
        out_ref[count:, :total] = jnp.concatenate(facts, axis=0).astype(jnp.bfloat16)
        for copy in moves:
            copy.wait()

    shape = jax.ShapeDtypeStruct((count + FACT_ROWS, width), rows.dtype)
    return on_core(
        body, shape, [ANYWHERE, VMEM, SMEM, SMEM, VMEM], [pltpu.SemaphoreType.DMA((4,))]
    )(rows, gates, block_list, block_count, owner)


def partial_sums(plan, sizes, parts, weights, places, before=None, send=True, waits=()):
    width, columns = weights[0].shape
    blocks = [
        block if isinstance(block, tuple) else (block,) for part in parts for block in part
    ]
    sources = [array for block in blocks for array in block]
    operands = [plan] + sources + [weights[place] for place in places] + [weights[2]]
    if before is not None:
        operands.append(before)
    specs = [SMEM] + [VMEM] * (len(operands) - 1 + len(waits))
    has_before = before is not None

    def body(plan_ref, *refs):
        source_refs, refs = refs[: len(sources)], refs[len(sources) :]
        weight_refs, refs = refs[: len(places) + 1], refs[len(places) + 1 :]
        before_ref, refs = (refs[0], refs[1:]) if has_before else (None, refs)
        results = refs[len(waits) :]
        start, source = 0, 0
        for part, size in enumerate(sizes):
            span = slice(start, start + size)
            start += size
            rows = []
            for index in range(len(places)):
                block = blocks[part * len(places) + index]
                value = source_refs[source][:size, :]
                if len(block) > 1:
                    other = source_refs[source + 1][:size, :]
                    value = jnp.where(plan_ref[INNER_AT] == 1, value, other)
                source += len(block)
                rows.append(value)
            for side in range(2):
                at = slice(side * columns, (side + 1) * columns)
                total = before_ref[span, at] if has_before else None
                for index, place in enumerate(places):
                    if side == 0:
                        weight = weight_refs[index][...]
                    else:
                        weight = weight_refs[-1][place * width : (place + 1) * width, :]
                    product = jnp.dot(rows[index], weight, preferred_element_type=jnp.float32)
                    total = product if total is None else total + product
                results[0][span, at] = total
                if send:
                    results[1][span, at] = total.astype(jnp.bfloat16)
        results[-1][...] = jnp.zeros(TOKEN.shape, TOKEN.dtype)

    shapes = [jax.ShapeDtypeStruct((sum(sizes), 2 * columns), jnp.float32)]
    if send:
        shapes.append(jax.ShapeDtypeStruct((sum(sizes), 2 * columns), jnp.bfloat16))
    return on_core(body, shapes + [TOKEN], specs)(*operands, *waits)


def hidden_rows(sums, got):
    units = sums.shape[1] // 4
    hidden = []
    for core in range(2):
        here, there = 2 * core * units, 2 * (1 - core) * units
        gate = sums[:, here : here + units] + got[:, there : there + units].astype(jnp.float32)
        up = sums[:, here + units : here + 2 * units]
        up = up + got[:, there + units : there + 2 * units].astype(jnp.float32)
        hidden.append((gate / (1.0 + jnp.exp(-gate)) * up).astype(jnp.bfloat16))
    return jnp.concatenate(hidden, axis=1)


def hide(sums, got):
    def body(sums_ref, got_ref, out_ref, token_ref):
        out_ref[...] = hidden_rows(sums_ref, got_ref)
        token_ref[...] = jnp.zeros(TOKEN.shape, TOKEN.dtype)

    shape = jax.ShapeDtypeStruct((sums.shape[0], sums.shape[1] // 2), jnp.bfloat16)
    return on_core(body, [shape, TOKEN], [VMEM, VMEM])(sums, got)


def factors_of(slot, plan, facts, rows):
    values = facts[:, :rows].astype(jnp.float32)
    kind = lax.broadcasted_iota(jnp.int32, (FACT_ROWS, 1), 0)
    mine = kind == plan[OFFSETS_AT + slot]
    factor = jnp.sum(jnp.where(mine, values, 0.0), axis=0, keepdims=True)
    return factor, values[4:5, :] * 256.0 + values[5:6, :]


def chunk_rows(owned, index, plan, factor, owner, hidden):
    first = (plan[index] * owned).astype(jnp.float32)
    token = first + lax.broadcasted_iota(jnp.int32, (owned, 1), 0).astype(jnp.float32)
    placing = jnp.where(owner == token, factor, 0.0).astype(jnp.bfloat16)
    return jnp.dot(placing, hidden, preferred_element_type=jnp.float32)


def facts_of(plan_ref, inner_ref, outer_ref, buffer, sem):
    last = inner_ref.shape[0] - FACT_ROWS

    def run(source):
        (copy,) = copies(source, last, buffer, FACT_ROWS, 1, sem, 0)
        copy.start()
        copy.wait()

    by_kind(plan_ref, (inner_ref, outer_ref), run)
    return buffer


def down(held, own_ref, lent_ref, sent_ref, kept_ref):
    units, width = own_ref.shape[0], kept_ref.shape[1]
    for out, at in ((kept_ref, slice(0, width)), (sent_ref, slice(width, 2 * width))):
        result = jnp.dot(held[:, :units], own_ref[:, at], preferred_element_type=jnp.float32)
        result += jnp.dot(held[:, units:], lent_ref[:, at], preferred_element_type=jnp.float32)
        out[...] = result.astype(out.dtype)


def fact_scratch(width):
    return [pltpu.VMEM((FACT_ROWS, width), jnp.bfloat16), pltpu.SemaphoreType.DMA((1,))]


def collect(owned, plan, hidden, sums, got, facts):
    rows, units = hidden[0].shape
    slots = len(facts)

    def body(plan_ref, *refs):
        hidden_refs, refs = refs[: slots - 1], refs[slots - 1 :]
        sums_ref, got_ref, refs = refs[0], refs[1], refs[2:]
        fact_refs, (out_ref, buffer, sem) = refs[: 2 * slots], refs[2 * slots :]
        factors = []
        for slot in range(slots):
            facts_of(plan_ref, *fact_refs[2 * slot : 2 * slot + 2], buffer, sem)
            factors.append(factors_of(slot, plan_ref, buffer, rows))
        factor = jnp.concatenate([pair[0] for pair in factors], axis=1)
        owner = jnp.concatenate([pair[1] for pair in factors], axis=1)
        every = [ref[...] for ref in hidden_refs] + [hidden_rows(sums_ref, got_ref)]
        every = jnp.concatenate(every, axis=0)
        for index in range(4):
            span = slice(index * owned, (index + 1) * owned)
            out_ref[span, :] = chunk_rows(owned, index, plan_ref, factor, owner, every)

    fact_blocks = [block for pair_of in facts for block in pair_of]
    specs = [SMEM] + [VMEM] * (slots + 1) + [ANYWHERE] * len(fact_blocks)
    shape = jax.ShapeDtypeStruct((4 * owned, units), jnp.float32)
    return on_core(body, shape, specs, fact_scratch(facts[0][0].shape[1]))(
        plan, *hidden, sums, got, *fact_blocks
    )


def finish(owned, slot, plan, sums, got, facts, before, down_own, down_lent):
    units = down_own.shape[0]
    width = down_own.shape[1] // 2
    pair = [
        jax.ShapeDtypeStruct((owned, width), jnp.bfloat16),
        jax.ShapeDtypeStruct((owned, width), jnp.float32),
    ]

    def first(plan_ref, sums_ref, got_ref, inner_ref, outer_ref, before_ref, *refs):
        own_ref, lent_ref, sent_ref, kept_ref, held_ref, buffer, sem = refs
        facts_of(plan_ref, inner_ref, outer_ref, buffer, sem)
        factor, owner = factors_of(slot, plan_ref, buffer, sums_ref.shape[0])
        hidden = hidden_rows(sums_ref, got_ref)
        for index in range(4):
            rows = chunk_rows(owned, index, plan_ref, factor, owner, hidden)
            rows = rows + before_ref[index * owned : (index + 1) * owned, :]
            held = rows.astype(jnp.bfloat16)
            if index == 0:
                down(held, own_ref, lent_ref, sent_ref, kept_ref)
            else:
                held_ref[(index - 1) * owned : index * owned, :] = held

    def others(indices, *waits):
        def body(held_ref, own_ref, lent_ref, *refs):
            out_refs = refs[len(waits) :]
            for place, index in enumerate(indices):
                held = held_ref[(index - 1) * owned : index * owned, :]
                down(held, own_ref, lent_ref, out_refs[2 * place], out_refs[2 * place + 1])

        operands = [held, down_own, down_lent, *waits]
        return on_core(body, pair * len(indices), [VMEM] * len(operands))(*operands)

    held_shape = jax.ShapeDtypeStruct((3 * owned, 2 * units), jnp.bfloat16)
    specs = [SMEM, VMEM, VMEM, ANYWHERE, ANYWHERE] + [VMEM] * 3
    sent, kept, held = on_core(
        first, pair + [held_shape], specs, fact_scratch(facts[0].shape[1])
    )(plan, sums, got, *facts, before, down_own, down_lent)
    rest = others([1, 2])
    chunks = [(sent, kept), (rest[0], rest[1]), (rest[2], rest[3])]
    return chunks, lambda *waits: others([3], *waits)


def rows_travel(
    tokens, gate_weight, up_weight, down_weight, route_gates, block_list, block_count, owner_token
):
    position = lax.axis_index("blk")
    share = lax.axis_index("tp")
    row_count, width = tokens.shape
    units = gate_weight.shape[2]
    owned = row_count // 2
    half = row_count // 2
    plan = jnp.asarray(PLAN, jnp.int32)[position]

    own_far = across_chips(tokens)
    own = with_facts(
        tokens, route_gates.T, jnp.transpose(block_list, (2, 0, 1)), block_count, owner_token
    )
    beside = along(own, BESIDE)
    middle = along(own, MIDDLE)

    gate_quarters = gate_weight[0].reshape(4, width, units)
    up_quarters = up_weight[0].reshape(4, width, units)

    def quarter(j):
        pair = [
            lax.dynamic_index_in_dim(q, share ^ j, 0, keepdims=False)
            for q in (gate_quarters, up_quarters)
        ]
        return jnp.concatenate(pair, axis=1)

    def down_part(j):
        return lax.dynamic_slice_in_dim(down_weight[0], (share ^ j) * width, width, 1)

    kept_down = jnp.concatenate([down_part(0), down_part(2)], axis=1)
    lend_down = jnp.concatenate([down_part(1), down_part(3)], axis=1)


    def at_kind(block, positions):
        pairs = [(4 * p + i, 4 * p + (i ^ 2)) for p in positions for i in range(4)]
        return lax.ppermute(block, ("blk", "tp"), pairs)

    inner_last = along(beside, MIDDLE)
    outer_next = along(middle, OUTWARD)
    beside_far = across_chips(beside)
    own_far_half = part_of(plan, own_far, own_far, half, half, flops=16 * 2**30)
    inward_far = along(own_far_half, INWARD)
    lend = jnp.concatenate([quarter(1), quarter(3)])
    lent = across_cores(after(lend, own))
    weights = [quarter(0), quarter(2), lent]
    whole = [row_count]
    sums_0, send_0, ready_0 = partial_sums(
        plan, whole, [(tokens, own_far)], weights, (0, 1), waits=[lend_down]
    )
    got_0 = across_cores(send_0)
    lent_down = across_cores(lend_down)

    outer_last = along(inner_last, OUTWARD)
    outer_next = after(outer_next, beside_far, inner_last, inward_far, ready_0)
    second = (middle, outer_next)
    second_far = (at_kind(middle, (1, 2)), at_kind(outer_next, (0, 3)))
    middle_far = along(inward_far, MIDDLE)
    sums_1, send_1, ready_1 = partial_sums(
        plan, whole, [(beside, beside_far)], weights, (0, 1)
    )
    got_1 = across_cores(send_1)

    last = (inner_last, outer_last)
    last_far_a = across_chips(
        part_of(plan, *last, 0, half, *second_far, middle_far, ready_0, ready_1)
    )
    outward_far = along(middle_far, OUTWARD)
    hidden_0, hidden_here = hide(sums_0, got_0)
    hidden_1, hidden_there = hide(sums_1, got_1)
    sums_2, send_2, _ = partial_sums(plan, whole, [(second, second_far)], weights, (0, 1))
    got_2 = across_cores(send_2)
    near, _ = partial_sums(plan, whole, [(last,)], weights, (0,), send=False)
    sums_3, send_3, _ = partial_sums(
        plan,
        [half, half],
        [(last_far_a,), ((middle_far, outward_far),)],
        weights,
        (1,),
        before=near,
        waits=[hidden_here, hidden_there],
    )
    got_3 = across_cores(send_3)
    total = collect(
        owned,
        plan,
        (hidden_0, hidden_1),
        sums_2,
        got_2,
        [(own, own), (beside, beside), second],
    )
    chunks, last_chunk = finish(
        owned, 3, plan, sums_3, got_3, last, total, kept_down, lent_down
    )

    def joined(sent, kept):
        return kept + across_chips(sent).astype(jnp.float32)

    first, second, third = [joined(*chunk).astype(jnp.bfloat16) for chunk in chunks]
    second = lax.optimization_barrier(second)
    inward = along(first, INWARD)
    middle = after(along(first, MIDDLE), flops=4 * 2**30)
    two_in = along(second, TWO_IN)
    passed = second.astype(jnp.float32) + inward.astype(jnp.float32)
    two_out = along(passed.astype(jnp.bfloat16), TWO_OUT)
    beside = along(third, BESIDE)
    total = lax.optimization_barrier(two_in.astype(jnp.float32) + two_out.astype(jnp.float32))
    total = lax.optimization_barrier(total + middle.astype(jnp.float32))
    own_sum = joined(*last_chunk(second))
    return (total + own_sum + beside.astype(jnp.float32)).astype(jnp.bfloat16)


def on_device(*args):
    block_list = args[5]
    sizes = (lax.axis_size("blk"), lax.axis_size("tp"), block_list.shape[1])
    if sizes == (4, 4, 4):
        return rows_travel(*args)
    return weights_travel(*args)


def solution(mesh):
    return jax.shard_map(
        on_device,
        mesh=mesh,
        in_specs=(
            P(("groups", "blk"), "tp"),
            P("blk", None, "tp"),
            P("blk", None, "tp"),
            P("blk", "tp", None),
            P(("groups", "blk"), None),
            P(("groups", "blk"), None, None),
            P(("groups", "blk"), None),
            P(("groups", "blk")),
        ),
        out_specs=P(("groups", "blk"), "tp"),
        check_vma=False,
    )
```

```python
import jax
import jax.numpy as jnp
from jax import lax
from jax.experimental import pallas as pl
from jax.experimental.pallas import tpu as pltpu
from jax.sharding import PartitionSpec as P


def shifted(block, axis, distance):
    devices = range(lax.axis_size(axis))
    route = [((i - distance) % len(devices), i) for i in devices]
    return lax.ppermute(block, axis, route)


def weights_travel(
    tokens, gate_weight, up_weight, down_weight, route_gates, block_list, block_count, owner_token
):
    whole_rows = lax.all_gather(tokens, "tp", axis=1, tiled=True)
    row_count = whole_rows.shape[0]
    width = whole_rows.shape[1]
    offsets_all = block_list.shape[1]
    block_total = block_list.shape[2]
    block_size = row_count // block_total
    blocks = whole_rows.reshape(block_total, block_size, width)
    gate_blocks = route_gates.reshape(block_total, block_size, offsets_all)
    totals = jnp.zeros((block_total, block_size, width), jnp.float32)

    def apply(totals, weights, offset, block_id):
        w_gate, w_up, w_down = weights
        block_rows = lax.dynamic_index_in_dim(blocks, block_id, 0, keepdims=False)
        gate_out = jnp.dot(block_rows, w_gate, preferred_element_type=jnp.float32)
        up_out = jnp.dot(block_rows, w_up, preferred_element_type=jnp.float32)
        hidden = (jax.nn.silu(gate_out) * up_out).astype(jnp.bfloat16)
        block_gates = lax.dynamic_index_in_dim(gate_blocks, block_id, 0, keepdims=False)
        factor = lax.dynamic_index_in_dim(block_gates, offset, 1, keepdims=False)
        product = jnp.dot(hidden, w_down, preferred_element_type=jnp.float32) * factor[:, None]
        before = lax.dynamic_index_in_dim(totals, block_id, 0, keepdims=False)
        return lax.dynamic_update_index_in_dim(totals, before + product, block_id, 0)

    resident = (gate_weight[0], up_weight[0], down_weight[0])
    arrived = [resident]
    holding = resident
    for offset in range(1, offsets_all):
        holding = shifted((holding[0], holding[1], holding[2]), "blk", 1)
        arrived.append(holding)
    for offset in range(offsets_all):
        weights = arrived[offset]

        def visit_block(position, totals, weights=weights, offset=offset):
            return apply(totals, weights, offset, block_list[0, offset, position])

        totals = lax.fori_loop(0, block_count[0, offset], visit_block, totals)
    summed = lax.psum_scatter(
        totals.reshape(row_count, width).astype(jnp.bfloat16), "tp", scatter_dimension=1, tiled=True
    )
    feature_share = summed.shape[1]
    cycle_size = lax.axis_size("blk")
    owned = row_count // 2
    capacity = max(2, 2 * row_count // cycle_size)
    target = owner_token // owned
    local_token = owner_token % owned
    target_table = (target[:, None] == jnp.arange(cycle_size, dtype=jnp.int32)[None, :]).astype(
        jnp.int32
    )
    running = jnp.cumsum(target_table, axis=0)
    rank = jnp.sum((running - 1) * target_table, axis=1)
    slot = target * capacity + rank
    send_rows = jnp.zeros((cycle_size * capacity, feature_share), jnp.bfloat16).at[slot].set(summed)
    send_index = jnp.full((cycle_size * capacity,), -1, jnp.int32).at[slot].set(local_token)
    send_rows = send_rows.reshape(cycle_size, capacity, feature_share)
    send_index = send_index.reshape(cycle_size, capacity)
    got_rows, got_index = (
        lax.all_to_all(send_rows, "blk", split_axis=0, concat_axis=0, tiled=True),
        lax.all_to_all(send_index, "blk", split_axis=0, concat_axis=0, tiled=True),
    )
    got_rows = got_rows.reshape(cycle_size * capacity, feature_share)
    got_index = got_index.reshape(cycle_size * capacity)
    placing = (got_index[:, None] == jnp.arange(owned, dtype=jnp.int32)[None, :]).astype(
        jnp.bfloat16
    )
    combined = lax.dot_general(
        placing, got_rows, (((0,), (0,)), ((), ())), preferred_element_type=jnp.float32
    )
    return combined.astype(jnp.bfloat16)


BESIDE = [(0, 1), (1, 0), (2, 3), (3, 2)]
MIDDLE = [(1, 2), (2, 1)]
INWARD = [(0, 1), (3, 2)]
OUTWARD = [(1, 0), (2, 3)]
TWO_IN = [(0, 2), (3, 1)]
TWO_OUT = [(1, 3), (2, 0)]
PLAN = [
    [3, 2, 1, 0, 0, 1, 2, 3, 0],
    [2, 3, 0, 1, 0, 3, 1, 2, 1],
    [1, 0, 3, 2, 0, 1, 3, 2, 1],
    [0, 1, 2, 3, 0, 3, 2, 1, 0],
]
OFFSETS_AT, INNER_AT = 4, 8
FACT_ROWS = 16
VMEM = pl.BlockSpec(memory_space=pltpu.VMEM)
SMEM = pl.BlockSpec(memory_space=pltpu.SMEM)
ANYWHERE = pl.BlockSpec(memory_space=pl.ANY)


def across_chips(block):
    return lax.ppermute(block, "tp", [(i, i ^ 2) for i in range(4)])


def across_cores(block):
    return lax.ppermute(block, "tp", [(i, i ^ 1) for i in range(4)])


def along(block, route):
    return lax.ppermute(block, "blk", route)


def cheap():
    return pl.CostEstimate(flops=1024, bytes_accessed=1024, transcendentals=0)


TOKEN = jax.ShapeDtypeStruct((8, 128), jnp.float32)
VMEM_LIMIT = 18 * 2**20


def on_core(body, out_shape, in_specs, scratch=()):
    return pl.pallas_call(
        body,
        out_shape=out_shape,
        in_specs=in_specs,
        out_specs=jax.tree.map(lambda _: VMEM, out_shape),
        scratch_shapes=scratch,
        compiler_params=pltpu.CompilerParams(vmem_limit_bytes=VMEM_LIMIT),
        cost_estimate=cheap(),
    )


def copies(source, start, target, size, pieces, sems, first):
    step = size // pieces
    return [
        pltpu.make_async_copy(
            source.at[pl.ds(start + index * step, step)],
            target.at[pl.ds(index * step, step)],
            sems.at[first + index],
        )
        for index in range(pieces)
    ]


def after(block, *others, flops=1024):
    return pl.pallas_call(
        lambda *refs: None,
        out_shape=jax.ShapeDtypeStruct(block.shape, block.dtype),
        in_specs=[ANYWHERE] * (1 + len(others)),
        out_specs=ANYWHERE,
        input_output_aliases={0: 0},
        cost_estimate=pl.CostEstimate(flops=flops, bytes_accessed=1024, transcendentals=0),
    )(block, *others)


def by_kind(plan_ref, kinds, run):
    if kinds[0] is kinds[1]:
        run(kinds[0])
        return
    for kind, value in zip(kinds, (1, 0)):

        @pl.when(plan_ref[INNER_AT] == value)
        def _(kind=kind):
            run(kind)


def part_of(plan, if_inner, if_outer, start, size, *others, flops=1024):
    shape = jax.ShapeDtypeStruct((size, if_inner.shape[1]), if_inner.dtype)
    pieces = 4

    def body(plan_ref, inner_ref, outer_ref, *rest):
        out_ref, buffer, in_sems, out_sems = rest[len(others) :]

        def run(source):
            inward = copies(source, start, buffer, size, pieces, in_sems, 0)
            outward = copies(buffer, 0, out_ref, size, pieces, out_sems, 0)
            for copy in inward:
                copy.start()
            for copy, next_copy in zip(inward, outward):
                copy.wait()
                next_copy.start()
            for copy in outward:
                copy.wait()

        by_kind(plan_ref, (inner_ref, inner_ref if if_outer is if_inner else outer_ref), run)

    return pl.pallas_call(
        body,
        out_shape=shape,
        in_specs=[SMEM] + [ANYWHERE] * (2 + len(others)),
        out_specs=ANYWHERE,
        scratch_shapes=[pltpu.VMEM(shape.shape, shape.dtype)]
        + [pltpu.SemaphoreType.DMA((pieces,))] * 2,
        compiler_params=pltpu.CompilerParams(vmem_limit_bytes=VMEM_LIMIT),
        cost_estimate=pl.CostEstimate(flops=flops, bytes_accessed=1024, transcendentals=0),
    )(plan, if_inner, if_outer, *others)


def with_facts(rows, gates, block_list, block_count, owner):
    count, width = rows.shape
    blocks, _, offsets = block_list.shape
    total = owner.shape[0]

    def body(rows_ref, gates_ref, list_ref, count_ref, owner_ref, out_ref, sems):
        moves = copies(rows_ref, 0, out_ref, count, 4, sems, 0)
        for copy in moves:
            copy.start()
        block_of = lax.broadcasted_iota(jnp.int32, (1, total), 1) // (total // blocks)
        facts = []
        for offset in range(offsets):
            mask = jnp.zeros((1, total), jnp.float32)
            for block in range(blocks):
                used = jnp.int32(0)
                for place in range(blocks):
                    found = (list_ref[place, 0, offset] == block) & (place < count_ref[0, offset])
                    used = used | found.astype(jnp.int32)
                mask = mask + jnp.where(block_of == block, used.astype(jnp.float32), 0.0)
            facts.append(gates_ref[offset : offset + 1, :] * mask)
        numbers = owner_ref[...].reshape(1, total)
        facts.append((numbers >> 8).astype(jnp.float32))
        facts.append((numbers & 255).astype(jnp.float32))
        facts.append(jnp.zeros((FACT_ROWS - len(facts), total), jnp.float32))
        out_ref[count:, :] = jnp.zeros((FACT_ROWS, width), jnp.bfloat16)
        out_ref[count:, :total] = jnp.concatenate(facts, axis=0).astype(jnp.bfloat16)
        for copy in moves:
            copy.wait()

    shape = jax.ShapeDtypeStruct((count + FACT_ROWS, width), rows.dtype)
    return on_core(
        body, shape, [ANYWHERE, VMEM, SMEM, SMEM, VMEM], [pltpu.SemaphoreType.DMA((4,))]
    )(rows, gates, block_list, block_count, owner)


def partial_sums(plan, sizes, parts, weights, places, before=None, send=True, waits=()):
    width, columns = weights[0].shape
    blocks = [
        block if isinstance(block, tuple) else (block,) for part in parts for block in part
    ]
    sources = [array for block in blocks for array in block]
    operands = [plan] + sources + [weights[place] for place in places] + [weights[2]]
    if before is not None:
        operands.append(before)
    specs = [SMEM] + [VMEM] * (len(operands) - 1 + len(waits))
    has_before = before is not None

    def body(plan_ref, *refs):
        source_refs, refs = refs[: len(sources)], refs[len(sources) :]
        weight_refs, refs = refs[: len(places) + 1], refs[len(places) + 1 :]
        before_ref, refs = (refs[0], refs[1:]) if has_before else (None, refs)
        results = refs[len(waits) :]
        start, source = 0, 0
        for part, size in enumerate(sizes):
            span = slice(start, start + size)
            start += size
            rows = []
            for index in range(len(places)):
                block = blocks[part * len(places) + index]
                value = source_refs[source][:size, :]
                if len(block) > 1:
                    other = source_refs[source + 1][:size, :]
                    value = jnp.where(plan_ref[INNER_AT] == 1, value, other)
                source += len(block)
                rows.append(value)
            for side in range(2):
                at = slice(side * columns, (side + 1) * columns)
                total = before_ref[span, at] if has_before else None
                for index, place in enumerate(places):
                    if side == 0:
                        weight = weight_refs[index][...]
                    else:
                        weight = weight_refs[-1][place * width : (place + 1) * width, :]
                    product = jnp.dot(rows[index], weight, preferred_element_type=jnp.float32)
                    total = product if total is None else total + product
                results[0][span, at] = total
                if send:
                    results[1][span, at] = total.astype(jnp.bfloat16)
        results[-1][...] = jnp.zeros(TOKEN.shape, TOKEN.dtype)

    shapes = [jax.ShapeDtypeStruct((sum(sizes), 2 * columns), jnp.float32)]
    if send:
        shapes.append(jax.ShapeDtypeStruct((sum(sizes), 2 * columns), jnp.bfloat16))
    return on_core(body, shapes + [TOKEN], specs)(*operands, *waits)


def hidden_rows(sums, got):
    units = sums.shape[1] // 4
    hidden = []
    for core in range(2):
        here, there = 2 * core * units, 2 * (1 - core) * units
        gate = sums[:, here : here + units] + got[:, there : there + units].astype(jnp.float32)
        up = sums[:, here + units : here + 2 * units]
        up = up + got[:, there + units : there + 2 * units].astype(jnp.float32)
        hidden.append((gate / (1.0 + jnp.exp(-gate)) * up).astype(jnp.bfloat16))
    return jnp.concatenate(hidden, axis=1)


def hide(sums, got):
    def body(sums_ref, got_ref, out_ref, token_ref):
        out_ref[...] = hidden_rows(sums_ref, got_ref)
        token_ref[...] = jnp.zeros(TOKEN.shape, TOKEN.dtype)

    shape = jax.ShapeDtypeStruct((sums.shape[0], sums.shape[1] // 2), jnp.bfloat16)
    return on_core(body, [shape, TOKEN], [VMEM, VMEM])(sums, got)


def factors_of(slot, plan, facts, rows):
    values = facts[:, :rows].astype(jnp.float32)
    kind = lax.broadcasted_iota(jnp.int32, (FACT_ROWS, 1), 0)
    mine = kind == plan[OFFSETS_AT + slot]
    factor = jnp.sum(jnp.where(mine, values, 0.0), axis=0, keepdims=True)
    return factor, values[4:5, :] * 256.0 + values[5:6, :]


def chunk_rows(owned, index, plan, factor, owner, hidden):
    first = (plan[index] * owned).astype(jnp.float32)
    token = first + lax.broadcasted_iota(jnp.int32, (owned, 1), 0).astype(jnp.float32)
    placing = jnp.where(owner == token, factor, 0.0).astype(jnp.bfloat16)
    return jnp.dot(placing, hidden, preferred_element_type=jnp.float32)


def facts_of(plan_ref, inner_ref, outer_ref, buffer, sem):
    last = inner_ref.shape[0] - FACT_ROWS

    def run(source):
        (copy,) = copies(source, last, buffer, FACT_ROWS, 1, sem, 0)
        copy.start()
        copy.wait()

    by_kind(plan_ref, (inner_ref, outer_ref), run)
    return buffer


def down(held, own_ref, lent_ref, sent_ref, kept_ref):
    units, width = own_ref.shape[0], kept_ref.shape[1]
    for out, at in ((kept_ref, slice(0, width)), (sent_ref, slice(width, 2 * width))):
        result = jnp.dot(held[:, :units], own_ref[:, at], preferred_element_type=jnp.float32)
        result += jnp.dot(held[:, units:], lent_ref[:, at], preferred_element_type=jnp.float32)
        out[...] = result.astype(out.dtype)


def fact_scratch(width):
    return [pltpu.VMEM((FACT_ROWS, width), jnp.bfloat16), pltpu.SemaphoreType.DMA((1,))]


def collect(owned, plan, hidden, sums, got, facts):
    rows, units = hidden[0].shape
    slots = len(facts)

    def body(plan_ref, *refs):
        hidden_refs, refs = refs[: slots - 1], refs[slots - 1 :]
        sums_ref, got_ref, refs = refs[0], refs[1], refs[2:]
        fact_refs, (out_ref, buffer, sem) = refs[: 2 * slots], refs[2 * slots :]
        factors = []
        for slot in range(slots):
            facts_of(plan_ref, *fact_refs[2 * slot : 2 * slot + 2], buffer, sem)
            factors.append(factors_of(slot, plan_ref, buffer, rows))
        factor = jnp.concatenate([pair[0] for pair in factors], axis=1)
        owner = jnp.concatenate([pair[1] for pair in factors], axis=1)
        every = [ref[...] for ref in hidden_refs] + [hidden_rows(sums_ref, got_ref)]
        every = jnp.concatenate(every, axis=0)
        for index in range(4):
            span = slice(index * owned, (index + 1) * owned)
            out_ref[span, :] = chunk_rows(owned, index, plan_ref, factor, owner, every)

    fact_blocks = [block for pair_of in facts for block in pair_of]
    specs = [SMEM] + [VMEM] * (slots + 1) + [ANYWHERE] * len(fact_blocks)
    shape = jax.ShapeDtypeStruct((4 * owned, units), jnp.float32)
    return on_core(body, shape, specs, fact_scratch(facts[0][0].shape[1]))(
        plan, *hidden, sums, got, *fact_blocks
    )


def finish(owned, slot, plan, sums, got, facts, before, down_own, down_lent):
    units = down_own.shape[0]
    width = down_own.shape[1] // 2
    pair = [
        jax.ShapeDtypeStruct((owned, width), jnp.bfloat16),
        jax.ShapeDtypeStruct((owned, width), jnp.float32),
    ]

    def first(plan_ref, sums_ref, got_ref, inner_ref, outer_ref, before_ref, *refs):
        own_ref, lent_ref, sent_ref, kept_ref, held_ref, buffer, sem = refs
        facts_of(plan_ref, inner_ref, outer_ref, buffer, sem)
        factor, owner = factors_of(slot, plan_ref, buffer, sums_ref.shape[0])
        hidden = hidden_rows(sums_ref, got_ref)
        for index in range(4):
            rows = chunk_rows(owned, index, plan_ref, factor, owner, hidden)
            rows = rows + before_ref[index * owned : (index + 1) * owned, :]
            held = rows.astype(jnp.bfloat16)
            if index == 0:
                down(held, own_ref, lent_ref, sent_ref, kept_ref)
            else:
                held_ref[(index - 1) * owned : index * owned, :] = held

    def others(indices, *waits):
        def body(held_ref, own_ref, lent_ref, *refs):
            out_refs = refs[len(waits) :]
            for place, index in enumerate(indices):
                held = held_ref[(index - 1) * owned : index * owned, :]
                down(held, own_ref, lent_ref, out_refs[2 * place], out_refs[2 * place + 1])

        operands = [held, down_own, down_lent, *waits]
        return on_core(body, pair * len(indices), [VMEM] * len(operands))(*operands)

    held_shape = jax.ShapeDtypeStruct((3 * owned, 2 * units), jnp.bfloat16)
    specs = [SMEM, VMEM, VMEM, ANYWHERE, ANYWHERE] + [VMEM] * 3
    sent, kept, held = on_core(
        first, pair + [held_shape], specs, fact_scratch(facts[0].shape[1])
    )(plan, sums, got, *facts, before, down_own, down_lent)
    return (sent, kept), lambda index, *waits: others([index], *waits)


def rows_travel(
    tokens, gate_weight, up_weight, down_weight, route_gates, block_list, block_count, owner_token
):
    position = lax.axis_index("blk")
    share = lax.axis_index("tp")
    row_count, width = tokens.shape
    units = gate_weight.shape[2]
    owned = row_count // 2
    half = row_count // 2
    plan = jnp.asarray(PLAN, jnp.int32)[position]

    own_far = across_chips(tokens)
    own = with_facts(
        tokens, route_gates.T, jnp.transpose(block_list, (2, 0, 1)), block_count, owner_token
    )
    beside = along(own, BESIDE)
    middle = along(own, MIDDLE)

    gate_quarters = gate_weight[0].reshape(4, width, units)
    up_quarters = up_weight[0].reshape(4, width, units)

    def quarter(j):
        pair = [
            lax.dynamic_index_in_dim(q, share ^ j, 0, keepdims=False)
            for q in (gate_quarters, up_quarters)
        ]
        return jnp.concatenate(pair, axis=1)

    def down_part(j):
        return lax.dynamic_slice_in_dim(down_weight[0], (share ^ j) * width, width, 1)

    kept_down = jnp.concatenate([down_part(0), down_part(2)], axis=1)
    lend_down = jnp.concatenate([down_part(1), down_part(3)], axis=1)


    def at_kind(block, positions):
        pairs = [(4 * p + i, 4 * p + (i ^ 2)) for p in positions for i in range(4)]
        return lax.ppermute(block, ("blk", "tp"), pairs)

    inner_last = along(beside, MIDDLE)
    outer_next = along(middle, OUTWARD)
    beside_far = across_chips(beside)
    own_far_half = part_of(plan, own_far, own_far, half, half, flops=16 * 2**30)
    inward_far = along(own_far_half, INWARD)
    lend = jnp.concatenate([quarter(1), quarter(3)])
    lent = across_cores(after(lend, own))
    weights = [quarter(0), quarter(2), lent]
    whole = [row_count]
    sums_0, send_0, ready_0 = partial_sums(
        plan, whole, [(tokens, own_far)], weights, (0, 1), waits=[lend_down]
    )
    got_0 = across_cores(send_0)
    lent_down = across_cores(lend_down)

    outer_last = along(inner_last, OUTWARD)
    outer_next = after(outer_next, beside_far, inner_last, inward_far, ready_0)
    second = (middle, outer_next)
    second_far = (at_kind(middle, (1, 2)), at_kind(outer_next, (0, 3)))
    middle_far = along(inward_far, MIDDLE)
    sums_1, send_1, ready_1 = partial_sums(
        plan, whole, [(beside, beside_far)], weights, (0, 1)
    )
    got_1 = across_cores(send_1)

    last = (inner_last, outer_last)
    last_far_a = across_chips(
        part_of(plan, *last, 0, half, *second_far, middle_far, ready_0, ready_1)
    )
    outward_far = along(middle_far, OUTWARD)
    hidden_0, hidden_here = hide(sums_0, got_0)
    hidden_1, hidden_there = hide(sums_1, got_1)
    sums_2, send_2, _ = partial_sums(plan, whole, [(second, second_far)], weights, (0, 1))
    got_2 = across_cores(send_2)
    near, _ = partial_sums(plan, whole, [(last,)], weights, (0,), send=False)
    sums_3, send_3, _ = partial_sums(
        plan,
        [half, half],
        [(last_far_a,), ((middle_far, outward_far),)],
        weights,
        (1,),
        before=near,
        waits=[hidden_here, hidden_there],
    )
    got_3 = across_cores(send_3)
    total = collect(
        owned,
        plan,
        (hidden_0, hidden_1),
        sums_2,
        got_2,
        [(own, own), (beside, beside), second],
    )
    first_chunk, chunk = finish(
        owned, 3, plan, sums_3, got_3, last, total, kept_down, lent_down
    )

    def joined(sent, kept):
        return kept + across_chips(sent).astype(jnp.float32)

    first = joined(*first_chunk).astype(jnp.bfloat16)
    second = lax.optimization_barrier(joined(*chunk(1)).astype(jnp.bfloat16))
    third = joined(*chunk(2, first)).astype(jnp.bfloat16)
    inward = along(first, INWARD)
    middle = after(along(first, MIDDLE), flops=2 * 2**30)
    two_in = along(second, TWO_IN)
    passed = second.astype(jnp.float32) + inward.astype(jnp.float32)
    two_out = along(passed.astype(jnp.bfloat16), TWO_OUT)
    beside = along(third, BESIDE)
    total = lax.optimization_barrier(two_in.astype(jnp.float32) + two_out.astype(jnp.float32))
    total = lax.optimization_barrier(total + middle.astype(jnp.float32))
    own_sum = joined(*chunk(3, second))
    return (total + own_sum + beside.astype(jnp.float32)).astype(jnp.bfloat16)


def on_device(*args):
    block_list = args[5]
    sizes = (lax.axis_size("blk"), lax.axis_size("tp"), block_list.shape[1])
    if sizes == (4, 4, 4):
        return rows_travel(*args)
    return weights_travel(*args)


def solution(mesh):
    return jax.shard_map(
        on_device,
        mesh=mesh,
        in_specs=(
            P(("groups", "blk"), "tp"),
            P("blk", None, "tp"),
            P("blk", None, "tp"),
            P("blk", "tp", None),
            P(("groups", "blk"), None),
            P(("groups", "blk"), None, None),
            P(("groups", "blk"), None),
            P(("groups", "blk")),
        ),
        out_specs=P(("groups", "blk"), "tp"),
        check_vma=False,
    )
```

```python
import jax
import jax.numpy as jnp
from jax import lax
from jax.experimental import pallas as pl
from jax.experimental.pallas import tpu as pltpu
from jax.sharding import PartitionSpec as P


def shifted(block, axis, distance):
    devices = range(lax.axis_size(axis))
    route = [((i - distance) % len(devices), i) for i in devices]
    return lax.ppermute(block, axis, route)


def weights_travel(
    tokens, gate_weight, up_weight, down_weight, route_gates, block_list, block_count, owner_token
):
    whole_rows = lax.all_gather(tokens, "tp", axis=1, tiled=True)
    row_count = whole_rows.shape[0]
    width = whole_rows.shape[1]
    offsets_all = block_list.shape[1]
    block_total = block_list.shape[2]
    block_size = row_count // block_total
    blocks = whole_rows.reshape(block_total, block_size, width)
    gate_blocks = route_gates.reshape(block_total, block_size, offsets_all)
    totals = jnp.zeros((block_total, block_size, width), jnp.float32)

    def apply(totals, weights, offset, block_id):
        w_gate, w_up, w_down = weights
        block_rows = lax.dynamic_index_in_dim(blocks, block_id, 0, keepdims=False)
        gate_out = jnp.dot(block_rows, w_gate, preferred_element_type=jnp.float32)
        up_out = jnp.dot(block_rows, w_up, preferred_element_type=jnp.float32)
        hidden = (jax.nn.silu(gate_out) * up_out).astype(jnp.bfloat16)
        block_gates = lax.dynamic_index_in_dim(gate_blocks, block_id, 0, keepdims=False)
        factor = lax.dynamic_index_in_dim(block_gates, offset, 1, keepdims=False)
        product = jnp.dot(hidden, w_down, preferred_element_type=jnp.float32) * factor[:, None]
        before = lax.dynamic_index_in_dim(totals, block_id, 0, keepdims=False)
        return lax.dynamic_update_index_in_dim(totals, before + product, block_id, 0)

    resident = (gate_weight[0], up_weight[0], down_weight[0])
    arrived = [resident]
    holding = resident
    for offset in range(1, offsets_all):
        holding = shifted((holding[0], holding[1], holding[2]), "blk", 1)
        arrived.append(holding)
    for offset in range(offsets_all):
        weights = arrived[offset]

        def visit_block(position, totals, weights=weights, offset=offset):
            return apply(totals, weights, offset, block_list[0, offset, position])

        totals = lax.fori_loop(0, block_count[0, offset], visit_block, totals)
    summed = lax.psum_scatter(
        totals.reshape(row_count, width).astype(jnp.bfloat16), "tp", scatter_dimension=1, tiled=True
    )
    feature_share = summed.shape[1]
    cycle_size = lax.axis_size("blk")
    owned = row_count // 2
    capacity = max(2, 2 * row_count // cycle_size)
    target = owner_token // owned
    local_token = owner_token % owned
    target_table = (target[:, None] == jnp.arange(cycle_size, dtype=jnp.int32)[None, :]).astype(
        jnp.int32
    )
    running = jnp.cumsum(target_table, axis=0)
    rank = jnp.sum((running - 1) * target_table, axis=1)
    slot = target * capacity + rank
    send_rows = jnp.zeros((cycle_size * capacity, feature_share), jnp.bfloat16).at[slot].set(summed)
    send_index = jnp.full((cycle_size * capacity,), -1, jnp.int32).at[slot].set(local_token)
    send_rows = send_rows.reshape(cycle_size, capacity, feature_share)
    send_index = send_index.reshape(cycle_size, capacity)
    got_rows, got_index = (
        lax.all_to_all(send_rows, "blk", split_axis=0, concat_axis=0, tiled=True),
        lax.all_to_all(send_index, "blk", split_axis=0, concat_axis=0, tiled=True),
    )
    got_rows = got_rows.reshape(cycle_size * capacity, feature_share)
    got_index = got_index.reshape(cycle_size * capacity)
    placing = (got_index[:, None] == jnp.arange(owned, dtype=jnp.int32)[None, :]).astype(
        jnp.bfloat16
    )
    combined = lax.dot_general(
        placing, got_rows, (((0,), (0,)), ((), ())), preferred_element_type=jnp.float32
    )
    return combined.astype(jnp.bfloat16)


BESIDE = [(0, 1), (1, 0), (2, 3), (3, 2)]
MIDDLE = [(1, 2), (2, 1)]
INWARD = [(0, 1), (3, 2)]
OUTWARD = [(1, 0), (2, 3)]
TWO_IN = [(0, 2), (3, 1)]
TWO_OUT = [(1, 3), (2, 0)]
PLAN = [
    [3, 2, 1, 0, 0, 1, 2, 3, 0],
    [2, 3, 0, 1, 0, 3, 1, 2, 1],
    [1, 0, 3, 2, 0, 1, 3, 2, 1],
    [0, 1, 2, 3, 0, 3, 2, 1, 0],
]
OFFSETS_AT, INNER_AT = 4, 8
FACT_ROWS = 16
VMEM = pl.BlockSpec(memory_space=pltpu.VMEM)
SMEM = pl.BlockSpec(memory_space=pltpu.SMEM)
ANYWHERE = pl.BlockSpec(memory_space=pl.ANY)


def across_chips(block):
    return lax.ppermute(block, "tp", [(i, i ^ 2) for i in range(4)])


def across_cores(block):
    return lax.ppermute(block, "tp", [(i, i ^ 1) for i in range(4)])


def along(block, route):
    return lax.ppermute(block, "blk", route)


def cheap():
    return pl.CostEstimate(flops=1024, bytes_accessed=1024, transcendentals=0)


TOKEN = jax.ShapeDtypeStruct((8, 128), jnp.float32)
VMEM_LIMIT = 18 * 2**20


def on_core(body, out_shape, in_specs, scratch=()):
    return pl.pallas_call(
        body,
        out_shape=out_shape,
        in_specs=in_specs,
        out_specs=jax.tree.map(lambda _: VMEM, out_shape),
        scratch_shapes=scratch,
        compiler_params=pltpu.CompilerParams(vmem_limit_bytes=VMEM_LIMIT),
        cost_estimate=cheap(),
    )


def copies(source, start, target, size, pieces, sems, first):
    step = size // pieces
    return [
        pltpu.make_async_copy(
            source.at[pl.ds(start + index * step, step)],
            target.at[pl.ds(index * step, step)],
            sems.at[first + index],
        )
        for index in range(pieces)
    ]


def after(block, *others, flops=1024):
    return pl.pallas_call(
        lambda *refs: None,
        out_shape=jax.ShapeDtypeStruct(block.shape, block.dtype),
        in_specs=[ANYWHERE] * (1 + len(others)),
        out_specs=ANYWHERE,
        input_output_aliases={0: 0},
        cost_estimate=pl.CostEstimate(flops=flops, bytes_accessed=1024, transcendentals=0),
    )(block, *others)


def by_kind(plan_ref, kinds, run):
    if kinds[0] is kinds[1]:
        run(kinds[0])
        return
    for kind, value in zip(kinds, (1, 0)):

        @pl.when(plan_ref[INNER_AT] == value)
        def _(kind=kind):
            run(kind)


def part_of(plan, if_inner, if_outer, start, size, *others, flops=1024):
    shape = jax.ShapeDtypeStruct((size, if_inner.shape[1]), if_inner.dtype)
    pieces = 4

    def body(plan_ref, inner_ref, outer_ref, *rest):
        out_ref, buffer, in_sems, out_sems = rest[len(others) :]

        def run(source):
            inward = copies(source, start, buffer, size, pieces, in_sems, 0)
            outward = copies(buffer, 0, out_ref, size, pieces, out_sems, 0)
            for copy in inward:
                copy.start()
            for copy, next_copy in zip(inward, outward):
                copy.wait()
                next_copy.start()
            for copy in outward:
                copy.wait()

        by_kind(plan_ref, (inner_ref, inner_ref if if_outer is if_inner else outer_ref), run)

    return pl.pallas_call(
        body,
        out_shape=shape,
        in_specs=[SMEM] + [ANYWHERE] * (2 + len(others)),
        out_specs=ANYWHERE,
        scratch_shapes=[pltpu.VMEM(shape.shape, shape.dtype)]
        + [pltpu.SemaphoreType.DMA((pieces,))] * 2,
        compiler_params=pltpu.CompilerParams(vmem_limit_bytes=VMEM_LIMIT),
        cost_estimate=pl.CostEstimate(flops=flops, bytes_accessed=1024, transcendentals=0),
    )(plan, if_inner, if_outer, *others)


def with_facts(rows, gates, block_list, block_count, owner):
    count, width = rows.shape
    blocks, _, offsets = block_list.shape
    total = owner.shape[0]

    def body(rows_ref, gates_ref, list_ref, count_ref, owner_ref, out_ref, sems):
        moves = copies(rows_ref, 0, out_ref, count, 4, sems, 0)
        for copy in moves:
            copy.start()
        block_of = lax.broadcasted_iota(jnp.int32, (1, total), 1) // (total // blocks)
        facts = []
        for offset in range(offsets):
            mask = jnp.zeros((1, total), jnp.float32)
            for block in range(blocks):
                used = jnp.int32(0)
                for place in range(blocks):
                    found = (list_ref[place, 0, offset] == block) & (place < count_ref[0, offset])
                    used = used | found.astype(jnp.int32)
                mask = mask + jnp.where(block_of == block, used.astype(jnp.float32), 0.0)
            facts.append(gates_ref[offset : offset + 1, :] * mask)
        numbers = owner_ref[...].reshape(1, total)
        facts.append((numbers >> 8).astype(jnp.float32))
        facts.append((numbers & 255).astype(jnp.float32))
        facts.append(jnp.zeros((FACT_ROWS - len(facts), total), jnp.float32))
        out_ref[count:, :] = jnp.zeros((FACT_ROWS, width), jnp.bfloat16)
        out_ref[count:, :total] = jnp.concatenate(facts, axis=0).astype(jnp.bfloat16)
        for copy in moves:
            copy.wait()

    shape = jax.ShapeDtypeStruct((count + FACT_ROWS, width), rows.dtype)
    return on_core(
        body, shape, [ANYWHERE, VMEM, SMEM, SMEM, VMEM], [pltpu.SemaphoreType.DMA((4,))]
    )(rows, gates, block_list, block_count, owner)


def partial_sums(plan, sizes, parts, weights, places, before=None, send=True, waits=()):
    width, columns = weights[0].shape
    blocks = [
        block if isinstance(block, tuple) else (block,) for part in parts for block in part
    ]
    sources = [array for block in blocks for array in block]
    operands = [plan] + sources + [weights[place] for place in places] + [weights[2]]
    if before is not None:
        operands.append(before)
    specs = [SMEM] + [VMEM] * (len(operands) - 1 + len(waits))
    has_before = before is not None

    def body(plan_ref, *refs):
        source_refs, refs = refs[: len(sources)], refs[len(sources) :]
        weight_refs, refs = refs[: len(places) + 1], refs[len(places) + 1 :]
        before_ref, refs = (refs[0], refs[1:]) if has_before else (None, refs)
        results = refs[len(waits) :]
        start, source = 0, 0
        for part, size in enumerate(sizes):
            span = slice(start, start + size)
            start += size
            rows = []
            for index in range(len(places)):
                block = blocks[part * len(places) + index]
                value = source_refs[source][:size, :]
                if len(block) > 1:
                    other = source_refs[source + 1][:size, :]
                    value = jnp.where(plan_ref[INNER_AT] == 1, value, other)
                source += len(block)
                rows.append(value)
            for side in range(2):
                at = slice(side * columns, (side + 1) * columns)
                total = before_ref[span, at] if has_before else None
                for index, place in enumerate(places):
                    if side == 0:
                        weight = weight_refs[index][...]
                    else:
                        weight = weight_refs[-1][place * width : (place + 1) * width, :]
                    product = jnp.dot(rows[index], weight, preferred_element_type=jnp.float32)
                    total = product if total is None else total + product
                results[0][span, at] = total
                if send:
                    results[1][span, at] = total.astype(jnp.bfloat16)
        results[-1][...] = jnp.zeros(TOKEN.shape, TOKEN.dtype)

    shapes = [jax.ShapeDtypeStruct((sum(sizes), 2 * columns), jnp.float32)]
    if send:
        shapes.append(jax.ShapeDtypeStruct((sum(sizes), 2 * columns), jnp.bfloat16))
    return on_core(body, shapes + [TOKEN], specs)(*operands, *waits)


def hidden_rows(sums, got):
    units = sums.shape[1] // 4
    hidden = []
    for core in range(2):
        here, there = 2 * core * units, 2 * (1 - core) * units
        gate = sums[:, here : here + units] + got[:, there : there + units].astype(jnp.float32)
        up = sums[:, here + units : here + 2 * units]
        up = up + got[:, there + units : there + 2 * units].astype(jnp.float32)
        hidden.append((gate / (1.0 + jnp.exp(-gate)) * up).astype(jnp.bfloat16))
    return jnp.concatenate(hidden, axis=1)


def hide(plan, sums, got, facts):
    shapes = [
        jax.ShapeDtypeStruct((sums.shape[0], sums.shape[1] // 2), jnp.bfloat16),
        jax.ShapeDtypeStruct((FACT_ROWS, facts.shape[1]), jnp.bfloat16),
        TOKEN,
    ]

    def body(plan_ref, sums_ref, got_ref, block_ref, out_ref, facts_ref, token_ref, sem):
        fetch = facts_of(plan_ref, block_ref, block_ref, facts_ref, sem)
        out_ref[...] = hidden_rows(sums_ref, got_ref)
        token_ref[...] = jnp.zeros(TOKEN.shape, TOKEN.dtype)
        fetch.wait()

    return on_core(
        body, shapes, [SMEM, VMEM, VMEM, ANYWHERE], [pltpu.SemaphoreType.DMA((1,))]
    )(plan, sums, got, facts)


def factors_of(slot, plan, facts, rows):
    values = facts[:, :rows].astype(jnp.float32)
    kind = lax.broadcasted_iota(jnp.int32, (FACT_ROWS, 1), 0)
    mine = kind == plan[OFFSETS_AT + slot]
    factor = jnp.sum(jnp.where(mine, values, 0.0), axis=0, keepdims=True)
    return factor, values[4:5, :] * 256.0 + values[5:6, :]


def chunk_rows(owned, index, plan, factor, owner, hidden):
    first = (plan[index] * owned).astype(jnp.float32)
    token = first + lax.broadcasted_iota(jnp.int32, (owned, 1), 0).astype(jnp.float32)
    placing = jnp.where(owner == token, factor, 0.0).astype(jnp.bfloat16)
    return jnp.dot(placing, hidden, preferred_element_type=jnp.float32)


def facts_of(plan_ref, inner_ref, outer_ref, buffer, sem):
    last = inner_ref.shape[0] - FACT_ROWS
    (fetch,) = copies(inner_ref, last, buffer, FACT_ROWS, 1, sem, 0)
    if inner_ref is outer_ref:
        fetch.start()
        return fetch
    (other,) = copies(outer_ref, last, buffer, FACT_ROWS, 1, sem, 0)
    by_kind(plan_ref, (fetch, other), lambda copy: copy.start())
    return fetch


def down(held, own_ref, lent_ref, sent_ref, kept_ref):
    units, width = own_ref.shape[0], kept_ref.shape[1]
    for out, at in ((kept_ref, slice(0, width)), (sent_ref, slice(width, 2 * width))):
        result = jnp.dot(held[:, :units], own_ref[:, at], preferred_element_type=jnp.float32)
        result += jnp.dot(held[:, units:], lent_ref[:, at], preferred_element_type=jnp.float32)
        out[...] = result.astype(out.dtype)


def collect(owned, plan, hidden, facts, sums, got, third, last):
    rows, units = hidden[0].shape
    width = facts[0].shape[1]

    def body(plan_ref, *refs):
        hidden_refs, fact_refs, refs = refs[:2], refs[2:4], refs[4:]
        sums_ref, got_ref, refs = refs[0], refs[1], refs[2:]
        third_refs, last_refs, refs = refs[:2], refs[2:4], refs[4:]
        out_ref, last_ref, buffer, sem, last_sem = refs
        fetch = facts_of(plan_ref, *third_refs, buffer, sem)
        fetch_last = facts_of(plan_ref, *last_refs, last_ref, last_sem)
        every = [ref[...] for ref in hidden_refs] + [hidden_rows(sums_ref, got_ref)]
        every = jnp.concatenate(every, axis=0)
        fetch.wait()
        factors = [
            factors_of(slot, plan_ref, ref, rows) for slot, ref in enumerate([*fact_refs, buffer])
        ]
        factor = jnp.concatenate([pair[0] for pair in factors], axis=1)
        owner = jnp.concatenate([pair[1] for pair in factors], axis=1)
        for index in range(4):
            span = slice(index * owned, (index + 1) * owned)
            out_ref[span, :] = chunk_rows(owned, index, plan_ref, factor, owner, every)
        fetch_last.wait()

    shapes = [
        jax.ShapeDtypeStruct((4 * owned, units), jnp.float32),
        jax.ShapeDtypeStruct((FACT_ROWS, width), jnp.bfloat16),
    ]
    scratch = [pltpu.VMEM((FACT_ROWS, width), jnp.bfloat16)]
    scratch += [pltpu.SemaphoreType.DMA((1,))] * 2
    return on_core(body, shapes, [SMEM] + [VMEM] * 6 + [ANYWHERE] * 4, scratch)(
        plan, *hidden, *facts, sums, got, *third, *last
    )


def finish(owned, slot, plan, sums, got, facts, before, down_own, down_lent):
    units = down_own.shape[0]
    width = down_own.shape[1] // 2
    pair = [
        jax.ShapeDtypeStruct((owned, width), jnp.bfloat16),
        jax.ShapeDtypeStruct((owned, width), jnp.float32),
    ]

    def first(plan_ref, sums_ref, got_ref, facts_ref, before_ref, *refs):
        own_ref, lent_ref, sent_ref, kept_ref, held_ref = refs
        factor, owner = factors_of(slot, plan_ref, facts_ref, sums_ref.shape[0])
        hidden = hidden_rows(sums_ref, got_ref)
        for index in range(4):
            rows = chunk_rows(owned, index, plan_ref, factor, owner, hidden)
            rows = rows + before_ref[index * owned : (index + 1) * owned, :]
            held = rows.astype(jnp.bfloat16)
            if index == 0:
                down(held, own_ref, lent_ref, sent_ref, kept_ref)
            else:
                held_ref[(index - 1) * owned : index * owned, :] = held

    def others(indices, *waits):
        def body(held_ref, own_ref, lent_ref, *refs):
            out_refs = refs[len(waits) :]
            for place, index in enumerate(indices):
                held = held_ref[(index - 1) * owned : index * owned, :]
                down(held, own_ref, lent_ref, out_refs[2 * place], out_refs[2 * place + 1])

        operands = [held, down_own, down_lent, *waits]
        return on_core(body, pair * len(indices), [VMEM] * len(operands))(*operands)

    held_shape = jax.ShapeDtypeStruct((3 * owned, 2 * units), jnp.bfloat16)
    sent, kept, held = on_core(first, pair + [held_shape], [SMEM] + [VMEM] * 6)(
        plan, sums, got, facts, before, down_own, down_lent
    )
    rest = others([1, 2])
    chunks = [(sent, kept), (rest[0], rest[1]), (rest[2], rest[3])]
    return chunks, lambda *waits: others([3], *waits)


def rows_travel(
    tokens, gate_weight, up_weight, down_weight, route_gates, block_list, block_count, owner_token
):
    position = lax.axis_index("blk")
    share = lax.axis_index("tp")
    row_count, width = tokens.shape
    units = gate_weight.shape[2]
    owned = row_count // 2
    half = row_count // 2
    plan = jnp.asarray(PLAN, jnp.int32)[position]

    own_far = across_chips(tokens)
    own = with_facts(
        tokens, route_gates.T, jnp.transpose(block_list, (2, 0, 1)), block_count, owner_token
    )
    beside = along(own, BESIDE)
    middle = along(own, MIDDLE)

    gate_quarters = gate_weight[0].reshape(4, width, units)
    up_quarters = up_weight[0].reshape(4, width, units)

    def quarter(j):
        pair = [
            lax.dynamic_index_in_dim(q, share ^ j, 0, keepdims=False)
            for q in (gate_quarters, up_quarters)
        ]
        return jnp.concatenate(pair, axis=1)

    def down_part(j):
        return lax.dynamic_slice_in_dim(down_weight[0], (share ^ j) * width, width, 1)

    kept_down = jnp.concatenate([down_part(0), down_part(2)], axis=1)
    lend_down = jnp.concatenate([down_part(1), down_part(3)], axis=1)


    def at_kind(block, positions):
        pairs = [(4 * p + i, 4 * p + (i ^ 2)) for p in positions for i in range(4)]
        return lax.ppermute(block, ("blk", "tp"), pairs)

    inner_last = along(beside, MIDDLE)
    outer_next = along(middle, OUTWARD)
    beside_far = across_chips(beside)
    own_far_half = part_of(plan, own_far, own_far, half, half, flops=16 * 2**30)
    inward_far = along(own_far_half, INWARD)
    lend = jnp.concatenate([quarter(1), quarter(3)])
    lent = across_cores(after(lend, own))
    weights = [quarter(0), quarter(2), lent]
    whole = [row_count]
    sums_0, send_0, ready_0 = partial_sums(
        plan, whole, [(tokens, own_far)], weights, (0, 1), waits=[lend_down]
    )
    got_0 = across_cores(send_0)
    lent_down = across_cores(lend_down)

    outer_last = along(inner_last, OUTWARD)
    outer_next = after(outer_next, beside_far, inner_last, inward_far, ready_0)
    second = (middle, outer_next)
    second_far = (at_kind(middle, (1, 2)), at_kind(outer_next, (0, 3)))
    middle_far = along(inward_far, MIDDLE)
    sums_1, send_1, ready_1 = partial_sums(
        plan, whole, [(beside, beside_far)], weights, (0, 1)
    )
    got_1 = across_cores(send_1)

    last = (inner_last, outer_last)
    last_far_a = across_chips(
        part_of(plan, *last, 0, half, *second_far, middle_far, ready_0, ready_1)
    )
    outward_far = along(middle_far, OUTWARD)
    hidden_0, facts_0, hidden_here = hide(plan, sums_0, got_0, own)
    hidden_1, facts_1, hidden_there = hide(plan, sums_1, got_1, beside)
    sums_2, send_2, _ = partial_sums(plan, whole, [(second, second_far)], weights, (0, 1))
    got_2 = across_cores(send_2)
    near, _ = partial_sums(plan, whole, [(last,)], weights, (0,), send=False)
    sums_3, send_3, _ = partial_sums(
        plan,
        [half, half],
        [(last_far_a,), ((middle_far, outward_far),)],
        weights,
        (1,),
        before=near,
        waits=[hidden_here, hidden_there],
    )
    got_3 = across_cores(send_3)
    hidden, facts = (hidden_0, hidden_1), (facts_0, facts_1)
    total, facts_3 = collect(owned, plan, hidden, facts, sums_2, got_2, second, last)
    chunks, last_chunk = finish(
        owned, 3, plan, sums_3, got_3, facts_3, total, kept_down, lent_down
    )

    def joined(sent, kept):
        return kept + across_chips(sent).astype(jnp.float32)

    first, second, third = [joined(*chunk).astype(jnp.bfloat16) for chunk in chunks]
    second = lax.optimization_barrier(second)
    inward = along(first, INWARD)
    middle = along(first, MIDDLE)
    two_in = along(second, TWO_IN)
    passed = second.astype(jnp.float32) + inward.astype(jnp.float32)
    two_out = along(passed.astype(jnp.bfloat16), TWO_OUT)
    beside = along(third, BESIDE)
    arrived = [block.astype(jnp.float32) for block in (middle, two_in, two_out)]
    total = lax.optimization_barrier(sum(arrived))
    own_sum = joined(*last_chunk(second))
    return (total + own_sum + beside.astype(jnp.float32)).astype(jnp.bfloat16)


def on_device(*args):
    block_list = args[5]
    sizes = (lax.axis_size("blk"), lax.axis_size("tp"), block_list.shape[1])
    if sizes == (4, 4, 4):
        return rows_travel(*args)
    return weights_travel(*args)


def solution(mesh):
    return jax.shard_map(
        on_device,
        mesh=mesh,
        in_specs=(
            P(("groups", "blk"), "tp"),
            P("blk", None, "tp"),
            P("blk", None, "tp"),
            P("blk", "tp", None),
            P(("groups", "blk"), None),
            P(("groups", "blk"), None, None),
            P(("groups", "blk"), None),
            P(("groups", "blk")),
        ),
        out_specs=P(("groups", "blk"), "tp"),
        check_vma=False,
    )
```
